32 devices in a mesh: parts: 2 (over y), ep: 4 (over x, core), tp: 4 (over z).
Axes of the slice: x: 2, y: 2, z: 4, core: 2. Of those that a mesh axis runs over, the one named last changes fastest.
Arguments:
- query_latent: bfloat16 [512, 32, 512], P(('parts', 'ep'), 'tp'), parts along dimension 0, may hold values from -63 to 63
- query_rope: bfloat16 [512, 2048], P(('parts', 'ep'), 'tp'), parts along dimension 0, may hold values from -5 to 5
- cache_latent: bfloat16 [512, 256, 512], P(('parts', 'ep')), parts along dimension 0, may hold values from -5 to 5
- cache_rope: bfloat16 [512, 64, 256], P(('parts', 'ep')), parts along dimension 0, may hold values from -4.5 to 4.5
- cache_length: int32 [512], P(('parts', 'ep')), parts along dimension 0, may hold values from 2 to 256, as said below
- value_up: bfloat16 [32, 512, 128], P('tp'), may hold values from -0.25 to 0.25
- output_weight: bfloat16 [4096, 7168], P('tp', 'ep'), may hold values from -0.1875 to 0.1875
- residual: bfloat16 [512, 7168], P('parts', 'ep'), parts along dimension 0, may hold values from -40 to 40
- norm_gain: float32 [7168], P('ep'), may hold values from 0.25 to 1.75
- routed_experts: int32 [512, 2], P('parts'), parts along dimension 0, may hold values from 0 to 3, all different within a row; in each aligned block of 64 rows (0 to 63, 64 to 127, ...) at most 64 rows name the same one
- expert_gates: float32 [512, 2], P('parts'), parts along dimension 0, may hold values from 0.2 to 1
- gate_weight: bfloat16 [4, 7168, 2048], P('ep', None, 'tp'), may hold values from -0.0625 to 0.0625
- up_weight: bfloat16 [4, 7168, 2048], P('ep', None, 'tp'), may hold values from -0.0625 to 0.0625
- down_weight: bfloat16 [4, 2048, 7168], P('ep', 'tp'), may hold values from -0.125 to 0.125
Outputs:
- stream_out: bfloat16 [512, 7168], P(('parts', 'tp'), 'ep'), parts along dimension 0
- expert_mix: bfloat16 [512, 7168], P(('parts', 'tp'), 'ep'), parts along dimension 0
The draws below stay inside these ranges and needn't reach their ends.
There are 2 independent parts, one for each index of `parts`. The reference program is written for one: setup_inputs(seed, part) draws one part's arguments, and reference() takes and returns one part's arrays. A program takes and returns all parts, laid end to end along the dimension named above; an argument that names none is the same for every part. Nothing has to cross between parts.
Inputs may be any that keep to these rules, and one draw needn't show every extreme that they name: Row r attends to cache positions 0 to cache_length[r] - 1; the first row of every group has all 256. `routed_experts`: each row names 2 different experts. Cut the rows into 4 aligned blocks of equal length: within one block no expert is named by more than 64 rows, and some expert reaches 64 in some block.
All inputs are finite; a program needn't handle non-finite values.
Results may differ from the reference program's by a relative error of at most 0.02.
Values may be sent and summed in bfloat16 or wider, within the bound.
No kernel may reach another device: no remote copies, remote signals or barrier semaphores. Data moves between devices by JAX's collectives and lax.ppermute only.
A program may use at most 128 MiB of HBM per device.

```python
import math
import jax
import jax.numpy as jnp
import numpy as np
from jax import lax

D = 7168
LATENT = 512
ROPE = 64
VHEAD = 128
FF = 2048
HEAD_DEV = 8
TOP = 2
LEN = 256
ROWS = 256
HEADS = 32
EXPERTS = 4
CAP = 64
N_TP = 4


def latent_base(key):
    return jnp.clip(jax.random.normal(key, (ROWS, LEN, LATENT), jnp.float32), -4.5, 4.5)


def draw_cache_latent(key, part):
    base = latent_base(key)
    return base.astype(jnp.bfloat16)


def draw_query_latent(key, part):
    key = jax.random.fold_in(key, 12)
    return jnp.clip(jax.random.normal(key, (ROWS, HEADS, LATENT), jnp.float32), -4.5, 4.5).astype(jnp.bfloat16)


def draw_query_rope(key, part):
    key = jax.random.fold_in(key, 13)
    return jnp.clip(jax.random.normal(key, (ROWS, HEADS * ROPE), jnp.float32), -4.5, 4.5).astype(jnp.bfloat16)


def draw_cache_length(key, part):
    key = jax.random.fold_in(key, 14)
    first_key, second_key = jax.random.split(key)
    first_part = jax.random.randint(first_key, (ROWS,), 0, LEN - 1)
    second_part = jax.random.randint(second_key, (ROWS,), 0, LEN - 1)
    lengths = 2 + first_part * second_part // max(LEN - 2, 1)
    lengths = jnp.minimum(lengths, LEN)
    return jnp.where(jnp.arange(ROWS) == 0, LEN, lengths).astype(jnp.int32)


def draw_residual(key, part):
    key = jax.random.fold_in(key, 15)
    row_key, column_key, value_key = jax.random.split(key, 3)
    row_scale = jnp.exp(jax.random.uniform(row_key, (ROWS,), jnp.float32, jnp.log(0.3), jnp.log(3.0)))
    ramp = 1.0 + 2.0 * jnp.arange(D, dtype=jnp.float32) / max(D - 1, 1)
    column_scale = jnp.exp(jax.random.uniform(column_key, (D,), jnp.float32, jnp.log(0.1), jnp.log(1.0))) * ramp
    values = jnp.clip(jax.random.normal(value_key, (ROWS, D), jnp.float32), -4.0, 4.0)
    return (values * row_scale[:, None] * column_scale[None, :]).astype(jnp.bfloat16)


def level_of(stream_key, shape, shards, least, high):
    level = 1.0
    for axis_at, parts in shards:
        draws = jax.random.uniform(jax.random.fold_in(jax.random.fold_in(stream_key, 6), axis_at), (parts,), jnp.float32, least / len(shards), high / len(shards))
        level = level * jnp.repeat(jnp.exp(draws), shape[axis_at] // parts).reshape((-1,) + (1,) * (len(shape) - 1 - axis_at))
    return level


def shared_out(key, own, number, rows, count, top, bound, skew):
    sequence = jax.random.permutation(key, count)
    heavy_load, usual = portions_of(count, rows * top, bound, skew, True), portions_of(count, rows * top, bound, skew, False)
    places = jnp.arange(count)

    def named(sizes, rotation):
        used = int((sizes > 0).sum())
        fixed = max(1, used // 4)
        moved = fixed + (places - fixed + rotation * (used - fixed)) % max(1, count - fixed)
        return jnp.zeros((count,), jnp.int32).at[sequence[jnp.where(places < fixed, places, moved)]].set(jnp.asarray(sizes, jnp.int32))

    sizes = jnp.where(number % 4 == 0, named(heavy_load, number // 4), named(usual, number - number // 4 - 1))
    mixed = jax.random.permutation(jax.random.fold_in(own, 3), count)
    giver, taker = mixed[0:count // 2 * 2:2], mixed[1:count // 2 * 2:2]
    room = jnp.minimum(sizes[giver] - 1, bound - sizes[taker]) // 2
    room = jnp.where((giver == sequence[0]) | (taker == sequence[0]) | (sizes[taker] == 0), 0, jnp.maximum(room, 0))
    moved = jax.random.randint(jax.random.fold_in(own, 4), (count // 2,), 0, 1 << 20) % (room + 1)
    sizes = sizes.at[giver].add(-moved).at[taker].add(moved)
    members = jnp.searchsorted(jnp.cumsum(sizes), jnp.arange(rows * top), side="right").astype(jnp.int32)
    listing = members.reshape(top, rows).T
    listing = listing[jax.random.permutation(jax.random.fold_in(own, 1), rows)]
    rotation = jax.random.randint(jax.random.fold_in(own, 2), (rows, 1), 0, top)
    return jnp.take_along_axis(listing, (jnp.arange(top)[None, :] + rotation) % top, axis=1)


def portions_of(amount, total, bound, lean, full):
    loads = [(1 << 20) // math.isqrt(rank ** lean) + 1 for rank in range(1, amount + 1)]
    largest = bound if full else min(bound, max(-(-total // amount), total * loads[0] // sum(loads)))
    least = 1 if total - largest >= amount - 1 else 0
    given, spare = [largest] + [least] * (amount - 1), total - largest - least * (amount - 1)
    while spare > 0:
        free = [i for i in range(1, amount) if given[i] < largest] or [i for i in range(1, amount) if given[i] < bound]
        mass, remaining = sum([loads[i] for i in free]), spare
        for i in free:
            extra = min(bound - given[i], max(1, remaining * loads[i] // mass), spare)
            given[i] = given[i] + extra
            spare = spare - extra
    return np.array(given)


def normal_values(own_key, extent, scale, most, shards=(), held_as=jnp.bfloat16):
    drawn = jax.random.normal(own_key, extent, jnp.float32) * scale
    if len(shards) > 0:
        drawn = level_of(own_key, extent, shards, -0.22, 0.18) * drawn
    return jnp.clip(drawn, min=-most, max=most).astype(held_as)


def setup_inputs(seed: int = 0, part: int = 0) -> dict:
    key_of = jax.random.split(jax.random.key(seed), 15)
    own_keys = jax.random.split(jax.random.fold_in(key_of[14], part), 15)
    query_latent = draw_query_latent(jax.random.fold_in(jax.random.fold_in(key_of[14], part), 71), part)
    query_rope = draw_query_rope(jax.random.fold_in(jax.random.fold_in(key_of[14], part), 71), part)
    cache_latent = draw_cache_latent(jax.random.fold_in(jax.random.fold_in(key_of[14], part), 71), part)
    cache_rope = normal_values(own_keys[3], (ROWS, ROPE, LEN), 1.0, 4.5, ((0, 4),))
    cache_length = draw_cache_length(jax.random.fold_in(jax.random.fold_in(key_of[14], part), 71), part)
    value_up = normal_values(key_of[5], (HEADS, LATENT, VHEAD), LATENT ** -0.5, 0.25, ((0, 4),))
    output_weight = normal_values(key_of[6], (HEADS * VHEAD, D), (HEAD_DEV * VHEAD) ** -0.5, 0.1875, ((0, 4), (1, 4)))
    residual = draw_residual(jax.random.fold_in(jax.random.fold_in(key_of[14], part), 71), part)
    norm_gain = jnp.clip(1.0 + 0.15 * jax.random.normal(key_of[8], (D,), jnp.float32), 0.25, 1.75)
    routed_experts_keys = jax.random.split(jax.random.fold_in(own_keys[9], 1), ROWS // (ROWS // N_TP))
    routed_experts_turns = jax.random.permutation(jax.random.fold_in(own_keys[9], 3), ROWS // (ROWS // N_TP))
    routed_experts = jax.vmap(lambda own, number: shared_out(jax.random.fold_in(own_keys[9], 2), own, number, ROWS // N_TP, EXPERTS, TOP, CAP, 2))(routed_experts_keys, routed_experts_turns).reshape((ROWS, TOP))
    expert_gates = jnp.clip(jax.random.uniform(own_keys[10], (ROWS, TOP), jnp.float32, 0.2, 1.0), 0.2, 1.0)
    gate_weight = normal_values(key_of[11], (EXPERTS, D, FF), D ** -0.5, 0.0625, ((0, 4), (2, 4)))
    up_weight = normal_values(key_of[12], (EXPERTS, D, FF), D ** -0.5, 0.0625, ((0, 4), (2, 4)))
    down_weight = normal_values(key_of[13], (EXPERTS, FF, D), FF ** -0.5, 0.125, ((0, 4), (1, 4)))
    return {"query_latent": query_latent, "query_rope": query_rope, "cache_latent": cache_latent, "cache_rope": cache_rope, "cache_length": cache_length, "value_up": value_up, "output_weight": output_weight, "residual": residual, "norm_gain": norm_gain, "routed_experts": routed_experts, "expert_gates": expert_gates, "gate_weight": gate_weight, "up_weight": up_weight, "down_weight": down_weight}


score_scale = 1.0 / 192.0 ** 0.5
norm_epsilon = 1e-06

def reference(query_latent, query_rope, cache_latent, cache_rope, cache_length, value_up, output_weight, residual, norm_gain, routed_experts, expert_gates, gate_weight, up_weight, down_weight):
    row_total = query_latent.shape[0]
    head_total = query_latent.shape[1]
    rope_query = query_rope.reshape(row_total, head_total, ROPE).astype(jnp.float32)
    cache_wide = cache_latent.astype(jnp.float32)
    latent_part = jnp.einsum('rhc,rlc->rhl', query_latent.astype(jnp.float32), cache_wide)
    rope_part = jnp.einsum('rhp,rpl->rhl', rope_query, cache_rope.astype(jnp.float32))
    scores = (latent_part + rope_part) * score_scale
    visible = jnp.arange(LEN, dtype=jnp.int32)[None, None, :] < cache_length[:, None, None]
    scores = jnp.where(visible, scores, -jnp.inf)
    peak_score = lax.optimization_barrier(jnp.max(scores, axis=-1, keepdims=True))
    weights = jnp.where(visible, jnp.exp(scores - peak_score), 0.0)
    probabilities = (weights / lax.optimization_barrier(jnp.sum(weights, axis=-1, keepdims=True))).astype(jnp.bfloat16)
    latent_out = jnp.einsum('rhl,rlc->rhc', probabilities.astype(jnp.float32), cache_wide).astype(jnp.bfloat16)
    head_out = jnp.einsum('rhc,hcv->rhv', latent_out.astype(jnp.float32), value_up.astype(jnp.float32)).astype(jnp.bfloat16)
    grouped = head_out.reshape(row_total, N_TP, HEAD_DEV * VHEAD).astype(jnp.float32)
    projection = output_weight.reshape(N_TP, HEAD_DEV * VHEAD, D).astype(jnp.float32)
    group_terms = jnp.einsum('rtk,tkd->rtd', grouped, projection).astype(jnp.bfloat16)
    group_terms = lax.optimization_barrier(group_terms)
    attention = lax.optimization_barrier(jnp.sum(group_terms.astype(jnp.float32), axis=1))
    stream_out = (residual.astype(jnp.float32) + attention).astype(jnp.bfloat16)
    stream_wide = stream_out.astype(jnp.float32)
    mean_square = lax.optimization_barrier(jnp.sum(stream_wide * stream_wide, axis=-1)) / D
    normed = (stream_wide * lax.rsqrt(mean_square + norm_epsilon)[:, None] * norm_gain).astype(jnp.bfloat16)

    def one_expert(expert_index):
        gate_part = jnp.dot(normed, gate_weight[expert_index], preferred_element_type=jnp.float32)
        up_part = jnp.dot(normed, up_weight[expert_index], preferred_element_type=jnp.float32)
        activation = (jax.nn.silu(gate_part) * up_part).astype(jnp.bfloat16)
        unit_groups = activation.reshape(row_total, N_TP, FF // N_TP).astype(jnp.float32)
        down_groups = down_weight[expert_index].reshape(N_TP, FF // N_TP, D).astype(jnp.float32)
        unit_terms = jnp.einsum('rtf,tfd->rtd', unit_groups, down_groups).astype(jnp.bfloat16)
        unit_terms = lax.optimization_barrier(unit_terms)
        expert_out = lax.optimization_barrier(jnp.sum(unit_terms.astype(jnp.float32), axis=1)).astype(jnp.bfloat16)
        row_weight = lax.optimization_barrier(jnp.sum(jnp.where(routed_experts == expert_index, expert_gates, 0.0), axis=-1))
        return row_weight[:, None] * expert_out.astype(jnp.float32)
    stacked = lax.map(one_expert, jnp.arange(EXPERTS, dtype=jnp.int32))
    expert_mix = lax.optimization_barrier(jnp.sum(stacked, axis=0)).astype(jnp.bfloat16)
    return (stream_out, expert_mix)
```

```python
import functools

import jax
import jax.numpy as jnp
from jax import lax
from jax.experimental import pallas as pl
from jax.experimental.pallas import tpu as pltpu
from jax.sharding import PartitionSpec as P

score_scale = 1.0 / 192.0**0.5
norm_epsilon = 1e-06
MIB = 1 << 20


def attention_kernel(step_rows, lengths, q_ref, qr_ref, k_ref, kr_ref, up_ref, out_ref, latent):
    step = pl.program_id(0)
    heads, positions = q_ref.shape[1], k_ref.shape[1]
    place = lax.broadcasted_iota(jnp.int32, (heads, positions), 1)
    lanes = latent.shape[2]
    scores = []
    for r in range(step_rows):
        score = lax.dot_general(
            q_ref[r], k_ref[r], (((1,), (1,)), ((), ())), preferred_element_type=jnp.float32
        )
        score += jnp.dot(qr_ref[r], kr_ref[r], preferred_element_type=jnp.float32)
        scores.append(score)
    probabilities = []
    for r in range(step_rows):
        visible = place < lengths[step * step_rows + r]
        score = jnp.where(visible, scores[r] * score_scale, -jnp.inf)
        weight = jnp.exp(score - jnp.max(score, axis=-1, keepdims=True))
        total = jnp.sum(weight, axis=-1, keepdims=True)
        probabilities.append((weight / total).astype(jnp.bfloat16))
    for r in range(step_rows):
        first = pl.multiple_of((step * step_rows + r) * heads, heads)
        mixed = jnp.dot(probabilities[r], k_ref[r], preferred_element_type=jnp.float32)
        for c in range(latent.shape[0]):
            latent[c, pl.ds(first, heads), :] = mixed[:, c * lanes : (c + 1) * lanes]

    @pl.when(step == pl.num_programs(0) - 1)
    def _():
        rows = out_ref.shape[0]
        width = up_ref.shape[2]
        for h in range(heads):
            parts = [latent[c, pl.ds(h, rows, stride=heads), :] for c in range(latent.shape[0])]
            part = jnp.concatenate(parts, axis=1).astype(jnp.bfloat16)
            out_ref[:, h * width : (h + 1) * width] = jnp.dot(
                part, up_ref[h], preferred_element_type=jnp.float32
            ).astype(jnp.bfloat16)


def attend(query_latent, rope_query, cache_latent, cache_rope, cache_length, value_up):
    rows, heads, latent_width = query_latent.shape
    positions = cache_latent.shape[1]
    rope_width = cache_rope.shape[1]
    value_width = value_up.shape[2]
    step_rows = 16
    by_row = lambda i, lengths: (i, 0, 0)
    return pl.pallas_call(
        functools.partial(attention_kernel, step_rows),
        out_shape=jax.ShapeDtypeStruct((rows, heads * value_width), jnp.bfloat16),
        grid_spec=pltpu.PrefetchScalarGridSpec(
            num_scalar_prefetch=1,
            grid=(rows // step_rows,),
            in_specs=[
                pl.BlockSpec((step_rows, heads, latent_width), by_row),
                pl.BlockSpec((step_rows, heads, rope_width), by_row),
                pl.BlockSpec((step_rows, positions, latent_width), by_row),
                pl.BlockSpec((step_rows, rope_width, positions), by_row),
                pl.BlockSpec(value_up.shape, lambda i, lengths: (0, 0, 0)),
            ],
            out_specs=pl.BlockSpec((rows, heads * value_width), lambda i, lengths: (0, 0)),
            scratch_shapes=[pltpu.VMEM((latent_width // 128, rows * heads, 128), jnp.float32)],
        ),
        compiler_params=pltpu.CompilerParams(vmem_limit_bytes=32 * MIB),
        name="attention",
    )(cache_length, query_latent, rope_query, cache_latent, cache_rope, value_up)


def projection_kernel(count, places, *refs):
    blocks, weight, outs = refs[:count], refs[count], refs[count + 1 : -2]
    gathered, result = refs[-2:]
    height = blocks[0].shape[0]
    for k in range(count):
        first = pl.multiple_of(places[k] * height, height)
        gathered[pl.ds(first, height), :] = blocks[k][...]
    columns = weight.shape[1]
    tile = 256 if columns % 256 == 0 else 128
    for j in range(columns // tile):
        result[:, j * tile : (j + 1) * tile] = jnp.dot(
            gathered[...], weight[:, j * tile : (j + 1) * tile], preferred_element_type=jnp.float32
        ).astype(jnp.bfloat16)
    out_height = outs[0].shape[0]
    for s in range(len(outs)):
        first = pl.multiple_of(places[count + s] * out_height, out_height)
        outs[s][...] = result[pl.ds(first, out_height), :]


def project(places, blocks, weight, out_count):
    count = len(blocks)
    height, depth = blocks[0].shape
    rows, columns = height * count, weight.shape[1]
    whole = pl.BlockSpec(memory_space=pltpu.VMEM)
    return pl.pallas_call(
        functools.partial(projection_kernel, count),
        out_shape=[jax.ShapeDtypeStruct((rows // out_count, columns), jnp.bfloat16)] * out_count,
        in_specs=[pl.BlockSpec(memory_space=pltpu.SMEM)] + [whole] * (count + 1),
        out_specs=[whole] * out_count,
        scratch_shapes=[
            pltpu.VMEM((rows, depth), jnp.bfloat16),
            pltpu.VMEM((rows, columns), jnp.bfloat16),
        ],
        compiler_params=pltpu.CompilerParams(vmem_limit_bytes=32 * MIB),
        name="projection",
    )(places, *blocks, weight)


def expert_kernel(row_blocks, column_blocks, model_width, places, *refs):
    count = row_blocks * column_blocks
    blocks, gains = refs[:count], refs[count : count + column_blocks]
    row_weight, gate_hbm, up_hbm, down_hbm = refs[count + column_blocks : count + column_blocks + 4]
    outs = refs[count + column_blocks + 4 : -8]
    x, gate, up, down, gate_sum, up_sum, active, sems = refs[-8:]
    height, width = blocks[0].shape
    hidden = gate.shape[2]
    copies = []
    for k in range(column_blocks):
        first = pl.multiple_of(places[k] * width, width)
        copies.append(
            (
                pltpu.make_async_copy(gate_hbm.at[0, pl.ds(first, width), :], gate.at[k], sems.at[0, k]),
                pltpu.make_async_copy(up_hbm.at[0, pl.ds(first, width), :], up.at[k], sems.at[1, k]),
                pltpu.make_async_copy(down_hbm.at[0, :, pl.ds(first, width)], down.at[k], sems.at[2, k]),
            )
        )
    for which in ((0, 1), (2,)):
        for k in range(column_blocks):
            for w in which:
                copies[k][w].start()
    squares = [jnp.zeros((height, 1), jnp.float32) for _ in range(row_blocks)]
    tile = min(256, hidden)
    for k in range(column_blocks):
        for s in range(row_blocks):
            wide = blocks[s * column_blocks + k][...].astype(jnp.float32)
            squares[s] += jnp.sum(wide * wide, axis=-1, keepdims=True)
            x[k, s * height : (s + 1) * height, :] = (wide * gains[k][...]).astype(jnp.bfloat16)
        copies[k][0].wait()
        copies[k][1].wait()
        for total, weight in ((gate_sum, gate), (up_sum, up)):
            for j in range(hidden // tile):
                cut = slice(j * tile, (j + 1) * tile)
                product = jnp.dot(x[k], weight[k, :, cut], preferred_element_type=jnp.float32)
                if k == 0:
                    total[:, cut] = product
                else:
                    total[:, cut] += product
    for s in range(row_blocks):
        rows = slice(s * height, (s + 1) * height)
        scale = lax.rsqrt(squares[s] / model_width + norm_epsilon)
        gate_part = gate_sum[rows, :] * scale
        up_part = up_sum[rows, :] * scale
        active[rows, :] = (gate_part / (1.0 + jnp.exp(-gate_part)) * up_part).astype(jnp.bfloat16)
    for k in range(column_blocks):
        copies[k][2].wait()
    tile = 256 if width % 256 == 0 else 128
    for k in range(column_blocks):
        for j in range(width // tile):
            cut = slice(j * tile, (j + 1) * tile)
            product = jnp.dot(active[...], down[k, :, cut], preferred_element_type=jnp.float32)
            for s in range(row_blocks):
                first = pl.multiple_of(places[column_blocks + s] * height, height)
                part = product[s * height : (s + 1) * height, :] * row_weight[pl.ds(first, height), :]
                outs[s * column_blocks + k][:, cut] = part.astype(jnp.bfloat16)


def run_expert(places, blocks, gains, row_weight, gate_weight, up_weight, down_weight):
    row_blocks, column_blocks = len(blocks), len(blocks[0])
    height, width = blocks[0][0].shape
    rows = row_blocks * height
    hidden = gate_weight.shape[2]
    whole = pl.BlockSpec(memory_space=pltpu.VMEM)
    count = row_blocks * column_blocks
    outs = pl.pallas_call(
        functools.partial(expert_kernel, row_blocks, column_blocks, gate_weight.shape[1]),
        out_shape=[jax.ShapeDtypeStruct((height, width), jnp.bfloat16)] * count,
        in_specs=[pl.BlockSpec(memory_space=pltpu.SMEM)]
        + [whole] * (count + column_blocks + 1)
        + [pl.BlockSpec(memory_space=pl.ANY)] * 3,
        out_specs=[whole] * count,
        scratch_shapes=[
            pltpu.VMEM((column_blocks, rows, width), jnp.bfloat16),
            pltpu.VMEM((column_blocks, width, hidden), jnp.bfloat16),
            pltpu.VMEM((column_blocks, width, hidden), jnp.bfloat16),
            pltpu.VMEM((column_blocks, hidden, width), jnp.bfloat16),
            pltpu.VMEM((rows, hidden), jnp.float32),
            pltpu.VMEM((rows, hidden), jnp.float32),
            pltpu.VMEM((rows, hidden), jnp.bfloat16),
            pltpu.SemaphoreType.DMA((3, column_blocks)),
        ],
        compiler_params=pltpu.CompilerParams(vmem_limit_bytes=48 * MIB),
        name="expert",
    )(places, *[b for row in blocks for b in row], *gains, row_weight, gate_weight, up_weight, down_weight)
    return [outs[s * column_blocks : (s + 1) * column_blocks] for s in range(row_blocks)]


def shards(
    query_latent,
    query_rope,
    cache_latent,
    cache_rope,
    cache_length,
    value_up,
    output_weight,
    residual,
    norm_gain,
    routed_experts,
    expert_gates,
    gate_weight,
    up_weight,
    down_weight,
):
    ep_count = lax.axis_size("ep")
    tp_count = lax.axis_size("tp")
    ep_index = lax.axis_index("ep")
    tp_index = lax.axis_index("tp")
    local_rows, local_heads, _ = query_latent.shape
    rope_width = cache_rope.shape[1]
    row_total = routed_experts.shape[0]
    block_rows = row_total // tp_count
    cores = 2
    chips = ep_count // cores

    def from_core(value):
        return lax.ppermute(value, "ep", [(i, i ^ 1) for i in range(ep_count)])

    def from_chip(value, back):
        step = cores * back
        return lax.ppermute(value, "ep", [(i, (i + step) % ep_count) for i in range(ep_count)])

    def from_tp(value, back):
        return lax.ppermute(value, "tp", [(i, (i + back) % tp_count) for i in range(tp_count)])

    def gather_ep(value):
        same = [value] + [from_chip(value, b) for b in range(1, chips)]
        other = [from_core(v) for v in same]
        return [v for pair in zip(same, other) for v in pair]

    chip, core = ep_index // cores, ep_index % cores
    ep_places = [
        (chip - b + chips) % chips * cores + (core if c == 0 else 1 - core)
        for b in range(chips)
        for c in range(cores)
    ]
    tp_places = [(tp_index - b + tp_count) % tp_count for b in range(tp_count)]
    places = jnp.stack(ep_places + tp_places).astype(jnp.int32)

    gains = gather_ep(norm_gain.reshape(1, -1))
    row_weight = jnp.sum(jnp.where(routed_experts == ep_index, expert_gates, 0.0), axis=-1, keepdims=True)

    head_out = attend(
        query_latent,
        query_rope.reshape(local_rows, local_heads, rope_width),
        cache_latent,
        cache_rope,
        cache_length,
        value_up,
    )
    partial = project(places, gather_ep(head_out), output_weight, tp_count)
    arrived = [partial[0]] + [from_tp(partial[b], tp_count - b) for b in range(1, tp_count)]
    own_residual = lax.dynamic_slice_in_dim(residual, tp_index * block_rows, block_rows, 0)
    attention = sum(a.astype(jnp.float32) for a in arrived)
    stream = (own_residual.astype(jnp.float32) + attention).astype(jnp.bfloat16)

    rows_of = [stream] + [from_tp(stream, b) for b in range(1, tp_count)]
    blocks = [gather_ep(r) for r in rows_of]
    outs = run_expert(places, blocks, gains, row_weight, gate_weight, up_weight, down_weight)

    def add(values):
        return sum(v.astype(jnp.float32) for v in values).astype(jnp.bfloat16)

    def back_to_ep(out):
        pairs = [add((out[b * cores], from_core(out[b * cores + 1]))) for b in range(chips)]
        return add([pairs[0]] + [from_chip(pairs[b], chips - b) for b in range(1, chips)])

    returned = [back_to_ep(out) for out in outs]
    mixed = add([returned[0]] + [from_tp(returned[b], tp_count - b) for b in range(1, tp_count)])
    return (stream, mixed)


def solution(mesh):
    return jax.shard_map(
        shards,
        mesh=mesh,
        in_specs=(
            P(("parts", "ep"), "tp", None),
            P(("parts", "ep"), "tp"),
            P(("parts", "ep"), None, None),
            P(("parts", "ep"), None, None),
            P(("parts", "ep")),
            P("tp", None, None),
            P("tp", "ep"),
            P("parts", "ep"),
            P("ep"),
            P("parts", None),
            P("parts", None),
            P("ep", None, "tp"),
            P("ep", None, "tp"),
            P("ep", "tp", None),
        ),
        out_specs=(P(("parts", "tp"), "ep"), P(("parts", "tp"), "ep")),
        check_vma=False,
    )
```

```python
import functools

import jax
import jax.numpy as jnp
from jax import lax
from jax.experimental import pallas as pl
from jax.experimental.pallas import tpu as pltpu
from jax.sharding import PartitionSpec as P

score_scale = 1.0 / 192.0**0.5
norm_epsilon = 1e-06
MIB = 1 << 20


def attention_kernel(step_rows, lengths, q_hbm, qr_hbm, k_hbm, kr_hbm, up_hbm, out_ref, *scratch):
    q, qr, k, kr, up, rope, latent, sems, key_sems = scratch
    rows = k.shape[0]
    positions, latent_width = k.shape[1:]
    rope_width = kr.shape[1]
    heads = q.shape[0] // rows
    steps = rows // step_rows
    copies = [
        pltpu.make_async_copy(source, target, sems.at[i])
        for i, (source, target) in enumerate(((qr_hbm, qr), (q_hbm, q), (up_hbm, up)))
    ]

    def key_copies(step):
        cut = pl.ds(step * step_rows, step_rows)
        return (
            pltpu.make_async_copy(k_hbm.at[cut], k.at[cut], key_sems.at[0, step]),
            pltpu.make_async_copy(kr_hbm.at[cut], kr.at[cut], key_sems.at[1, step]),
        )

    copies[0].start()
    copies[1].start()
    for step in range(steps):
        for copy in key_copies(step):
            copy.start()
    copies[2].start()

    copies[0].wait()
    lane = lax.broadcasted_iota(jnp.int32, (heads, heads * rope_width), 1)
    head = lax.broadcasted_iota(jnp.int32, (heads, heads * rope_width), 0)
    own = jnp.where(lane // rope_width == head, 1.0, 0.0)
    spread = (qr[...].astype(jnp.float32)[:, None, :] * own[None, :, :]).reshape(rows * heads, heads * rope_width)
    lane = lax.broadcasted_iota(jnp.int32, (heads * rope_width, rope_width), 0)
    column = lax.broadcasted_iota(jnp.int32, (heads * rope_width, rope_width), 1)
    fold = jnp.where(lane % rope_width == column, 1.0, 0.0).astype(jnp.bfloat16)
    rope[...] = jnp.dot(spread.astype(jnp.bfloat16), fold, preferred_element_type=jnp.float32).astype(jnp.bfloat16)
    copies[1].wait()

    place = lax.broadcasted_iota(jnp.int32, (heads, positions), 1)
    lanes = latent.shape[2]

    def attend_rows(step, carry):
        for copy in key_copies(step):
            copy.wait()
        scores = []
        for pair in range(step_rows // 2):
            first = step * step_rows + 2 * pair
            cut = pl.ds(pl.multiple_of(first * heads, 2 * heads), 2 * heads)
            for r in range(2):
                score = lax.dot_general(
                    q[cut, :], k[first + r], (((1,), (1,)), ((), ())), preferred_element_type=jnp.float32
                )
                score += jnp.dot(rope[cut, :], kr[first + r], preferred_element_type=jnp.float32)
                scores.append(score[r * heads : (r + 1) * heads, :])
        probabilities = []
        for r in range(step_rows):
            visible = place < lengths[step * step_rows + r]
            score = jnp.where(visible, scores[r] * score_scale, -jnp.inf)
            weight = jnp.exp(score - jnp.max(score, axis=-1, keepdims=True))
            total = jnp.sum(weight, axis=-1, keepdims=True)
            probabilities.append((weight / total).astype(jnp.bfloat16))
        for r in range(step_rows):
            row = step * step_rows + r
            mixed = jnp.dot(probabilities[r], k[row], preferred_element_type=jnp.float32)
            for c in range(latent.shape[0]):
                latent[c, pl.ds(pl.multiple_of(row * heads, heads), heads), :] = mixed[:, c * lanes : (c + 1) * lanes]
        return carry

    lax.fori_loop(0, steps, attend_rows, 0)
    copies[2].wait()
    width = up.shape[2]
    for h in range(heads):
        parts = [latent[c, pl.ds(h, rows, stride=heads), :] for c in range(latent.shape[0])]
        part = jnp.concatenate(parts, axis=1).astype(jnp.bfloat16)
        out_ref[:, h * width : (h + 1) * width] = jnp.dot(
            part, up[h], preferred_element_type=jnp.float32
        ).astype(jnp.bfloat16)


def attend(query_latent, query_rope, cache_latent, cache_rope, cache_length, value_up):
    rows, heads, latent_width = query_latent.shape
    step_rows = 16
    steps = rows // step_rows
    hbm = pl.BlockSpec(memory_space=pltpu.HBM)
    return pl.pallas_call(
        functools.partial(attention_kernel, step_rows),
        out_shape=jax.ShapeDtypeStruct((rows, heads * value_up.shape[2]), jnp.bfloat16),
        in_specs=[pl.BlockSpec(memory_space=pltpu.SMEM)] + [hbm] * 5,
        out_specs=pl.BlockSpec(memory_space=pltpu.VMEM),
        scratch_shapes=[
            pltpu.VMEM((rows * heads, latent_width), jnp.bfloat16),
            pltpu.VMEM(query_rope.shape, jnp.bfloat16),
            pltpu.VMEM(cache_latent.shape, jnp.bfloat16),
            pltpu.VMEM(cache_rope.shape, jnp.bfloat16),
            pltpu.VMEM(value_up.shape, jnp.bfloat16),
            pltpu.VMEM((rows * heads, cache_rope.shape[1]), jnp.bfloat16),
            pltpu.VMEM((latent_width // 128, rows * heads, 128), jnp.float32),
            pltpu.SemaphoreType.DMA((3,)),
            pltpu.SemaphoreType.DMA((2, steps)),
        ],
        compiler_params=pltpu.CompilerParams(vmem_limit_bytes=28 * MIB),
        name="attention",
    )(
        cache_length,
        query_latent.reshape(rows * heads, latent_width),
        query_rope,
        cache_latent,
        cache_rope,
        value_up,
    )


def projection_kernel(count, places, *refs):
    blocks, weight, outs = refs[:count], refs[count], refs[count + 1 : -2]
    gathered, result = refs[-2:]
    height = blocks[0].shape[0]
    for k in range(count):
        first = pl.multiple_of(places[k] * height, height)
        gathered[pl.ds(first, height), :] = blocks[k][...]
    columns = weight.shape[1]
    tile = 256 if columns % 256 == 0 else 128
    for j in range(columns // tile):
        result[:, j * tile : (j + 1) * tile] = jnp.dot(
            gathered[...], weight[:, j * tile : (j + 1) * tile], preferred_element_type=jnp.float32
        ).astype(jnp.bfloat16)
    out_height = outs[0].shape[0]
    for s in range(len(outs)):
        first = pl.multiple_of(places[count + s] * out_height, out_height)
        outs[s][...] = result[pl.ds(first, out_height), :]


def project(places, blocks, weight, out_count):
    count = len(blocks)
    height, depth = blocks[0].shape
    rows, columns = height * count, weight.shape[1]
    whole = pl.BlockSpec(memory_space=pltpu.VMEM)
    return pl.pallas_call(
        functools.partial(projection_kernel, count),
        out_shape=[jax.ShapeDtypeStruct((rows // out_count, columns), jnp.bfloat16)] * out_count,
        in_specs=[pl.BlockSpec(memory_space=pltpu.SMEM)] + [whole] * (count + 1),
        out_specs=[whole] * out_count,
        scratch_shapes=[
            pltpu.VMEM((rows, depth), jnp.bfloat16),
            pltpu.VMEM((rows, columns), jnp.bfloat16),
        ],
        compiler_params=pltpu.CompilerParams(vmem_limit_bytes=32 * MIB),
        name="projection",
    )(places, *blocks, weight)


def expert_kernel(row_blocks, column_blocks, cores, model_width, places, *refs):
    count = row_blocks * column_blocks
    blocks, gains = refs[:count], refs[count : count + column_blocks]
    row_weight, gate, up, down = refs[count + column_blocks : count + column_blocks + 4]
    outs = refs[count + column_blocks + 4 : -4]
    x, gate_sum, up_sum, active = refs[-4:]
    height, width = blocks[0].shape
    hidden = gate.shape[2]
    squares = [jnp.zeros((height, 1), jnp.float32) for _ in range(row_blocks)]
    tile = min(256, hidden)
    for k in range(column_blocks):
        for s in range(row_blocks):
            wide = blocks[s * column_blocks + k][...].astype(jnp.float32)
            squares[s] += jnp.sum(wide * wide, axis=-1, keepdims=True)
            x[k, s * height : (s + 1) * height, :] = (wide * gains[k][...]).astype(jnp.bfloat16)
        depth = pl.ds(pl.multiple_of(places[k] * width, 128), width)
        for total, weight in ((gate_sum, gate), (up_sum, up)):
            for j in range(hidden // tile):
                cut = slice(j * tile, (j + 1) * tile)
                product = jnp.dot(x[k], weight[0, depth, cut], preferred_element_type=jnp.float32)
                if k == 0:
                    total[:, cut] = product
                else:
                    total[:, cut] += product
    for s in range(row_blocks):
        rows = slice(s * height, (s + 1) * height)
        scale = lax.rsqrt(squares[s] / model_width + norm_epsilon)
        gate_part = gate_sum[rows, :] * scale
        up_part = up_sum[rows, :] * scale
        active[rows, :] = (gate_part / (1.0 + jnp.exp(-gate_part)) * up_part).astype(jnp.bfloat16)
    tile = 256 if width % 256 == 0 else 128
    weights = []
    for s in range(row_blocks):
        first = pl.multiple_of(places[column_blocks + s] * height, height)
        weights.append(row_weight[pl.ds(first, height), :])
    for c in reversed(range(cores)):
        for b in range(column_blocks // cores):
            start = pl.multiple_of(places[b * cores + c] * width, 128)
            for j in range(width // tile):
                cut = slice(j * tile, (j + 1) * tile)
                product = jnp.dot(
                    active[...], down[0, :, pl.ds(start + j * tile, tile)], preferred_element_type=jnp.float32
                )
                for s in range(row_blocks):
                    part = product[s * height : (s + 1) * height, :] * weights[s]
                    outs[s * cores + c][b * height : (b + 1) * height, cut] = part.astype(jnp.bfloat16)


def run_expert(places, blocks, gains, row_weight, gate_weight, up_weight, down_weight, cores):
    row_blocks, column_blocks = len(blocks), len(blocks[0])
    height, width = blocks[0][0].shape
    rows = row_blocks * height
    hidden = gate_weight.shape[2]
    whole = pl.BlockSpec(memory_space=pltpu.VMEM)
    count = row_blocks * column_blocks
    out = jax.ShapeDtypeStruct((height * (column_blocks // cores), width), jnp.bfloat16)
    outs = pl.pallas_call(
        functools.partial(expert_kernel, row_blocks, column_blocks, cores, gate_weight.shape[1]),
        out_shape=[out] * (row_blocks * cores),
        in_specs=[pl.BlockSpec(memory_space=pltpu.SMEM)] + [whole] * (count + column_blocks + 4),
        out_specs=[whole] * (row_blocks * cores),
        scratch_shapes=[
            pltpu.VMEM((column_blocks, rows, width), jnp.bfloat16),
            pltpu.VMEM((rows, hidden), jnp.float32),
            pltpu.VMEM((rows, hidden), jnp.float32),
            pltpu.VMEM((rows, hidden), jnp.bfloat16),
        ],
        compiler_params=pltpu.CompilerParams(vmem_limit_bytes=14 * MIB),
        name="expert",
    )(places, *[b for row in blocks for b in row], *gains, row_weight, gate_weight, up_weight, down_weight)
    return [outs[s * cores : (s + 1) * cores] for s in range(row_blocks)]


def add_kernel(groups, *refs):
    used = sum(len(g) for g in groups)
    outs = refs[-len(groups) :]
    at = 0
    for group, out in zip(groups, outs):
        total = None
        for first in group:
            value = refs[at][first : first + out.shape[0], :].astype(jnp.float32)
            total = value if total is None else total + value
            at += 1
        out[...] = total.astype(jnp.bfloat16)


def add(groups, height, after=()):
    values = [value for group in groups for value, _ in group]
    width = values[0].shape[1]
    whole = pl.BlockSpec(memory_space=pltpu.VMEM)
    return pl.pallas_call(
        functools.partial(add_kernel, [[first for _, first in group] for group in groups]),
        out_shape=[jax.ShapeDtypeStruct((height, width), jnp.bfloat16)] * len(groups),
        in_specs=[whole] * len(values) + [pl.BlockSpec(memory_space=pl.ANY)] * len(after),
        out_specs=[whole] * len(groups),
        compiler_params=pltpu.CompilerParams(vmem_limit_bytes=8 * MIB),
        name="add",
    )(*values, *after)


def shards(
    query_latent,
    query_rope,
    cache_latent,
    cache_rope,
    cache_length,
    value_up,
    output_weight,
    residual,
    norm_gain,
    routed_experts,
    expert_gates,
    gate_weight,
    up_weight,
    down_weight,
):
    ep_count = lax.axis_size("ep")
    tp_count = lax.axis_size("tp")
    ep_index = lax.axis_index("ep")
    tp_index = lax.axis_index("tp")
    row_total = routed_experts.shape[0]
    block_rows = row_total // tp_count
    cores = 2
    chips = ep_count // cores

    def from_core(value):
        return lax.ppermute(value, "ep", [(i, i ^ 1) for i in range(ep_count)])

    def from_chip(value, back):
        step = cores * back
        return lax.ppermute(value, "ep", [(i, (i + step) % ep_count) for i in range(ep_count)])

    def from_tp(value, back):
        return lax.ppermute(value, "tp", [(i, (i + back) % tp_count) for i in range(tp_count)])

    def gather_ep(value):
        same = [value] + [from_chip(value, b) for b in range(1, chips)]
        other = [from_core(v) for v in same]
        return [v for pair in zip(same, other) for v in pair]

    chip, core = ep_index // cores, ep_index % cores
    ep_places = [
        (chip - b + chips) % chips * cores + (core if c == 0 else 1 - core)
        for b in range(chips)
        for c in range(cores)
    ]
    tp_places = [(tp_index - b + tp_count) % tp_count for b in range(tp_count)]
    places = jnp.stack(ep_places + tp_places).astype(jnp.int32)

    gains = gather_ep(norm_gain.reshape(1, -1))
    row_weight = jnp.sum(jnp.where(routed_experts == ep_index, expert_gates, 0.0), axis=-1, keepdims=True)

    head_out = attend(query_latent, query_rope, cache_latent, cache_rope, cache_length, value_up)
    partial = project(places, gather_ep(head_out), output_weight, tp_count)
    arrived = [partial[0]] + [from_tp(partial[b], tp_count - b) for b in range(1, tp_count)]
    own_residual = lax.dynamic_slice_in_dim(residual, tp_index * block_rows, block_rows, 0)
    attention = sum(a.astype(jnp.float32) for a in arrived)
    stream = (own_residual.astype(jnp.float32) + attention).astype(jnp.bfloat16)

    near = [b for b in range(1, tp_count) if b != tp_count // 2]
    far = [b for b in range(1, tp_count) if b == tp_count // 2]
    rows_of = {0: stream}
    for b in near:
        rows_of[b] = from_tp(stream, b)
    if far:
        (again,) = add([[(stream, 0)]], block_rows, [rows_of[b] for b in near])
        for b in far:
            rows_of[b] = from_tp(again, b)
    blocks = [gather_ep(rows_of[b]) for b in range(tp_count)]
    outs = run_expert(places, blocks, gains, row_weight, gate_weight, up_weight, down_weight, cores)

    swapped = [from_core(out[1]) for out in outs]
    order = far + near + [0]
    kept, across = {}, {}
    for at, b in enumerate(order):
        before = across[order[at - 2]] if at >= 2 else []
        pair = [[(outs[b][0], c * block_rows), (swapped[b], c * block_rows)] for c in range(chips)]
        sums = add(pair, block_rows, before)
        kept[b] = sums[0]
        across[b] = [from_chip(sums[c], chips - c) for c in range(1, chips)]
    finals = []
    for b in far + near:
        (total,) = add([[(v, 0) for v in [kept[b]] + across[b]]], block_rows)
        finals.append(from_tp(total, tp_count - b))
    (mixed,) = add([[(v, 0) for v in [kept[0]] + across[0] + finals]], block_rows)
    return (stream, mixed)


def solution(mesh):
    return jax.shard_map(
        shards,
        mesh=mesh,
        in_specs=(
            P(("parts", "ep"), "tp", None),
            P(("parts", "ep"), "tp"),
            P(("parts", "ep"), None, None),
            P(("parts", "ep"), None, None),
            P(("parts", "ep")),
            P("tp", None, None),
            P("tp", "ep"),
            P("parts", "ep"),
            P("ep"),
            P("parts", None),
            P("parts", None),
            P("ep", None, "tp"),
            P("ep", None, "tp"),
            P("ep", "tp", None),
        ),
        out_specs=(P(("parts", "tp"), "ep"), P(("parts", "tp"), "ep")),
        check_vma=False,
    )
```

```python
import functools

import jax
import jax.numpy as jnp
from jax import lax
from jax.experimental import pallas as pl
from jax.experimental.pallas import tpu as pltpu
from jax.sharding import PartitionSpec as P

score_scale = 1.0 / 192.0**0.5
norm_epsilon = 1e-06
MIB = 1 << 20


def attention_kernel(step_rows, lengths, q_hbm, qr_hbm, k_hbm, kr_hbm, up_hbm, out_ref, *scratch):
    q, qr, k, kr, up, rope, latent, sems, key_sems = scratch
    rows = k.shape[0]
    positions, latent_width = k.shape[1:]
    rope_width = kr.shape[1]
    heads = q.shape[0] // rows
    steps = rows // step_rows
    copies = [
        pltpu.make_async_copy(source, target, sems.at[i])
        for i, (source, target) in enumerate(((qr_hbm, qr), (q_hbm, q), (up_hbm, up)))
    ]

    def key_copies(step):
        cut = pl.ds(step * step_rows, step_rows)
        return (
            pltpu.make_async_copy(k_hbm.at[cut], k.at[cut], key_sems.at[0, step]),
            pltpu.make_async_copy(kr_hbm.at[cut], kr.at[cut], key_sems.at[1, step]),
        )

    copies[0].start()
    copies[1].start()
    for step in range(steps):
        for copy in key_copies(step):
            copy.start()
    copies[2].start()

    copies[0].wait()
    lane = lax.broadcasted_iota(jnp.int32, (heads, heads * rope_width), 1)
    head = lax.broadcasted_iota(jnp.int32, (heads, heads * rope_width), 0)
    own = jnp.where(lane // rope_width == head, 1.0, 0.0)
    spread = (qr[...].astype(jnp.float32)[:, None, :] * own[None, :, :]).reshape(rows * heads, heads * rope_width)
    lane = lax.broadcasted_iota(jnp.int32, (heads * rope_width, rope_width), 0)
    column = lax.broadcasted_iota(jnp.int32, (heads * rope_width, rope_width), 1)
    fold = jnp.where(lane % rope_width == column, 1.0, 0.0).astype(jnp.bfloat16)
    rope[...] = jnp.dot(spread.astype(jnp.bfloat16), fold, preferred_element_type=jnp.float32).astype(jnp.bfloat16)
    copies[1].wait()

    place = lax.broadcasted_iota(jnp.int32, (heads, positions), 1)
    lanes = latent.shape[2]

    def attend_rows(step, carry):
        for copy in key_copies(step):
            copy.wait()
        scores = []
        for pair in range(step_rows // 2):
            first = step * step_rows + 2 * pair
            cut = pl.ds(pl.multiple_of(first * heads, 2 * heads), 2 * heads)
            for r in range(2):
                score = lax.dot_general(
                    q[cut, :], k[first + r], (((1,), (1,)), ((), ())), preferred_element_type=jnp.float32
                )
                score += jnp.dot(rope[cut, :], kr[first + r], preferred_element_type=jnp.float32)
                scores.append(score[r * heads : (r + 1) * heads, :])
        probabilities = []
        for r in range(step_rows):
            visible = place < lengths[step * step_rows + r]
            score = jnp.where(visible, scores[r] * score_scale, -jnp.inf)
            weight = jnp.exp(score - jnp.max(score, axis=-1, keepdims=True))
            total = jnp.sum(weight, axis=-1, keepdims=True)
            probabilities.append((weight / total).astype(jnp.bfloat16))
        for r in range(step_rows):
            row = step * step_rows + r
            mixed = jnp.dot(probabilities[r], k[row], preferred_element_type=jnp.float32)
            for c in range(latent.shape[0]):
                latent[c, pl.ds(pl.multiple_of(row * heads, heads), heads), :] = mixed[:, c * lanes : (c + 1) * lanes]
        return carry

    lax.fori_loop(0, steps, attend_rows, 0)
    copies[2].wait()
    width = up.shape[2]
    for h in range(heads):
        parts = [latent[c, pl.ds(h, rows, stride=heads), :] for c in range(latent.shape[0])]
        part = jnp.concatenate(parts, axis=1).astype(jnp.bfloat16)
        out_ref[:, h * width : (h + 1) * width] = jnp.dot(
            part, up[h], preferred_element_type=jnp.float32
        ).astype(jnp.bfloat16)


def attend(query_latent, query_rope, cache_latent, cache_rope, cache_length, value_up):
    rows, heads, latent_width = query_latent.shape
    step_rows = 16
    steps = rows // step_rows
    hbm = pl.BlockSpec(memory_space=pltpu.HBM)
    return pl.pallas_call(
        functools.partial(attention_kernel, step_rows),
        out_shape=jax.ShapeDtypeStruct((rows, heads * value_up.shape[2]), jnp.bfloat16),
        in_specs=[pl.BlockSpec(memory_space=pltpu.SMEM)] + [hbm] * 5,
        out_specs=pl.BlockSpec(memory_space=pltpu.VMEM),
        scratch_shapes=[
            pltpu.VMEM((rows * heads, latent_width), jnp.bfloat16),
            pltpu.VMEM(query_rope.shape, jnp.bfloat16),
            pltpu.VMEM(cache_latent.shape, jnp.bfloat16),
            pltpu.VMEM(cache_rope.shape, jnp.bfloat16),
            pltpu.VMEM(value_up.shape, jnp.bfloat16),
            pltpu.VMEM((rows * heads, cache_rope.shape[1]), jnp.bfloat16),
            pltpu.VMEM((latent_width // 128, rows * heads, 128), jnp.float32),
            pltpu.SemaphoreType.DMA((3,)),
            pltpu.SemaphoreType.DMA((2, steps)),
        ],
        cost_estimate=pl.CostEstimate(
            flops=64 * heads * cache_latent.size, bytes_accessed=2 * cache_latent.size, transcendentals=0
        ),
        compiler_params=pltpu.CompilerParams(vmem_limit_bytes=58 * MIB),
        name="attention",
    )(
        cache_length,
        query_latent.reshape(rows * heads, latent_width),
        query_rope,
        cache_latent,
        cache_rope,
        value_up,
    )


def projection_kernel(count, out_count, places, *refs):
    blocks, weight, outs = refs[:count], refs[count], refs[-2 - out_count : -2]
    gathered, result = refs[-2:]
    height = blocks[0].shape[0]
    for k in range(count):
        first = pl.multiple_of(places[k] * height, height)
        gathered[pl.ds(first, height), :] = blocks[k][...]
    columns = weight.shape[1]
    tile = 256 if columns % 256 == 0 else 128
    for j in range(columns // tile):
        result[:, j * tile : (j + 1) * tile] = jnp.dot(
            gathered[...], weight[:, j * tile : (j + 1) * tile], preferred_element_type=jnp.float32
        ).astype(jnp.bfloat16)
    out_height = outs[0].shape[0]
    for s in range(len(outs)):
        first = pl.multiple_of(places[count + s] * out_height, out_height)
        outs[s][...] = result[pl.ds(first, out_height), :]


def project(places, blocks, weight, out_count, after):
    count = len(blocks)
    height, depth = blocks[0].shape
    rows, columns = height * count, weight.shape[1]
    whole = pl.BlockSpec(memory_space=pltpu.VMEM)
    return pl.pallas_call(
        functools.partial(projection_kernel, count, out_count),
        out_shape=[jax.ShapeDtypeStruct((rows // out_count, columns), jnp.bfloat16)] * out_count,
        in_specs=[pl.BlockSpec(memory_space=pltpu.SMEM)]
        + [whole] * (count + 1)
        + [pl.BlockSpec(memory_space=pl.ANY)] * len(after),
        out_specs=[whole] * out_count,
        scratch_shapes=[
            pltpu.VMEM((rows, depth), jnp.bfloat16),
            pltpu.VMEM((rows, columns), jnp.bfloat16),
        ],
        cost_estimate=pl.CostEstimate(flops=2 * rows * depth * columns, bytes_accessed=4 * MIB, transcendentals=0),
        compiler_params=pltpu.CompilerParams(vmem_limit_bytes=8 * MIB),
        name="projection",
    )(places, *blocks, weight, *after)


def touch_kernel(*refs):
    refs[-1][...] = jnp.zeros(refs[-1].shape, jnp.float32)


def touch(values, after):
    return pl.pallas_call(
        touch_kernel,
        out_shape=jax.ShapeDtypeStruct((8, 128), jnp.float32),
        in_specs=[pl.BlockSpec(memory_space=pltpu.VMEM)] * len(values)
        + [pl.BlockSpec(memory_space=pl.ANY)] * len(after),
        out_specs=pl.BlockSpec(memory_space=pltpu.VMEM),
        compiler_params=pltpu.CompilerParams(vmem_limit_bytes=24 * MIB),
        name="touch",
    )(*values, *after)


def expert_kernel(row_blocks, column_blocks, cores, model_width, places, *refs):
    count = row_blocks * column_blocks
    blocks, gains = refs[:count], refs[count : count + column_blocks]
    row_weight, gate, up, down = refs[count + column_blocks : count + column_blocks + 4]
    outs = refs[count + column_blocks + 4 : -4]
    x, gate_sum, up_sum, active = refs[-4:]
    height, width = blocks[0].shape
    hidden = gate.shape[2]
    squares = [jnp.zeros((height, 1), jnp.float32) for _ in range(row_blocks)]
    tile = min(256, hidden)
    for k in range(column_blocks):
        for s in range(row_blocks):
            wide = blocks[s * column_blocks + k][...].astype(jnp.float32)
            squares[s] += jnp.sum(wide * wide, axis=-1, keepdims=True)
            x[k, s * height : (s + 1) * height, :] = (wide * gains[k][...]).astype(jnp.bfloat16)
        depth = pl.ds(pl.multiple_of(places[k] * width, 128), width)
        for total, weight in ((gate_sum, gate), (up_sum, up)):
            for j in range(hidden // tile):
                cut = slice(j * tile, (j + 1) * tile)
                product = jnp.dot(x[k], weight[0, depth, cut], preferred_element_type=jnp.float32)
                if k == 0:
                    total[:, cut] = product
                else:
                    total[:, cut] += product
    for s in range(row_blocks):
        rows = slice(s * height, (s + 1) * height)
        scale = lax.rsqrt(squares[s] / model_width + norm_epsilon)
        gate_part = gate_sum[rows, :] * scale
        up_part = up_sum[rows, :] * scale
        active[rows, :] = (gate_part / (1.0 + jnp.exp(-gate_part)) * up_part).astype(jnp.bfloat16)
    tile = 256 if width % 256 == 0 else 128
    weights = []
    for s in range(row_blocks):
        first = pl.multiple_of(places[column_blocks + s] * height, height)
        weights.append(row_weight[pl.ds(first, height), :])
    for c in reversed(range(cores)):
        for b in range(column_blocks // cores):
            start = pl.multiple_of(places[b * cores + c] * width, 128)
            for j in range(width // tile):
                cut = slice(j * tile, (j + 1) * tile)
                product = jnp.dot(
                    active[...], down[0, :, pl.ds(start + j * tile, tile)], preferred_element_type=jnp.float32
                )
                for s in range(row_blocks):
                    part = product[s * height : (s + 1) * height, :] * weights[s]
                    outs[s * cores + c][b * height : (b + 1) * height, cut] = part.astype(jnp.bfloat16)


def run_expert(places, blocks, gains, row_weight, gate_weight, up_weight, down_weight, cores):
    row_blocks, column_blocks = len(blocks), len(blocks[0])
    height, width = blocks[0][0].shape
    rows = row_blocks * height
    hidden = gate_weight.shape[2]
    whole = pl.BlockSpec(memory_space=pltpu.VMEM)
    count = row_blocks * column_blocks
    out = jax.ShapeDtypeStruct((height * (column_blocks // cores), width), jnp.bfloat16)
    outs = pl.pallas_call(
        functools.partial(expert_kernel, row_blocks, column_blocks, cores, gate_weight.shape[1]),
        out_shape=[out] * (row_blocks * cores),
        in_specs=[pl.BlockSpec(memory_space=pltpu.SMEM)] + [whole] * (count + column_blocks + 4),
        out_specs=[whole] * (row_blocks * cores),
        scratch_shapes=[
            pltpu.VMEM((column_blocks, rows, width), jnp.bfloat16),
            pltpu.VMEM((rows, hidden), jnp.float32),
            pltpu.VMEM((rows, hidden), jnp.float32),
            pltpu.VMEM((rows, hidden), jnp.bfloat16),
        ],
        cost_estimate=pl.CostEstimate(
            flops=6 * rows * hidden * gate_weight.shape[1], bytes_accessed=8 * MIB, transcendentals=rows * hidden
        ),
        compiler_params=pltpu.CompilerParams(vmem_limit_bytes=2 * rows * (gate_weight.shape[1] + 5 * hidden) + 5 * MIB),
        name="expert",
    )(places, *[b for row in blocks for b in row], *gains, row_weight, gate_weight, up_weight, down_weight)
    return [outs[s * cores : (s + 1) * cores] for s in range(row_blocks)]


def add_kernel(groups, *refs):
    used = sum(len(g) for g in groups)
    outs = refs[-len(groups) :]
    at = 0
    for group, out in zip(groups, outs):
        total = None
        for first in group:
            value = refs[at][first : first + out.shape[0], :].astype(jnp.float32)
            total = value if total is None else total + value
            at += 1
        out[...] = total.astype(jnp.bfloat16)


def add(groups, height, after=()):
    values = [value for group in groups for value, _ in group]
    width = values[0].shape[1]
    whole = pl.BlockSpec(memory_space=pltpu.VMEM)
    return pl.pallas_call(
        functools.partial(add_kernel, [[first for _, first in group] for group in groups]),
        out_shape=[jax.ShapeDtypeStruct((height, width), jnp.bfloat16)] * len(groups),
        in_specs=[whole] * len(values) + [pl.BlockSpec(memory_space=pl.ANY)] * len(after),
        out_specs=[whole] * len(groups),
        compiler_params=pltpu.CompilerParams(vmem_limit_bytes=8 * MIB),
        name="add",
    )(*values, *after)


def shards(
    query_latent,
    query_rope,
    cache_latent,
    cache_rope,
    cache_length,
    value_up,
    output_weight,
    residual,
    norm_gain,
    routed_experts,
    expert_gates,
    gate_weight,
    up_weight,
    down_weight,
):
    ep_count = lax.axis_size("ep")
    tp_count = lax.axis_size("tp")
    ep_index = lax.axis_index("ep")
    tp_index = lax.axis_index("tp")
    row_total = routed_experts.shape[0]
    block_rows = row_total // tp_count
    cores = 2
    chips = ep_count // cores

    def from_core(value):
        return lax.ppermute(value, "ep", [(i, i ^ 1) for i in range(ep_count)])

    def from_chip(value, back):
        step = cores * back
        return lax.ppermute(value, "ep", [(i, (i + step) % ep_count) for i in range(ep_count)])

    def from_tp(value, bits):
        return lax.ppermute(value, "tp", [(i, i ^ bits) for i in range(tp_count)])

    def gather_ep(value):
        same = [value] + [from_chip(value, b) for b in range(1, chips)]
        other = [from_core(v) for v in same]
        return [v for pair in zip(same, other) for v in pair]

    chip, core = ep_index // cores, ep_index % cores
    ep_places = [
        (chip - b + chips) % chips * cores + (core if c == 0 else 1 - core)
        for b in range(chips)
        for c in range(cores)
    ]
    tp_places = [tp_index ^ k for k in range(tp_count)]
    places = jnp.stack(ep_places + tp_places).astype(jnp.int32)

    gains = gather_ep(norm_gain.reshape(1, -1))
    row_weight = jnp.sum(jnp.where(routed_experts == ep_index, expert_gates, 0.0), axis=-1, keepdims=True)

    head_out = attend(query_latent, query_rope, cache_latent, cache_rope, cache_length, value_up)
    partial = project(places, gather_ep(head_out), output_weight, tp_count, gains)
    expert_weights = [gate_weight, up_weight, down_weight]
    touched = touch(expert_weights, [partial[0]])

    own_residual = lax.dynamic_slice_in_dim(residual, tp_index * block_rows, block_rows, 0)
    terms = [[(value, 0)] for value in partial]
    for k in reversed(range(1, tp_count)):
        total = add([terms[k]], block_rows)[0] if len(terms[k]) > 1 else terms[k][0][0]
        low = k & -k
        terms[k ^ low].append((from_tp(total, low), 0))
    (stream,) = add([terms[0] + [(own_residual, 0)]], block_rows, [touched])

    rows_of = {0: stream}
    for k in range(1, tp_count):
        low = k & -k
        rows_of[k] = from_tp(rows_of[k ^ low], low)
    blocks = [gather_ep(rows_of[k]) for k in range(tp_count)]
    outs = run_expert(places, blocks, gains, row_weight, *expert_weights, cores)

    swapped = [from_core(out[1]) for out in outs]
    terms = [[] for _ in range(tp_count)]
    arrivals = []
    for k in reversed(range(tp_count)):
        before = []
        if len(arrivals) == 1:
            before = arrivals[0]
        elif len(arrivals) > 1:
            before = arrivals[-2]
        pair = [[(outs[k][0], c * block_rows), (swapped[k], c * block_rows)] for c in range(chips)]
        sums = add(pair, block_rows, before)
        across = [from_chip(sums[c], chips - c) for c in range(1, chips)]
        arrivals.append(across)
        terms[k] += [(value, 0) for value in [sums[0]] + across]
        if k:
            (total,) = add([terms[k]], block_rows)
            low = k & -k
            terms[k ^ low].append((from_tp(total, low), 0))
    (mixed,) = add([terms[0]], block_rows)
    return (stream, mixed)


def solution(mesh):
    return jax.shard_map(
        shards,
        mesh=mesh,
        in_specs=(
            P(("parts", "ep"), "tp", None),
            P(("parts", "ep"), "tp"),
            P(("parts", "ep"), None, None),
            P(("parts", "ep"), None, None),
            P(("parts", "ep")),
            P("tp", None, None),
            P("tp", "ep"),
            P("parts", "ep"),
            P("ep"),
            P("parts", None),
            P("parts", None),
            P("ep", None, "tp"),
            P("ep", None, "tp"),
            P("ep", "tp", None),
        ),
        out_specs=(P(("parts", "tp"), "ep"), P(("parts", "tp"), "ep")),
        check_vma=False,
    )
```

```python
import functools

import jax
import jax.numpy as jnp
from jax import lax
from jax.experimental import pallas as pl
from jax.experimental.pallas import tpu as pltpu
from jax.sharding import PartitionSpec as P

score_scale = 1.0 / 192.0**0.5
norm_epsilon = 1e-06
MIB = 1 << 20


def attention_kernel(step_rows, lengths, q_hbm, qr_hbm, k_hbm, kr_hbm, up_hbm, out_ref, *scratch):
    q, qr, k, kr, up, rope, latent, sems, key_sems = scratch
    rows = k.shape[0]
    positions, latent_width = k.shape[1:]
    rope_width = kr.shape[1]
    heads = q.shape[0] // rows
    steps = rows // step_rows
    copies = [
        pltpu.make_async_copy(source, target, sems.at[i])
        for i, (source, target) in enumerate(((qr_hbm, qr), (q_hbm, q), (up_hbm, up)))
    ]

    def key_copies(step):
        cut = pl.ds(step * step_rows, step_rows)
        return (
            pltpu.make_async_copy(k_hbm.at[cut], k.at[cut], key_sems.at[0, step]),
            pltpu.make_async_copy(kr_hbm.at[cut], kr.at[cut], key_sems.at[1, step]),
        )

    copies[0].start()
    copies[1].start()
    for step in range(steps):
        for copy in key_copies(step):
            copy.start()
    copies[2].start()

    copies[0].wait()
    lane = lax.broadcasted_iota(jnp.int32, (heads, heads * rope_width), 1)
    head = lax.broadcasted_iota(jnp.int32, (heads, heads * rope_width), 0)
    own = jnp.where(lane // rope_width == head, 1.0, 0.0)
    spread = (qr[...].astype(jnp.float32)[:, None, :] * own[None, :, :]).reshape(rows * heads, heads * rope_width)
    lane = lax.broadcasted_iota(jnp.int32, (heads * rope_width, rope_width), 0)
    column = lax.broadcasted_iota(jnp.int32, (heads * rope_width, rope_width), 1)
    fold = jnp.where(lane % rope_width == column, 1.0, 0.0).astype(jnp.bfloat16)
    rope[...] = jnp.dot(spread.astype(jnp.bfloat16), fold, preferred_element_type=jnp.float32).astype(jnp.bfloat16)
    copies[1].wait()

    place = lax.broadcasted_iota(jnp.int32, (heads, positions), 1)
    lanes = latent.shape[2]

    def score_rows(step):
        scores = []
        for pair in range(step_rows // 2):
            first = step * step_rows + 2 * pair
            cut = slice(first * heads, (first + 2) * heads)
            for r in range(2):
                score = lax.dot_general(
                    q[cut, :], k[first + r], (((1,), (1,)), ((), ())), preferred_element_type=jnp.float32
                )
                score += jnp.dot(rope[cut, :], kr[first + r], preferred_element_type=jnp.float32)
                scores.append(score[r * heads : (r + 1) * heads, :])
        return scores

    def mix_rows(step, probabilities):
        for r in range(step_rows):
            row = step * step_rows + r
            mixed = jnp.dot(probabilities[r], k[row], preferred_element_type=jnp.float32)
            for c in range(latent.shape[0]):
                latent[c, row * heads : (row + 1) * heads, :] = mixed[:, c * lanes : (c + 1) * lanes]

    probabilities = None
    for step in range(steps):
        for copy in key_copies(step):
            copy.wait()
        scores = score_rows(step)
        if step:
            mix_rows(step - 1, probabilities)
        probabilities = []
        for r in range(step_rows):
            visible = place < lengths[step * step_rows + r]
            score = jnp.where(visible, scores[r] * score_scale, -jnp.inf)
            weight = jnp.exp(score - jnp.max(score, axis=-1, keepdims=True))
            total = jnp.sum(weight, axis=-1, keepdims=True)
            probabilities.append((weight / total).astype(jnp.bfloat16))
    mix_rows(steps - 1, probabilities)
    copies[2].wait()
    width = up.shape[2]
    for h in range(heads):
        parts = [latent[c, pl.ds(h, rows, stride=heads), :] for c in range(latent.shape[0])]
        part = jnp.concatenate(parts, axis=1).astype(jnp.bfloat16)
        out_ref[:, h * width : (h + 1) * width] = jnp.dot(
            part, up[h], preferred_element_type=jnp.float32
        ).astype(jnp.bfloat16)


def attend(query_latent, query_rope, cache_latent, cache_rope, cache_length, value_up):
    rows, heads, latent_width = query_latent.shape
    step_rows = 8
    steps = rows // step_rows
    hbm = pl.BlockSpec(memory_space=pltpu.HBM)
    return pl.pallas_call(
        functools.partial(attention_kernel, step_rows),
        out_shape=jax.ShapeDtypeStruct((rows, heads * value_up.shape[2]), jnp.bfloat16),
        in_specs=[pl.BlockSpec(memory_space=pltpu.SMEM)] + [hbm] * 5,
        out_specs=pl.BlockSpec(memory_space=pltpu.VMEM),
        scratch_shapes=[
            pltpu.VMEM((rows * heads, latent_width), jnp.bfloat16),
            pltpu.VMEM(query_rope.shape, jnp.bfloat16),
            pltpu.VMEM(cache_latent.shape, jnp.bfloat16),
            pltpu.VMEM(cache_rope.shape, jnp.bfloat16),
            pltpu.VMEM(value_up.shape, jnp.bfloat16),
            pltpu.VMEM((rows * heads, cache_rope.shape[1]), jnp.bfloat16),
            pltpu.VMEM((latent_width // 128, rows * heads, 128), jnp.float32),
            pltpu.SemaphoreType.DMA((3,)),
            pltpu.SemaphoreType.DMA((2, steps)),
        ],
        cost_estimate=pl.CostEstimate(
            flops=64 * heads * cache_latent.size, bytes_accessed=2 * cache_latent.size, transcendentals=0
        ),
        compiler_params=pltpu.CompilerParams(vmem_limit_bytes=60 * MIB),
        name="attention",
    )(
        cache_length,
        query_latent.reshape(rows * heads, latent_width),
        query_rope,
        cache_latent,
        cache_rope,
        value_up,
    )


def projection_kernel(count, parts, out_count, places, *refs):
    blocks, weight_hbm = refs[:count], refs[count]
    outs, (gathered, weight, sums, result, sems, weight_sems) = refs[-6 - out_count : -6], refs[-6:]
    height = blocks[0].shape[0]
    depth, columns = weight.shape
    step = depth // parts
    weight_copies = [
        pltpu.make_async_copy(
            weight_hbm.at[pl.ds(i * step, step)], weight.at[pl.ds(i * step, step)], weight_sems.at[i]
        )
        for i in range(parts)
    ]
    copies = []
    for k in range(count):
        first = pl.multiple_of(places[k] * height, height)
        copies.append(pltpu.make_async_copy(blocks[k], gathered.at[pl.ds(first, height), :], sems.at[k]))
    for copy in copies + weight_copies:
        copy.start()
    for copy in copies:
        copy.wait()
    tile = 256 if columns % 256 == 0 else 128
    for i in range(parts):
        weight_copies[i].wait()
        rows = slice(i * step, (i + 1) * step)
        for j in range(columns // tile):
            cut = slice(j * tile, (j + 1) * tile)
            product = jnp.dot(gathered[:, rows], weight[rows, cut], preferred_element_type=jnp.float32)
            if i:
                product += sums[:, cut]
            if i < parts - 1:
                sums[:, cut] = product
            else:
                result[:, cut] = product.astype(jnp.bfloat16)
    out_height = outs[0].shape[0]
    for s in range(out_count):
        first = pl.multiple_of(places[count + s] * out_height, out_height)
        outs[s][...] = result[pl.ds(first, out_height), :]


def project(places, blocks, weight, out_count):
    count, parts = len(blocks), 2
    height, depth = blocks[0].shape
    rows, columns = height * count, weight.shape[1]
    return pl.pallas_call(
        functools.partial(projection_kernel, count, parts, out_count),
        out_shape=[jax.ShapeDtypeStruct((rows // out_count, columns), jnp.bfloat16)] * out_count,
        in_specs=[pl.BlockSpec(memory_space=pltpu.SMEM)] + [pl.BlockSpec(memory_space=pl.ANY)] * (count + 1),
        out_specs=[pl.BlockSpec(memory_space=pltpu.VMEM)] * out_count,
        scratch_shapes=[
            pltpu.VMEM((rows, depth), jnp.bfloat16),
            pltpu.VMEM(weight.shape, jnp.bfloat16),
            pltpu.VMEM((rows, columns), jnp.float32),
            pltpu.VMEM((rows, columns), jnp.bfloat16),
            pltpu.SemaphoreType.DMA((count,)),
            pltpu.SemaphoreType.DMA((parts,)),
        ],
        cost_estimate=pl.CostEstimate(flops=2 * rows * depth * columns, bytes_accessed=2 * weight.size, transcendentals=0),
        compiler_params=pltpu.CompilerParams(vmem_limit_bytes=53 * MIB),
        name="projection",
    )(places, *blocks, weight)


def gate_kernel(row_blocks, column_blocks, model_width, places, *refs):
    count = row_blocks * column_blocks
    blocks, gains = refs[:count], refs[count : count + column_blocks]
    gate_hbm, up_hbm = refs[count + column_blocks : count + column_blocks + 2]
    active, x, gate, up, gate_sum, up_sum, sems = refs[-7:]
    height, width = blocks[0].shape
    hidden = gate.shape[2]
    copies = []
    for k in range(column_blocks):
        first = pl.multiple_of(places[k] * width, width)
        copies.append(
            (
                pltpu.make_async_copy(gate_hbm.at[0, pl.ds(first, width), :], gate.at[k], sems.at[0, k]),
                pltpu.make_async_copy(up_hbm.at[0, pl.ds(first, width), :], up.at[k], sems.at[1, k]),
            )
        )
        copies[k][0].start()
        copies[k][1].start()
    squares = [jnp.zeros((height, 1), jnp.float32) for _ in range(row_blocks)]
    tile = min(256, hidden)
    for k in range(column_blocks):
        for s in range(row_blocks):
            wide = blocks[s * column_blocks + k][...].astype(jnp.float32)
            squares[s] += jnp.sum(wide * wide, axis=-1, keepdims=True)
            x[k, s * height : (s + 1) * height, :] = (wide * gains[k][...]).astype(jnp.bfloat16)
        for w, total, weight in ((0, gate_sum, gate), (1, up_sum, up)):
            copies[k][w].wait()
            for j in range(hidden // tile):
                cut = slice(j * tile, (j + 1) * tile)
                product = jnp.dot(x[k], weight[k, :, cut], preferred_element_type=jnp.float32)
                if k == 0:
                    total[:, cut] = product
                else:
                    total[:, cut] += product
    for s in range(row_blocks):
        rows = slice(s * height, (s + 1) * height)
        scale = lax.rsqrt(squares[s] / model_width + norm_epsilon)
        gate_part = gate_sum[rows, :] * scale
        up_part = up_sum[rows, :] * scale
        active[rows, :] = (gate_part / (1.0 + jnp.exp(-gate_part)) * up_part).astype(jnp.bfloat16)


def activate(places, blocks, gains, gate_weight, up_weight, after):
    row_blocks, column_blocks = len(blocks), len(blocks[0])
    height, width = blocks[0][0].shape
    rows = row_blocks * height
    model_width, hidden = gate_weight.shape[1:]
    whole = pl.BlockSpec(memory_space=pltpu.VMEM)
    count = row_blocks * column_blocks
    return pl.pallas_call(
        functools.partial(gate_kernel, row_blocks, column_blocks, model_width),
        out_shape=jax.ShapeDtypeStruct((rows, hidden), jnp.bfloat16),
        in_specs=[pl.BlockSpec(memory_space=pltpu.SMEM)]
        + [whole] * (count + column_blocks)
        + [pl.BlockSpec(memory_space=pl.ANY)] * (2 + len(after)),
        out_specs=whole,
        scratch_shapes=[
            pltpu.VMEM((column_blocks, rows, width), jnp.bfloat16),
            pltpu.VMEM((column_blocks, width, hidden), jnp.bfloat16),
            pltpu.VMEM((column_blocks, width, hidden), jnp.bfloat16),
            pltpu.VMEM((rows, hidden), jnp.float32),
            pltpu.VMEM((rows, hidden), jnp.float32),
            pltpu.SemaphoreType.DMA((2, column_blocks)),
        ],
        cost_estimate=pl.CostEstimate(
            flops=4 * rows * gate_weight.size, bytes_accessed=4 * gate_weight.size, transcendentals=rows * hidden
        ),
        compiler_params=pltpu.CompilerParams(vmem_limit_bytes=49 * MIB),
        name="activate",
    )(places, *[b for row in blocks for b in row], *gains, gate_weight, up_weight, *after)


def down_kernel(row_blocks, column_blocks, cores, places, active, row_weight, down_hbm, *refs):
    outs = refs[-2 - row_blocks * cores : -2]
    down, sems = refs[-2:]
    width = down.shape[2]
    height = active.shape[0] // row_blocks
    order = [b * cores + c for c in reversed(range(cores)) for b in range(column_blocks // cores)]
    copies = {}
    for k in order:
        first = pl.multiple_of(places[k] * width, width)
        copies[k] = pltpu.make_async_copy(down_hbm.at[0, :, pl.ds(first, width)], down.at[k], sems.at[k])
        copies[k].start()
    tile = 256 if width % 256 == 0 else 128
    weights = []
    for s in range(row_blocks):
        first = pl.multiple_of(places[column_blocks + s] * height, height)
        weights.append(row_weight[pl.ds(first, height), :])
    for k in order:
        b, c = k // cores, k % cores
        copies[k].wait()
        for j in range(width // tile):
            cut = slice(j * tile, (j + 1) * tile)
            product = jnp.dot(active[...], down[k, :, cut], preferred_element_type=jnp.float32)
            for s in range(row_blocks):
                part = product[s * height : (s + 1) * height, :] * weights[s]
                outs[s * cores + c][b * height : (b + 1) * height, cut] = part.astype(jnp.bfloat16)


def project_down(places, active, row_weight, down_weight, row_blocks, column_blocks, cores, after):
    rows, hidden = active.shape
    width = down_weight.shape[2] // column_blocks
    whole = pl.BlockSpec(memory_space=pltpu.VMEM)
    out = jax.ShapeDtypeStruct((rows // row_blocks * (column_blocks // cores), width), jnp.bfloat16)
    outs = pl.pallas_call(
        functools.partial(down_kernel, row_blocks, column_blocks, cores),
        out_shape=[out] * (row_blocks * cores),
        in_specs=[pl.BlockSpec(memory_space=pltpu.SMEM)]
        + [whole] * 2
        + [pl.BlockSpec(memory_space=pl.ANY)] * (1 + len(after)),
        out_specs=[whole] * (row_blocks * cores),
        scratch_shapes=[
            pltpu.VMEM((column_blocks, hidden, width), jnp.bfloat16),
            pltpu.SemaphoreType.DMA((column_blocks,)),
        ],
        cost_estimate=pl.CostEstimate(
            flops=2 * rows * down_weight.size, bytes_accessed=2 * down_weight.size, transcendentals=0
        ),
        compiler_params=pltpu.CompilerParams(vmem_limit_bytes=49 * MIB),
        name="down",
    )(places, active, row_weight, down_weight, *after)
    return [outs[s * cores : (s + 1) * cores] for s in range(row_blocks)]


def add_kernel(groups, *refs):
    used = sum(len(g) for g in groups)
    outs = refs[-len(groups) :]
    at = 0
    for group, out in zip(groups, outs):
        total = None
        for first in group:
            value = refs[at][first : first + out.shape[0], :].astype(jnp.float32)
            total = value if total is None else total + value
            at += 1
        out[...] = total.astype(jnp.bfloat16)


def add(groups, height, after=()):
    values = [value for group in groups for value, _ in group]
    width = values[0].shape[1]
    whole = pl.BlockSpec(memory_space=pltpu.VMEM)
    return pl.pallas_call(
        functools.partial(add_kernel, [[first for _, first in group] for group in groups]),
        out_shape=[jax.ShapeDtypeStruct((height, width), jnp.bfloat16)] * len(groups),
        in_specs=[whole] * len(values) + [pl.BlockSpec(memory_space=pl.ANY)] * len(after),
        out_specs=[whole] * len(groups),
        compiler_params=pltpu.CompilerParams(vmem_limit_bytes=8 * MIB),
        name="add",
    )(*values, *after)


def shards(
    query_latent,
    query_rope,
    cache_latent,
    cache_rope,
    cache_length,
    value_up,
    output_weight,
    residual,
    norm_gain,
    routed_experts,
    expert_gates,
    gate_weight,
    up_weight,
    down_weight,
):
    ep_count = lax.axis_size("ep")
    tp_count = lax.axis_size("tp")
    ep_index = lax.axis_index("ep")
    tp_index = lax.axis_index("tp")
    row_total = routed_experts.shape[0]
    block_rows = row_total // tp_count
    cores = 2
    chips = ep_count // cores

    def from_core(value):
        return lax.ppermute(value, "ep", [(i, i ^ 1) for i in range(ep_count)])

    def from_chip(value, back):
        step = cores * back
        return lax.ppermute(value, "ep", [(i, (i + step) % ep_count) for i in range(ep_count)])

    def from_tp(value, bits):
        return lax.ppermute(value, "tp", [(i, i ^ bits) for i in range(tp_count)])

    def gather_ep(value):
        same = [value] + [from_chip(value, b) for b in range(1, chips)]
        other = [from_core(v) for v in same]
        return [v for pair in zip(same, other) for v in pair]

    chip, core = ep_index // cores, ep_index % cores
    ep_places = [
        (chip - b + chips) % chips * cores + (core if c == 0 else 1 - core)
        for b in range(chips)
        for c in range(cores)
    ]
    tp_places = [tp_index ^ k for k in range(tp_count)]
    places = jnp.stack(ep_places + tp_places).astype(jnp.int32)

    gains = gather_ep(norm_gain.reshape(1, -1))
    row_weight = jnp.sum(jnp.where(routed_experts == ep_index, expert_gates, 0.0), axis=-1, keepdims=True)

    head_out = attend(query_latent, query_rope, cache_latent, cache_rope, cache_length, value_up)
    partial = project(places, gather_ep(head_out), output_weight, tp_count)

    own_residual = lax.dynamic_slice_in_dim(residual, tp_index * block_rows, block_rows, 0)
    terms = [[(value, 0)] for value in partial]
    first = []
    for k in reversed(range(1, tp_count)):
        total = terms[k][0][0]
        if len(terms[k]) > 1 or (k == 1 and first):
            (total,) = add([terms[k]], block_rows, first)
        low = k & -k
        arrived = from_tp(total, low)
        terms[k ^ low].append((arrived, 0))
        first = first or [arrived]
    stream_terms = terms[0] + [(own_residual, 0)]
    stream, stream_out = add([stream_terms, stream_terms], block_rows, gains)

    rows_of = {0: stream}
    for k in range(1, tp_count):
        low = k & -k
        rows_of[k] = from_tp(rows_of[k ^ low], low)
    blocks = [gather_ep(rows_of[k]) for k in range(tp_count)]

    half = tp_count // 2
    groups = [list(reversed(range(1, half + 1))), list(reversed(range(half + 1, tp_count))) + [0]]
    terms = [[] for _ in range(tp_count)]
    arrivals = []
    hold_gate, hold_down = blocks[0], [blocks[tp_count - 1][-2]]
    for group in groups:
        chosen = jnp.stack(ep_places + [tp_places[k] for k in group]).astype(jnp.int32)
        active = activate(chosen, [blocks[k] for k in group], gains, gate_weight, up_weight, hold_gate)
        outs = project_down(
            chosen, active, row_weight, down_weight, len(group), ep_count, cores, hold_down
        )
        swapped = [from_core(out[1]) for out in outs]
        for at, k in enumerate(group):
            pair = [[(outs[at][0], c * block_rows), (swapped[at], c * block_rows)] for c in range(chips)]
            wait = arrivals[0] if len(arrivals) == 1 else arrivals[-2] if arrivals else []
            sums = add(pair, block_rows, wait)
            across = [from_chip(sums[c], chips - c) for c in range(1, chips)]
            if not arrivals:
                hold_gate, hold_down = [sums[-1]], across
            arrivals.append(across)
            terms[k] += [(value, 0) for value in [sums[0]] + across]
    for group in groups:
        for k in group:
            if k:
                (total,) = add([terms[k]], block_rows)
                terms[0].append((from_tp(total, k), 0))
    (mixed,) = add([terms[0]], block_rows)
    return (stream_out, mixed)


def solution(mesh):
    return jax.shard_map(
        shards,
        mesh=mesh,
        in_specs=(
            P(("parts", "ep"), "tp", None),
            P(("parts", "ep"), "tp"),
            P(("parts", "ep"), None, None),
            P(("parts", "ep"), None, None),
            P(("parts", "ep")),
            P("tp", None, None),
            P("tp", "ep"),
            P("parts", "ep"),
            P("ep"),
            P("parts", None),
            P("parts", None),
            P("ep", None, "tp"),
            P("ep", None, "tp"),
            P("ep", "tp", None),
        ),
        out_specs=(P(("parts", "tp"), "ep"), P(("parts", "tp"), "ep")),
        check_vma=False,
    )
```

```python
import functools

import jax
import jax.numpy as jnp
from jax import lax
from jax.experimental import pallas as pl
from jax.experimental.pallas import tpu as pltpu
from jax.sharding import PartitionSpec as P

score_scale = 1.0 / 192.0**0.5
norm_epsilon = 1e-06
MIB = 1 << 20


def in_hbm(value):
    return pltpu.with_memory_space_constraint(value, pltpu.HBM)


def in_vmem(value):
    return pltpu.with_memory_space_constraint(value, pltpu.VMEM)


def fetch_kernel(parts, *refs):
    source, target, sems = refs[0], refs[-2], refs[-1]
    step = source.shape[-2] // parts
    copies = []
    for i in range(parts):
        cut = (slice(None),) * (len(source.shape) - 2) + (pl.ds(i * step, step),)
        copies.append(pltpu.make_async_copy(source.at[cut], target.at[cut], sems.at[i]))
    for copy in copies:
        copy.start()
    for copy in copies:
        copy.wait()


def fetch(value, after):
    parts = 4
    return pl.pallas_call(
        functools.partial(fetch_kernel, parts),
        out_shape=pltpu.VMEM(value.shape, value.dtype),
        in_specs=[pl.BlockSpec(memory_space=pl.ANY)] * (1 + len(after)),
        out_specs=pl.BlockSpec(memory_space=pltpu.VMEM),
        scratch_shapes=[pltpu.SemaphoreType.DMA((parts,))],
        cost_estimate=pl.CostEstimate(flops=0, bytes_accessed=4 * value.size, transcendentals=0),
        compiler_params=pltpu.CompilerParams(vmem_limit_bytes=1 * MIB),
        name="fetch",
    )(in_hbm(value), *after)


def attention_kernel(step_rows, lengths, q_ref, qr_ref, k_ref, kr_ref, up_ref, out_ref, latent, rope):
    step = pl.program_id(0)
    heads, positions = q_ref.shape[1], k_ref.shape[1]
    rope_width = kr_ref.shape[1]

    @pl.when(step == 0)
    def _():
        all_rows = qr_ref.shape[0]
        width = heads * rope_width
        lane = lax.broadcasted_iota(jnp.int32, (heads, width), 1)
        head = lax.broadcasted_iota(jnp.int32, (heads, width), 0)
        own = jnp.where(lane // rope_width == head, 1.0, 0.0)
        spread = qr_ref[...].astype(jnp.float32)[:, None, :] * own[None, :, :]
        spread = spread.reshape(all_rows * heads, width).astype(jnp.bfloat16)
        lane = lax.broadcasted_iota(jnp.int32, (width, rope_width), 0)
        column = lax.broadcasted_iota(jnp.int32, (width, rope_width), 1)
        fold = jnp.where(lane % rope_width == column, 1.0, 0.0).astype(jnp.bfloat16)
        rope[...] = jnp.dot(spread, fold, preferred_element_type=jnp.float32)

    place = lax.broadcasted_iota(jnp.int32, (heads, positions), 1)
    lanes = latent.shape[2]
    lanes = latent.shape[2]
    scores = []
    for r in range(step_rows):
        first = pl.multiple_of((step * step_rows + r) * heads, heads)
        score = lax.dot_general(
            q_ref[r], k_ref[r], (((1,), (1,)), ((), ())), preferred_element_type=jnp.float32
        )
        score += jnp.dot(
            rope[pl.ds(first, heads), :].astype(jnp.bfloat16), kr_ref[r], preferred_element_type=jnp.float32
        )
        scores.append(score)
    probabilities = []
    for r in range(step_rows):
        visible = place < lengths[step * step_rows + r]
        score = jnp.where(visible, scores[r] * score_scale, -jnp.inf)
        weight = jnp.exp(score - jnp.max(score, axis=-1, keepdims=True))
        total = jnp.sum(weight, axis=-1, keepdims=True)
        probabilities.append((weight / total).astype(jnp.bfloat16))
    for r in range(step_rows):
        first = pl.multiple_of((step * step_rows + r) * heads, heads)
        mixed = jnp.dot(probabilities[r], k_ref[r], preferred_element_type=jnp.float32)
        for c in range(latent.shape[0]):
            latent[c, pl.ds(first, heads), :] = mixed[:, c * lanes : (c + 1) * lanes]

    @pl.when(step == pl.num_programs(0) - 1)
    def _():
        rows = out_ref.shape[0]
        width = up_ref.shape[2]
        for h in range(heads):
            parts = [latent[c, pl.ds(h, rows, stride=heads), :] for c in range(latent.shape[0])]
            part = jnp.concatenate(parts, axis=1).astype(jnp.bfloat16)
            out_ref[:, h * width : (h + 1) * width] = jnp.dot(
                part, up_ref[h], preferred_element_type=jnp.float32
            ).astype(jnp.bfloat16)


def attend(query_latent, query_rope, cache_latent, cache_rope, cache_length, value_up):
    rows, heads, latent_width = query_latent.shape
    positions = cache_latent.shape[1]
    rope_width = cache_rope.shape[1]
    value_width = value_up.shape[2]
    step_rows = 16
    by_row = lambda i, lengths: (i, 0, 0)
    return pl.pallas_call(
        functools.partial(attention_kernel, step_rows),
        out_shape=jax.ShapeDtypeStruct((rows, heads * value_width), jnp.bfloat16),
        grid_spec=pltpu.PrefetchScalarGridSpec(
            num_scalar_prefetch=1,
            grid=(rows // step_rows,),
            in_specs=[
                pl.BlockSpec((step_rows, heads, latent_width), by_row),
                pl.BlockSpec(query_rope.shape, lambda i, lengths: (0, 0)),
                pl.BlockSpec((step_rows, positions, latent_width), by_row),
                pl.BlockSpec((step_rows, rope_width, positions), by_row),
                pl.BlockSpec(value_up.shape, lambda i, lengths: (0, 0, 0)),
            ],
            out_specs=pl.BlockSpec((rows, heads * value_width), lambda i, lengths: (0, 0)),
            scratch_shapes=[
                pltpu.VMEM((latent_width // 128, rows * heads, 128), jnp.float32),
                pltpu.VMEM((rows * heads, rope_width), jnp.float32),
            ],
        ),
        cost_estimate=pl.CostEstimate(
            flops=64 * heads * cache_latent.size, bytes_accessed=2 * cache_latent.size, transcendentals=0
        ),
        compiler_params=pltpu.CompilerParams(vmem_limit_bytes=20 * MIB),
        name="attention",
    )(
        cache_length,
        in_hbm(query_latent),
        in_hbm(query_rope),
        in_hbm(cache_latent),
        in_hbm(cache_rope),
        in_hbm(value_up),
    )


def projection_kernel(count, out_count, places, *refs):
    blocks, weight, outs = refs[:count], refs[count], refs[-2 - out_count : -2]
    gathered, result = refs[-2:]
    height = blocks[0].shape[0]
    for k in range(count):
        first = pl.multiple_of(places[k] * height, height)
        gathered[pl.ds(first, height), :] = blocks[k][...]
    columns = weight.shape[1]
    tile = 256 if columns % 256 == 0 else 128
    for j in range(columns // tile):
        result[:, j * tile : (j + 1) * tile] = jnp.dot(
            gathered[...], weight[:, j * tile : (j + 1) * tile], preferred_element_type=jnp.float32
        ).astype(jnp.bfloat16)
    out_height = outs[0].shape[0]
    for s in range(len(outs)):
        first = pl.multiple_of(places[count + s] * out_height, out_height)
        outs[s][...] = result[pl.ds(first, out_height), :]


def project(places, blocks, weight, out_count):
    count = len(blocks)
    height, depth = blocks[0].shape
    rows, columns = height * count, weight.shape[1]
    whole = pl.BlockSpec(memory_space=pltpu.VMEM)
    return pl.pallas_call(
        functools.partial(projection_kernel, count, out_count),
        out_shape=[jax.ShapeDtypeStruct((rows // out_count, columns), jnp.bfloat16)] * out_count,
        in_specs=[pl.BlockSpec(memory_space=pltpu.SMEM)] + [whole] * (count + 1),
        out_specs=[whole] * out_count,
        scratch_shapes=[
            pltpu.VMEM((rows, depth), jnp.bfloat16),
            pltpu.VMEM((rows, columns), jnp.bfloat16),
        ],
        cost_estimate=pl.CostEstimate(flops=2 * rows * depth * columns, bytes_accessed=4 * MIB, transcendentals=0),
        compiler_params=pltpu.CompilerParams(vmem_limit_bytes=8 * MIB),
        name="projection",
    )(places, *blocks, in_vmem(weight))


def gate_kernel(row_blocks, column_blocks, model_width, places, *refs):
    count = row_blocks * column_blocks
    blocks, gains = refs[:count], refs[count : count + column_blocks]
    gate, up = refs[count + column_blocks : count + column_blocks + 2]
    active, x, gate_sum, up_sum = refs[-4:]
    height, width = blocks[0].shape
    hidden = gate.shape[2]
    squares = [jnp.zeros((height, 1), jnp.float32) for _ in range(row_blocks)]
    tile = min(256, hidden)
    for k in range(column_blocks):
        for s in range(row_blocks):
            wide = blocks[s * column_blocks + k][...].astype(jnp.float32)
            squares[s] += jnp.sum(wide * wide, axis=-1, keepdims=True)
            x[k, s * height : (s + 1) * height, :] = (wide * gains[k][...]).astype(jnp.bfloat16)
        depth = pl.ds(pl.multiple_of(places[k] * width, 128), width)
        for total, weight in ((gate_sum, gate), (up_sum, up)):
            for j in range(hidden // tile):
                cut = slice(j * tile, (j + 1) * tile)
                product = jnp.dot(x[k], weight[0, depth, cut], preferred_element_type=jnp.float32)
                if k == 0:
                    total[:, cut] = product
                else:
                    total[:, cut] += product
    for s in range(row_blocks):
        rows = slice(s * height, (s + 1) * height)
        scale = lax.rsqrt(squares[s] / model_width + norm_epsilon)
        gate_part = gate_sum[rows, :] * scale
        up_part = up_sum[rows, :] * scale
        active[rows, :] = (gate_part / (1.0 + jnp.exp(-gate_part)) * up_part).astype(jnp.bfloat16)


def activate(places, blocks, gains, gate_weight, up_weight, after):
    row_blocks, column_blocks = len(blocks), len(blocks[0])
    height, width = blocks[0][0].shape
    rows = row_blocks * height
    model_width, hidden = gate_weight.shape[1:]
    whole = pl.BlockSpec(memory_space=pltpu.VMEM)
    count = row_blocks * column_blocks
    return pl.pallas_call(
        functools.partial(gate_kernel, row_blocks, column_blocks, model_width),
        out_shape=jax.ShapeDtypeStruct((rows, hidden), jnp.bfloat16),
        in_specs=[pl.BlockSpec(memory_space=pltpu.SMEM)]
        + [whole] * (count + column_blocks + 2)
        + [pl.BlockSpec(memory_space=pl.ANY)] * len(after),
        out_specs=whole,
        scratch_shapes=[
            pltpu.VMEM((column_blocks, rows, width), jnp.bfloat16),
            pltpu.VMEM((rows, hidden), jnp.float32),
            pltpu.VMEM((rows, hidden), jnp.float32),
        ],
        cost_estimate=pl.CostEstimate(
            flops=4 * rows * gate_weight.size, bytes_accessed=4 * gate_weight.size, transcendentals=rows * hidden
        ),
        compiler_params=pltpu.CompilerParams(vmem_limit_bytes=2 * rows * (model_width + 4 * hidden) + 4 * MIB),
        name="activate",
    )(places, *[b for row in blocks for b in row], *gains, in_vmem(gate_weight), in_vmem(up_weight), *after)


def down_kernel(row_blocks, column_blocks, cores, places, active, row_weight, down, *refs):
    outs = refs[-row_blocks * cores :]
    width = down.shape[2] // column_blocks
    height = active.shape[0] // row_blocks
    order = [b * cores + c for c in reversed(range(cores)) for b in range(column_blocks // cores)]
    tile = 256 if width % 256 == 0 else 128
    weights = []
    for s in range(row_blocks):
        first = pl.multiple_of(places[column_blocks + s] * height, height)
        weights.append(row_weight[pl.ds(first, height), :])
    for k in order:
        b, c = k // cores, k % cores
        start = pl.multiple_of(places[k] * width, 128)
        for j in range(width // tile):
            cut = slice(j * tile, (j + 1) * tile)
            product = jnp.dot(
                active[...], down[0, :, pl.ds(start + j * tile, tile)], preferred_element_type=jnp.float32
            )
            for s in range(row_blocks):
                part = product[s * height : (s + 1) * height, :] * weights[s]
                outs[s * cores + c][b * height : (b + 1) * height, cut] = part.astype(jnp.bfloat16)


def project_down(places, active, row_weight, down_weight, row_blocks, column_blocks, cores, after):
    rows, hidden = active.shape
    width = down_weight.shape[2] // column_blocks
    whole = pl.BlockSpec(memory_space=pltpu.VMEM)
    out = jax.ShapeDtypeStruct((rows // row_blocks * (column_blocks // cores), width), jnp.bfloat16)
    outs = pl.pallas_call(
        functools.partial(down_kernel, row_blocks, column_blocks, cores),
        out_shape=[out] * (row_blocks * cores),
        in_specs=[pl.BlockSpec(memory_space=pltpu.SMEM)]
        + [whole] * 3
        + [pl.BlockSpec(memory_space=pl.ANY)] * len(after),
        out_specs=[whole] * (row_blocks * cores),
        cost_estimate=pl.CostEstimate(
            flops=2 * rows * down_weight.size, bytes_accessed=2 * down_weight.size, transcendentals=0
        ),
        compiler_params=pltpu.CompilerParams(vmem_limit_bytes=4 * MIB),
        name="down",
    )(places, active, row_weight, in_vmem(down_weight), *after)
    return [outs[s * cores : (s + 1) * cores] for s in range(row_blocks)]


def add_kernel(groups, *refs):
    used = sum(len(g) for g in groups)
    outs = refs[-len(groups) :]
    at = 0
    for group, out in zip(groups, outs):
        total = None
        for first in group:
            value = refs[at][first : first + out.shape[0], :].astype(jnp.float32)
            total = value if total is None else total + value
            at += 1
        out[...] = total.astype(jnp.bfloat16)


def add(groups, height, after=()):
    values = [value for group in groups for value, _ in group]
    width = values[0].shape[1]
    whole = pl.BlockSpec(memory_space=pltpu.VMEM)
    return pl.pallas_call(
        functools.partial(add_kernel, [[first for _, first in group] for group in groups]),
        out_shape=[jax.ShapeDtypeStruct((height, width), jnp.bfloat16)] * len(groups),
        in_specs=[whole] * len(values) + [pl.BlockSpec(memory_space=pl.ANY)] * len(after),
        out_specs=[whole] * len(groups),
        compiler_params=pltpu.CompilerParams(vmem_limit_bytes=8 * MIB),
        name="add",
    )(*values, *after)


def shards(
    query_latent,
    query_rope,
    cache_latent,
    cache_rope,
    cache_length,
    value_up,
    output_weight,
    residual,
    norm_gain,
    routed_experts,
    expert_gates,
    gate_weight,
    up_weight,
    down_weight,
):
    ep_count = lax.axis_size("ep")
    tp_count = lax.axis_size("tp")
    ep_index = lax.axis_index("ep")
    tp_index = lax.axis_index("tp")
    row_total = routed_experts.shape[0]
    block_rows = row_total // tp_count
    cores = 2
    chips = ep_count // cores

    def from_core(value):
        return lax.ppermute(value, "ep", [(i, i ^ 1) for i in range(ep_count)])

    def from_chip(value, back):
        step = cores * back
        return lax.ppermute(value, "ep", [(i, (i + step) % ep_count) for i in range(ep_count)])

    def from_tp(value, bits):
        return lax.ppermute(value, "tp", [(i, i ^ bits) for i in range(tp_count)])

    def gather_ep(value):
        same = [value] + [from_chip(value, b) for b in range(1, chips)]
        other = [from_core(v) for v in same]
        return [v for pair in zip(same, other) for v in pair]

    chip, core = ep_index // cores, ep_index % cores
    ep_places = [
        (chip - b + chips) % chips * cores + (core if c == 0 else 1 - core)
        for b in range(chips)
        for c in range(cores)
    ]
    tp_places = [tp_index ^ k for k in range(tp_count)]
    places = jnp.stack(ep_places + tp_places).astype(jnp.int32)

    gains = gather_ep(norm_gain.reshape(1, -1))
    row_weight = jnp.sum(jnp.where(routed_experts == ep_index, expert_gates, 0.0), axis=-1, keepdims=True)

    head_out = attend(query_latent, query_rope, cache_latent, cache_rope, cache_length, value_up)
    output_weight = fetch(output_weight, [head_out])
    partial = project(places, gather_ep(head_out), output_weight, tp_count)

    own_residual = lax.dynamic_slice_in_dim(residual, tp_index * block_rows, block_rows, 0)
    gate_weight = fetch(gate_weight, [partial[0]])
    terms = [[(value, 0)] for value in partial]
    first = []
    for k in reversed(range(1, tp_count)):
        total = terms[k][0][0]
        if len(terms[k]) > 1 or (k == 1 and first):
            (total,) = add([terms[k]], block_rows, first)
        low = k & -k
        arrived = from_tp(total, low)
        terms[k ^ low].append((arrived, 0))
        first = [total] if first else [arrived]
    up_weight = fetch(up_weight, [total])
    down_weight = fetch(down_weight, [total])
    stream_terms = terms[0] + [(own_residual, 0)]
    stream, stream_out = add([stream_terms, stream_terms], block_rows, gains + [gate_weight, up_weight, down_weight])

    rows_of = {0: stream}
    for k in range(1, tp_count):
        low = k & -k
        rows_of[k] = from_tp(rows_of[k ^ low], low)
    blocks = [gather_ep(rows_of[k]) for k in range(tp_count)]

    half = tp_count // 2
    groups = [list(reversed(range(1, half + 1))), list(reversed(range(half + 1, tp_count))) + [0]]
    terms = [[] for _ in range(tp_count)]
    arrivals = []
    hold_gate, hold_down = blocks[0], [blocks[tp_count - 1][-2]]
    for group in groups:
        chosen = jnp.stack(ep_places + [tp_places[k] for k in group]).astype(jnp.int32)
        active = activate(chosen, [blocks[k] for k in group], gains, gate_weight, up_weight, hold_gate)
        outs = project_down(
            chosen, active, row_weight, down_weight, len(group), ep_count, cores, hold_down
        )
        swapped = [from_core(out[1]) for out in outs]
        for at, k in enumerate(group):
            pair = [[(outs[at][0], c * block_rows), (swapped[at], c * block_rows)] for c in range(chips)]
            wait = arrivals[0] if len(arrivals) == 1 else arrivals[-2] if arrivals else []
            sums = add(pair, block_rows, wait)
            across = [from_chip(sums[c], chips - c) for c in range(1, chips)]
            if not arrivals:
                hold_gate, hold_down = [sums[-1]], across
            arrivals.append(across)
            terms[k] += [(value, 0) for value in [sums[0]] + across]
    for group in groups:
        for k in group:
            if k:
                (total,) = add([terms[k]], block_rows)
                terms[0].append((from_tp(total, k), 0))
    (mixed,) = add([terms[0]], block_rows)
    return (stream_out, mixed)


def solution(mesh):
    return jax.shard_map(
        shards,
        mesh=mesh,
        in_specs=(
            P(("parts", "ep"), "tp", None),
            P(("parts", "ep"), "tp"),
            P(("parts", "ep"), None, None),
            P(("parts", "ep"), None, None),
            P(("parts", "ep")),
            P("tp", None, None),
            P("tp", "ep"),
            P("parts", "ep"),
            P("ep"),
            P("parts", None),
            P("parts", None),
            P("ep", None, "tp"),
            P("ep", None, "tp"),
            P("ep", "tp", None),
        ),
        out_specs=(P(("parts", "tp"), "ep"), P(("parts", "tp"), "ep")),
        check_vma=False,
    )
```

```python
import functools

import jax
import jax.numpy as jnp
from jax import lax
from jax.experimental import pallas as pl
from jax.experimental.pallas import tpu as pltpu
from jax.sharding import PartitionSpec as P

score_scale = 1.0 / 192.0**0.5
norm_epsilon = 1e-06
MIB = 1 << 20


def in_hbm(value):
    return pltpu.with_memory_space_constraint(value, pltpu.HBM)


def in_vmem(value):
    return pltpu.with_memory_space_constraint(value, pltpu.VMEM)


def fetch_kernel(parts, *refs):
    source, target, sems = refs[0], refs[-2], refs[-1]
    step = source.shape[-2] // parts
    copies = []
    for i in range(parts):
        cut = (slice(None),) * (len(source.shape) - 2) + (pl.ds(i * step, step),)
        copies.append(pltpu.make_async_copy(source.at[cut], target.at[cut], sems.at[i]))
    for copy in copies:
        copy.start()
    for copy in copies:
        copy.wait()


def fetch(value, after):
    parts = 4
    return pl.pallas_call(
        functools.partial(fetch_kernel, parts),
        out_shape=pltpu.VMEM(value.shape, value.dtype),
        in_specs=[pl.BlockSpec(memory_space=pl.ANY)] * (1 + len(after)),
        out_specs=pl.BlockSpec(memory_space=pltpu.VMEM),
        scratch_shapes=[pltpu.SemaphoreType.DMA((parts,))],
        cost_estimate=pl.CostEstimate(flops=0, bytes_accessed=4 * value.size, transcendentals=0),
        compiler_params=pltpu.CompilerParams(vmem_limit_bytes=1 * MIB),
        name="fetch",
    )(in_hbm(value), *after)


def attention_kernel(step_rows, lengths, q_ref, qr_ref, k_ref, kr_ref, up_ref, *refs):
    out_ref, latent, rope = refs[-3:]
    step = pl.program_id(0)
    heads, positions = q_ref.shape[1], k_ref.shape[1]
    rope_width = kr_ref.shape[1]

    @pl.when(step == 0)
    def _():
        all_rows = qr_ref.shape[0]
        width = heads * rope_width
        lane = lax.broadcasted_iota(jnp.int32, (heads, width), 1)
        head = lax.broadcasted_iota(jnp.int32, (heads, width), 0)
        own = jnp.where(lane // rope_width == head, 1.0, 0.0)
        spread = qr_ref[...].astype(jnp.float32)[:, None, :] * own[None, :, :]
        spread = spread.reshape(all_rows * heads, width).astype(jnp.bfloat16)
        lane = lax.broadcasted_iota(jnp.int32, (width, rope_width), 0)
        column = lax.broadcasted_iota(jnp.int32, (width, rope_width), 1)
        fold = jnp.where(lane % rope_width == column, 1.0, 0.0).astype(jnp.bfloat16)
        rope[...] = jnp.dot(spread, fold, preferred_element_type=jnp.float32)

    place = lax.broadcasted_iota(jnp.int32, (heads, positions), 1)
    lanes = latent.shape[2]
    lanes = latent.shape[2]
    scores = []
    for r in range(step_rows):
        first = pl.multiple_of((step * step_rows + r) * heads, heads)
        score = lax.dot_general(
            q_ref[r], k_ref[r], (((1,), (1,)), ((), ())), preferred_element_type=jnp.float32
        )
        score += jnp.dot(
            rope[pl.ds(first, heads), :].astype(jnp.bfloat16), kr_ref[r], preferred_element_type=jnp.float32
        )
        scores.append(score)
    probabilities = []
    for r in range(step_rows):
        visible = place < lengths[step * step_rows + r]
        score = jnp.where(visible, scores[r] * score_scale, -jnp.inf)
        weight = jnp.exp(score - jnp.max(score, axis=-1, keepdims=True))
        total = jnp.sum(weight, axis=-1, keepdims=True)
        probabilities.append((weight / total).astype(jnp.bfloat16))
    for r in range(step_rows):
        first = pl.multiple_of((step * step_rows + r) * heads, heads)
        mixed = jnp.dot(probabilities[r], k_ref[r], preferred_element_type=jnp.float32)
        for c in range(latent.shape[0]):
            latent[c, pl.ds(first, heads), :] = mixed[:, c * lanes : (c + 1) * lanes]

    @pl.when(step == pl.num_programs(0) - 1)
    def _():
        rows = out_ref.shape[0]
        width = up_ref.shape[2]
        for h in range(heads):
            parts = [latent[c, pl.ds(h, rows, stride=heads), :] for c in range(latent.shape[0])]
            part = jnp.concatenate(parts, axis=1).astype(jnp.bfloat16)
            out_ref[:, h * width : (h + 1) * width] = jnp.dot(
                part, up_ref[h], preferred_element_type=jnp.float32
            ).astype(jnp.bfloat16)


def attend(query_latent, query_rope, cache_latent, cache_rope, cache_length, value_up, after):
    rows, heads, latent_width = query_latent.shape
    positions = cache_latent.shape[1]
    rope_width = cache_rope.shape[1]
    value_width = value_up.shape[2]
    step_rows = 16
    by_row = lambda i, lengths: (i, 0, 0)
    return pl.pallas_call(
        functools.partial(attention_kernel, step_rows),
        out_shape=jax.ShapeDtypeStruct((rows, heads * value_width), jnp.bfloat16),
        grid_spec=pltpu.PrefetchScalarGridSpec(
            num_scalar_prefetch=1,
            grid=(rows // step_rows,),
            in_specs=[
                pl.BlockSpec((step_rows, heads, latent_width), by_row),
                pl.BlockSpec(query_rope.shape, lambda i, lengths: (0, 0)),
                pl.BlockSpec((step_rows, positions, latent_width), by_row),
                pl.BlockSpec((step_rows, rope_width, positions), by_row),
                pl.BlockSpec(value_up.shape, lambda i, lengths: (0, 0, 0)),
            ]
            + [pl.BlockSpec(memory_space=pl.ANY)] * len(after),
            out_specs=pl.BlockSpec((rows, heads * value_width), lambda i, lengths: (0, 0)),
            scratch_shapes=[
                pltpu.VMEM((latent_width // 128, rows * heads, 128), jnp.float32),
                pltpu.VMEM((rows * heads, rope_width), jnp.float32),
            ],
        ),
        cost_estimate=pl.CostEstimate(
            flops=64 * heads * cache_latent.size, bytes_accessed=2 * cache_latent.size, transcendentals=0
        ),
        compiler_params=pltpu.CompilerParams(vmem_limit_bytes=20 * MIB),
        name="attention",
    )(
        cache_length,
        in_hbm(query_latent),
        in_hbm(query_rope),
        in_hbm(cache_latent),
        in_hbm(cache_rope),
        in_hbm(value_up),
        *after,
    )


def projection_kernel(count, out_count, places, *refs):
    blocks, weight, outs = refs[:count], refs[count], refs[-2 - out_count : -2]
    gathered, result = refs[-2:]
    height = blocks[0].shape[0]
    for k in range(count):
        first = pl.multiple_of(places[k] * height, height)
        gathered[pl.ds(first, height), :] = blocks[k][...]
    columns = weight.shape[1]
    tile = 256 if columns % 256 == 0 else 128
    for j in range(columns // tile):
        result[:, j * tile : (j + 1) * tile] = jnp.dot(
            gathered[...], weight[:, j * tile : (j + 1) * tile], preferred_element_type=jnp.float32
        ).astype(jnp.bfloat16)
    out_height = outs[0].shape[0]
    for s in range(len(outs)):
        first = pl.multiple_of(places[count + s] * out_height, out_height)
        outs[s][...] = result[pl.ds(first, out_height), :]


def project(places, blocks, weight, out_count):
    count = len(blocks)
    height, depth = blocks[0].shape
    rows, columns = height * count, weight.shape[1]
    whole = pl.BlockSpec(memory_space=pltpu.VMEM)
    return pl.pallas_call(
        functools.partial(projection_kernel, count, out_count),
        out_shape=[jax.ShapeDtypeStruct((rows // out_count, columns), jnp.bfloat16)] * out_count,
        in_specs=[pl.BlockSpec(memory_space=pltpu.SMEM)] + [whole] * (count + 1),
        out_specs=[whole] * out_count,
        scratch_shapes=[
            pltpu.VMEM((rows, depth), jnp.bfloat16),
            pltpu.VMEM((rows, columns), jnp.bfloat16),
        ],
        cost_estimate=pl.CostEstimate(flops=2 * rows * depth * columns, bytes_accessed=4 * MIB, transcendentals=0),
        compiler_params=pltpu.CompilerParams(vmem_limit_bytes=8 * MIB),
        name="projection",
    )(places, *blocks, in_vmem(weight))


def gate_kernel(row_blocks, column_blocks, model_width, places, *refs):
    count = row_blocks * column_blocks
    blocks, gains = refs[:count], refs[count : count + column_blocks]
    gate, up = refs[count + column_blocks : count + column_blocks + 2]
    active, x, gate_sum, up_sum = refs[-4:]
    height, width = blocks[0].shape
    hidden = gate.shape[2]
    squares = [jnp.zeros((height, 1), jnp.float32) for _ in range(row_blocks)]
    tile = min(256, hidden)
    for k in range(column_blocks):
        for s in range(row_blocks):
            wide = blocks[s * column_blocks + k][...].astype(jnp.float32)
            squares[s] += jnp.sum(wide * wide, axis=-1, keepdims=True)
            x[k, s * height : (s + 1) * height, :] = (wide * gains[k][...]).astype(jnp.bfloat16)
        depth = pl.ds(pl.multiple_of(places[k] * width, 128), width)
        for total, weight in ((gate_sum, gate), (up_sum, up)):
            for j in range(hidden // tile):
                cut = slice(j * tile, (j + 1) * tile)
                product = jnp.dot(x[k], weight[0, depth, cut], preferred_element_type=jnp.float32)
                if k == 0:
                    total[:, cut] = product
                else:
                    total[:, cut] += product
    for s in range(row_blocks):
        rows = slice(s * height, (s + 1) * height)
        scale = lax.rsqrt(squares[s] / model_width + norm_epsilon)
        gate_part = gate_sum[rows, :] * scale
        up_part = up_sum[rows, :] * scale
        active[rows, :] = (gate_part / (1.0 + jnp.exp(-gate_part)) * up_part).astype(jnp.bfloat16)


def activate(places, blocks, gains, gate_weight, up_weight, after):
    row_blocks, column_blocks = len(blocks), len(blocks[0])
    height, width = blocks[0][0].shape
    rows = row_blocks * height
    model_width, hidden = gate_weight.shape[1:]
    whole = pl.BlockSpec(memory_space=pltpu.VMEM)
    count = row_blocks * column_blocks
    return pl.pallas_call(
        functools.partial(gate_kernel, row_blocks, column_blocks, model_width),
        out_shape=jax.ShapeDtypeStruct((rows, hidden), jnp.bfloat16),
        in_specs=[pl.BlockSpec(memory_space=pltpu.SMEM)]
        + [whole] * (count + column_blocks + 2)
        + [pl.BlockSpec(memory_space=pl.ANY)] * len(after),
        out_specs=whole,
        scratch_shapes=[
            pltpu.VMEM((column_blocks, rows, width), jnp.bfloat16),
            pltpu.VMEM((rows, hidden), jnp.float32),
            pltpu.VMEM((rows, hidden), jnp.float32),
        ],
        cost_estimate=pl.CostEstimate(
            flops=4 * rows * gate_weight.size, bytes_accessed=4 * gate_weight.size, transcendentals=rows * hidden
        ),
        compiler_params=pltpu.CompilerParams(vmem_limit_bytes=2 * rows * (model_width + 4 * hidden) + 4 * MIB),
        name="activate",
    )(places, *[b for row in blocks for b in row], *gains, in_vmem(gate_weight), in_vmem(up_weight), *after)


def down_kernel(slots, column_blocks, cores, places, active, row_weight, down, *refs):
    row_blocks = len(slots)
    outs = refs[-row_blocks * cores :]
    width = down.shape[2] // column_blocks
    height = active.shape[0] // row_blocks
    order = [b * cores + c for c in reversed(range(cores)) for b in range(column_blocks // cores)]
    tile = 256 if width % 256 == 0 else 128
    weights = []
    for s in range(row_blocks):
        first = pl.multiple_of(places[column_blocks + slots[s]] * height, height)
        weights.append(row_weight[pl.ds(first, height), :])
    for k in order:
        b, c = k // cores, k % cores
        start = pl.multiple_of(places[k] * width, 128)
        for j in range(width // tile):
            cut = slice(j * tile, (j + 1) * tile)
            product = jnp.dot(
                active[...], down[0, :, pl.ds(start + j * tile, tile)], preferred_element_type=jnp.float32
            )
            for s in range(row_blocks):
                part = product[s * height : (s + 1) * height, :] * weights[s]
                outs[s * cores + c][b * height : (b + 1) * height, cut] = part.astype(jnp.bfloat16)


def project_down(places, active, row_weight, down_weight, slots, column_blocks, cores, after):
    row_blocks = len(slots)
    rows, hidden = active.shape
    width = down_weight.shape[2] // column_blocks
    whole = pl.BlockSpec(memory_space=pltpu.VMEM)
    out = jax.ShapeDtypeStruct((rows // row_blocks * (column_blocks // cores), width), jnp.bfloat16)
    outs = pl.pallas_call(
        functools.partial(down_kernel, slots, column_blocks, cores),
        out_shape=[out] * (row_blocks * cores),
        in_specs=[pl.BlockSpec(memory_space=pltpu.SMEM)]
        + [whole] * 3
        + [pl.BlockSpec(memory_space=pl.ANY)] * len(after),
        out_specs=[whole] * (row_blocks * cores),
        cost_estimate=pl.CostEstimate(
            flops=2 * rows * down_weight.size, bytes_accessed=2 * down_weight.size, transcendentals=0
        ),
        compiler_params=pltpu.CompilerParams(vmem_limit_bytes=4 * MIB),
        name="down",
    )(places, active, row_weight, in_vmem(down_weight), *after)
    return [outs[s * cores : (s + 1) * cores] for s in range(row_blocks)]


def add_kernel(groups, *refs):
    used = sum(len(g) for g in groups)
    outs = refs[-len(groups) :]
    at = 0
    for group, out in zip(groups, outs):
        total = None
        for first in group:
            value = refs[at][first : first + out.shape[0], :].astype(jnp.float32)
            total = value if total is None else total + value
            at += 1
        out[...] = total.astype(jnp.bfloat16)


def add(groups, height, after=()):
    values = [value for group in groups for value, _ in group]
    width = values[0].shape[1]
    whole = pl.BlockSpec(memory_space=pltpu.VMEM)
    return pl.pallas_call(
        functools.partial(add_kernel, [[first for _, first in group] for group in groups]),
        out_shape=[jax.ShapeDtypeStruct((height, width), jnp.bfloat16)] * len(groups),
        in_specs=[whole] * len(values) + [pl.BlockSpec(memory_space=pl.ANY)] * len(after),
        out_specs=[whole] * len(groups),
        compiler_params=pltpu.CompilerParams(vmem_limit_bytes=8 * MIB),
        name="add",
    )(*values, *after)


def shards(
    query_latent,
    query_rope,
    cache_latent,
    cache_rope,
    cache_length,
    value_up,
    output_weight,
    residual,
    norm_gain,
    routed_experts,
    expert_gates,
    gate_weight,
    up_weight,
    down_weight,
):
    ep_count = lax.axis_size("ep")
    tp_count = lax.axis_size("tp")
    ep_index = lax.axis_index("ep")
    tp_index = lax.axis_index("tp")
    row_total = routed_experts.shape[0]
    block_rows = row_total // tp_count
    cores = 2
    chips = ep_count // cores

    def from_core(value):
        return lax.ppermute(value, "ep", [(i, i ^ 1) for i in range(ep_count)])

    def from_chip(value, back):
        step = cores * back
        return lax.ppermute(value, "ep", [(i, (i + step) % ep_count) for i in range(ep_count)])

    def from_tp(value, bits):
        return lax.ppermute(value, "tp", [(i, i ^ bits) for i in range(tp_count)])

    def gather_ep(value):
        same = [value] + [from_chip(value, b) for b in range(1, chips)]
        other = [from_core(v) for v in same]
        return [v for pair in zip(same, other) for v in pair]

    chip, core = ep_index // cores, ep_index % cores
    ep_places = [
        (chip - b + chips) % chips * cores + (core if c == 0 else 1 - core)
        for b in range(chips)
        for c in range(cores)
    ]
    tp_places = [tp_index ^ k for k in range(tp_count)]
    places = jnp.stack(ep_places + tp_places).astype(jnp.int32)

    gain = norm_gain.reshape(1, -1)
    gains = gather_ep(gain)
    own_residual = lax.dynamic_slice_in_dim(residual, tp_index * block_rows, block_rows, 0)
    row_weight = jnp.sum(jnp.where(routed_experts == ep_index, expert_gates, 0.0), axis=-1, keepdims=True)

    head_out = attend(query_latent, query_rope, cache_latent, cache_rope, cache_length, value_up, [places])
    output_weight = fetch(output_weight, [head_out, row_weight, own_residual, gain])
    partial = project(places, gather_ep(head_out), output_weight, tp_count)

    gate_weight = fetch(gate_weight, [partial[0]])
    terms = [[(value, 0)] for value in partial]
    for k in reversed(range(1, tp_count)):
        total = terms[k][0][0]
        if len(terms[k]) > 1 or k == 1:
            (total,) = add([terms[k]], block_rows, [gate_weight] if k == 1 else [])
        low = k & -k
        arrived = from_tp(total, low)
        terms[k ^ low].append((arrived, 0))
    up_weight = fetch(up_weight, [total])
    down_weight = fetch(down_weight, [total])
    stream_terms = terms[0] + [(own_residual, 0)]
    stream, stream_out = add([stream_terms, stream_terms], block_rows, gains + [gate_weight, up_weight, down_weight])

    rows_of = {0: stream}
    for k in range(1, tp_count):
        low = k & -k
        rows_of[k] = from_tp(rows_of[k ^ low], low)
    blocks = [gather_ep(rows_of[k]) for k in range(tp_count)]

    half = tp_count // 2
    groups = [list(reversed(range(1, half + 1))), list(reversed(range(half + 1, tp_count))) + [0]]
    terms = [[] for _ in range(tp_count)]
    arrivals = []
    hold_gate, hold_down = blocks[0], [blocks[tp_count - 1][-2]]
    for group in groups:
        active = activate(places, [blocks[k] for k in group], gains, gate_weight, up_weight, hold_gate)
        outs = project_down(places, active, row_weight, down_weight, group, ep_count, cores, hold_down)
        swapped = [from_core(out[1]) for out in outs]
        for at, k in enumerate(group):
            pair = [[(outs[at][0], c * block_rows), (swapped[at], c * block_rows)] for c in range(chips)]
            wait = arrivals[0] if len(arrivals) == 1 else arrivals[-2] if arrivals else []
            sums = add(pair, block_rows, wait)
            across = [from_chip(sums[c], chips - c) for c in range(1, chips)]
            if not arrivals:
                hold_gate, hold_down = [sums[-1]], across
            arrivals.append(across)
            terms[k] += [(value, 0) for value in [sums[0]] + across]
    for group in groups:
        for k in group:
            if k:
                (total,) = add([terms[k]], block_rows)
                terms[0].append((from_tp(total, k), 0))
    (mixed,) = add([terms[0]], block_rows)
    return (stream_out, mixed)


def solution(mesh):
    return jax.shard_map(
        shards,
        mesh=mesh,
        in_specs=(
            P(("parts", "ep"), "tp", None),
            P(("parts", "ep"), "tp"),
            P(("parts", "ep"), None, None),
            P(("parts", "ep"), None, None),
            P(("parts", "ep")),
            P("tp", None, None),
            P("tp", "ep"),
            P("parts", "ep"),
            P("ep"),
            P("parts", None),
            P("parts", None),
            P("ep", None, "tp"),
            P("ep", None, "tp"),
            P("ep", "tp", None),
        ),
        out_specs=(P(("parts", "tp"), "ep"), P(("parts", "tp"), "ep")),
        check_vma=False,
    )
```

```python
import functools

import jax
import jax.numpy as jnp
from jax import lax
from jax.experimental import pallas as pl
from jax.experimental.pallas import tpu as pltpu
from jax.sharding import PartitionSpec as P

score_scale = 1.0 / 192.0**0.5
norm_epsilon = 1e-06
MIB = 1 << 20
light = pl.CostEstimate(flops=1, bytes_accessed=1, transcendentals=0)


def in_hbm(value):
    return pltpu.with_memory_space_constraint(value, pltpu.HBM)


def in_vmem(value):
    return pltpu.with_memory_space_constraint(value, pltpu.VMEM)


def fetch_kernel(parts, *refs):
    source, target, sems = refs[0], refs[-2], refs[-1]
    step = source.shape[-2] // parts
    copies = []
    for i in range(parts):
        cut = (slice(None),) * (len(source.shape) - 2) + (pl.ds(i * step, step),)
        copies.append(pltpu.make_async_copy(source.at[cut], target.at[cut], sems.at[i]))
    for copy in copies:
        copy.start()
    for copy in copies:
        copy.wait()


def fetch(value, after):
    parts = 4
    return pl.pallas_call(
        functools.partial(fetch_kernel, parts),
        out_shape=pltpu.VMEM(value.shape, value.dtype),
        in_specs=[pl.BlockSpec(memory_space=pl.ANY)] * (1 + len(after)),
        out_specs=pl.BlockSpec(memory_space=pltpu.VMEM),
        scratch_shapes=[pltpu.SemaphoreType.DMA((parts,))],
        cost_estimate=pl.CostEstimate(flops=0, bytes_accessed=4 * value.size, transcendentals=0),
        compiler_params=pltpu.CompilerParams(vmem_limit_bytes=1 * MIB),
        name="fetch",
    )(in_hbm(value), *after)


def attention_kernel(step_rows, lengths, q_ref, qr_ref, k_ref, kr_ref, up_ref, *refs):
    out_ref, latent, rope = refs[-3:]
    step = pl.program_id(0)
    heads, positions = q_ref.shape[1], k_ref.shape[1]
    rope_width = kr_ref.shape[1]

    @pl.when(step == 0)
    def _():
        all_rows = qr_ref.shape[0]
        width = heads * rope_width
        lane = lax.broadcasted_iota(jnp.int32, (heads, width), 1)
        head = lax.broadcasted_iota(jnp.int32, (heads, width), 0)
        own = jnp.where(lane // rope_width == head, 1.0, 0.0)
        spread = qr_ref[...].astype(jnp.float32)[:, None, :] * own[None, :, :]
        spread = spread.reshape(all_rows * heads, width).astype(jnp.bfloat16)
        lane = lax.broadcasted_iota(jnp.int32, (width, rope_width), 0)
        column = lax.broadcasted_iota(jnp.int32, (width, rope_width), 1)
        fold = jnp.where(lane % rope_width == column, 1.0, 0.0).astype(jnp.bfloat16)
        rope[...] = jnp.dot(spread, fold, preferred_element_type=jnp.float32)

    place = lax.broadcasted_iota(jnp.int32, (heads, positions), 1)
    lanes = latent.shape[2]
    lanes = latent.shape[2]
    scores = []
    for r in range(step_rows):
        first = pl.multiple_of((step * step_rows + r) * heads, heads)
        score = lax.dot_general(
            q_ref[r], k_ref[r], (((1,), (1,)), ((), ())), preferred_element_type=jnp.float32
        )
        score += jnp.dot(
            rope[pl.ds(first, heads), :].astype(jnp.bfloat16), kr_ref[r], preferred_element_type=jnp.float32
        )
        scores.append(score)
    probabilities = []
    for r in range(step_rows):
        visible = place < lengths[step * step_rows + r]
        score = jnp.where(visible, scores[r] * score_scale, -jnp.inf)
        weight = jnp.exp(score - jnp.max(score, axis=-1, keepdims=True))
        total = jnp.sum(weight, axis=-1, keepdims=True)
        probabilities.append((weight / total).astype(jnp.bfloat16))
    for r in range(step_rows):
        first = pl.multiple_of((step * step_rows + r) * heads, heads)
        mixed = jnp.dot(probabilities[r], k_ref[r], preferred_element_type=jnp.float32)
        for c in range(latent.shape[0]):
            latent[c, pl.ds(first, heads), :] = mixed[:, c * lanes : (c + 1) * lanes]

    @pl.when(step == pl.num_programs(0) - 1)
    def _():
        rows = out_ref.shape[0]
        width = up_ref.shape[2]
        for h in range(heads):
            parts = [latent[c, pl.ds(h, rows, stride=heads), :] for c in range(latent.shape[0])]
            part = jnp.concatenate(parts, axis=1).astype(jnp.bfloat16)
            out_ref[:, h * width : (h + 1) * width] = jnp.dot(
                part, up_ref[h], preferred_element_type=jnp.float32
            ).astype(jnp.bfloat16)


def attend(query_latent, query_rope, cache_latent, cache_rope, cache_length, value_up, after):
    rows, heads, latent_width = query_latent.shape
    positions = cache_latent.shape[1]
    rope_width = cache_rope.shape[1]
    value_width = value_up.shape[2]
    step_rows = 16
    by_row = lambda i, lengths: (i, 0, 0)
    return pl.pallas_call(
        functools.partial(attention_kernel, step_rows),
        out_shape=jax.ShapeDtypeStruct((rows, heads * value_width), jnp.bfloat16),
        grid_spec=pltpu.PrefetchScalarGridSpec(
            num_scalar_prefetch=1,
            grid=(rows // step_rows,),
            in_specs=[
                pl.BlockSpec((step_rows, heads, latent_width), by_row),
                pl.BlockSpec(query_rope.shape, lambda i, lengths: (0, 0)),
                pl.BlockSpec((step_rows, positions, latent_width), by_row),
                pl.BlockSpec((step_rows, rope_width, positions), by_row),
                pl.BlockSpec(value_up.shape, lambda i, lengths: (0, 0, 0)),
            ]
            + [pl.BlockSpec(memory_space=pl.ANY)] * len(after),
            out_specs=pl.BlockSpec((rows, heads * value_width), lambda i, lengths: (0, 0)),
            scratch_shapes=[
                pltpu.VMEM((latent_width // 128, rows * heads, 128), jnp.float32),
                pltpu.VMEM((rows * heads, rope_width), jnp.float32),
            ],
        ),
        cost_estimate=pl.CostEstimate(
            flops=64 * heads * cache_latent.size, bytes_accessed=2 * cache_latent.size, transcendentals=0
        ),
        compiler_params=pltpu.CompilerParams(vmem_limit_bytes=20 * MIB),
        name="attention",
    )(
        cache_length,
        in_hbm(query_latent),
        in_hbm(query_rope),
        in_hbm(cache_latent),
        in_hbm(cache_rope),
        in_hbm(value_up),
        *after,
    )


def projection_kernel(count, out_count, places, *refs):
    blocks, weight, outs = refs[:count], refs[count], refs[-2 - out_count : -2]
    gathered, result = refs[-2:]
    height = blocks[0].shape[0]
    for k in range(count):
        first = pl.multiple_of(places[k] * height, height)
        gathered[pl.ds(first, height), :] = blocks[k][...]
    columns = weight.shape[1]
    tile = 256 if columns % 256 == 0 else 128
    for j in range(columns // tile):
        result[:, j * tile : (j + 1) * tile] = jnp.dot(
            gathered[...], weight[:, j * tile : (j + 1) * tile], preferred_element_type=jnp.float32
        ).astype(jnp.bfloat16)
    out_height = outs[0].shape[0]
    for s in range(len(outs)):
        first = pl.multiple_of(places[count + s] * out_height, out_height)
        outs[s][...] = result[pl.ds(first, out_height), :]


def project(places, blocks, weight, out_count):
    count = len(blocks)
    height, depth = blocks[0].shape
    rows, columns = height * count, weight.shape[1]
    whole = pl.BlockSpec(memory_space=pltpu.VMEM)
    return pl.pallas_call(
        functools.partial(projection_kernel, count, out_count),
        out_shape=[jax.ShapeDtypeStruct((rows // out_count, columns), jnp.bfloat16)] * out_count,
        in_specs=[pl.BlockSpec(memory_space=pltpu.SMEM)] + [whole] * (count + 1),
        out_specs=[whole] * out_count,
        scratch_shapes=[
            pltpu.VMEM((rows, depth), jnp.bfloat16),
            pltpu.VMEM((rows, columns), jnp.bfloat16),
        ],
        cost_estimate=pl.CostEstimate(flops=2 * rows * depth * columns, bytes_accessed=4 * MIB, transcendentals=0),
        compiler_params=pltpu.CompilerParams(vmem_limit_bytes=8 * MIB),
        name="projection",
    )(places, *blocks, in_vmem(weight))


def gate_kernel(row_blocks, column_blocks, model_width, places, *refs):
    count = row_blocks * column_blocks
    blocks, gains = refs[:count], refs[count : count + column_blocks]
    gate, up = refs[count + column_blocks : count + column_blocks + 2]
    active, x, gate_sum, up_sum = refs[-4:]
    height, width = blocks[0].shape
    hidden = gate.shape[2]
    squares = [jnp.zeros((height, 1), jnp.float32) for _ in range(row_blocks)]
    tile = min(256, hidden)
    for k in range(column_blocks):
        for s in range(row_blocks):
            wide = blocks[s * column_blocks + k][...].astype(jnp.float32)
            squares[s] += jnp.sum(wide * wide, axis=-1, keepdims=True)
            x[k, s * height : (s + 1) * height, :] = (wide * gains[k][...]).astype(jnp.bfloat16)
        depth = pl.ds(pl.multiple_of(places[k] * width, 128), width)
        for total, weight in ((gate_sum, gate), (up_sum, up)):
            for j in range(hidden // tile):
                cut = slice(j * tile, (j + 1) * tile)
                product = jnp.dot(x[k], weight[0, depth, cut], preferred_element_type=jnp.float32)
                if k == 0:
                    total[:, cut] = product
                else:
                    total[:, cut] += product
    for s in range(row_blocks):
        rows = slice(s * height, (s + 1) * height)
        scale = lax.rsqrt(squares[s] / model_width + norm_epsilon)
        gate_part = gate_sum[rows, :] * scale
        up_part = up_sum[rows, :] * scale
        active[rows, :] = (gate_part / (1.0 + jnp.exp(-gate_part)) * up_part).astype(jnp.bfloat16)


def activate(places, blocks, gains, gate_weight, up_weight, after):
    row_blocks, column_blocks = len(blocks), len(blocks[0])
    height, width = blocks[0][0].shape
    rows = row_blocks * height
    model_width, hidden = gate_weight.shape[1:]
    whole = pl.BlockSpec(memory_space=pltpu.VMEM)
    count = row_blocks * column_blocks
    return pl.pallas_call(
        functools.partial(gate_kernel, row_blocks, column_blocks, model_width),
        out_shape=jax.ShapeDtypeStruct((rows, hidden), jnp.bfloat16),
        in_specs=[pl.BlockSpec(memory_space=pltpu.SMEM)]
        + [whole] * (count + column_blocks + 2)
        + [pl.BlockSpec(memory_space=pl.ANY)] * len(after),
        out_specs=whole,
        scratch_shapes=[
            pltpu.VMEM((column_blocks, rows, width), jnp.bfloat16),
            pltpu.VMEM((rows, hidden), jnp.float32),
            pltpu.VMEM((rows, hidden), jnp.float32),
        ],
        cost_estimate=light,
        compiler_params=pltpu.CompilerParams(vmem_limit_bytes=2 * rows * (model_width + 4 * hidden) + 4 * MIB),
        name="activate",
    )(places, *[b for row in blocks for b in row], *gains, in_vmem(gate_weight), in_vmem(up_weight), *after)


def down_kernel(slots, column_blocks, cores, places, active, row_weight, down, *refs):
    row_blocks = len(slots)
    outs = refs[-row_blocks * cores :]
    width = down.shape[2] // column_blocks
    height = active.shape[0] // row_blocks
    order = [b * cores + c for c in reversed(range(cores)) for b in range(column_blocks // cores)]
    tile = 256 if width % 256 == 0 else 128
    weights = []
    for s in range(row_blocks):
        first = pl.multiple_of(places[column_blocks + slots[s]] * height, height)
        weights.append(row_weight[pl.ds(first, height), :])
    for k in order:
        b, c = k // cores, k % cores
        start = pl.multiple_of(places[k] * width, 128)
        for j in range(width // tile):
            cut = slice(j * tile, (j + 1) * tile)
            product = jnp.dot(
                active[...], down[0, :, pl.ds(start + j * tile, tile)], preferred_element_type=jnp.float32
            )
            for s in range(row_blocks):
                part = product[s * height : (s + 1) * height, :] * weights[s]
                outs[s * cores + c][b * height : (b + 1) * height, cut] = part.astype(jnp.bfloat16)


def project_down(places, active, row_weight, down_weight, slots, column_blocks, cores, after):
    row_blocks = len(slots)
    rows, hidden = active.shape
    width = down_weight.shape[2] // column_blocks
    whole = pl.BlockSpec(memory_space=pltpu.VMEM)
    out = jax.ShapeDtypeStruct((rows // row_blocks * (column_blocks // cores), width), jnp.bfloat16)
    outs = pl.pallas_call(
        functools.partial(down_kernel, slots, column_blocks, cores),
        out_shape=[out] * (row_blocks * cores),
        in_specs=[pl.BlockSpec(memory_space=pltpu.SMEM)]
        + [whole] * 3
        + [pl.BlockSpec(memory_space=pl.ANY)] * len(after),
        out_specs=[whole] * (row_blocks * cores),
        cost_estimate=light,
        compiler_params=pltpu.CompilerParams(vmem_limit_bytes=4 * MIB),
        name="down",
    )(places, active, row_weight, in_vmem(down_weight), *after)
    return [outs[s * cores : (s + 1) * cores] for s in range(row_blocks)]


def add_kernel(groups, *refs):
    used = sum(len(g) for g in groups)
    outs = refs[-len(groups) :]
    at = 0
    for group, out in zip(groups, outs):
        total = None
        for first in group:
            value = refs[at][first : first + out.shape[0], :].astype(jnp.float32)
            total = value if total is None else total + value
            at += 1
        out[...] = total.astype(jnp.bfloat16)


def add(groups, height, after=()):
    values = [value for group in groups for value, _ in group]
    width = values[0].shape[1]
    whole = pl.BlockSpec(memory_space=pltpu.VMEM)
    return pl.pallas_call(
        functools.partial(add_kernel, [[first for _, first in group] for group in groups]),
        out_shape=[jax.ShapeDtypeStruct((height, width), jnp.bfloat16)] * len(groups),
        in_specs=[whole] * len(values) + [pl.BlockSpec(memory_space=pl.ANY)] * len(after),
        out_specs=[whole] * len(groups),
        cost_estimate=light,
        compiler_params=pltpu.CompilerParams(vmem_limit_bytes=8 * MIB),
        name="add",
    )(*values, *after)


def shards(
    query_latent,
    query_rope,
    cache_latent,
    cache_rope,
    cache_length,
    value_up,
    output_weight,
    residual,
    norm_gain,
    routed_experts,
    expert_gates,
    gate_weight,
    up_weight,
    down_weight,
):
    ep_count = lax.axis_size("ep")
    tp_count = lax.axis_size("tp")
    ep_index = lax.axis_index("ep")
    tp_index = lax.axis_index("tp")
    row_total = routed_experts.shape[0]
    block_rows = row_total // tp_count
    cores = 2
    chips = ep_count // cores

    def from_core(value):
        return lax.ppermute(value, "ep", [(i, i ^ 1) for i in range(ep_count)])

    def from_chip(value, back):
        step = cores * back
        return lax.ppermute(value, "ep", [(i, (i + step) % ep_count) for i in range(ep_count)])

    def from_tp(value, bits):
        return lax.ppermute(value, "tp", [(i, i ^ bits) for i in range(tp_count)])

    def gather_ep(value):
        same = [value] + [from_chip(value, b) for b in range(1, chips)]
        other = [from_core(v) for v in same]
        return [v for pair in zip(same, other) for v in pair]

    chip, core = ep_index // cores, ep_index % cores
    ep_places = [
        (chip - b + chips) % chips * cores + (core if c == 0 else 1 - core)
        for b in range(chips)
        for c in range(cores)
    ]
    tp_places = [tp_index ^ k for k in range(tp_count)]
    places = jnp.stack(ep_places + tp_places).astype(jnp.int32)

    gain = norm_gain.reshape(1, -1)
    gains = gather_ep(gain)
    own_residual = lax.dynamic_slice_in_dim(residual, tp_index * block_rows, block_rows, 0)
    row_weight = jnp.sum(jnp.where(routed_experts == ep_index, expert_gates, 0.0), axis=-1, keepdims=True)

    head_out = attend(query_latent, query_rope, cache_latent, cache_rope, cache_length, value_up, [places])
    output_weight = fetch(output_weight, [head_out, row_weight, own_residual, gain])
    partial = project(places, gather_ep(head_out), output_weight, tp_count)

    gate_weight = fetch(gate_weight, [partial[0]])
    terms = [[(value, 0)] for value in partial]
    for k in reversed(range(1, tp_count)):
        total = terms[k][0][0]
        if len(terms[k]) > 1 or k == 1:
            (total,) = add([terms[k]], block_rows, [gate_weight] if k == 1 else [])
        low = k & -k
        arrived = from_tp(total, low)
        terms[k ^ low].append((arrived, 0))
    up_weight = fetch(up_weight, [total])
    down_weight = fetch(down_weight, [total])
    stream_terms = terms[0] + [(own_residual, 0)]
    stream, stream_out = add([stream_terms, stream_terms], block_rows, gains + [gate_weight, up_weight, down_weight])

    rows_of = {0: stream}
    for k in range(1, tp_count):
        low = k & -k
        rows_of[k] = from_tp(rows_of[k ^ low], low)
    blocks = [gather_ep(rows_of[k]) for k in range(tp_count)]

    half = tp_count // 2
    groups = [list(range(half, 0, -1)), list(range(tp_count - 1, half, -1))]
    if tp_count == 4:
        groups = [[2, 0], [3, 1]]
    else:
        groups[1].append(0)
    late = groups[1]
    hold_gate, hold_down, across = [rows_of[late[0]]], blocks[late[1]][-2:-1], blocks[late[0]][-2:-1]
    terms = [[] for _ in range(tp_count)]
    for group in groups:
        active = activate(places, [blocks[k] for k in group], gains, gate_weight, up_weight, hold_gate)
        outs = project_down(places, active, row_weight, down_weight, group, ep_count, cores, hold_down)
        swapped = [from_core(out[1]) for out in outs]
        for at, k in enumerate(group):
            pair = [[(outs[at][0], c * block_rows), (swapped[at], c * block_rows)] for c in range(chips)]
            sums = add(pair, block_rows, across)
            across = [from_chip(sums[c], chips - c) for c in range(1, chips)]
            terms[k] += [(value, 0) for value in [sums[0]] + across]
            if at == 0:
                hold_gate, hold_down = sums[1:], across
        across = []
    before = []
    for group in groups:
        for k in group:
            if k:
                (total,) = add([terms[k]], block_rows, before)
                before = [from_tp(total, k)]
                terms[0].append((before[0], 0))
                if k < half:
                    before = []
    (mixed,) = add([terms[0]], block_rows)
    return (stream_out, mixed)


def solution(mesh):
    return jax.shard_map(
        shards,
        mesh=mesh,
        in_specs=(
            P(("parts", "ep"), "tp", None),
            P(("parts", "ep"), "tp"),
            P(("parts", "ep"), None, None),
            P(("parts", "ep"), None, None),
            P(("parts", "ep")),
            P("tp", None, None),
            P("tp", "ep"),
            P("parts", "ep"),
            P("ep"),
            P("parts", None),
            P("parts", None),
            P("ep", None, "tp"),
            P("ep", None, "tp"),
            P("ep", "tp", None),
        ),
        out_specs=(P(("parts", "tp"), "ep"), P(("parts", "tp"), "ep")),
        check_vma=False,
    )
```

```python
import functools

import jax
import jax.numpy as jnp
from jax import lax
from jax.experimental import pallas as pl
from jax.experimental.pallas import tpu as pltpu
from jax.sharding import PartitionSpec as P

score_scale = 1.0 / 192.0**0.5
norm_epsilon = 1e-06
MIB = 1 << 20


def in_hbm(value):
    return pltpu.with_memory_space_constraint(value, pltpu.HBM)


def in_vmem(value):
    return pltpu.with_memory_space_constraint(value, pltpu.VMEM)


def fetch_kernel(parts, *refs):
    source, target, sems = refs[0], refs[-2], refs[-1]
    step = source.shape[-2] // parts
    copies = []
    for i in range(parts):
        cut = (slice(None),) * (len(source.shape) - 2) + (pl.ds(i * step, step),)
        copies.append(pltpu.make_async_copy(source.at[cut], target.at[cut], sems.at[i]))
    for copy in copies:
        copy.start()
    for copy in copies:
        copy.wait()


def fetch(value, after):
    parts = 4
    return pl.pallas_call(
        functools.partial(fetch_kernel, parts),
        out_shape=pltpu.VMEM(value.shape, value.dtype),
        in_specs=[pl.BlockSpec(memory_space=pl.ANY)] * (1 + len(after)),
        out_specs=pl.BlockSpec(memory_space=pltpu.VMEM),
        scratch_shapes=[pltpu.SemaphoreType.DMA((parts,))],
        cost_estimate=pl.CostEstimate(flops=0, bytes_accessed=4 * value.size, transcendentals=0),
        compiler_params=pltpu.CompilerParams(vmem_limit_bytes=1 * MIB),
        name="fetch",
    )(in_hbm(value), *after)


def attention_kernel(step_rows, lengths, q_ref, qr_ref, k_ref, kr_ref, up_ref, *refs):
    out_ref, latent, rope = refs[-3:]
    step = pl.program_id(0)
    heads, positions = q_ref.shape[1], k_ref.shape[1]
    rope_width = kr_ref.shape[1]

    @pl.when(step == 0)
    def _():
        all_rows = qr_ref.shape[0]
        width = heads * rope_width
        lane = lax.broadcasted_iota(jnp.int32, (heads, width), 1)
        head = lax.broadcasted_iota(jnp.int32, (heads, width), 0)
        own = jnp.where(lane // rope_width == head, 1.0, 0.0)
        spread = qr_ref[...].astype(jnp.float32)[:, None, :] * own[None, :, :]
        spread = spread.reshape(all_rows * heads, width).astype(jnp.bfloat16)
        lane = lax.broadcasted_iota(jnp.int32, (width, rope_width), 0)
        column = lax.broadcasted_iota(jnp.int32, (width, rope_width), 1)
        fold = jnp.where(lane % rope_width == column, 1.0, 0.0).astype(jnp.bfloat16)
        rope[...] = jnp.dot(spread, fold, preferred_element_type=jnp.float32)

    place = lax.broadcasted_iota(jnp.int32, (heads, positions), 1)
    lanes = latent.shape[2]
    lanes = latent.shape[2]
    scores = []
    for r in range(step_rows):
        first = pl.multiple_of((step * step_rows + r) * heads, heads)
        score = lax.dot_general(
            q_ref[r], k_ref[r], (((1,), (1,)), ((), ())), preferred_element_type=jnp.float32
        )
        score += jnp.dot(
            rope[pl.ds(first, heads), :].astype(jnp.bfloat16), kr_ref[r], preferred_element_type=jnp.float32
        )
        scores.append(score)
    probabilities = []
    for r in range(step_rows):
        visible = place < lengths[step * step_rows + r]
        score = jnp.where(visible, scores[r] * score_scale, -jnp.inf)
        weight = jnp.exp(score - jnp.max(score, axis=-1, keepdims=True))
        total = jnp.sum(weight, axis=-1, keepdims=True)
        probabilities.append((weight / total).astype(jnp.bfloat16))
    for r in range(step_rows):
        first = pl.multiple_of((step * step_rows + r) * heads, heads)
        mixed = jnp.dot(probabilities[r], k_ref[r], preferred_element_type=jnp.float32)
        for c in range(latent.shape[0]):
            latent[c, pl.ds(first, heads), :] = mixed[:, c * lanes : (c + 1) * lanes]

    @pl.when(step == pl.num_programs(0) - 1)
    def _():
        rows = out_ref.shape[0]
        width = up_ref.shape[2]
        for h in range(heads):
            parts = [latent[c, pl.ds(h, rows, stride=heads), :] for c in range(latent.shape[0])]
            part = jnp.concatenate(parts, axis=1).astype(jnp.bfloat16)
            out_ref[:, h * width : (h + 1) * width] = jnp.dot(
                part, up_ref[h], preferred_element_type=jnp.float32
            ).astype(jnp.bfloat16)


def attend(query_latent, query_rope, cache_latent, cache_rope, cache_length, value_up, after):
    rows, heads, latent_width = query_latent.shape
    positions = cache_latent.shape[1]
    rope_width = cache_rope.shape[1]
    value_width = value_up.shape[2]
    step_rows = 16
    by_row = lambda i, lengths: (i, 0, 0)
    return pl.pallas_call(
        functools.partial(attention_kernel, step_rows),
        out_shape=jax.ShapeDtypeStruct((rows, heads * value_width), jnp.bfloat16),
        grid_spec=pltpu.PrefetchScalarGridSpec(
            num_scalar_prefetch=1,
            grid=(rows // step_rows,),
            in_specs=[
                pl.BlockSpec((step_rows, heads, latent_width), by_row),
                pl.BlockSpec(query_rope.shape, lambda i, lengths: (0, 0)),
                pl.BlockSpec((step_rows, positions, latent_width), by_row),
                pl.BlockSpec((step_rows, rope_width, positions), by_row),
                pl.BlockSpec(value_up.shape, lambda i, lengths: (0, 0, 0)),
            ]
            + [pl.BlockSpec(memory_space=pl.ANY)] * len(after),
            out_specs=pl.BlockSpec((rows, heads * value_width), lambda i, lengths: (0, 0)),
            scratch_shapes=[
                pltpu.VMEM((latent_width // 128, rows * heads, 128), jnp.float32),
                pltpu.VMEM((rows * heads, rope_width), jnp.float32),
            ],
        ),
        cost_estimate=pl.CostEstimate(
            flops=64 * heads * cache_latent.size, bytes_accessed=2 * cache_latent.size, transcendentals=0
        ),
        compiler_params=pltpu.CompilerParams(vmem_limit_bytes=20 * MIB),
        name="attention",
    )(
        cache_length,
        in_hbm(query_latent),
        in_hbm(query_rope),
        in_hbm(cache_latent),
        in_hbm(cache_rope),
        in_hbm(value_up),
        *after,
    )


def projection_kernel(count, out_count, places, *refs):
    blocks, weight, outs = refs[:count], refs[count], refs[-2 - out_count : -2]
    gathered, result = refs[-2:]
    height = blocks[0].shape[0]
    for k in range(count):
        first = pl.multiple_of(places[k] * height, height)
        gathered[pl.ds(first, height), :] = blocks[k][...]
    columns = weight.shape[1]
    tile = 256 if columns % 256 == 0 else 128
    for j in range(columns // tile):
        result[:, j * tile : (j + 1) * tile] = jnp.dot(
            gathered[...], weight[:, j * tile : (j + 1) * tile], preferred_element_type=jnp.float32
        ).astype(jnp.bfloat16)
    out_height = outs[0].shape[0]
    for s in range(len(outs)):
        first = pl.multiple_of(places[count + s] * out_height, out_height)
        outs[s][...] = result[pl.ds(first, out_height), :]


def project(places, blocks, weight, out_count):
    count = len(blocks)
    height, depth = blocks[0].shape
    rows, columns = height * count, weight.shape[1]
    whole = pl.BlockSpec(memory_space=pltpu.VMEM)
    return pl.pallas_call(
        functools.partial(projection_kernel, count, out_count),
        out_shape=[jax.ShapeDtypeStruct((rows // out_count, columns), jnp.bfloat16)] * out_count,
        in_specs=[pl.BlockSpec(memory_space=pltpu.SMEM)] + [whole] * (count + 1),
        out_specs=[whole] * out_count,
        scratch_shapes=[
            pltpu.VMEM((rows, depth), jnp.bfloat16),
            pltpu.VMEM((rows, columns), jnp.bfloat16),
        ],
        cost_estimate=pl.CostEstimate(flops=2 * rows * depth * columns, bytes_accessed=4 * MIB, transcendentals=0),
        compiler_params=pltpu.CompilerParams(vmem_limit_bytes=8 * MIB),
        name="projection",
    )(places, *blocks, in_vmem(weight))


def gate_kernel(row_blocks, column_blocks, model_width, places, *refs):
    count = row_blocks * column_blocks
    blocks, gains = refs[:count], refs[count : count + column_blocks]
    gate, up = refs[count + column_blocks : count + column_blocks + 2]
    active, x, gate_sum, up_sum = refs[-4:]
    height, width = blocks[0].shape
    hidden = gate.shape[2]
    squares = [jnp.zeros((height, 1), jnp.float32) for _ in range(row_blocks)]
    tile = min(256, hidden)
    for k in range(column_blocks):
        for s in range(row_blocks):
            wide = blocks[s * column_blocks + k][...].astype(jnp.float32)
            squares[s] += jnp.sum(wide * wide, axis=-1, keepdims=True)
            x[k, s * height : (s + 1) * height, :] = (wide * gains[k][...]).astype(jnp.bfloat16)
        depth = pl.ds(pl.multiple_of(places[k] * width, 128), width)
        for total, weight in ((gate_sum, gate), (up_sum, up)):
            for j in range(hidden // tile):
                cut = slice(j * tile, (j + 1) * tile)
                product = jnp.dot(x[k], weight[0, depth, cut], preferred_element_type=jnp.float32)
                if k == 0:
                    total[:, cut] = product
                else:
                    total[:, cut] += product
    for s in range(row_blocks):
        rows = slice(s * height, (s + 1) * height)
        scale = lax.rsqrt(squares[s] / model_width + norm_epsilon)
        gate_part = gate_sum[rows, :] * scale
        up_part = up_sum[rows, :] * scale
        active[rows, :] = (gate_part / (1.0 + jnp.exp(-gate_part)) * up_part).astype(jnp.bfloat16)


def activate(places, blocks, gains, gate_weight, up_weight, after):
    row_blocks, column_blocks = len(blocks), len(blocks[0])
    height, width = blocks[0][0].shape
    rows = row_blocks * height
    model_width, hidden = gate_weight.shape[1:]
    whole = pl.BlockSpec(memory_space=pltpu.VMEM)
    count = row_blocks * column_blocks
    return pl.pallas_call(
        functools.partial(gate_kernel, row_blocks, column_blocks, model_width),
        out_shape=jax.ShapeDtypeStruct((rows, hidden), jnp.bfloat16),
        in_specs=[pl.BlockSpec(memory_space=pltpu.SMEM)]
        + [whole] * (count + column_blocks + 2)
        + [pl.BlockSpec(memory_space=pl.ANY)] * len(after),
        out_specs=whole,
        scratch_shapes=[
            pltpu.VMEM((column_blocks, rows, width), jnp.bfloat16),
            pltpu.VMEM((rows, hidden), jnp.float32),
            pltpu.VMEM((rows, hidden), jnp.float32),
        ],
        cost_estimate=pl.CostEstimate(
            flops=4 * rows * gate_weight.size, bytes_accessed=4 * gate_weight.size, transcendentals=rows * hidden
        ),
        compiler_params=pltpu.CompilerParams(vmem_limit_bytes=2 * rows * (model_width + 4 * hidden) + 4 * MIB),
        name="activate",
    )(places, *[b for row in blocks for b in row], *gains, in_vmem(gate_weight), in_vmem(up_weight), *after)


def down_kernel(slots, column_blocks, cores, places, active, row_weight, down, *refs):
    row_blocks = len(slots)
    outs = refs[-row_blocks * cores :]
    width = down.shape[2] // column_blocks
    height = active.shape[0] // row_blocks
    order = [b * cores + c for c in reversed(range(cores)) for b in range(column_blocks // cores)]
    tile = 256 if width % 256 == 0 else 128
    weights = []
    for s in range(row_blocks):
        first = pl.multiple_of(places[column_blocks + slots[s]] * height, height)
        weights.append(row_weight[pl.ds(first, height), :])
    for k in order:
        b, c = k // cores, k % cores
        start = pl.multiple_of(places[k] * width, 128)
        for j in range(width // tile):
            cut = slice(j * tile, (j + 1) * tile)
            product = jnp.dot(
                active[...], down[0, :, pl.ds(start + j * tile, tile)], preferred_element_type=jnp.float32
            )
            for s in range(row_blocks):
                part = product[s * height : (s + 1) * height, :] * weights[s]
                outs[s * cores + c][b * height : (b + 1) * height, cut] = part.astype(jnp.bfloat16)


def project_down(places, active, row_weight, down_weight, slots, column_blocks, cores, after):
    row_blocks = len(slots)
    rows, hidden = active.shape
    width = down_weight.shape[2] // column_blocks
    whole = pl.BlockSpec(memory_space=pltpu.VMEM)
    out = jax.ShapeDtypeStruct((rows // row_blocks * (column_blocks // cores), width), jnp.bfloat16)
    outs = pl.pallas_call(
        functools.partial(down_kernel, slots, column_blocks, cores),
        out_shape=[out] * (row_blocks * cores),
        in_specs=[pl.BlockSpec(memory_space=pltpu.SMEM)]
        + [whole] * 3
        + [pl.BlockSpec(memory_space=pl.ANY)] * len(after),
        out_specs=[whole] * (row_blocks * cores),
        cost_estimate=pl.CostEstimate(
            flops=2 * rows * down_weight.size, bytes_accessed=2 * down_weight.size, transcendentals=0
        ),
        compiler_params=pltpu.CompilerParams(vmem_limit_bytes=4 * MIB),
        name="down",
    )(places, active, row_weight, in_vmem(down_weight), *after)
    return [outs[s * cores : (s + 1) * cores] for s in range(row_blocks)]


def add_kernel(groups, *refs):
    used = sum(len(g) for g in groups)
    outs = refs[-len(groups) :]
    at = 0
    for group, out in zip(groups, outs):
        total = None
        for first in group:
            value = refs[at][first : first + out.shape[0], :].astype(jnp.float32)
            total = value if total is None else total + value
            at += 1
        out[...] = total.astype(jnp.bfloat16)


def add(groups, height, after=()):
    values = [value for group in groups for value, _ in group]
    width = values[0].shape[1]
    whole = pl.BlockSpec(memory_space=pltpu.VMEM)
    return pl.pallas_call(
        functools.partial(add_kernel, [[first for _, first in group] for group in groups]),
        out_shape=[jax.ShapeDtypeStruct((height, width), jnp.bfloat16)] * len(groups),
        in_specs=[whole] * len(values) + [pl.BlockSpec(memory_space=pl.ANY)] * len(after),
        out_specs=[whole] * len(groups),
        compiler_params=pltpu.CompilerParams(vmem_limit_bytes=8 * MIB),
        name="add",
    )(*values, *after)


def shards(
    query_latent,
    query_rope,
    cache_latent,
    cache_rope,
    cache_length,
    value_up,
    output_weight,
    residual,
    norm_gain,
    routed_experts,
    expert_gates,
    gate_weight,
    up_weight,
    down_weight,
):
    ep_count = lax.axis_size("ep")
    tp_count = lax.axis_size("tp")
    ep_index = lax.axis_index("ep")
    tp_index = lax.axis_index("tp")
    row_total = routed_experts.shape[0]
    block_rows = row_total // tp_count
    cores = 2
    chips = ep_count // cores

    def from_core(value):
        return lax.ppermute(value, "ep", [(i, i ^ 1) for i in range(ep_count)])

    def from_chip(value, back):
        step = cores * back
        return lax.ppermute(value, "ep", [(i, (i + step) % ep_count) for i in range(ep_count)])

    def from_tp(value, bits):
        return lax.ppermute(value, "tp", [(i, i ^ bits) for i in range(tp_count)])

    def gather_ep(value):
        same = [value] + [from_chip(value, b) for b in range(1, chips)]
        other = [from_core(v) for v in same]
        return [v for pair in zip(same, other) for v in pair]

    chip, core = ep_index // cores, ep_index % cores
    ep_places = [
        (chip - b + chips) % chips * cores + (core if c == 0 else 1 - core)
        for b in range(chips)
        for c in range(cores)
    ]
    tp_places = [tp_index ^ k for k in range(tp_count)]
    places = jnp.stack(ep_places + tp_places).astype(jnp.int32)

    gain = norm_gain.reshape(1, -1)
    gains = gather_ep(gain)
    own_residual = lax.dynamic_slice_in_dim(residual, tp_index * block_rows, block_rows, 0)
    row_weight = jnp.sum(jnp.where(routed_experts == ep_index, expert_gates, 0.0), axis=-1, keepdims=True)

    head_out = attend(query_latent, query_rope, cache_latent, cache_rope, cache_length, value_up, [places])
    output_weight = fetch(output_weight, [head_out, row_weight, own_residual, gain])
    partial = project(places, gather_ep(head_out), output_weight, tp_count)

    gate_weight = fetch(gate_weight, [partial[0]])
    terms = [[(value, 0)] for value in partial]
    for k in reversed(range(1, tp_count)):
        total = terms[k][0][0]
        if len(terms[k]) > 1 or k == 1:
            (total,) = add([terms[k]], block_rows, [gate_weight] if k == 1 else [])
        low = k & -k
        arrived = from_tp(total, low)
        terms[k ^ low].append((arrived, 0))
    up_weight = fetch(up_weight, [total])
    down_weight = fetch(down_weight, [total])
    stream_terms = terms[0] + [(own_residual, 0)]
    stream, stream_out = add([stream_terms, stream_terms], block_rows, gains + [gate_weight, up_weight, down_weight])

    rows_of = {0: stream}
    for k in range(1, tp_count):
        low = k & -k
        rows_of[k] = from_tp(rows_of[k ^ low], low)
    blocks = [gather_ep(rows_of[k]) for k in range(tp_count)]

    slots = list(reversed(range(tp_count)))
    active = activate(places, [blocks[k] for k in slots], gains, gate_weight, up_weight, [])
    outs = project_down(places, active, row_weight, down_weight, slots, ep_count, cores, [])
    swapped = [from_core(out[1]) for out in outs]
    terms = [[] for _ in range(tp_count)]
    arrivals = []
    for at, k in enumerate(slots):
        before = arrivals[0] if len(arrivals) == 1 else arrivals[-2] if arrivals else []
        pair = [[(outs[at][0], c * block_rows), (swapped[at], c * block_rows)] for c in range(chips)]
        sums = add(pair, block_rows, before)
        across = [from_chip(sums[c], chips - c) for c in range(1, chips)]
        arrivals.append(across)
        terms[k] += [(value, 0) for value in [sums[0]] + across]
        if k:
            (total,) = add([terms[k]], block_rows)
            low = k & -k
            terms[k ^ low].append((from_tp(total, low), 0))
    (mixed,) = add([terms[0]], block_rows)
    return (stream_out, mixed)


def solution(mesh):
    return jax.shard_map(
        shards,
        mesh=mesh,
        in_specs=(
            P(("parts", "ep"), "tp", None),
            P(("parts", "ep"), "tp"),
            P(("parts", "ep"), None, None),
            P(("parts", "ep"), None, None),
            P(("parts", "ep")),
            P("tp", None, None),
            P("tp", "ep"),
            P("parts", "ep"),
            P("ep"),
            P("parts", None),
            P("parts", None),
            P("ep", None, "tp"),
            P("ep", None, "tp"),
            P("ep", "tp", None),
        ),
        out_specs=(P(("parts", "tp"), "ep"), P(("parts", "tp"), "ep")),
        check_vma=False,
    )
```

```python
import functools

import jax
import jax.numpy as jnp
from jax import lax
from jax.experimental import pallas as pl
from jax.experimental.pallas import tpu as pltpu
from jax.sharding import PartitionSpec as P

score_scale = 1.0 / 192.0**0.5
norm_epsilon = 1e-06
MIB = 1 << 20
light = pl.CostEstimate(flops=1, bytes_accessed=1, transcendentals=0)


def in_hbm(value):
    return pltpu.with_memory_space_constraint(value, pltpu.HBM)


def in_vmem(value):
    return pltpu.with_memory_space_constraint(value, pltpu.VMEM)


def fetch_kernel(parts, *refs):
    source, target, sems = refs[0], refs[-2], refs[-1]
    step = source.shape[-2] // parts
    copies = []
    for i in range(parts):
        cut = (slice(None),) * (len(source.shape) - 2) + (pl.ds(i * step, step),)
        copies.append(pltpu.make_async_copy(source.at[cut], target.at[cut], sems.at[i]))
    for copy in copies:
        copy.start()
    for copy in copies:
        copy.wait()


def fetch(value, after):
    parts = 4
    return pl.pallas_call(
        functools.partial(fetch_kernel, parts),
        out_shape=pltpu.VMEM(value.shape, value.dtype),
        in_specs=[pl.BlockSpec(memory_space=pl.ANY)] * (1 + len(after)),
        out_specs=pl.BlockSpec(memory_space=pltpu.VMEM),
        scratch_shapes=[pltpu.SemaphoreType.DMA((parts,))],
        cost_estimate=pl.CostEstimate(flops=0, bytes_accessed=4 * value.size, transcendentals=0),
        compiler_params=pltpu.CompilerParams(vmem_limit_bytes=1 * MIB),
        name="fetch",
    )(in_hbm(value), *after)


def attention_kernel(step_rows, parts, lengths, q_ref, qr_ref, k_ref, kr_ref, up_ref, weight_hbm, *refs):
    out_ref, weight, latent, rope, sems = refs[-5:]
    step = pl.program_id(0)
    height = weight_hbm.shape[0] // parts
    copies = []
    for i in range(parts):
        cut = pl.ds(i * height, height)
        copies.append(pltpu.make_async_copy(weight_hbm.at[cut], weight.at[cut], sems.at[i]))
    heads, positions = q_ref.shape[1], k_ref.shape[1]
    rope_width = kr_ref.shape[1]

    @pl.when(step == 0)
    def _():
        for copy in copies:
            copy.start()
        all_rows = qr_ref.shape[0]
        width = heads * rope_width
        lane = lax.broadcasted_iota(jnp.int32, (heads, width), 1)
        head = lax.broadcasted_iota(jnp.int32, (heads, width), 0)
        own = jnp.where(lane // rope_width == head, 1.0, 0.0)
        spread = qr_ref[...].astype(jnp.float32)[:, None, :] * own[None, :, :]
        spread = spread.reshape(all_rows * heads, width).astype(jnp.bfloat16)
        lane = lax.broadcasted_iota(jnp.int32, (width, rope_width), 0)
        column = lax.broadcasted_iota(jnp.int32, (width, rope_width), 1)
        fold = jnp.where(lane % rope_width == column, 1.0, 0.0).astype(jnp.bfloat16)
        rope[...] = jnp.dot(spread, fold, preferred_element_type=jnp.float32)

    place = lax.broadcasted_iota(jnp.int32, (heads, positions), 1)
    lanes = latent.shape[2]
    lanes = latent.shape[2]
    scores = []
    for r in range(step_rows):
        first = pl.multiple_of((step * step_rows + r) * heads, heads)
        score = lax.dot_general(
            q_ref[r], k_ref[r], (((1,), (1,)), ((), ())), preferred_element_type=jnp.float32
        )
        score += jnp.dot(
            rope[pl.ds(first, heads), :].astype(jnp.bfloat16), kr_ref[r], preferred_element_type=jnp.float32
        )
        scores.append(score)
    probabilities = []
    for r in range(step_rows):
        visible = place < lengths[step * step_rows + r]
        score = jnp.where(visible, scores[r] * score_scale, -jnp.inf)
        weight = jnp.exp(score - jnp.max(score, axis=-1, keepdims=True))
        total = jnp.sum(weight, axis=-1, keepdims=True)
        probabilities.append((weight / total).astype(jnp.bfloat16))
    for r in range(step_rows):
        first = pl.multiple_of((step * step_rows + r) * heads, heads)
        mixed = jnp.dot(probabilities[r], k_ref[r], preferred_element_type=jnp.float32)
        for c in range(latent.shape[0]):
            latent[c, pl.ds(first, heads), :] = mixed[:, c * lanes : (c + 1) * lanes]

    @pl.when(step == pl.num_programs(0) - 1)
    def _():
        for copy in copies:
            copy.wait()
        rows = out_ref.shape[0]
        width = up_ref.shape[2]
        for h in range(heads):
            parts = [latent[c, pl.ds(h, rows, stride=heads), :] for c in range(latent.shape[0])]
            part = jnp.concatenate(parts, axis=1).astype(jnp.bfloat16)
            out_ref[:, h * width : (h + 1) * width] = jnp.dot(
                part, up_ref[h], preferred_element_type=jnp.float32
            ).astype(jnp.bfloat16)


def attend(query_latent, query_rope, cache_latent, cache_rope, cache_length, value_up, output_weight, after):
    rows, heads, latent_width = query_latent.shape
    positions = cache_latent.shape[1]
    rope_width = cache_rope.shape[1]
    value_width = value_up.shape[2]
    step_rows, parts = 16, 4
    by_row = lambda i, lengths: (i, 0, 0)
    return pl.pallas_call(
        functools.partial(attention_kernel, step_rows, parts),
        out_shape=[
            jax.ShapeDtypeStruct((rows, heads * value_width), jnp.bfloat16),
            pltpu.VMEM(output_weight.shape, output_weight.dtype),
        ],
        grid_spec=pltpu.PrefetchScalarGridSpec(
            num_scalar_prefetch=1,
            grid=(rows // step_rows,),
            in_specs=[
                pl.BlockSpec((step_rows, heads, latent_width), by_row),
                pl.BlockSpec(query_rope.shape, lambda i, lengths: (0, 0)),
                pl.BlockSpec((step_rows, positions, latent_width), by_row),
                pl.BlockSpec((step_rows, rope_width, positions), by_row),
                pl.BlockSpec(value_up.shape, lambda i, lengths: (0, 0, 0)),
            ]
            + [pl.BlockSpec(memory_space=pl.ANY)] * (1 + len(after)),
            out_specs=[
                pl.BlockSpec((rows, heads * value_width), lambda i, lengths: (0, 0)),
                pl.BlockSpec(memory_space=pl.ANY),
            ],
            scratch_shapes=[
                pltpu.VMEM((latent_width // 128, rows * heads, 128), jnp.float32),
                pltpu.VMEM((rows * heads, rope_width), jnp.float32),
                pltpu.SemaphoreType.DMA((parts,)),
            ],
        ),
        cost_estimate=pl.CostEstimate(
            flops=64 * heads * cache_latent.size, bytes_accessed=2 * cache_latent.size, transcendentals=0
        ),
        compiler_params=pltpu.CompilerParams(vmem_limit_bytes=20 * MIB),
        name="attention",
    )(
        cache_length,
        in_hbm(query_latent),
        in_hbm(query_rope),
        in_hbm(cache_latent),
        in_hbm(cache_rope),
        in_hbm(value_up),
        in_hbm(output_weight),
        *after,
    )


def projection_kernel(count, out_count, halves, places, *refs):
    blocks, weight, residual_hbm = refs[:count], refs[count], refs[count + 1]
    outs, (gathered, result, residual, sem) = refs[-4 - out_count * halves : -4], refs[-4:]
    height = blocks[0].shape[0]
    columns = weight.shape[1]
    out_height = result.shape[0] // out_count
    half = out_height // halves
    own = pl.multiple_of(places[count] * out_height, out_height)
    copy = pltpu.make_async_copy(residual_hbm.at[pl.ds(own, out_height), :], residual, sem)
    copy.start()
    for k in range(count):
        first = pl.multiple_of(places[k] * height, height)
        gathered[pl.ds(first, height), :] = blocks[k][...]
    tile = 256 if columns % 256 == 0 else 128
    for j in range(columns // tile):
        result[:, j * tile : (j + 1) * tile] = jnp.dot(
            gathered[...], weight[:, j * tile : (j + 1) * tile], preferred_element_type=jnp.float32
        )
    copy.wait()
    for h in range(halves):
        for s in range(out_count):
            first = pl.multiple_of(places[count + s] * out_height + h * half, half)
            part = result[pl.ds(first, half), :]
            if s == 0:
                part += residual[h * half : (h + 1) * half, :].astype(jnp.float32)
            outs[h * out_count + s][...] = part.astype(outs[h * out_count + s].dtype)


def project(places, blocks, weight, residual, out_count, halves):
    count = len(blocks)
    height, depth = blocks[0].shape
    rows, columns = height * count, weight.shape[1]
    half = rows // out_count // halves
    whole = pl.BlockSpec(memory_space=pltpu.VMEM)
    kinds = ([jnp.float32] + [jnp.bfloat16] * (out_count - 1)) * halves
    outs = pl.pallas_call(
        functools.partial(projection_kernel, count, out_count, halves),
        out_shape=[jax.ShapeDtypeStruct((half, columns), kind) for kind in kinds],
        in_specs=[pl.BlockSpec(memory_space=pltpu.SMEM)]
        + [whole] * (count + 1)
        + [pl.BlockSpec(memory_space=pl.ANY)],
        out_specs=[whole] * len(kinds),
        scratch_shapes=[
            pltpu.VMEM((rows, depth), jnp.bfloat16),
            pltpu.VMEM((rows, columns), jnp.float32),
            pltpu.VMEM((half * halves, columns), jnp.bfloat16),
            pltpu.SemaphoreType.DMA,
        ],
        cost_estimate=light,
        compiler_params=pltpu.CompilerParams(vmem_limit_bytes=8 * MIB),
        name="projection",
    )(places, *blocks, in_vmem(weight), in_hbm(residual))
    return [outs[h * out_count : (h + 1) * out_count] for h in range(halves)]


def gate_kernel(row_blocks, column_blocks, model_width, places, *refs):
    count = row_blocks * column_blocks
    blocks, gains = refs[:count], refs[count : count + column_blocks]
    gate, up = refs[count + column_blocks : count + column_blocks + 2]
    active, x, gate_sum, up_sum = refs[-4:]
    height, width = blocks[0].shape
    hidden = gate.shape[2]
    squares = [jnp.zeros((height, 1), jnp.float32) for _ in range(row_blocks)]
    tile = min(256, hidden)
    for k in range(column_blocks):
        for s in range(row_blocks):
            wide = blocks[s * column_blocks + k][...].astype(jnp.float32)
            squares[s] += jnp.sum(wide * wide, axis=-1, keepdims=True)
            x[k, s * height : (s + 1) * height, :] = (wide * gains[k][...]).astype(jnp.bfloat16)
        depth = pl.ds(pl.multiple_of(places[k] * width, 128), width)
        for total, weight in ((gate_sum, gate), (up_sum, up)):
            for j in range(hidden // tile):
                cut = slice(j * tile, (j + 1) * tile)
                product = jnp.dot(x[k], weight[0, depth, cut], preferred_element_type=jnp.float32)
                if k == 0:
                    total[:, cut] = product
                else:
                    total[:, cut] += product
    for s in range(row_blocks):
        rows = slice(s * height, (s + 1) * height)
        scale = lax.rsqrt(squares[s] / model_width + norm_epsilon)
        gate_part = gate_sum[rows, :] * scale
        up_part = up_sum[rows, :] * scale
        active[rows, :] = (gate_part / (1.0 + jnp.exp(-gate_part)) * up_part).astype(jnp.bfloat16)


def activate(places, blocks, gains, gate_weight, up_weight, after):
    row_blocks, column_blocks = len(blocks), len(blocks[0])
    height, width = blocks[0][0].shape
    rows = row_blocks * height
    model_width, hidden = gate_weight.shape[1:]
    whole = pl.BlockSpec(memory_space=pltpu.VMEM)
    count = row_blocks * column_blocks
    return pl.pallas_call(
        functools.partial(gate_kernel, row_blocks, column_blocks, model_width),
        out_shape=jax.ShapeDtypeStruct((rows, hidden), jnp.bfloat16),
        in_specs=[pl.BlockSpec(memory_space=pltpu.SMEM)]
        + [whole] * (count + column_blocks + 2)
        + [pl.BlockSpec(memory_space=pl.ANY)] * len(after),
        out_specs=whole,
        scratch_shapes=[
            pltpu.VMEM((column_blocks, rows, width), jnp.bfloat16),
            pltpu.VMEM((rows, hidden), jnp.float32),
            pltpu.VMEM((rows, hidden), jnp.float32),
        ],
        cost_estimate=light,
        compiler_params=pltpu.CompilerParams(vmem_limit_bytes=2 * rows * (model_width + 4 * hidden) + 4 * MIB),
        name="activate",
    )(places, *[b for row in blocks for b in row], *gains, in_vmem(gate_weight), in_vmem(up_weight), *after)


def down_kernel(groups, half, height, column_blocks, cores, places, active, routed, gates, down, *refs):
    outs = refs[-len(groups) * cores :]
    width = down.shape[2] // column_blocks
    rows = routed.shape[1]
    chips = column_blocks // cores
    order = [b * cores + c for c in reversed(range(cores)) for b in range(chips)]
    tile = 256 if width % 256 == 0 else 128
    block_rows = rows // sum(len(g) for g in groups)
    gate = jnp.sum(jnp.where(routed[...] == places[0], gates[...], 0.0), axis=0, keepdims=True)
    line = lax.broadcasted_iota(jnp.int32, (height, rows), 0)
    column = lax.broadcasted_iota(jnp.int32, (height, rows), 1)
    weights, spots = [], []
    for g, group in enumerate(groups):
        for at, k in enumerate(group):
            first = places[column_blocks + k] * block_rows + half * height
            weights.append(jnp.sum(jnp.where(column == line + first, gate, 0.0), axis=1, keepdims=True))
            spots.append((g, at * chips))
    for k in order:
        b, c = k // cores, k % cores
        start = pl.multiple_of(places[k] * width, 128)
        for j in range(width // tile):
            cut = slice(j * tile, (j + 1) * tile)
            product = jnp.dot(
                active[...], down[0, :, pl.ds(start + j * tile, tile)], preferred_element_type=jnp.float32
            )
            for s, (g, base) in enumerate(spots):
                part = product[s * height : (s + 1) * height, :] * weights[s]
                outs[g * cores + c][(base + b) * height : (base + b + 1) * height, cut] = part.astype(jnp.bfloat16)


def project_down(places, active, routed, gates, down_weight, groups, half, height, column_blocks, cores, after):
    width = down_weight.shape[2] // column_blocks
    chips = column_blocks // cores
    whole = pl.BlockSpec(memory_space=pltpu.VMEM)
    kinds = [
        jax.ShapeDtypeStruct((len(g) * chips * height, width), jnp.bfloat16) for g in groups for _ in range(cores)
    ]
    outs = pl.pallas_call(
        functools.partial(down_kernel, groups, half, height, column_blocks, cores),
        out_shape=kinds,
        in_specs=[pl.BlockSpec(memory_space=pltpu.SMEM)]
        + [whole] * 4
        + [pl.BlockSpec(memory_space=pl.ANY)] * len(after),
        out_specs=[whole] * len(kinds),
        cost_estimate=light,
        compiler_params=pltpu.CompilerParams(vmem_limit_bytes=4 * MIB),
        name="down",
    )(places, active, routed, gates, in_vmem(down_weight), *after)
    return [outs[g * cores : (g + 1) * cores] for g in range(len(groups))]


def add_kernel(plan, height, *refs):
    outs = refs[-len(plan) :]
    at = 0
    for pieces, out in zip(plan, outs):
        for p, piece in enumerate(pieces):
            total = None
            for first in piece:
                value = refs[at][first : first + height, :].astype(jnp.float32)
                total = value if total is None else total + value
                at += 1
            out[p * height : (p + 1) * height, :] = total.astype(jnp.bfloat16)


def add(outputs, height, after=()):
    values = [value for pieces in outputs for piece in pieces for value, _ in piece]
    width = values[0].shape[1]
    whole = pl.BlockSpec(memory_space=pltpu.VMEM)
    plan = [[[first for _, first in piece] for piece in pieces] for pieces in outputs]
    return pl.pallas_call(
        functools.partial(add_kernel, plan, height),
        out_shape=[jax.ShapeDtypeStruct((height * len(pieces), width), jnp.bfloat16) for pieces in outputs],
        in_specs=[whole] * len(values) + [pl.BlockSpec(memory_space=pl.ANY)] * len(after),
        out_specs=[whole] * len(outputs),
        cost_estimate=light,
        compiler_params=pltpu.CompilerParams(vmem_limit_bytes=8 * MIB),
        name="add",
    )(*values, *after)


def shards(
    query_latent,
    query_rope,
    cache_latent,
    cache_rope,
    cache_length,
    value_up,
    output_weight,
    residual,
    norm_gain,
    routed_experts,
    expert_gates,
    gate_weight,
    up_weight,
    down_weight,
):
    ep_count = lax.axis_size("ep")
    tp_count = lax.axis_size("tp")
    ep_index = lax.axis_index("ep")
    tp_index = lax.axis_index("tp")
    row_total = routed_experts.shape[0]
    block_rows = row_total // tp_count
    cores = 2
    chips = ep_count // cores

    def from_core(value):
        return lax.ppermute(value, "ep", [(i, i ^ 1) for i in range(ep_count)])

    def from_chip(value, back):
        step = cores * back
        return lax.ppermute(value, "ep", [(i, (i + step) % ep_count) for i in range(ep_count)])

    def from_tp(value, bits):
        return lax.ppermute(value, "tp", [(i, i ^ bits) for i in range(tp_count)])

    def spread_tp(value):
        rows = [value]
        for k in range(1, tp_count):
            low = k & -k
            rows.append(from_tp(rows[k ^ low], low))
        return rows

    def gather_ep(value):
        same = [value] + [from_chip(value, b) for b in range(1, chips)]
        other = [from_core(v) for v in same]
        return [v for pair in zip(same, other) for v in pair]

    chip, core = ep_index // cores, ep_index % cores
    ep_places = [
        (chip - b + chips) % chips * cores + (core if c == 0 else 1 - core)
        for b in range(chips)
        for c in range(cores)
    ]
    tp_places = [tp_index ^ k for k in range(tp_count)]
    places = jnp.stack(ep_places + tp_places).astype(jnp.int32)

    halves = 2
    half_rows = block_rows // halves
    gain = norm_gain.reshape(1, -1)
    gains = gather_ep(gain)
    routed, gates = routed_experts.T, expert_gates.T

    head_out, output_weight = attend(
        query_latent,
        query_rope,
        cache_latent,
        cache_rope,
        cache_length,
        value_up,
        output_weight,
        [places, gain],
    )
    partial = project(places, gather_ep(head_out), output_weight, residual, tp_count, halves)

    gate_weight = fetch(gate_weight, [partial[0][0]])
    terms = [[[(value, 0)] for value in partial[h]] for h in range(halves)]
    first_arrival, second_sum = None, None
    streams, rows_of, blocks = [], [], []

    def send_back(h, k, after):
        total = terms[h][k][0][0]
        if len(terms[h][k]) > 1 or after:
            (total,) = add([[terms[h][k]]], half_rows, after)
        low = k & -k
        arrived = from_tp(total, low)
        terms[h][k ^ low].append((arrived, 0))
        return total, arrived

    last = tp_count - 1
    _, first_arrival = send_back(0, last, [])
    totals = [send_back(0, k, [gate_weight] if k == 1 else []) for k in reversed(range(1, last))]
    up_weight = fetch(up_weight, [totals[0][0]])
    _, late_arrival = send_back(1, last, [totals[0][0]])
    (stream,) = add([[terms[0][0]]], half_rows, [up_weight, *gains])
    streams.append(stream)
    rows_of.append(spread_tp(stream))
    late = [send_back(1, k, [stream]) for k in reversed(range(1, last))]
    down_weight = fetch(down_weight, [stream])
    (stream,) = add([[terms[1][0]]], half_rows, [rows_of[0][tp_count // 2], down_weight])
    streams.append(stream)
    rows_of.append(spread_tp(stream))
    blocks = [[gather_ep(rows) for rows in rows_of[h]] for h in range(halves)]

    slots = list(reversed(range(tp_count)))
    groups = [slots[i : i + 2] for i in range(0, tp_count, 2)]
    terms = [[[] for _ in range(tp_count)] for _ in range(halves)]

    def run_expert(h, hold_gate, hold_down):
        active = activate(places, [blocks[h][k] for k in slots], gains, gate_weight, up_weight, hold_gate)
        outs = project_down(
            places, active, routed, gates, down_weight, groups, h, half_rows, ep_count, cores, hold_down
        )
        return outs, [from_core(out[1]) for out in outs]

    def add_cores(h, g, outs, swapped, after):
        def rows(at, b):
            first = (at * chips + b) * half_rows
            return [(outs[g][0], first), (swapped[g], first)]

        count = len(groups[g])
        return add([[rows(at, b) for at in range(count)] for b in range(chips)], half_rows, after)

    def cross(h, g, sums):
        across = [from_chip(sums[b], chips - b) for b in range(1, chips)]
        for at, k in enumerate(groups[g]):
            terms[h][k] += [(value, at * half_rows) for value in [sums[0]] + across]
        return across

    late_rows = [rows_of[1][last]] + [blocks[1][k][-2] for k in range(last)]
    outs, swapped = run_expert(0, late_rows, blocks[1][last][-2:-1])
    sums = add_cores(0, 0, outs, swapped, [])
    across = cross(0, 0, sums)
    sent = {last: send_back(0, last, [])}
    rest = [add_cores(0, g, outs, swapped, across) for g in range(1, len(groups))]
    late_outs, late_swapped = run_expert(1, sums[-1:], sent[last][:1] + rest[0][-1:])
    for g in range(1, len(groups)):
        across = cross(0, g, rest[g - 1])
    across = cross(1, 0, add_cores(1, 0, late_outs, late_swapped, across + [sent[last][1]]))
    for k in reversed(range(1, last)):
        sent[k] = send_back(0, k, [])
    early = [sent[k][0] for k in range(1, last)]
    for g in range(1, len(groups)):
        across = cross(1, g, add_cores(1, g, late_outs, late_swapped, across + early))
    for k in reversed(range(1, tp_count)):
        send_back(1, k, [sent[k][1]])
    (mixed,) = add([[terms[h][0] for h in range(halves)]], half_rows)
    (stream_out,) = add([[[(stream, 0)] for stream in streams]], half_rows)
    return (stream_out, mixed)


def solution(mesh):
    return jax.shard_map(
        shards,
        mesh=mesh,
        in_specs=(
            P(("parts", "ep"), "tp", None),
            P(("parts", "ep"), "tp"),
            P(("parts", "ep"), None, None),
            P(("parts", "ep"), None, None),
            P(("parts", "ep")),
            P("tp", None, None),
            P("tp", "ep"),
            P("parts", "ep"),
            P("ep"),
            P("parts", None),
            P("parts", None),
            P("ep", None, "tp"),
            P("ep", None, "tp"),
            P("ep", "tp", None),
        ),
        out_specs=(P(("parts", "tp"), "ep"), P(("parts", "tp"), "ep")),
        check_vma=False,
    )
```

```python
import functools

import jax
import jax.numpy as jnp
from jax import lax
from jax.experimental import pallas as pl
from jax.experimental.pallas import tpu as pltpu
from jax.sharding import PartitionSpec as P

score_scale = 1.0 / 192.0**0.5
norm_epsilon = 1e-06
MIB = 1 << 20


def in_hbm(value):
    return pltpu.with_memory_space_constraint(value, pltpu.HBM)


def in_vmem(value):
    return pltpu.with_memory_space_constraint(value, pltpu.VMEM)


def fetch_kernel(parts, *refs):
    source, target, sems = refs[0], refs[-2], refs[-1]
    step = source.shape[-2] // parts
    copies = []
    for i in range(parts):
        cut = (slice(None),) * (len(source.shape) - 2) + (pl.ds(i * step, step),)
        copies.append(pltpu.make_async_copy(source.at[cut], target.at[cut], sems.at[i]))
    for copy in copies:
        copy.start()
    for copy in copies:
        copy.wait()


def fetch(value, after):
    parts = 4
    return pl.pallas_call(
        functools.partial(fetch_kernel, parts),
        out_shape=pltpu.VMEM(value.shape, value.dtype),
        in_specs=[pl.BlockSpec(memory_space=pl.ANY)] * (1 + len(after)),
        out_specs=pl.BlockSpec(memory_space=pltpu.VMEM),
        scratch_shapes=[pltpu.SemaphoreType.DMA((parts,))],
        cost_estimate=pl.CostEstimate(flops=0, bytes_accessed=4 * value.size, transcendentals=0),
        compiler_params=pltpu.CompilerParams(vmem_limit_bytes=1 * MIB),
        name="fetch",
    )(in_hbm(value), *after)


def attention_kernel(step_rows, pieces, lengths, q_ref, qr_ref, k_hbm, kr_hbm, up_ref, *refs):
    out_ref, latent, rope, k_ref, kr_ref, sems = refs[-6:]
    step = pl.program_id(0)
    heads, positions = q_ref.shape[1], k_ref.shape[1]
    rope_width = kr_ref.shape[1]

    def copies(at):
        whole = pl.ds(at * step_rows, step_rows)
        made = [pltpu.make_async_copy(kr_hbm.at[whole], kr_ref.at[whole], sems.at[at, pieces])]
        for i in range(pieces):
            part = pl.ds(at * step_rows + i * (step_rows // pieces), step_rows // pieces)
            made.append(pltpu.make_async_copy(k_hbm.at[part], k_ref.at[part], sems.at[at, i]))
        return made

    @pl.when(step == 0)
    def _():
        for at in range(k_ref.shape[0] // step_rows):
            for copy in copies(at):
                copy.start()
        all_rows = qr_ref.shape[0]
        width = heads * rope_width
        lane = lax.broadcasted_iota(jnp.int32, (heads, width), 1)
        head = lax.broadcasted_iota(jnp.int32, (heads, width), 0)
        own = jnp.where(lane // rope_width == head, 1.0, 0.0)
        spread = qr_ref[...].astype(jnp.float32)[:, None, :] * own[None, :, :]
        spread = spread.reshape(all_rows * heads, width).astype(jnp.bfloat16)
        lane = lax.broadcasted_iota(jnp.int32, (width, rope_width), 0)
        column = lax.broadcasted_iota(jnp.int32, (width, rope_width), 1)
        fold = jnp.where(lane % rope_width == column, 1.0, 0.0).astype(jnp.bfloat16)
        rope[...] = jnp.dot(spread, fold, preferred_element_type=jnp.float32)

    for copy in copies(step):
        copy.wait()
    place = lax.broadcasted_iota(jnp.int32, (heads, positions), 1)
    lanes = latent.shape[2]
    lanes = latent.shape[2]
    scores = []
    for r in range(step_rows):
        first = pl.multiple_of((step * step_rows + r) * heads, heads)
        score = lax.dot_general(
            q_ref[r], k_ref[step * step_rows + r], (((1,), (1,)), ((), ())), preferred_element_type=jnp.float32
        )
        score += jnp.dot(
            rope[pl.ds(first, heads), :].astype(jnp.bfloat16), kr_ref[step * step_rows + r], preferred_element_type=jnp.float32
        )
        scores.append(score)
    probabilities = []
    for r in range(step_rows):
        visible = place < lengths[step * step_rows + r]
        score = jnp.where(visible, scores[r] * score_scale, -jnp.inf)
        weight = jnp.exp(score - jnp.max(score, axis=-1, keepdims=True))
        total = jnp.sum(weight, axis=-1, keepdims=True)
        probabilities.append((weight / total).astype(jnp.bfloat16))
    for r in range(step_rows):
        first = pl.multiple_of((step * step_rows + r) * heads, heads)
        mixed = jnp.dot(probabilities[r], k_ref[step * step_rows + r], preferred_element_type=jnp.float32)
        for c in range(latent.shape[0]):
            latent[c, pl.ds(first, heads), :] = mixed[:, c * lanes : (c + 1) * lanes]

    @pl.when(step == pl.num_programs(0) - 1)
    def _():
        rows = out_ref.shape[0]
        width = up_ref.shape[2]
        for h in range(heads):
            parts = [latent[c, pl.ds(h, rows, stride=heads), :] for c in range(latent.shape[0])]
            part = jnp.concatenate(parts, axis=1).astype(jnp.bfloat16)
            out_ref[:, h * width : (h + 1) * width] = jnp.dot(
                part, up_ref[h], preferred_element_type=jnp.float32
            ).astype(jnp.bfloat16)


def attend(query_latent, query_rope, cache_latent, cache_rope, cache_length, value_up, after):
    rows, heads, latent_width = query_latent.shape
    rope_width = cache_rope.shape[1]
    value_width = value_up.shape[2]
    step_rows, pieces = 16, 2
    by_row = lambda i, lengths: (i, 0, 0)
    return pl.pallas_call(
        functools.partial(attention_kernel, step_rows, pieces),
        out_shape=jax.ShapeDtypeStruct((rows, heads * value_width), jnp.bfloat16),
        grid_spec=pltpu.PrefetchScalarGridSpec(
            num_scalar_prefetch=1,
            grid=(rows // step_rows,),
            in_specs=[
                pl.BlockSpec((step_rows, heads, latent_width), by_row),
                pl.BlockSpec(query_rope.shape, lambda i, lengths: (0, 0)),
                pl.BlockSpec(memory_space=pl.ANY),
                pl.BlockSpec(memory_space=pl.ANY),
                pl.BlockSpec(value_up.shape, lambda i, lengths: (0, 0, 0)),
            ]
            + [pl.BlockSpec(memory_space=pl.ANY)] * len(after),
            out_specs=pl.BlockSpec((rows, heads * value_width), lambda i, lengths: (0, 0)),
            scratch_shapes=[
                pltpu.VMEM((latent_width // 128, rows * heads, 128), jnp.float32),
                pltpu.VMEM((rows * heads, rope_width), jnp.float32),
                pltpu.VMEM(cache_latent.shape, jnp.bfloat16),
                pltpu.VMEM(cache_rope.shape, jnp.bfloat16),
                pltpu.SemaphoreType.DMA((rows // step_rows, pieces + 1)),
            ],
        ),
        cost_estimate=pl.CostEstimate(
            flops=64 * heads * cache_latent.size, bytes_accessed=2 * cache_latent.size, transcendentals=0
        ),
        compiler_params=pltpu.CompilerParams(vmem_limit_bytes=28 * MIB),
        name="attention",
    )(
        cache_length,
        in_hbm(query_latent),
        in_hbm(query_rope),
        in_hbm(cache_latent),
        in_hbm(cache_rope),
        in_hbm(value_up),
        *after,
    )


def projection_kernel(count, out_count, places, *refs):
    blocks, weight, outs = refs[:count], refs[count], refs[-2 - out_count : -2]
    gathered, result = refs[-2:]
    height = blocks[0].shape[0]
    for k in range(count):
        first = pl.multiple_of(places[k] * height, height)
        gathered[pl.ds(first, height), :] = blocks[k][...]
    columns = weight.shape[1]
    tile = 256 if columns % 256 == 0 else 128
    for j in range(columns // tile):
        result[:, j * tile : (j + 1) * tile] = jnp.dot(
            gathered[...], weight[:, j * tile : (j + 1) * tile], preferred_element_type=jnp.float32
        ).astype(jnp.bfloat16)
    out_height = outs[0].shape[0]
    for s in range(len(outs)):
        first = pl.multiple_of(places[count + s] * out_height, out_height)
        outs[s][...] = result[pl.ds(first, out_height), :]


def project(places, blocks, weight, out_count):
    count = len(blocks)
    height, depth = blocks[0].shape
    rows, columns = height * count, weight.shape[1]
    whole = pl.BlockSpec(memory_space=pltpu.VMEM)
    return pl.pallas_call(
        functools.partial(projection_kernel, count, out_count),
        out_shape=[jax.ShapeDtypeStruct((rows // out_count, columns), jnp.bfloat16)] * out_count,
        in_specs=[pl.BlockSpec(memory_space=pltpu.SMEM)] + [whole] * (count + 1),
        out_specs=[whole] * out_count,
        scratch_shapes=[
            pltpu.VMEM((rows, depth), jnp.bfloat16),
            pltpu.VMEM((rows, columns), jnp.bfloat16),
        ],
        cost_estimate=pl.CostEstimate(flops=2 * rows * depth * columns, bytes_accessed=4 * MIB, transcendentals=0),
        compiler_params=pltpu.CompilerParams(vmem_limit_bytes=8 * MIB),
        name="projection",
    )(places, *blocks, in_vmem(weight))


def gate_kernel(row_blocks, column_blocks, model_width, places, *refs):
    count = row_blocks * column_blocks
    blocks, gains = refs[:count], refs[count : count + column_blocks]
    gate, up = refs[count + column_blocks : count + column_blocks + 2]
    active, x, gate_sum, up_sum = refs[-4:]
    height, width = blocks[0].shape
    hidden = gate.shape[2]
    squares = [jnp.zeros((height, 1), jnp.float32) for _ in range(row_blocks)]
    tile = min(256, hidden)
    for k in range(column_blocks):
        for s in range(row_blocks):
            wide = blocks[s * column_blocks + k][...].astype(jnp.float32)
            squares[s] += jnp.sum(wide * wide, axis=-1, keepdims=True)
            x[k, s * height : (s + 1) * height, :] = (wide * gains[k][...]).astype(jnp.bfloat16)
        depth = pl.ds(pl.multiple_of(places[k] * width, 128), width)
        for total, weight in ((gate_sum, gate), (up_sum, up)):
            for j in range(hidden // tile):
                cut = slice(j * tile, (j + 1) * tile)
                product = jnp.dot(x[k], weight[0, depth, cut], preferred_element_type=jnp.float32)
                if k == 0:
                    total[:, cut] = product
                else:
                    total[:, cut] += product
    for s in range(row_blocks):
        rows = slice(s * height, (s + 1) * height)
        scale = lax.rsqrt(squares[s] / model_width + norm_epsilon)
        gate_part = gate_sum[rows, :] * scale
        up_part = up_sum[rows, :] * scale
        active[rows, :] = (gate_part / (1.0 + jnp.exp(-gate_part)) * up_part).astype(jnp.bfloat16)


def activate(places, blocks, gains, gate_weight, up_weight, after):
    row_blocks, column_blocks = len(blocks), len(blocks[0])
    height, width = blocks[0][0].shape
    rows = row_blocks * height
    model_width, hidden = gate_weight.shape[1:]
    whole = pl.BlockSpec(memory_space=pltpu.VMEM)
    count = row_blocks * column_blocks
    return pl.pallas_call(
        functools.partial(gate_kernel, row_blocks, column_blocks, model_width),
        out_shape=jax.ShapeDtypeStruct((rows, hidden), jnp.bfloat16),
        in_specs=[pl.BlockSpec(memory_space=pltpu.SMEM)]
        + [whole] * (count + column_blocks + 2)
        + [pl.BlockSpec(memory_space=pl.ANY)] * len(after),
        out_specs=whole,
        scratch_shapes=[
            pltpu.VMEM((column_blocks, rows, width), jnp.bfloat16),
            pltpu.VMEM((rows, hidden), jnp.float32),
            pltpu.VMEM((rows, hidden), jnp.float32),
        ],
        cost_estimate=pl.CostEstimate(
            flops=4 * rows * gate_weight.size, bytes_accessed=4 * gate_weight.size, transcendentals=rows * hidden
        ),
        compiler_params=pltpu.CompilerParams(vmem_limit_bytes=2 * rows * (model_width + 4 * hidden) + 4 * MIB),
        name="activate",
    )(places, *[b for row in blocks for b in row], *gains, in_vmem(gate_weight), in_vmem(up_weight), *after)


def down_kernel(slots, column_blocks, cores, core, places, active, row_weight, down, *refs):
    row_blocks = len(slots)
    outs = refs[-row_blocks:]
    width = down.shape[2] // column_blocks
    height = active.shape[0] // row_blocks
    tile = 256 if width % 256 == 0 else 128
    weights = []
    for s in range(row_blocks):
        first = pl.multiple_of(places[column_blocks + slots[s]] * height, height)
        weights.append(row_weight[pl.ds(first, height), :])
    for b in range(column_blocks // cores):
        k = b * cores + core
        start = pl.multiple_of(places[k] * width, 128)
        for j in range(width // tile):
            cut = slice(j * tile, (j + 1) * tile)
            product = jnp.dot(
                active[...], down[0, :, pl.ds(start + j * tile, tile)], preferred_element_type=jnp.float32
            )
            for s in range(row_blocks):
                part = product[s * height : (s + 1) * height, :] * weights[s]
                outs[s][b * height : (b + 1) * height, cut] = part.astype(jnp.bfloat16)


def project_down(places, active, row_weight, down_weight, slots, column_blocks, cores, core, after):
    row_blocks = len(slots)
    rows = active.shape[0]
    width = down_weight.shape[2] // column_blocks
    whole = pl.BlockSpec(memory_space=pltpu.VMEM)
    out = jax.ShapeDtypeStruct((rows // row_blocks * (column_blocks // cores), width), jnp.bfloat16)
    outs = pl.pallas_call(
        functools.partial(down_kernel, slots, column_blocks, cores, core),
        out_shape=[out] * row_blocks,
        in_specs=[pl.BlockSpec(memory_space=pltpu.SMEM)]
        + [whole] * 3
        + [pl.BlockSpec(memory_space=pl.ANY)] * len(after),
        out_specs=[whole] * row_blocks,
        cost_estimate=pl.CostEstimate(
            flops=2 * rows * down_weight.size // cores, bytes_accessed=2 * down_weight.size // cores, transcendentals=0
        ),
        compiler_params=pltpu.CompilerParams(vmem_limit_bytes=4 * MIB),
        name="down",
    )(places, active, row_weight, in_vmem(down_weight), *after)
    return outs


def add_kernel(groups, *refs):
    used = sum(len(g) for g in groups)
    outs = refs[-len(groups) :]
    at = 0
    for group, out in zip(groups, outs):
        total = None
        for first in group:
            value = refs[at][first : first + out.shape[0], :].astype(jnp.float32)
            total = value if total is None else total + value
            at += 1
        out[...] = total.astype(jnp.bfloat16)


def add(groups, height, after=()):
    values = [value for group in groups for value, _ in group]
    width = values[0].shape[1]
    whole = pl.BlockSpec(memory_space=pltpu.VMEM)
    return pl.pallas_call(
        functools.partial(add_kernel, [[first for _, first in group] for group in groups]),
        out_shape=[jax.ShapeDtypeStruct((height, width), jnp.bfloat16)] * len(groups),
        in_specs=[whole] * len(values) + [pl.BlockSpec(memory_space=pl.ANY)] * len(after),
        out_specs=[whole] * len(groups),
        compiler_params=pltpu.CompilerParams(vmem_limit_bytes=8 * MIB),
        name="add",
    )(*values, *after)


def shards(
    query_latent,
    query_rope,
    cache_latent,
    cache_rope,
    cache_length,
    value_up,
    output_weight,
    residual,
    norm_gain,
    routed_experts,
    expert_gates,
    gate_weight,
    up_weight,
    down_weight,
):
    ep_count = lax.axis_size("ep")
    tp_count = lax.axis_size("tp")
    ep_index = lax.axis_index("ep")
    tp_index = lax.axis_index("tp")
    row_total = routed_experts.shape[0]
    block_rows = row_total // tp_count
    cores = 2
    chips = ep_count // cores

    def from_core(value):
        return lax.ppermute(value, "ep", [(i, i ^ 1) for i in range(ep_count)])

    def from_chip(value, back):
        step = cores * back
        return lax.ppermute(value, "ep", [(i, (i + step) % ep_count) for i in range(ep_count)])

    def from_tp(value, bits):
        return lax.ppermute(value, "tp", [(i, i ^ bits) for i in range(tp_count)])

    def gather_ep(value):
        same = [value] + [from_chip(value, b) for b in range(1, chips)]
        other = [from_core(v) for v in same]
        return [v for pair in zip(same, other) for v in pair]

    chip, core = ep_index // cores, ep_index % cores
    ep_places = [
        (chip - b + chips) % chips * cores + (core if c == 0 else 1 - core)
        for b in range(chips)
        for c in range(cores)
    ]
    tp_places = [tp_index ^ k for k in range(tp_count)]
    places = jnp.stack(ep_places + tp_places).astype(jnp.int32)

    gain = norm_gain.reshape(1, -1)
    gains = gather_ep(gain)
    own_residual = lax.dynamic_slice_in_dim(residual, tp_index * block_rows, block_rows, 0)
    row_weight = jnp.sum(jnp.where(routed_experts == ep_index, expert_gates, 0.0), axis=-1, keepdims=True)

    head_out = attend(query_latent, query_rope, cache_latent, cache_rope, cache_length, value_up, [places])
    output_weight = fetch(output_weight, [head_out, row_weight, own_residual, gain])
    partial = project(places, gather_ep(head_out), output_weight, tp_count)

    up_weight = fetch(up_weight, [partial[0]])
    terms = [[(value, 0)] for value in partial]
    for k in reversed(range(1, tp_count)):
        total = terms[k][0][0]
        if len(terms[k]) > 1 or k == 1:
            (total,) = add([terms[k]], block_rows, [gate_weight if k == 1 else up_weight])
        if k == tp_count // 2:
            gate_weight = fetch(gate_weight, [total])
        low = k & -k
        arrived = from_tp(total, low)
        terms[k ^ low].append((arrived, 0))
    down_weight = fetch(down_weight, [total])
    stream_terms = terms[0] + [(own_residual, 0)]
    stream, stream_out = add([stream_terms, stream_terms], block_rows, gains + [gate_weight, up_weight, down_weight])

    rows_of = {0: stream}
    for k in range(1, tp_count):
        low = k & -k
        rows_of[k] = from_tp(rows_of[k ^ low], low)
    blocks = [gather_ep(rows_of[k]) for k in range(tp_count)]

    slots = list(reversed(range(tp_count)))
    active = activate(places, [blocks[k] for k in slots], gains, gate_weight, up_weight, [])
    others = project_down(places, active, row_weight, down_weight, slots, ep_count, cores, 1, [])
    swapped = [from_core(out) for out in others]
    outs = project_down(places, active, row_weight, down_weight, slots, ep_count, cores, 0, others[:1])
    terms = [[] for _ in range(tp_count)]
    across = []
    for at, k in enumerate(slots):
        pair = [[(outs[at], c * block_rows), (swapped[at], c * block_rows)] for c in range(chips)]
        sums = add(pair, block_rows, across)
        across = [from_chip(sums[c], chips - c) for c in range(1, chips)]
        terms[k] += [(value, 0) for value in [sums[0]] + across]
        if k:
            (total,) = add([terms[k]], block_rows)
            low = k & -k
            terms[k ^ low].append((from_tp(total, low), 0))
    (mixed,) = add([terms[0]], block_rows)
    return (stream_out, mixed)


def solution(mesh):
    return jax.shard_map(
        shards,
        mesh=mesh,
        in_specs=(
            P(("parts", "ep"), "tp", None),
            P(("parts", "ep"), "tp"),
            P(("parts", "ep"), None, None),
            P(("parts", "ep"), None, None),
            P(("parts", "ep")),
            P("tp", None, None),
            P("tp", "ep"),
            P("parts", "ep"),
            P("ep"),
            P("parts", None),
            P("parts", None),
            P("ep", None, "tp"),
            P("ep", None, "tp"),
            P("ep", "tp", None),
        ),
        out_specs=(P(("parts", "tp"), "ep"), P(("parts", "tp"), "ep")),
        check_vma=False,
    )
```

```python
import functools

import jax
import jax.numpy as jnp
from jax import lax
from jax.experimental import pallas as pl
from jax.experimental.pallas import tpu as pltpu
from jax.sharding import PartitionSpec as P

score_scale = 1.0 / 192.0**0.5
norm_epsilon = 1e-06
MIB = 1 << 20


def in_hbm(value):
    return pltpu.with_memory_space_constraint(value, pltpu.HBM)


def in_vmem(value):
    return pltpu.with_memory_space_constraint(value, pltpu.VMEM)


def fetch_kernel(parts, *refs):
    source, target, sems = refs[0], refs[-2], refs[-1]
    step = source.shape[-2] // parts
    copies = []
    for i in range(parts):
        cut = (slice(None),) * (len(source.shape) - 2) + (pl.ds(i * step, step),)
        copies.append(pltpu.make_async_copy(source.at[cut], target.at[cut], sems.at[i]))
    for copy in copies:
        copy.start()
    for copy in copies:
        copy.wait()


def fetch(value, after):
    parts = 4
    return pl.pallas_call(
        functools.partial(fetch_kernel, parts),
        out_shape=pltpu.VMEM(value.shape, value.dtype),
        in_specs=[pl.BlockSpec(memory_space=pl.ANY)] * (1 + len(after)),
        out_specs=pl.BlockSpec(memory_space=pltpu.VMEM),
        scratch_shapes=[pltpu.SemaphoreType.DMA((parts,))],
        cost_estimate=pl.CostEstimate(flops=0, bytes_accessed=4 * value.size, transcendentals=0),
        compiler_params=pltpu.CompilerParams(vmem_limit_bytes=1 * MIB),
        name="fetch",
    )(in_hbm(value), *after)


def attention_kernel(step_rows, pieces, ahead, lengths, q_ref, qr_ref, k_hbm, kr_hbm, up_ref, *refs):
    out_ref, latent, rope, k_ref, kr_ref, sems = refs[-6:]
    step = pl.program_id(0)
    steps = k_ref.shape[0] // step_rows
    heads, positions = q_ref.shape[1], k_ref.shape[1]
    rope_width = kr_ref.shape[1]

    def copies(at):
        whole = pl.ds(at * step_rows, step_rows)
        made = [pltpu.make_async_copy(kr_hbm.at[whole], kr_ref.at[whole], sems.at[at, pieces])]
        for i in range(pieces):
            part = pl.ds(at * step_rows + i * (step_rows // pieces), step_rows // pieces)
            made.append(pltpu.make_async_copy(k_hbm.at[part], k_ref.at[part], sems.at[at, i]))
        return made

    @pl.when(step == 0)
    def _():
        for at in range(min(ahead, steps)):
            for copy in copies(at):
                copy.start()
        all_rows = qr_ref.shape[0]
        width = heads * rope_width
        lane = lax.broadcasted_iota(jnp.int32, (heads, width), 1)
        head = lax.broadcasted_iota(jnp.int32, (heads, width), 0)
        own = jnp.where(lane // rope_width == head, 1.0, 0.0)
        spread = qr_ref[...].astype(jnp.float32)[:, None, :] * own[None, :, :]
        spread = spread.reshape(all_rows * heads, width).astype(jnp.bfloat16)
        lane = lax.broadcasted_iota(jnp.int32, (width, rope_width), 0)
        column = lax.broadcasted_iota(jnp.int32, (width, rope_width), 1)
        fold = jnp.where(lane % rope_width == column, 1.0, 0.0).astype(jnp.bfloat16)
        rope[...] = jnp.dot(spread, fold, preferred_element_type=jnp.float32)

    @pl.when(step + ahead < steps)
    def _():
        for copy in copies(step + ahead):
            copy.start()

    for copy in copies(step):
        copy.wait()
    place = lax.broadcasted_iota(jnp.int32, (heads, positions), 1)
    lanes = latent.shape[2]
    lanes = latent.shape[2]
    scores = []
    for r in range(step_rows):
        first = pl.multiple_of((step * step_rows + r) * heads, heads)
        score = lax.dot_general(
            q_ref[r], k_ref[step * step_rows + r], (((1,), (1,)), ((), ())), preferred_element_type=jnp.float32
        )
        score += jnp.dot(
            rope[pl.ds(first, heads), :].astype(jnp.bfloat16), kr_ref[step * step_rows + r], preferred_element_type=jnp.float32
        )
        scores.append(score)
    probabilities = []
    for r in range(step_rows):
        visible = place < lengths[step * step_rows + r]
        score = jnp.where(visible, scores[r] * score_scale, -jnp.inf)
        weight = jnp.exp(score - jnp.max(score, axis=-1, keepdims=True))
        total = jnp.sum(weight, axis=-1, keepdims=True)
        probabilities.append((weight / total).astype(jnp.bfloat16))
    for r in range(step_rows):
        first = pl.multiple_of((step * step_rows + r) * heads, heads)
        mixed = jnp.dot(probabilities[r], k_ref[step * step_rows + r], preferred_element_type=jnp.float32)
        for c in range(latent.shape[0]):
            latent[c, pl.ds(first, heads), :] = mixed[:, c * lanes : (c + 1) * lanes]

    @pl.when(step == pl.num_programs(0) - 1)
    def _():
        rows = out_ref.shape[0]
        width = up_ref.shape[2]
        for h in range(heads):
            parts = [latent[c, pl.ds(h, rows, stride=heads), :] for c in range(latent.shape[0])]
            part = jnp.concatenate(parts, axis=1).astype(jnp.bfloat16)
            out_ref[:, h * width : (h + 1) * width] = jnp.dot(
                part, up_ref[h], preferred_element_type=jnp.float32
            ).astype(jnp.bfloat16)


def attend(query_latent, query_rope, cache_latent, cache_rope, cache_length, value_up, after):
    rows, heads, latent_width = query_latent.shape
    rope_width = cache_rope.shape[1]
    value_width = value_up.shape[2]
    step_rows, pieces, ahead = 8, 1, 3
    by_row = lambda i, lengths: (i, 0, 0)
    return pl.pallas_call(
        functools.partial(attention_kernel, step_rows, pieces, ahead),
        out_shape=jax.ShapeDtypeStruct((rows, heads * value_width), jnp.bfloat16),
        grid_spec=pltpu.PrefetchScalarGridSpec(
            num_scalar_prefetch=1,
            grid=(rows // step_rows,),
            in_specs=[
                pl.BlockSpec((step_rows, heads, latent_width), by_row),
                pl.BlockSpec(query_rope.shape, lambda i, lengths: (0, 0)),
                pl.BlockSpec(memory_space=pl.ANY),
                pl.BlockSpec(memory_space=pl.ANY),
                pl.BlockSpec(value_up.shape, lambda i, lengths: (0, 0, 0)),
            ]
            + [pl.BlockSpec(memory_space=pl.ANY)] * len(after),
            out_specs=pl.BlockSpec((rows, heads * value_width), lambda i, lengths: (0, 0)),
            scratch_shapes=[
                pltpu.VMEM((latent_width // 128, rows * heads, 128), jnp.float32),
                pltpu.VMEM((rows * heads, rope_width), jnp.float32),
                pltpu.VMEM(cache_latent.shape, jnp.bfloat16),
                pltpu.VMEM(cache_rope.shape, jnp.bfloat16),
                pltpu.SemaphoreType.DMA((rows // step_rows, pieces + 1)),
            ],
        ),
        cost_estimate=pl.CostEstimate(
            flops=64 * heads * cache_latent.size, bytes_accessed=2 * cache_latent.size, transcendentals=0
        ),
        compiler_params=pltpu.CompilerParams(vmem_limit_bytes=28 * MIB),
        name="attention",
    )(
        cache_length,
        in_hbm(query_latent),
        in_hbm(query_rope),
        in_hbm(cache_latent),
        in_hbm(cache_rope),
        in_hbm(value_up),
        *after,
    )


def projection_kernel(count, out_count, places, *refs):
    blocks, weight, outs = refs[:count], refs[count], refs[-2 - out_count : -2]
    gathered, result = refs[-2:]
    height = blocks[0].shape[0]
    for k in range(count):
        first = pl.multiple_of(places[k] * height, height)
        gathered[pl.ds(first, height), :] = blocks[k][...]
    columns = weight.shape[1]
    tile = 256 if columns % 256 == 0 else 128
    for j in range(columns // tile):
        result[:, j * tile : (j + 1) * tile] = jnp.dot(
            gathered[...], weight[:, j * tile : (j + 1) * tile], preferred_element_type=jnp.float32
        ).astype(jnp.bfloat16)
    out_height = outs[0].shape[0]
    for s in range(len(outs)):
        first = pl.multiple_of(places[count + s] * out_height, out_height)
        outs[s][...] = result[pl.ds(first, out_height), :]


def project(places, blocks, weight, out_count):
    count = len(blocks)
    height, depth = blocks[0].shape
    rows, columns = height * count, weight.shape[1]
    whole = pl.BlockSpec(memory_space=pltpu.VMEM)
    return pl.pallas_call(
        functools.partial(projection_kernel, count, out_count),
        out_shape=[jax.ShapeDtypeStruct((rows // out_count, columns), jnp.bfloat16)] * out_count,
        in_specs=[pl.BlockSpec(memory_space=pltpu.SMEM)] + [whole] * (count + 1),
        out_specs=[whole] * out_count,
        scratch_shapes=[
            pltpu.VMEM((rows, depth), jnp.bfloat16),
            pltpu.VMEM((rows, columns), jnp.bfloat16),
        ],
        cost_estimate=pl.CostEstimate(flops=2 * rows * depth * columns, bytes_accessed=4 * MIB, transcendentals=0),
        compiler_params=pltpu.CompilerParams(vmem_limit_bytes=8 * MIB),
        name="projection",
    )(places, *blocks, in_vmem(weight))


def gate_kernel(row_blocks, cores, first, count, model_width, places, *refs):
    blocks, gains = refs[: row_blocks * count], refs[row_blocks * count : (row_blocks + 1) * count]
    refs = refs[(row_blocks + 1) * count :]
    gate, up, refs = refs[0], refs[1], refs[2:]
    if first:
        before, (active, x) = refs[:3], refs[-2:]
        gate_sum, up_sum, squares = before
    else:
        gate_sum, up_sum, squares, x = refs[-4:]
    height, width = blocks[0].shape
    hidden = gate.shape[2]
    tile = min(256, hidden)
    sums = [[None] * (hidden // tile), [None] * (hidden // tile)]
    totals = [squares[s * height : (s + 1) * height, :] if first else 0.0 for s in range(row_blocks)]
    for k in range(count):
        for s in range(row_blocks):
            wide = blocks[s * count + k][...].astype(jnp.float32)
            totals[s] += jnp.sum(wide * wide, axis=-1, keepdims=True)
            x[s * height : (s + 1) * height, k * width : (k + 1) * width] = (wide * gains[k][...]).astype(jnp.bfloat16)
    for w, (weight, start) in enumerate(((gate, gate_sum), (up, up_sum))):
        for j in range(hidden // tile):
            cut = slice(j * tile, (j + 1) * tile)
            total = start[:, cut] if first else None
            for k in range(count):
                depth = pl.ds(pl.multiple_of(places[first + k] * width, 128), width)
                product = jnp.dot(
                    x[:, k * width : (k + 1) * width], weight[0, depth, cut], preferred_element_type=jnp.float32
                )
                total = product if total is None else total + product
            sums[w][j] = total
            if not first:
                start[:, cut] = total
    if not first:
        for s in range(row_blocks):
            squares[s * height : (s + 1) * height, :] = totals[s]
        return
    scale = jnp.concatenate([lax.rsqrt(t / model_width + norm_epsilon) for t in totals], axis=0)
    for j in range(hidden // tile):
        gate_part = sums[0][j] * scale
        up_part = sums[1][j] * scale
        active[:, j * tile : (j + 1) * tile] = (gate_part / (1.0 + jnp.exp(-gate_part)) * up_part).astype(jnp.bfloat16)


def activate(places, blocks, gains, gate_weight, up_weight, cores, first, before):
    row_blocks, count = len(blocks), len(blocks[0])
    height, width = blocks[0][0].shape
    rows = row_blocks * height
    model_width, hidden = gate_weight.shape[1:]
    whole = pl.BlockSpec(memory_space=pltpu.VMEM)
    if first:
        kinds = jax.ShapeDtypeStruct((rows, hidden), jnp.bfloat16)
    else:
        kinds = [jax.ShapeDtypeStruct((rows, n), jnp.float32) for n in (hidden, hidden, 1)]
    return pl.pallas_call(
        functools.partial(gate_kernel, row_blocks, cores, first, count, model_width),
        out_shape=kinds,
        in_specs=[pl.BlockSpec(memory_space=pltpu.SMEM)] + [whole] * ((row_blocks + 1) * count + 2 + len(before)),
        out_specs=whole if first else [whole] * 3,
        scratch_shapes=[pltpu.VMEM((rows, count * width), jnp.bfloat16)],
        cost_estimate=pl.CostEstimate(
            flops=4 * rows * hidden * count * width, bytes_accessed=4 * hidden * count * width, transcendentals=0
        ),
        compiler_params=pltpu.CompilerParams(vmem_limit_bytes=2 * rows * (count * width + 8 * hidden) + 4 * MIB),
        name="activate",
    )(places, *[b for row in blocks for b in row], *gains, in_vmem(gate_weight), in_vmem(up_weight), *before)


def down_kernel(slots, at, column_blocks, cores, places, active, row_weight, down, *refs):
    row_blocks = len(slots)
    outs = refs[-row_blocks * cores :]
    width = down.shape[2] // column_blocks
    height = outs[0].shape[0] * cores // column_blocks
    mine = slice(at * row_blocks * height, (at + 1) * row_blocks * height)
    order = [b * cores + c for c in reversed(range(cores)) for b in range(column_blocks // cores)]
    tile = 256 if width % 256 == 0 else 128
    weights = []
    for s in range(row_blocks):
        first = pl.multiple_of(places[column_blocks + slots[s]] * height, height)
        weights.append(row_weight[pl.ds(first, height), :])
    for k in order:
        b, c = k // cores, k % cores
        start = pl.multiple_of(places[k] * width, 128)
        for j in range(width // tile):
            cut = slice(j * tile, (j + 1) * tile)
            product = jnp.dot(
                active[mine, :], down[0, :, pl.ds(start + j * tile, tile)], preferred_element_type=jnp.float32
            )
            for s in range(row_blocks):
                part = product[s * height : (s + 1) * height, :] * weights[s]
                outs[s * cores + c][b * height : (b + 1) * height, cut] = part.astype(jnp.bfloat16)


def project_down(places, active, row_weight, down_weight, slots, at, height, column_blocks, cores, after):
    row_blocks = len(slots)
    rows = row_blocks * height
    width = down_weight.shape[2] // column_blocks
    whole = pl.BlockSpec(memory_space=pltpu.VMEM)
    out = jax.ShapeDtypeStruct((height * (column_blocks // cores), width), jnp.bfloat16)
    outs = pl.pallas_call(
        functools.partial(down_kernel, slots, at, column_blocks, cores),
        out_shape=[out] * (row_blocks * cores),
        in_specs=[pl.BlockSpec(memory_space=pltpu.SMEM)]
        + [whole] * 3
        + [pl.BlockSpec(memory_space=pl.ANY)] * len(after),
        out_specs=[whole] * (row_blocks * cores),
        cost_estimate=pl.CostEstimate(
            flops=2 * rows * down_weight.size, bytes_accessed=2 * down_weight.size, transcendentals=0
        ),
        compiler_params=pltpu.CompilerParams(vmem_limit_bytes=4 * MIB),
        name="down",
    )(places, active, row_weight, in_vmem(down_weight), *after)
    return [outs[s * cores : (s + 1) * cores] for s in range(row_blocks)]


def add_kernel(groups, *refs):
    used = sum(len(g) for g in groups)
    outs = refs[-len(groups) :]
    at = 0
    for group, out in zip(groups, outs):
        total = None
        for first in group:
            value = refs[at][first : first + out.shape[0], :].astype(jnp.float32)
            total = value if total is None else total + value
            at += 1
        out[...] = total.astype(jnp.bfloat16)


def add(groups, height, after=()):
    values = [value for group in groups for value, _ in group]
    width = values[0].shape[1]
    whole = pl.BlockSpec(memory_space=pltpu.VMEM)
    return pl.pallas_call(
        functools.partial(add_kernel, [[first for _, first in group] for group in groups]),
        out_shape=[jax.ShapeDtypeStruct((height, width), jnp.bfloat16)] * len(groups),
        in_specs=[whole] * len(values) + [pl.BlockSpec(memory_space=pl.ANY)] * len(after),
        out_specs=[whole] * len(groups),
        compiler_params=pltpu.CompilerParams(vmem_limit_bytes=8 * MIB),
        name="add",
    )(*values, *after)


def shards(
    query_latent,
    query_rope,
    cache_latent,
    cache_rope,
    cache_length,
    value_up,
    output_weight,
    residual,
    norm_gain,
    routed_experts,
    expert_gates,
    gate_weight,
    up_weight,
    down_weight,
):
    ep_count = lax.axis_size("ep")
    tp_count = lax.axis_size("tp")
    ep_index = lax.axis_index("ep")
    tp_index = lax.axis_index("tp")
    row_total = routed_experts.shape[0]
    block_rows = row_total // tp_count
    cores = 2
    chips = ep_count // cores

    def from_core(value):
        return lax.ppermute(value, "ep", [(i, i ^ 1) for i in range(ep_count)])

    def from_chip(value, back):
        step = cores * back
        return lax.ppermute(value, "ep", [(i, (i + step) % ep_count) for i in range(ep_count)])

    def from_tp(value, bits):
        return lax.ppermute(value, "tp", [(i, i ^ bits) for i in range(tp_count)])

    def gather_ep(value):
        same = [value] + [from_chip(value, b) for b in range(1, chips)]
        other = [from_core(v) for v in same]
        return [v for pair in zip(same, other) for v in pair]

    chip, core = ep_index // cores, ep_index % cores
    ep_places = [
        (chip - b + chips) % chips * cores + (core if c == 0 else 1 - core)
        for b in range(chips)
        for c in range(cores)
    ]
    tp_places = [tp_index ^ k for k in range(tp_count)]
    places = jnp.stack(ep_places + tp_places).astype(jnp.int32)

    gain = norm_gain.reshape(1, -1)
    gains = gather_ep(gain)
    own_residual = lax.dynamic_slice_in_dim(residual, tp_index * block_rows, block_rows, 0)
    row_weight = jnp.sum(jnp.where(routed_experts == ep_index, expert_gates, 0.0), axis=-1, keepdims=True)

    head_out = attend(query_latent, query_rope, cache_latent, cache_rope, cache_length, value_up, [places])
    output_weight = fetch(output_weight, [head_out, row_weight, own_residual, gain])
    partial = project(places, gather_ep(head_out), output_weight, tp_count)

    gate_weight = fetch(gate_weight, [partial[0]])
    terms = [[(value, 0)] for value in partial]
    for k in reversed(range(1, tp_count)):
        total = terms[k][0][0]
        if len(terms[k]) > 1 or k == 1:
            (total,) = add([terms[k]], block_rows, [gate_weight] if k == 1 else [])
        low = k & -k
        arrived = from_tp(total, low)
        terms[k ^ low].append((arrived, 0))
    up_weight = fetch(up_weight, [total])
    down_weight = fetch(down_weight, [total])
    stream_terms = terms[0] + [(own_residual, 0)]
    stream, stream_out = add([stream_terms, stream_terms], block_rows, gains + [gate_weight, up_weight, down_weight])

    rows_of = {0: stream}
    crossed = [from_chip(stream, b) for b in range(1, chips)]
    for k in range(1, tp_count):
        low = k & -k
        source = rows_of[k ^ low]
        if k == tp_count - 1:
            (source,) = add([[(source, 0)]], block_rows, crossed)
        rows_of[k] = from_tp(source, low)
    slots = list(reversed(range(tp_count)))
    near = {k: [rows_of[k], from_core(rows_of[k])] for k in slots}
    sums = activate(places, [near[k] for k in slots], gains[:cores], gate_weight, up_weight, cores, 0, [])
    far = {}
    for k in [0] + slots[:-1]:
        far[k] = []
        for b in range(1, chips):
            value = from_chip(rows_of[k], b) if k else crossed[b - 1]
            (later,) = add([[(value, 0)]], block_rows, sums[-1:]) if k == 0 else (value,)
            far[k] += [value, from_core(later)]
    active = activate(places, [far[k] for k in slots], gains[cores:], gate_weight, up_weight, cores, cores, sums)

    def send_back(k, after):
        total = list(add([terms[k]], block_rows, after))
        low = k & -k
        terms[k ^ low].append((from_tp(total[0], low), 0))
        return total

    terms = [[] for _ in range(tp_count)]
    arrivals = []
    outs = project_down(places, active, row_weight, down_weight, slots, 0, block_rows, ep_count, cores, [])
    swapped = [from_core(out[1]) for out in outs]
    for at, k in enumerate(slots):
        before = arrivals[-2] + sent if len(arrivals) > 1 else []
        pair = [[(outs[at][0], c * block_rows), (swapped[at], c * block_rows)] for c in range(chips)]
        added = add(pair, block_rows, before)
        across = [from_chip(added[c], chips - c) for c in range(1, chips)]
        arrivals.append(across)
        terms[k] += [(value, 0) for value in [added[0]] + across]
        if at == 0:
            sent = send_back(k, [])
    for k in slots[1:-1]:
        sent = send_back(k, sent)
    (mixed,) = add([terms[0]], block_rows)
    return (stream_out, mixed)


def solution(mesh):
    return jax.shard_map(
        shards,
        mesh=mesh,
        in_specs=(
            P(("parts", "ep"), "tp", None),
            P(("parts", "ep"), "tp"),
            P(("parts", "ep"), None, None),
            P(("parts", "ep"), None, None),
            P(("parts", "ep")),
            P("tp", None, None),
            P("tp", "ep"),
            P("parts", "ep"),
            P("ep"),
            P("parts", None),
            P("parts", None),
            P("ep", None, "tp"),
            P("ep", None, "tp"),
            P("ep", "tp", None),
        ),
        out_specs=(P(("parts", "tp"), "ep"), P(("parts", "tp"), "ep")),
        check_vma=False,
    )
```

```python
import functools

import jax
import jax.numpy as jnp
from jax import lax
from jax.experimental import pallas as pl
from jax.experimental.pallas import tpu as pltpu
from jax.sharding import PartitionSpec as P

score_scale = 1.0 / 192.0**0.5
norm_epsilon = 1e-06
MIB = 1 << 20


def in_hbm(value):
    return pltpu.with_memory_space_constraint(value, pltpu.HBM)


def in_vmem(value):
    return pltpu.with_memory_space_constraint(value, pltpu.VMEM)


def fetch_kernel(parts, *refs):
    source, target, sems = refs[0], refs[-2], refs[-1]
    step = source.shape[-2] // parts
    copies = []
    for i in range(parts):
        cut = (slice(None),) * (len(source.shape) - 2) + (pl.ds(i * step, step),)
        copies.append(pltpu.make_async_copy(source.at[cut], target.at[cut], sems.at[i]))
    for copy in copies:
        copy.start()
    for copy in copies:
        copy.wait()


def fetch(value, after):
    parts = 4
    return pl.pallas_call(
        functools.partial(fetch_kernel, parts),
        out_shape=pltpu.VMEM(value.shape, value.dtype),
        in_specs=[pl.BlockSpec(memory_space=pl.ANY)] * (1 + len(after)),
        out_specs=pl.BlockSpec(memory_space=pltpu.VMEM),
        scratch_shapes=[pltpu.SemaphoreType.DMA((parts,))],
        cost_estimate=pl.CostEstimate(flops=0, bytes_accessed=4 * value.size, transcendentals=0),
        compiler_params=pltpu.CompilerParams(vmem_limit_bytes=1 * MIB),
        name="fetch",
    )(in_hbm(value), *after)


def attention_kernel(step_rows, pieces, ahead, lengths, q_ref, qr_ref, k_hbm, kr_hbm, up_hbm, *refs):
    out_ref, latent, rope, k_ref, kr_ref, up_ref, sems, up_sem = refs[-8:]
    step = pl.program_id(0)
    steps = k_ref.shape[0] // step_rows
    heads, positions = q_ref.shape[1], k_ref.shape[1]
    rope_width = kr_ref.shape[1]

    def copies(at):
        whole = pl.ds(at * step_rows, step_rows)
        made = [pltpu.make_async_copy(kr_hbm.at[whole], kr_ref.at[whole], sems.at[at, pieces])]
        for i in range(pieces):
            part = pl.ds(at * step_rows + i * (step_rows // pieces), step_rows // pieces)
            made.append(pltpu.make_async_copy(k_hbm.at[part], k_ref.at[part], sems.at[at, i]))
        return made

    @pl.when(step == 0)
    def _():
        for at in range(min(ahead, steps)):
            for copy in copies(at):
                copy.start()
        pltpu.make_async_copy(up_hbm, up_ref, up_sem).start()
        all_rows = qr_ref.shape[0]
        width = heads * rope_width
        lane = lax.broadcasted_iota(jnp.int32, (heads, width), 1)
        head = lax.broadcasted_iota(jnp.int32, (heads, width), 0)
        own = jnp.where(lane // rope_width == head, 1.0, 0.0)
        spread = qr_ref[...].astype(jnp.float32)[:, None, :] * own[None, :, :]
        spread = spread.reshape(all_rows * heads, width).astype(jnp.bfloat16)
        lane = lax.broadcasted_iota(jnp.int32, (width, rope_width), 0)
        column = lax.broadcasted_iota(jnp.int32, (width, rope_width), 1)
        fold = jnp.where(lane % rope_width == column, 1.0, 0.0).astype(jnp.bfloat16)
        rope[...] = jnp.dot(spread, fold, preferred_element_type=jnp.float32)

    @pl.when(step + ahead < steps)
    def _():
        for copy in copies(step + ahead):
            copy.start()

    for copy in copies(step):
        copy.wait()
    place = lax.broadcasted_iota(jnp.int32, (heads, positions), 1)
    lanes = latent.shape[2]
    lanes = latent.shape[2]
    scores = []
    for r in range(step_rows):
        first = pl.multiple_of((step * step_rows + r) * heads, heads)
        score = lax.dot_general(
            q_ref[r], k_ref[step * step_rows + r], (((1,), (1,)), ((), ())), preferred_element_type=jnp.float32
        )
        score += jnp.dot(
            rope[pl.ds(first, heads), :].astype(jnp.bfloat16), kr_ref[step * step_rows + r], preferred_element_type=jnp.float32
        )
        scores.append(score)
    probabilities = []
    for r in range(step_rows):
        visible = place < lengths[step * step_rows + r]
        score = jnp.where(visible, scores[r] * score_scale, -jnp.inf)
        weight = jnp.exp(score - jnp.max(score, axis=-1, keepdims=True))
        total = jnp.sum(weight, axis=-1, keepdims=True)
        probabilities.append((weight / total).astype(jnp.bfloat16))
    for r in range(step_rows):
        first = pl.multiple_of((step * step_rows + r) * heads, heads)
        mixed = jnp.dot(probabilities[r], k_ref[step * step_rows + r], preferred_element_type=jnp.float32)
        for c in range(latent.shape[0]):
            latent[c, pl.ds(first, heads), :] = mixed[:, c * lanes : (c + 1) * lanes]

    @pl.when(step == pl.num_programs(0) - 1)
    def _():
        pltpu.make_async_copy(up_hbm, up_ref, up_sem).wait()
        rows = out_ref.shape[0]
        width = up_ref.shape[2]
        for h in range(heads):
            parts = [latent[c, pl.ds(h, rows, stride=heads), :] for c in range(latent.shape[0])]
            part = jnp.concatenate(parts, axis=1).astype(jnp.bfloat16)
            out_ref[:, h * width : (h + 1) * width] = jnp.dot(
                part, up_ref[h], preferred_element_type=jnp.float32
            ).astype(jnp.bfloat16)


def attend(query_latent, query_rope, cache_latent, cache_rope, cache_length, value_up, after):
    rows, heads, latent_width = query_latent.shape
    rope_width = cache_rope.shape[1]
    value_width = value_up.shape[2]
    step_rows, pieces, ahead = 8, 1, 3
    by_row = lambda i, lengths: (i, 0, 0)
    return pl.pallas_call(
        functools.partial(attention_kernel, step_rows, pieces, ahead),
        out_shape=jax.ShapeDtypeStruct((rows, heads * value_width), jnp.bfloat16),
        grid_spec=pltpu.PrefetchScalarGridSpec(
            num_scalar_prefetch=1,
            grid=(rows // step_rows,),
            in_specs=[
                pl.BlockSpec((step_rows, heads, latent_width), by_row),
                pl.BlockSpec(query_rope.shape, lambda i, lengths: (0, 0)),
                pl.BlockSpec(memory_space=pl.ANY),
                pl.BlockSpec(memory_space=pl.ANY),
                pl.BlockSpec(memory_space=pl.ANY),
            ]
            + [pl.BlockSpec(memory_space=pl.ANY)] * len(after),
            out_specs=pl.BlockSpec((rows, heads * value_width), lambda i, lengths: (0, 0)),
            scratch_shapes=[
                pltpu.VMEM((latent_width // 128, rows * heads, 128), jnp.float32),
                pltpu.VMEM((rows * heads, rope_width), jnp.float32),
                pltpu.VMEM(cache_latent.shape, jnp.bfloat16),
                pltpu.VMEM(cache_rope.shape, jnp.bfloat16),
                pltpu.VMEM(value_up.shape, jnp.bfloat16),
                pltpu.SemaphoreType.DMA((rows // step_rows, pieces + 1)),
                pltpu.SemaphoreType.DMA,
            ],
        ),
        cost_estimate=pl.CostEstimate(
            flops=64 * heads * cache_latent.size, bytes_accessed=2 * cache_latent.size, transcendentals=0
        ),
        compiler_params=pltpu.CompilerParams(vmem_limit_bytes=28 * MIB),
        name="attention",
    )(
        cache_length,
        in_hbm(query_latent),
        in_hbm(query_rope),
        in_hbm(cache_latent),
        in_hbm(cache_rope),
        in_hbm(value_up),
        *after,
    )


def projection_kernel(count, out_count, places, *refs):
    blocks, weight, outs = refs[:count], refs[count], refs[-2 - out_count : -2]
    gathered, result = refs[-2:]
    height = blocks[0].shape[0]
    for k in range(count):
        first = pl.multiple_of(places[k] * height, height)
        gathered[pl.ds(first, height), :] = blocks[k][...]
    columns = weight.shape[1]
    tile = 256 if columns % 256 == 0 else 128
    for j in range(columns // tile):
        result[:, j * tile : (j + 1) * tile] = jnp.dot(
            gathered[...], weight[:, j * tile : (j + 1) * tile], preferred_element_type=jnp.float32
        ).astype(jnp.bfloat16)
    out_height = outs[0].shape[0]
    for s in range(len(outs)):
        first = pl.multiple_of(places[count + s] * out_height, out_height)
        outs[s][...] = result[pl.ds(first, out_height), :]


def project(places, blocks, weight, out_count):
    count = len(blocks)
    height, depth = blocks[0].shape
    rows, columns = height * count, weight.shape[1]
    whole = pl.BlockSpec(memory_space=pltpu.VMEM)
    return pl.pallas_call(
        functools.partial(projection_kernel, count, out_count),
        out_shape=[jax.ShapeDtypeStruct((rows // out_count, columns), jnp.bfloat16)] * out_count,
        in_specs=[pl.BlockSpec(memory_space=pltpu.SMEM)] + [whole] * (count + 1),
        out_specs=[whole] * out_count,
        scratch_shapes=[
            pltpu.VMEM((rows, depth), jnp.bfloat16),
            pltpu.VMEM((rows, columns), jnp.bfloat16),
        ],
        cost_estimate=pl.CostEstimate(flops=2 * rows * depth * columns, bytes_accessed=4 * MIB, transcendentals=0),
        compiler_params=pltpu.CompilerParams(vmem_limit_bytes=8 * MIB),
        name="projection",
    )(places, *blocks, in_vmem(weight))


def gate_kernel(row_blocks, cores, first, count, model_width, places, *refs):
    blocks, gains = refs[: row_blocks * count], refs[row_blocks * count : (row_blocks + 1) * count]
    refs = refs[(row_blocks + 1) * count :]
    gate, up, refs = refs[0], refs[1], refs[2:]
    if first:
        before, (active, x) = refs[:3], refs[-2:]
        gate_sum, up_sum, squares = before
    else:
        gate_sum, up_sum, squares, x = refs[-4:]
    height, width = blocks[0].shape
    hidden = gate.shape[2]
    tile = min(256, hidden)
    sums = [[None] * (hidden // tile), [None] * (hidden // tile)]
    totals = [squares[s * height : (s + 1) * height, :] if first else 0.0 for s in range(row_blocks)]
    for k in range(count):
        for s in range(row_blocks):
            wide = blocks[s * count + k][...].astype(jnp.float32)
            totals[s] += jnp.sum(wide * wide, axis=-1, keepdims=True)
            x[s * height : (s + 1) * height, k * width : (k + 1) * width] = (wide * gains[k][...]).astype(jnp.bfloat16)
    for w, (weight, start) in enumerate(((gate, gate_sum), (up, up_sum))):
        for j in range(hidden // tile):
            cut = slice(j * tile, (j + 1) * tile)
            total = start[:, cut] if first else None
            for k in range(count):
                depth = pl.ds(pl.multiple_of(places[first + k] * width, 128), width)
                product = jnp.dot(
                    x[:, k * width : (k + 1) * width], weight[0, depth, cut], preferred_element_type=jnp.float32
                )
                total = product if total is None else total + product
            sums[w][j] = total
            if not first:
                start[:, cut] = total
    if not first:
        for s in range(row_blocks):
            squares[s * height : (s + 1) * height, :] = totals[s]
        return
    scale = jnp.concatenate([lax.rsqrt(t / model_width + norm_epsilon) for t in totals], axis=0)
    for j in range(hidden // tile):
        gate_part = sums[0][j] * scale
        up_part = sums[1][j] * scale
        active[:, j * tile : (j + 1) * tile] = (gate_part / (1.0 + jnp.exp(-gate_part)) * up_part).astype(jnp.bfloat16)


def activate(places, blocks, gains, gate_weight, up_weight, cores, first, before):
    row_blocks, count = len(blocks), len(blocks[0])
    height, width = blocks[0][0].shape
    rows = row_blocks * height
    model_width, hidden = gate_weight.shape[1:]
    whole = pl.BlockSpec(memory_space=pltpu.VMEM)
    if first:
        kinds = jax.ShapeDtypeStruct((rows, hidden), jnp.bfloat16)
    else:
        kinds = [jax.ShapeDtypeStruct((rows, n), jnp.float32) for n in (hidden, hidden, 1)]
    return pl.pallas_call(
        functools.partial(gate_kernel, row_blocks, cores, first, count, model_width),
        out_shape=kinds,
        in_specs=[pl.BlockSpec(memory_space=pltpu.SMEM)] + [whole] * ((row_blocks + 1) * count + 2 + len(before)),
        out_specs=whole if first else [whole] * 3,
        scratch_shapes=[pltpu.VMEM((rows, count * width), jnp.bfloat16)],
        cost_estimate=pl.CostEstimate(
            flops=4 * rows * hidden * count * width, bytes_accessed=4 * hidden * count * width, transcendentals=0
        ),
        compiler_params=pltpu.CompilerParams(vmem_limit_bytes=2 * rows * (count * width + 8 * hidden) + 12 * MIB),
        name="activate",
    )(places, *[b for row in blocks for b in row], *gains, in_vmem(gate_weight), in_vmem(up_weight), *before)


def down_kernel(slots, at, column_blocks, cores, places, active, row_weight, down, *refs):
    row_blocks = len(slots)
    outs = refs[-row_blocks * cores :]
    width = down.shape[2] // column_blocks
    height = outs[0].shape[0] * cores // column_blocks
    mine = slice(at * row_blocks * height, (at + 1) * row_blocks * height)
    order = [b * cores + c for c in reversed(range(cores)) for b in range(column_blocks // cores)]
    tile = 256 if width % 256 == 0 else 128
    weights = []
    for s in range(row_blocks):
        first = pl.multiple_of(places[column_blocks + slots[s]] * height, height)
        weights.append(row_weight[pl.ds(first, height), :])
    for k in order:
        b, c = k // cores, k % cores
        start = pl.multiple_of(places[k] * width, 128)
        for j in range(width // tile):
            cut = slice(j * tile, (j + 1) * tile)
            product = jnp.dot(
                active[mine, :], down[0, :, pl.ds(start + j * tile, tile)], preferred_element_type=jnp.float32
            )
            for s in range(row_blocks):
                part = product[s * height : (s + 1) * height, :] * weights[s]
                outs[s * cores + c][b * height : (b + 1) * height, cut] = part.astype(jnp.bfloat16)


def project_down(places, active, row_weight, down_weight, slots, at, height, column_blocks, cores, after):
    row_blocks = len(slots)
    rows = row_blocks * height
    width = down_weight.shape[2] // column_blocks
    whole = pl.BlockSpec(memory_space=pltpu.VMEM)
    out = jax.ShapeDtypeStruct((height * (column_blocks // cores), width), jnp.bfloat16)
    outs = pl.pallas_call(
        functools.partial(down_kernel, slots, at, column_blocks, cores),
        out_shape=[out] * (row_blocks * cores),
        in_specs=[pl.BlockSpec(memory_space=pltpu.SMEM)]
        + [whole] * 3
        + [pl.BlockSpec(memory_space=pl.ANY)] * len(after),
        out_specs=[whole] * (row_blocks * cores),
        cost_estimate=pl.CostEstimate(
            flops=2 * rows * down_weight.size, bytes_accessed=2 * down_weight.size, transcendentals=0
        ),
        compiler_params=pltpu.CompilerParams(vmem_limit_bytes=4 * MIB),
        name="down",
    )(places, active, row_weight, in_vmem(down_weight), *after)
    return [outs[s * cores : (s + 1) * cores] for s in range(row_blocks)]


def add_kernel(groups, *refs):
    used = sum(len(g) for g in groups)
    outs = refs[-len(groups) :]
    at = 0
    for group, out in zip(groups, outs):
        total = None
        for first in group:
            value = refs[at][first : first + out.shape[0], :].astype(jnp.float32)
            total = value if total is None else total + value
            at += 1
        out[...] = total.astype(out.dtype)


def add(groups, height, after=(), kind=jnp.bfloat16):
    values = [value for group in groups for value, _ in group]
    width = values[0].shape[1]
    whole = pl.BlockSpec(memory_space=pltpu.VMEM)
    return pl.pallas_call(
        functools.partial(add_kernel, [[first for _, first in group] for group in groups]),
        out_shape=[jax.ShapeDtypeStruct((height, width), kind)] * len(groups),
        in_specs=[whole] * len(values) + [pl.BlockSpec(memory_space=pl.ANY)] * len(after),
        out_specs=[whole] * len(groups),
        compiler_params=pltpu.CompilerParams(vmem_limit_bytes=8 * MIB),
        name="add",
    )(*values, *after)


def shards(
    query_latent,
    query_rope,
    cache_latent,
    cache_rope,
    cache_length,
    value_up,
    output_weight,
    residual,
    norm_gain,
    routed_experts,
    expert_gates,
    gate_weight,
    up_weight,
    down_weight,
):
    ep_count = lax.axis_size("ep")
    tp_count = lax.axis_size("tp")
    ep_index = lax.axis_index("ep")
    tp_index = lax.axis_index("tp")
    row_total = routed_experts.shape[0]
    block_rows = row_total // tp_count
    cores = 2
    chips = ep_count // cores

    def from_core(value):
        return lax.ppermute(value, "ep", [(i, i ^ 1) for i in range(ep_count)])

    def from_chip(value, back):
        step = cores * back
        return lax.ppermute(value, "ep", [(i, (i + step) % ep_count) for i in range(ep_count)])

    def from_tp(value, bits):
        return lax.ppermute(value, "tp", [(i, i ^ bits) for i in range(tp_count)])

    def gather_ep(value):
        same = [value] + [from_chip(value, b) for b in range(1, chips)]
        other = [from_core(v) for v in same]
        return [v for pair in zip(same, other) for v in pair]

    chip, core = ep_index // cores, ep_index % cores
    ep_places = [
        (chip - b + chips) % chips * cores + (core if c == 0 else 1 - core)
        for b in range(chips)
        for c in range(cores)
    ]
    tp_places = [tp_index ^ k for k in range(tp_count)]
    places = jnp.stack(ep_places + tp_places).astype(jnp.int32)

    gain = norm_gain.reshape(1, -1)
    gains = gather_ep(gain)
    own_residual = lax.dynamic_slice_in_dim(residual, tp_index * block_rows, block_rows, 0)
    row_weight = jnp.sum(jnp.where(routed_experts == ep_index, expert_gates, 0.0), axis=-1, keepdims=True)

    head_out = attend(query_latent, query_rope, cache_latent, cache_rope, cache_length, value_up, [places])
    output_weight = fetch(output_weight, [head_out, row_weight, own_residual, gain])
    partial = project(places, gather_ep(head_out), output_weight, tp_count)

    gate_weight = fetch(gate_weight, [partial[0]])
    terms = [[(value, 0)] for value in partial]
    for k in reversed(range(1, tp_count)):
        total = terms[k][0][0]
        if len(terms[k]) > 1 or k == 1:
            (total,) = add([terms[k]], block_rows, [gate_weight] if k == 1 else [])
        low = k & -k
        arrived = from_tp(total, low)
        terms[k ^ low].append((arrived, 0))
    up_weight = fetch(up_weight, [total])
    down_weight = fetch(down_weight, [total])
    stream_terms = terms[0] + [(own_residual, 0)]
    stream, stream_out = add([stream_terms, stream_terms], block_rows, gains + [gate_weight, up_weight, down_weight])

    rows_of = {0: stream}
    crossed = [from_chip(stream, b) for b in range(1, chips)]
    for k in range(1, tp_count):
        low = k & -k
        source = rows_of[k ^ low]
        if k == tp_count - 1:
            (source,) = add([[(source, 0)]], block_rows, crossed)
        rows_of[k] = from_tp(source, low)
    slots = list(reversed(range(tp_count)))
    near = {k: [rows_of[k], from_core(rows_of[k])] for k in slots}
    sums = activate(places, [near[k] for k in slots], gains[:cores], gate_weight, up_weight, cores, 0, [])
    far = {}
    for k in [0] + slots[:-1]:
        far[k] = []
        for b in range(1, chips):
            value = from_chip(rows_of[k], b) if k else crossed[b - 1]
            (later,) = add([[(value, 0)]], block_rows, sums[-1:]) if k == 0 else (value,)
            far[k] += [value, from_core(later)]
    active = activate(places, [far[k] for k in slots], gains[cores:], gate_weight, up_weight, cores, cores, sums)

    def send_back(k, after):
        total = list(add([terms[k]], block_rows, after))
        low = k & -k
        terms[k ^ low].append((from_tp(total[0], low), 0))
        return total

    terms = [[] for _ in range(tp_count)]
    arrivals, sent = [], []
    outs = project_down(places, active, row_weight, down_weight, slots, 0, block_rows, ep_count, cores, [])
    swapped = [from_core(out[1]) for out in outs]
    for at, k in enumerate(slots):
        before = arrivals[-2] + sent[0] if len(arrivals) > 1 else []
        pair = [[(outs[at][0], c * block_rows), (swapped[at], c * block_rows)] for c in range(chips)]
        added = add(pair, block_rows, before)
        across = [from_chip(added[c], chips - c) for c in range(1, chips)]
        arrivals.append(across)
        terms[k] += [(value, 0) for value in [added[0]] + across]
        if at == 0:
            sent = [send_back(k, [])]
    for k in slots[1:-1]:
        send_back(k, [])
    (most,) = add([terms[0][:-1]], block_rows, (), jnp.float32)
    (mixed,) = add([[(most, 0), terms[0][-1]]], block_rows)
    return (stream_out, mixed)


def solution(mesh):
    return jax.shard_map(
        shards,
        mesh=mesh,
        in_specs=(
            P(("parts", "ep"), "tp", None),
            P(("parts", "ep"), "tp"),
            P(("parts", "ep"), None, None),
            P(("parts", "ep"), None, None),
            P(("parts", "ep")),
            P("tp", None, None),
            P("tp", "ep"),
            P("parts", "ep"),
            P("ep"),
            P("parts", None),
            P("parts", None),
            P("ep", None, "tp"),
            P("ep", None, "tp"),
            P("ep", "tp", None),
        ),
        out_specs=(P(("parts", "tp"), "ep"), P(("parts", "tp"), "ep")),
        check_vma=False,
    )
```

```python
import functools

import jax
import jax.numpy as jnp
from jax import lax
from jax.experimental import pallas as pl
from jax.experimental.pallas import tpu as pltpu
from jax.sharding import PartitionSpec as P

score_scale = 1.0 / 192.0**0.5
norm_epsilon = 1e-06
MIB = 1 << 20


def in_hbm(value):
    return pltpu.with_memory_space_constraint(value, pltpu.HBM)


def in_vmem(value):
    return pltpu.with_memory_space_constraint(value, pltpu.VMEM)


def fetch_kernel(parts, *refs):
    source, target, sems = refs[0], refs[-2], refs[-1]
    step = source.shape[-2] // parts
    copies = []
    for i in range(parts):
        cut = (slice(None),) * (len(source.shape) - 2) + (pl.ds(i * step, step),)
        copies.append(pltpu.make_async_copy(source.at[cut], target.at[cut], sems.at[i]))
    for copy in copies:
        copy.start()
    for copy in copies:
        copy.wait()


def fetch(value, after):
    parts = 4
    return pl.pallas_call(
        functools.partial(fetch_kernel, parts),
        out_shape=pltpu.VMEM(value.shape, value.dtype),
        in_specs=[pl.BlockSpec(memory_space=pl.ANY)] * (1 + len(after)),
        out_specs=pl.BlockSpec(memory_space=pltpu.VMEM),
        scratch_shapes=[pltpu.SemaphoreType.DMA((parts,))],
        cost_estimate=pl.CostEstimate(flops=0, bytes_accessed=4 * value.size, transcendentals=0),
        compiler_params=pltpu.CompilerParams(vmem_limit_bytes=1 * MIB),
        name="fetch",
    )(in_hbm(value), *after)


def attention_kernel(step_rows, pieces, ahead, lengths, q_ref, qr_ref, k_hbm, kr_hbm, up_hbm, *refs):
    out_ref, latent, rope, k_ref, kr_ref, up_ref, sems, up_sem = refs[-8:]
    step = pl.program_id(0)
    steps = k_ref.shape[0] // step_rows
    heads, positions = q_ref.shape[1], k_ref.shape[1]
    rope_width = kr_ref.shape[1]

    def copies(at):
        whole = pl.ds(at * step_rows, step_rows)
        made = [pltpu.make_async_copy(kr_hbm.at[whole], kr_ref.at[whole], sems.at[at, pieces])]
        for i in range(pieces):
            part = pl.ds(at * step_rows + i * (step_rows // pieces), step_rows // pieces)
            made.append(pltpu.make_async_copy(k_hbm.at[part], k_ref.at[part], sems.at[at, i]))
        return made

    @pl.when(step == 0)
    def _():
        for at in range(min(ahead, steps)):
            for copy in copies(at):
                copy.start()
        pltpu.make_async_copy(up_hbm, up_ref, up_sem).start()
        all_rows = qr_ref.shape[0]
        width = heads * rope_width
        lane = lax.broadcasted_iota(jnp.int32, (heads, width), 1)
        head = lax.broadcasted_iota(jnp.int32, (heads, width), 0)
        own = jnp.where(lane // rope_width == head, 1.0, 0.0)
        spread = qr_ref[...].astype(jnp.float32)[:, None, :] * own[None, :, :]
        spread = spread.reshape(all_rows * heads, width).astype(jnp.bfloat16)
        lane = lax.broadcasted_iota(jnp.int32, (width, rope_width), 0)
        column = lax.broadcasted_iota(jnp.int32, (width, rope_width), 1)
        fold = jnp.where(lane % rope_width == column, 1.0, 0.0).astype(jnp.bfloat16)
        rope[...] = jnp.dot(spread, fold, preferred_element_type=jnp.float32)

    @pl.when(step + ahead < steps)
    def _():
        for copy in copies(step + ahead):
            copy.start()

    for copy in copies(step):
        copy.wait()
    place = lax.broadcasted_iota(jnp.int32, (heads, positions), 1)
    lanes = latent.shape[2]
    lanes = latent.shape[2]
    scores = []
    for r in range(step_rows):
        first = pl.multiple_of((step * step_rows + r) * heads, heads)
        score = lax.dot_general(
            q_ref[r], k_ref[step * step_rows + r], (((1,), (1,)), ((), ())), preferred_element_type=jnp.float32
        )
        score += jnp.dot(
            rope[pl.ds(first, heads), :].astype(jnp.bfloat16), kr_ref[step * step_rows + r], preferred_element_type=jnp.float32
        )
        scores.append(score)
    probabilities = []
    for r in range(step_rows):
        visible = place < lengths[step * step_rows + r]
        score = jnp.where(visible, scores[r] * score_scale, -jnp.inf)
        weight = jnp.exp(score - jnp.max(score, axis=-1, keepdims=True))
        total = jnp.sum(weight, axis=-1, keepdims=True)
        probabilities.append((weight / total).astype(jnp.bfloat16))
    for r in range(step_rows):
        first = pl.multiple_of((step * step_rows + r) * heads, heads)
        mixed = jnp.dot(probabilities[r], k_ref[step * step_rows + r], preferred_element_type=jnp.float32)
        for c in range(latent.shape[0]):
            latent[c, pl.ds(first, heads), :] = mixed[:, c * lanes : (c + 1) * lanes]

    @pl.when(step == pl.num_programs(0) - 1)
    def _():
        pltpu.make_async_copy(up_hbm, up_ref, up_sem).wait()
        rows = out_ref.shape[0]
        width = up_ref.shape[2]
        for h in range(heads):
            parts = [latent[c, pl.ds(h, rows, stride=heads), :] for c in range(latent.shape[0])]
            part = jnp.concatenate(parts, axis=1).astype(jnp.bfloat16)
            out_ref[:, h * width : (h + 1) * width] = jnp.dot(
                part, up_ref[h], preferred_element_type=jnp.float32
            ).astype(jnp.bfloat16)


def attend(query_latent, query_rope, cache_latent, cache_rope, cache_length, value_up, after):
    rows, heads, latent_width = query_latent.shape
    rope_width = cache_rope.shape[1]
    value_width = value_up.shape[2]
    step_rows, pieces, ahead = 8, 1, 3
    by_row = lambda i, lengths: (i, 0, 0)
    return pl.pallas_call(
        functools.partial(attention_kernel, step_rows, pieces, ahead),
        out_shape=jax.ShapeDtypeStruct((rows, heads * value_width), jnp.bfloat16),
        grid_spec=pltpu.PrefetchScalarGridSpec(
            num_scalar_prefetch=1,
            grid=(rows // step_rows,),
            in_specs=[
                pl.BlockSpec((step_rows, heads, latent_width), by_row),
                pl.BlockSpec(query_rope.shape, lambda i, lengths: (0, 0)),
                pl.BlockSpec(memory_space=pl.ANY),
                pl.BlockSpec(memory_space=pl.ANY),
                pl.BlockSpec(memory_space=pl.ANY),
            ]
            + [pl.BlockSpec(memory_space=pl.ANY)] * len(after),
            out_specs=pl.BlockSpec((rows, heads * value_width), lambda i, lengths: (0, 0)),
            scratch_shapes=[
                pltpu.VMEM((latent_width // 128, rows * heads, 128), jnp.float32),
                pltpu.VMEM((rows * heads, rope_width), jnp.float32),
                pltpu.VMEM(cache_latent.shape, jnp.bfloat16),
                pltpu.VMEM(cache_rope.shape, jnp.bfloat16),
                pltpu.VMEM(value_up.shape, jnp.bfloat16),
                pltpu.SemaphoreType.DMA((rows // step_rows, pieces + 1)),
                pltpu.SemaphoreType.DMA,
            ],
        ),
        cost_estimate=pl.CostEstimate(
            flops=64 * heads * cache_latent.size, bytes_accessed=2 * cache_latent.size, transcendentals=0
        ),
        compiler_params=pltpu.CompilerParams(vmem_limit_bytes=28 * MIB),
        name="attention",
    )(
        cache_length,
        in_hbm(query_latent),
        in_hbm(query_rope),
        in_hbm(cache_latent),
        in_hbm(cache_rope),
        in_hbm(value_up),
        *after,
    )


def projection_kernel(count, out_count, places, *refs):
    blocks, weight, outs = refs[:count], refs[count], refs[-2 - out_count : -2]
    gathered, result = refs[-2:]
    height = blocks[0].shape[0]
    for k in range(count):
        first = pl.multiple_of(places[k] * height, height)
        gathered[pl.ds(first, height), :] = blocks[k][...]
    columns = weight.shape[1]
    tile = 256 if columns % 256 == 0 else 128
    for j in range(columns // tile):
        result[:, j * tile : (j + 1) * tile] = jnp.dot(
            gathered[...], weight[:, j * tile : (j + 1) * tile], preferred_element_type=jnp.float32
        ).astype(jnp.bfloat16)
    out_height = outs[0].shape[0]
    for s in range(len(outs)):
        first = pl.multiple_of(places[count + s] * out_height, out_height)
        outs[s][...] = result[pl.ds(first, out_height), :]


def project(places, blocks, weight, out_count):
    count = len(blocks)
    height, depth = blocks[0].shape
    rows, columns = height * count, weight.shape[1]
    whole = pl.BlockSpec(memory_space=pltpu.VMEM)
    return pl.pallas_call(
        functools.partial(projection_kernel, count, out_count),
        out_shape=[jax.ShapeDtypeStruct((rows // out_count, columns), jnp.bfloat16)] * out_count,
        in_specs=[pl.BlockSpec(memory_space=pltpu.SMEM)] + [whole] * (count + 1),
        out_specs=[whole] * out_count,
        scratch_shapes=[
            pltpu.VMEM((rows, depth), jnp.bfloat16),
            pltpu.VMEM((rows, columns), jnp.bfloat16),
        ],
        cost_estimate=pl.CostEstimate(flops=2 * rows * depth * columns, bytes_accessed=4 * MIB, transcendentals=0),
        compiler_params=pltpu.CompilerParams(vmem_limit_bytes=8 * MIB),
        name="projection",
    )(places, *blocks, in_vmem(weight))


def gate_kernel(row_blocks, cores, first, count, model_width, places, *refs):
    blocks, gains = refs[: row_blocks * count], refs[row_blocks * count : (row_blocks + 1) * count]
    refs = refs[(row_blocks + 1) * count :]
    gate, up, refs = refs[0], refs[1], refs[2:]
    if first:
        before, (active, x) = refs[:3], refs[-2:]
        gate_sum, up_sum, squares = before
    else:
        gate_sum, up_sum, squares, x = refs[-4:]
    height, width = blocks[0].shape
    hidden = gate.shape[2]
    tile = min(256, hidden)
    sums = [[None] * (hidden // tile), [None] * (hidden // tile)]
    totals = [squares[s * height : (s + 1) * height, :] if first else 0.0 for s in range(row_blocks)]
    for k in range(count):
        for s in range(row_blocks):
            wide = blocks[s * count + k][...].astype(jnp.float32)
            totals[s] += jnp.sum(wide * wide, axis=-1, keepdims=True)
            x[s * height : (s + 1) * height, k * width : (k + 1) * width] = (wide * gains[k][...]).astype(jnp.bfloat16)
    for w, (weight, start) in enumerate(((gate, gate_sum), (up, up_sum))):
        for j in range(hidden // tile):
            cut = slice(j * tile, (j + 1) * tile)
            total = start[:, cut] if first else None
            for k in range(count):
                depth = pl.ds(pl.multiple_of(places[first + k] * width, 128), width)
                product = jnp.dot(
                    x[:, k * width : (k + 1) * width], weight[0, depth, cut], preferred_element_type=jnp.float32
                )
                total = product if total is None else total + product
            sums[w][j] = total
            if not first:
                start[:, cut] = total
    if not first:
        for s in range(row_blocks):
            squares[s * height : (s + 1) * height, :] = totals[s]
        return
    scale = jnp.concatenate([lax.rsqrt(t / model_width + norm_epsilon) for t in totals], axis=0)
    for j in range(hidden // tile):
        gate_part = sums[0][j] * scale
        up_part = sums[1][j] * scale
        active[:, j * tile : (j + 1) * tile] = (gate_part / (1.0 + jnp.exp(-gate_part)) * up_part).astype(jnp.bfloat16)


def activate(places, blocks, gains, gate_weight, up_weight, cores, first, before):
    row_blocks, count = len(blocks), len(blocks[0])
    height, width = blocks[0][0].shape
    rows = row_blocks * height
    model_width, hidden = gate_weight.shape[1:]
    whole = pl.BlockSpec(memory_space=pltpu.VMEM)
    if first:
        kinds = jax.ShapeDtypeStruct((rows, hidden), jnp.bfloat16)
    else:
        kinds = [jax.ShapeDtypeStruct((rows, n), jnp.float32) for n in (hidden, hidden, 1)]
    return pl.pallas_call(
        functools.partial(gate_kernel, row_blocks, cores, first, count, model_width),
        out_shape=kinds,
        in_specs=[pl.BlockSpec(memory_space=pltpu.SMEM)] + [whole] * ((row_blocks + 1) * count + 2 + len(before)),
        out_specs=whole if first else [whole] * 3,
        scratch_shapes=[pltpu.VMEM((rows, count * width), jnp.bfloat16)],
        cost_estimate=pl.CostEstimate(
            flops=4 * rows * hidden * count * width, bytes_accessed=4 * hidden * count * width, transcendentals=0
        ),
        compiler_params=pltpu.CompilerParams(vmem_limit_bytes=2 * rows * (count * width + 8 * hidden) + 12 * MIB),
        name="activate",
    )(places, *[b for row in blocks for b in row], *gains, in_vmem(gate_weight), in_vmem(up_weight), *before)


def down_kernel(slots, at, column_blocks, cores, places, active, row_weight, down, *refs):
    row_blocks = len(slots)
    outs = refs[-row_blocks * cores :]
    width = down.shape[2] // column_blocks
    height = outs[0].shape[0] * cores // column_blocks
    mine = slice(at * row_blocks * height, (at + 1) * row_blocks * height)
    order = [b * cores + c for c in reversed(range(cores)) for b in range(column_blocks // cores)]
    tile = 256 if width % 256 == 0 else 128
    weights = []
    for s in range(row_blocks):
        first = pl.multiple_of(places[column_blocks + slots[s]] * height, height)
        weights.append(row_weight[pl.ds(first, height), :])
    for k in order:
        b, c = k // cores, k % cores
        start = pl.multiple_of(places[k] * width, 128)
        for j in range(width // tile):
            cut = slice(j * tile, (j + 1) * tile)
            product = jnp.dot(
                active[mine, :], down[0, :, pl.ds(start + j * tile, tile)], preferred_element_type=jnp.float32
            )
            for s in range(row_blocks):
                part = product[s * height : (s + 1) * height, :] * weights[s]
                outs[s * cores + c][b * height : (b + 1) * height, cut] = part.astype(jnp.bfloat16)


def project_down(places, active, row_weight, down_weight, slots, at, height, column_blocks, cores, after):
    row_blocks = len(slots)
    rows = row_blocks * height
    width = down_weight.shape[2] // column_blocks
    whole = pl.BlockSpec(memory_space=pltpu.VMEM)
    out = jax.ShapeDtypeStruct((height * (column_blocks // cores), width), jnp.bfloat16)
    outs = pl.pallas_call(
        functools.partial(down_kernel, slots, at, column_blocks, cores),
        out_shape=[out] * (row_blocks * cores),
        in_specs=[pl.BlockSpec(memory_space=pltpu.SMEM)]
        + [whole] * 3
        + [pl.BlockSpec(memory_space=pl.ANY)] * len(after),
        out_specs=[whole] * (row_blocks * cores),
        cost_estimate=pl.CostEstimate(
            flops=2 * rows * down_weight.size, bytes_accessed=2 * down_weight.size, transcendentals=0
        ),
        compiler_params=pltpu.CompilerParams(vmem_limit_bytes=4 * MIB),
        name="down",
    )(places, active, row_weight, in_vmem(down_weight), *after)
    return [outs[s * cores : (s + 1) * cores] for s in range(row_blocks)]


def add_kernel(groups, *refs):
    used = sum(len(g) for g in groups)
    outs = refs[-len(groups) :]
    at = 0
    for group, out in zip(groups, outs):
        total = None
        for first in group:
            value = refs[at][first : first + out.shape[0], :].astype(jnp.float32)
            total = value if total is None else total + value
            at += 1
        out[...] = total.astype(out.dtype)


def add(groups, height, after=(), kind=jnp.bfloat16):
    values = [value for group in groups for value, _ in group]
    width = values[0].shape[1]
    whole = pl.BlockSpec(memory_space=pltpu.VMEM)
    return pl.pallas_call(
        functools.partial(add_kernel, [[first for _, first in group] for group in groups]),
        out_shape=[jax.ShapeDtypeStruct((height, width), kind)] * len(groups),
        in_specs=[whole] * len(values) + [pl.BlockSpec(memory_space=pl.ANY)] * len(after),
        out_specs=[whole] * len(groups),
        compiler_params=pltpu.CompilerParams(vmem_limit_bytes=8 * MIB),
        name="add",
    )(*values, *after)


def shards(
    query_latent,
    query_rope,
    cache_latent,
    cache_rope,
    cache_length,
    value_up,
    output_weight,
    residual,
    norm_gain,
    routed_experts,
    expert_gates,
    gate_weight,
    up_weight,
    down_weight,
):
    ep_count = lax.axis_size("ep")
    tp_count = lax.axis_size("tp")
    ep_index = lax.axis_index("ep")
    tp_index = lax.axis_index("tp")
    row_total = routed_experts.shape[0]
    block_rows = row_total // tp_count
    cores = 2
    chips = ep_count // cores

    def from_core(value):
        return lax.ppermute(value, "ep", [(i, i ^ 1) for i in range(ep_count)])

    def from_chip(value, back):
        step = cores * back
        return lax.ppermute(value, "ep", [(i, (i + step) % ep_count) for i in range(ep_count)])

    def from_tp(value, bits):
        return lax.ppermute(value, "tp", [(i, i ^ bits) for i in range(tp_count)])

    def gather_ep(value):
        same = [value] + [from_chip(value, b) for b in range(1, chips)]
        other = [from_core(v) for v in same]
        return [v for pair in zip(same, other) for v in pair]

    chip, core = ep_index // cores, ep_index % cores
    ep_places = [
        (chip - b + chips) % chips * cores + (core if c == 0 else 1 - core)
        for b in range(chips)
        for c in range(cores)
    ]
    tp_places = [tp_index ^ k for k in range(tp_count)]
    places = jnp.stack(ep_places + tp_places).astype(jnp.int32)

    gain = norm_gain.reshape(1, -1)
    gains = gather_ep(gain)
    own_residual = lax.dynamic_slice_in_dim(residual, tp_index * block_rows, block_rows, 0)
    row_weight = jnp.sum(jnp.where(routed_experts == ep_index, expert_gates, 0.0), axis=-1, keepdims=True)

    head_out = attend(query_latent, query_rope, cache_latent, cache_rope, cache_length, value_up, [places])
    output_weight = fetch(output_weight, [head_out, row_weight, own_residual, gain])
    partial = project(places, gather_ep(head_out), output_weight, tp_count)

    gate_weight = fetch(gate_weight, [partial[0]])
    terms = [[(value, 0)] for value in partial]
    for k in reversed(range(1, tp_count)):
        total = terms[k][0][0]
        if len(terms[k]) > 1 or k == 1:
            (total,) = add([terms[k]], block_rows, [gate_weight] if k == 1 else [])
        low = k & -k
        arrived = from_tp(total, low)
        terms[k ^ low].append((arrived, 0))
    up_weight = fetch(up_weight, [total])
    down_weight = fetch(down_weight, [total])
    stream_terms = terms[0] + [(own_residual, 0)]
    stream, stream_out = add([stream_terms, stream_terms], block_rows, gains + [gate_weight, up_weight, down_weight])

    rows_of = {0: stream}
    crossed = [from_chip(stream, b) for b in range(1, chips)]
    for k in range(1, tp_count):
        low = k & -k
        source = rows_of[k ^ low]
        if k == tp_count - 1:
            (source,) = add([[(source, 0)]], block_rows, crossed)
        rows_of[k] = from_tp(source, low)
    slots = list(reversed(range(tp_count)))
    near = {k: [rows_of[k], from_core(rows_of[k])] for k in slots}
    sums = activate(places, [near[k] for k in slots], gains[:cores], gate_weight, up_weight, cores, 0, [])
    far = {}
    for k in [0] + slots[:-1]:
        far[k] = []
        for b in range(1, chips):
            if k == 0:
                value = crossed[b - 1]
            elif k == 1:
                value = from_tp(crossed[b - 1], 1)
            else:
                value = from_chip(rows_of[k], b)
            (later,) = add([[(value, 0)]], block_rows, sums[-1:]) if k == 0 else (value,)
            far[k] += [value, from_core(later)]
    active = activate(places, [far[k] for k in slots], gains[cores:], gate_weight, up_weight, cores, cores, sums)

    def send_back(k, after):
        total = list(add([terms[k]], block_rows, after))
        low = k & -k
        terms[k ^ low].append((from_tp(total[0], low), 0))
        return total

    terms = [[] for _ in range(tp_count)]
    arrivals, sent = [], []
    outs = project_down(places, active, row_weight, down_weight, slots, 0, block_rows, ep_count, cores, [])
    swapped = [from_core(out[1]) for out in outs]
    def core_sums(k, after):
        at = slots.index(k)
        rows = [[(outs[at][0], c * block_rows), (swapped[at], c * block_rows)] for c in range(chips)]
        return rows, after

    def cross(k, extra, after):
        rows, after = core_sums(k, after)
        added = add([row + more for row, more in zip(rows, extra)], block_rows, after)
        across = [from_chip(added[c], chips - c) for c in range(1, chips)]
        arrivals.append(across)
        terms[k] += [(value, 0) for value in [added[0]] + across]

    none = [[] for _ in range(chips)]
    for k in slots[:-2]:
        cross(k, none, arrivals[-2] if len(arrivals) > 1 else [])
    rows, _ = core_sums(1, [])
    added = add(rows, block_rows)
    joined = [[]] + [[(from_tp(added[c], 1), 0)] for c in range(1, chips)]
    early = [value for more in joined for value, _ in more]
    sent = send_back(slots[0], early)
    cross(0, joined, sent)
    for k in slots[1:-2]:
        send_back(k, [])
    terms[1].insert(0, (added[0], 0))
    (kept,) = add([terms[1]], block_rows) if len(terms[1]) > 1 else (added[0],)
    (most,) = add([terms[0]], block_rows, (), jnp.float32)
    (mixed,) = add([[(most, 0), (from_tp(kept, 1), 0)]], block_rows)
    return (stream_out, mixed)


def solution(mesh):
    return jax.shard_map(
        shards,
        mesh=mesh,
        in_specs=(
            P(("parts", "ep"), "tp", None),
            P(("parts", "ep"), "tp"),
            P(("parts", "ep"), None, None),
            P(("parts", "ep"), None, None),
            P(("parts", "ep")),
            P("tp", None, None),
            P("tp", "ep"),
            P("parts", "ep"),
            P("ep"),
            P("parts", None),
            P("parts", None),
            P("ep", None, "tp"),
            P("ep", None, "tp"),
            P("ep", "tp", None),
        ),
        out_specs=(P(("parts", "tp"), "ep"), P(("parts", "tp"), "ep")),
        check_vma=False,
    )
```

```python
import functools

import jax
import jax.numpy as jnp
from jax import lax
from jax.experimental import pallas as pl
from jax.experimental.pallas import tpu as pltpu
from jax.sharding import PartitionSpec as P

score_scale = 1.0 / 192.0**0.5
norm_epsilon = 1e-06
MIB = 1 << 20


def in_hbm(value):
    return pltpu.with_memory_space_constraint(value, pltpu.HBM)


def in_vmem(value):
    return pltpu.with_memory_space_constraint(value, pltpu.VMEM)


def fetch_kernel(parts, *refs):
    source, target, sems = refs[0], refs[-2], refs[-1]
    step = source.shape[-2] // parts
    copies = []
    for i in range(parts):
        cut = (slice(None),) * (len(source.shape) - 2) + (pl.ds(i * step, step),)
        copies.append(pltpu.make_async_copy(source.at[cut], target.at[cut], sems.at[i]))
    for copy in copies:
        copy.start()
    for copy in copies:
        copy.wait()


def fetch(value, after):
    parts = 4
    return pl.pallas_call(
        functools.partial(fetch_kernel, parts),
        out_shape=pltpu.VMEM(value.shape, value.dtype),
        in_specs=[pl.BlockSpec(memory_space=pl.ANY)] * (1 + len(after)),
        out_specs=pl.BlockSpec(memory_space=pltpu.VMEM),
        scratch_shapes=[pltpu.SemaphoreType.DMA((parts,))],
        cost_estimate=pl.CostEstimate(flops=0, bytes_accessed=4 * value.size, transcendentals=0),
        compiler_params=pltpu.CompilerParams(vmem_limit_bytes=1 * MIB),
        name="fetch",
    )(in_hbm(value), *after)


def attention_kernel(step_rows, pieces, ahead, lengths, q_ref, qr_ref, k_hbm, kr_hbm, up_hbm, *refs):
    out_ref, latent, rope, k_ref, kr_ref, up_ref, sems, up_sem = refs[-8:]
    step = pl.program_id(0)
    steps = k_ref.shape[0] // step_rows
    heads, positions = q_ref.shape[1], k_ref.shape[1]
    rope_width = kr_ref.shape[1]

    def copies(at):
        whole = pl.ds(at * step_rows, step_rows)
        made = [pltpu.make_async_copy(kr_hbm.at[whole], kr_ref.at[whole], sems.at[at, pieces])]
        for i in range(pieces):
            part = pl.ds(at * step_rows + i * (step_rows // pieces), step_rows // pieces)
            made.append(pltpu.make_async_copy(k_hbm.at[part], k_ref.at[part], sems.at[at, i]))
        return made

    @pl.when(step == 0)
    def _():
        for at in range(min(ahead, steps)):
            for copy in copies(at):
                copy.start()
        pltpu.make_async_copy(up_hbm, up_ref, up_sem).start()
        all_rows = qr_ref.shape[0]
        width = heads * rope_width
        lane = lax.broadcasted_iota(jnp.int32, (heads, width), 1)
        head = lax.broadcasted_iota(jnp.int32, (heads, width), 0)
        own = jnp.where(lane // rope_width == head, 1.0, 0.0)
        spread = qr_ref[...].astype(jnp.float32)[:, None, :] * own[None, :, :]
        spread = spread.reshape(all_rows * heads, width).astype(jnp.bfloat16)
        lane = lax.broadcasted_iota(jnp.int32, (width, rope_width), 0)
        column = lax.broadcasted_iota(jnp.int32, (width, rope_width), 1)
        fold = jnp.where(lane % rope_width == column, 1.0, 0.0).astype(jnp.bfloat16)
        rope[...] = jnp.dot(spread, fold, preferred_element_type=jnp.float32)

    @pl.when(step + ahead < steps)
    def _():
        for copy in copies(step + ahead):
            copy.start()

    for copy in copies(step):
        copy.wait()
    place = lax.broadcasted_iota(jnp.int32, (heads, positions), 1)
    lanes = latent.shape[2]
    lanes = latent.shape[2]
    scores = []
    for r in range(step_rows):
        first = pl.multiple_of((step * step_rows + r) * heads, heads)
        score = lax.dot_general(
            q_ref[r], k_ref[step * step_rows + r], (((1,), (1,)), ((), ())), preferred_element_type=jnp.float32
        )
        score += jnp.dot(
            rope[pl.ds(first, heads), :].astype(jnp.bfloat16), kr_ref[step * step_rows + r], preferred_element_type=jnp.float32
        )
        scores.append(score)
    probabilities = []
    for r in range(step_rows):
        visible = place < lengths[step * step_rows + r]
        score = jnp.where(visible, scores[r] * score_scale, -jnp.inf)
        weight = jnp.exp(score - jnp.max(score, axis=-1, keepdims=True))
        total = jnp.sum(weight, axis=-1, keepdims=True)
        probabilities.append((weight / total).astype(jnp.bfloat16))
    for r in range(step_rows):
        first = pl.multiple_of((step * step_rows + r) * heads, heads)
        mixed = jnp.dot(probabilities[r], k_ref[step * step_rows + r], preferred_element_type=jnp.float32)
        for c in range(latent.shape[0]):
            latent[c, pl.ds(first, heads), :] = mixed[:, c * lanes : (c + 1) * lanes]

    @pl.when(step == pl.num_programs(0) - 1)
    def _():
        pltpu.make_async_copy(up_hbm, up_ref, up_sem).wait()
        rows = out_ref.shape[0]
        width = up_ref.shape[2]
        for h in range(heads):
            parts = [latent[c, pl.ds(h, rows, stride=heads), :] for c in range(latent.shape[0])]
            part = jnp.concatenate(parts, axis=1).astype(jnp.bfloat16)
            out_ref[:, h * width : (h + 1) * width] = jnp.dot(
                part, up_ref[h], preferred_element_type=jnp.float32
            ).astype(jnp.bfloat16)


def attend(query_latent, query_rope, cache_latent, cache_rope, cache_length, value_up, after):
    rows, heads, latent_width = query_latent.shape
    rope_width = cache_rope.shape[1]
    value_width = value_up.shape[2]
    step_rows, pieces, ahead = 8, 1, 3
    by_row = lambda i, lengths: (i, 0, 0)
    return pl.pallas_call(
        functools.partial(attention_kernel, step_rows, pieces, ahead),
        out_shape=jax.ShapeDtypeStruct((rows, heads * value_width), jnp.bfloat16),
        grid_spec=pltpu.PrefetchScalarGridSpec(
            num_scalar_prefetch=1,
            grid=(rows // step_rows,),
            in_specs=[
                pl.BlockSpec((step_rows, heads, latent_width), by_row),
                pl.BlockSpec(query_rope.shape, lambda i, lengths: (0, 0)),
                pl.BlockSpec(memory_space=pl.ANY),
                pl.BlockSpec(memory_space=pl.ANY),
                pl.BlockSpec(memory_space=pl.ANY),
            ]
            + [pl.BlockSpec(memory_space=pl.ANY)] * len(after),
            out_specs=pl.BlockSpec((rows, heads * value_width), lambda i, lengths: (0, 0)),
            scratch_shapes=[
                pltpu.VMEM((latent_width // 128, rows * heads, 128), jnp.float32),
                pltpu.VMEM((rows * heads, rope_width), jnp.float32),
                pltpu.VMEM(cache_latent.shape, jnp.bfloat16),
                pltpu.VMEM(cache_rope.shape, jnp.bfloat16),
                pltpu.VMEM(value_up.shape, jnp.bfloat16),
                pltpu.SemaphoreType.DMA((rows // step_rows, pieces + 1)),
                pltpu.SemaphoreType.DMA,
            ],
        ),
        cost_estimate=pl.CostEstimate(
            flops=64 * heads * cache_latent.size, bytes_accessed=2 * cache_latent.size, transcendentals=0
        ),
        compiler_params=pltpu.CompilerParams(vmem_limit_bytes=28 * MIB),
        name="attention",
    )(
        cache_length,
        in_hbm(query_latent),
        in_hbm(query_rope),
        in_hbm(cache_latent),
        in_hbm(cache_rope),
        in_hbm(value_up),
        *after,
    )


def projection_kernel(count, out_count, places, *refs):
    blocks, weight, outs = refs[:count], refs[count], refs[-2 - out_count : -2]
    gathered, result = refs[-2:]
    height = blocks[0].shape[0]
    for k in range(count):
        first = pl.multiple_of(places[k] * height, height)
        gathered[pl.ds(first, height), :] = blocks[k][...]
    columns = weight.shape[1]
    tile = 256 if columns % 256 == 0 else 128
    for j in range(columns // tile):
        result[:, j * tile : (j + 1) * tile] = jnp.dot(
            gathered[...], weight[:, j * tile : (j + 1) * tile], preferred_element_type=jnp.float32
        ).astype(jnp.bfloat16)
    out_height = outs[0].shape[0]
    for s in range(len(outs)):
        first = pl.multiple_of(places[count + s] * out_height, out_height)
        outs[s][...] = result[pl.ds(first, out_height), :]


def project(places, blocks, weight, out_count):
    count = len(blocks)
    height, depth = blocks[0].shape
    rows, columns = height * count, weight.shape[1]
    whole = pl.BlockSpec(memory_space=pltpu.VMEM)
    return pl.pallas_call(
        functools.partial(projection_kernel, count, out_count),
        out_shape=[jax.ShapeDtypeStruct((rows // out_count, columns), jnp.bfloat16)] * out_count,
        in_specs=[pl.BlockSpec(memory_space=pltpu.SMEM)] + [whole] * (count + 1),
        out_specs=[whole] * out_count,
        scratch_shapes=[
            pltpu.VMEM((rows, depth), jnp.bfloat16),
            pltpu.VMEM((rows, columns), jnp.bfloat16),
        ],
        cost_estimate=pl.CostEstimate(flops=2 * rows * depth * columns, bytes_accessed=4 * MIB, transcendentals=0),
        compiler_params=pltpu.CompilerParams(vmem_limit_bytes=8 * MIB),
        name="projection",
    )(places, *blocks, in_vmem(weight))


def gate_kernel(row_blocks, cores, first, count, model_width, places, *refs):
    blocks, gains = refs[: row_blocks * count], refs[row_blocks * count : (row_blocks + 1) * count]
    refs = refs[(row_blocks + 1) * count :]
    gate, up, refs = refs[0], refs[1], refs[2:]
    if first:
        before, (active, x) = refs[:3], refs[-2:]
        gate_sum, up_sum, squares = before
    else:
        gate_sum, up_sum, squares, x = refs[-4:]
    height, width = blocks[0].shape
    hidden = gate.shape[2]
    tile = min(256, hidden)
    sums = [[None] * (hidden // tile), [None] * (hidden // tile)]
    totals = [squares[s * height : (s + 1) * height, :] if first else 0.0 for s in range(row_blocks)]
    for k in range(count):
        for s in range(row_blocks):
            wide = blocks[s * count + k][...].astype(jnp.float32)
            totals[s] += jnp.sum(wide * wide, axis=-1, keepdims=True)
            x[s * height : (s + 1) * height, k * width : (k + 1) * width] = (wide * gains[k][...]).astype(jnp.bfloat16)
    for w, (weight, start) in enumerate(((gate, gate_sum), (up, up_sum))):
        for j in range(hidden // tile):
            cut = slice(j * tile, (j + 1) * tile)
            total = start[:, cut] if first else None
            for k in range(count):
                depth = pl.ds(pl.multiple_of(places[first + k] * width, 128), width)
                product = jnp.dot(
                    x[:, k * width : (k + 1) * width], weight[0, depth, cut], preferred_element_type=jnp.float32
                )
                total = product if total is None else total + product
            sums[w][j] = total
            if not first:
                start[:, cut] = total
    if not first:
        for s in range(row_blocks):
            squares[s * height : (s + 1) * height, :] = totals[s]
        return
    scale = jnp.concatenate([lax.rsqrt(t / model_width + norm_epsilon) for t in totals], axis=0)
    for j in range(hidden // tile):
        gate_part = sums[0][j] * scale
        up_part = sums[1][j] * scale
        active[:, j * tile : (j + 1) * tile] = (gate_part / (1.0 + jnp.exp(-gate_part)) * up_part).astype(jnp.bfloat16)


def activate(places, blocks, gains, gate_weight, up_weight, cores, first, before):
    row_blocks, count = len(blocks), len(blocks[0])
    height, width = blocks[0][0].shape
    rows = row_blocks * height
    model_width, hidden = gate_weight.shape[1:]
    whole = pl.BlockSpec(memory_space=pltpu.VMEM)
    if first:
        kinds = jax.ShapeDtypeStruct((rows, hidden), jnp.bfloat16)
    else:
        kinds = [jax.ShapeDtypeStruct((rows, n), jnp.float32) for n in (hidden, hidden, 1)]
    return pl.pallas_call(
        functools.partial(gate_kernel, row_blocks, cores, first, count, model_width),
        out_shape=kinds,
        in_specs=[pl.BlockSpec(memory_space=pltpu.SMEM)] + [whole] * ((row_blocks + 1) * count + 2 + len(before)),
        out_specs=whole if first else [whole] * 3,
        scratch_shapes=[pltpu.VMEM((rows, count * width), jnp.bfloat16)],
        cost_estimate=pl.CostEstimate(
            flops=4 * rows * hidden * count * width, bytes_accessed=4 * hidden * count * width, transcendentals=0
        ),
        compiler_params=pltpu.CompilerParams(vmem_limit_bytes=2 * rows * (count * width + 8 * hidden) + 12 * MIB),
        name="activate",
    )(places, *[b for row in blocks for b in row], *gains, in_vmem(gate_weight), in_vmem(up_weight), *before)


def down_kernel(slots, at, column_blocks, cores, places, active, row_weight, down, *refs):
    row_blocks = len(slots)
    outs = refs[-row_blocks * cores :]
    width = down.shape[2] // column_blocks
    height = outs[0].shape[0] * cores // column_blocks
    mine = slice(at * row_blocks * height, (at + 1) * row_blocks * height)
    order = [b * cores + c for c in reversed(range(cores)) for b in range(column_blocks // cores)]
    tile = 256 if width % 256 == 0 else 128
    weights = []
    for s in range(row_blocks):
        first = pl.multiple_of(places[column_blocks + slots[s]] * height, height)
        weights.append(row_weight[pl.ds(first, height), :])
    for k in order:
        b, c = k // cores, k % cores
        start = pl.multiple_of(places[k] * width, 128)
        for j in range(width // tile):
            cut = slice(j * tile, (j + 1) * tile)
            product = jnp.dot(
                active[mine, :], down[0, :, pl.ds(start + j * tile, tile)], preferred_element_type=jnp.float32
            )
            for s in range(row_blocks):
                part = product[s * height : (s + 1) * height, :] * weights[s]
                outs[s * cores + c][b * height : (b + 1) * height, cut] = part.astype(jnp.bfloat16)


def project_down(places, active, row_weight, down_weight, slots, at, height, column_blocks, cores, after):
    row_blocks = len(slots)
    rows = row_blocks * height
    width = down_weight.shape[2] // column_blocks
    whole = pl.BlockSpec(memory_space=pltpu.VMEM)
    out = jax.ShapeDtypeStruct((height * (column_blocks // cores), width), jnp.bfloat16)
    outs = pl.pallas_call(
        functools.partial(down_kernel, slots, at, column_blocks, cores),
        out_shape=[out] * (row_blocks * cores),
        in_specs=[pl.BlockSpec(memory_space=pltpu.SMEM)]
        + [whole] * 3
        + [pl.BlockSpec(memory_space=pl.ANY)] * len(after),
        out_specs=[whole] * (row_blocks * cores),
        cost_estimate=pl.CostEstimate(
            flops=2 * rows * down_weight.size, bytes_accessed=2 * down_weight.size, transcendentals=0
        ),
        compiler_params=pltpu.CompilerParams(vmem_limit_bytes=4 * MIB),
        name="down",
    )(places, active, row_weight, in_vmem(down_weight), *after)
    return [outs[s * cores : (s + 1) * cores] for s in range(row_blocks)]


def add_kernel(groups, *refs):
    used = sum(len(g) for g in groups)
    outs = refs[-len(groups) :]
    at = 0
    for group, out in zip(groups, outs):
        total = None
        for first in group:
            value = refs[at][first : first + out.shape[0], :].astype(jnp.float32)
            total = value if total is None else total + value
            at += 1
        out[...] = total.astype(out.dtype)


def add(groups, height, after=(), kind=jnp.bfloat16):
    values = [value for group in groups for value, _ in group]
    width = values[0].shape[1]
    whole = pl.BlockSpec(memory_space=pltpu.VMEM)
    return pl.pallas_call(
        functools.partial(add_kernel, [[first for _, first in group] for group in groups]),
        out_shape=[jax.ShapeDtypeStruct((height, width), kind)] * len(groups),
        in_specs=[whole] * len(values) + [pl.BlockSpec(memory_space=pl.ANY)] * len(after),
        out_specs=[whole] * len(groups),
        compiler_params=pltpu.CompilerParams(vmem_limit_bytes=8 * MIB),
        name="add",
    )(*values, *after)


def shards(
    query_latent,
    query_rope,
    cache_latent,
    cache_rope,
    cache_length,
    value_up,
    output_weight,
    residual,
    norm_gain,
    routed_experts,
    expert_gates,
    gate_weight,
    up_weight,
    down_weight,
):
    ep_count = lax.axis_size("ep")
    tp_count = lax.axis_size("tp")
    ep_index = lax.axis_index("ep")
    tp_index = lax.axis_index("tp")
    row_total = routed_experts.shape[0]
    block_rows = row_total // tp_count
    cores = 2
    chips = ep_count // cores

    def from_core(value):
        return lax.ppermute(value, "ep", [(i, i ^ 1) for i in range(ep_count)])

    def from_chip(value, back):
        step = cores * back
        return lax.ppermute(value, "ep", [(i, (i + step) % ep_count) for i in range(ep_count)])

    def from_tp(value, bits):
        return lax.ppermute(value, "tp", [(i, i ^ bits) for i in range(tp_count)])

    def gather_ep(value, after=()):
        same = [value] + [from_chip(value, b) for b in range(1, chips)]
        if after:
            same[1:] = [add([[(v, 0)]], v.shape[0], after)[0] for v in same[1:]]
        other = [from_core(v) for v in same]
        return [v for pair in zip(same, other) for v in pair]

    chip, core = ep_index // cores, ep_index % cores
    ep_places = [
        (chip - b + chips) % chips * cores + (core if c == 0 else 1 - core)
        for b in range(chips)
        for c in range(cores)
    ]
    tp_places = [tp_index ^ k for k in range(tp_count)]
    places = jnp.stack(ep_places + tp_places).astype(jnp.int32)

    gain = norm_gain.reshape(1, -1)
    gains = gather_ep(gain)
    own_residual = lax.dynamic_slice_in_dim(residual, tp_index * block_rows, block_rows, 0)
    row_weight = jnp.sum(jnp.where(routed_experts == ep_index, expert_gates, 0.0), axis=-1, keepdims=True)

    head_out = attend(query_latent, query_rope, cache_latent, cache_rope, cache_length, value_up, [places])
    output_weight = fetch(output_weight, [head_out, row_weight, own_residual, gain])
    partial = project(places, gather_ep(head_out, [output_weight]), output_weight, tp_count)

    gate_weight = fetch(gate_weight, [partial[0]])
    terms = [[(value, 0)] for value in partial]
    for k in reversed(range(1, tp_count)):
        total = terms[k][0][0]
        if len(terms[k]) > 1 or k == 1:
            (total,) = add([terms[k]], block_rows, [gate_weight] if k == 1 else [])
        low = k & -k
        arrived = from_tp(total, low)
        terms[k ^ low].append((arrived, 0))
    up_weight = fetch(up_weight, [total])
    down_weight = fetch(down_weight, [total])
    stream_terms = terms[0] + [(own_residual, 0)]
    stream, stream_out = add([stream_terms, stream_terms], block_rows, gains + [gate_weight, up_weight, down_weight])

    rows_of = {0: stream}
    crossed = [from_chip(stream, b) for b in range(1, chips)]
    for k in range(1, tp_count):
        low = k & -k
        source = rows_of[k ^ low]
        if k == tp_count - 1:
            (source,) = add([[(source, 0)]], block_rows, crossed)
        rows_of[k] = from_tp(source, low)
    slots = list(reversed(range(tp_count)))
    near = {k: [rows_of[k], from_core(rows_of[k])] for k in slots}
    sums = activate(places, [near[k] for k in slots], gains[:cores], gate_weight, up_weight, cores, 0, [])
    far = {}
    for k in [0] + slots[:-1]:
        far[k] = []
        for b in range(1, chips):
            if k == 0:
                value = crossed[b - 1]
            elif k == 1:
                (source,) = add([[(crossed[b - 1], 0)]], block_rows, [rows_of[tp_count - 1]])
                value = from_tp(source, 1)
            else:
                value = from_chip(rows_of[k], b)
            (later,) = add([[(value, 0)]], block_rows, sums[-1:]) if k == tp_count - 1 else (value,)
            far[k] += [value, from_core(later)]
    active = activate(places, [far[k] for k in slots], gains[cores:], gate_weight, up_weight, cores, cores, sums)

    def send_back(k, after):
        total = list(add([terms[k]], block_rows, after))
        low = k & -k
        terms[k ^ low].append((from_tp(total[0], low), 0))
        return total

    terms = [[] for _ in range(tp_count)]
    arrivals, sent = [], []
    outs = project_down(places, active, row_weight, down_weight, slots, 0, block_rows, ep_count, cores, [])
    swapped = [from_core(out[1]) for out in outs]
    def core_sums(k, after):
        at = slots.index(k)
        rows = [[(outs[at][0], c * block_rows), (swapped[at], c * block_rows)] for c in range(chips)]
        return rows, after

    def cross(k, extra, after):
        rows, after = core_sums(k, after)
        added = add([row + more for row, more in zip(rows, extra)], block_rows, after)
        across = [from_chip(added[c], chips - c) for c in range(1, chips)]
        arrivals.append(across)
        terms[k] += [(value, 0) for value in [added[0]] + across]

    none = [[] for _ in range(chips)]
    for k in slots[:-2]:
        cross(k, none, arrivals[-2] if len(arrivals) > 1 else [])
    rows, _ = core_sums(1, [])
    added = add(rows, block_rows)
    joined = [[]] + [[(from_tp(added[c], 1), 0)] for c in range(1, chips)]
    early = [value for more in joined for value, _ in more]
    sent = send_back(slots[0], early)
    cross(0, joined, sent)
    for k in slots[1:-2]:
        send_back(k, [])
    terms[1].insert(0, (added[0], 0))
    (kept,) = add([terms[1]], block_rows) if len(terms[1]) > 1 else (added[0],)
    (most,) = add([terms[0]], block_rows, (), jnp.float32)
    (mixed,) = add([[(most, 0), (from_tp(kept, 1), 0)]], block_rows)
    return (stream_out, mixed)


def solution(mesh):
    return jax.shard_map(
        shards,
        mesh=mesh,
        in_specs=(
            P(("parts", "ep"), "tp", None),
            P(("parts", "ep"), "tp"),
            P(("parts", "ep"), None, None),
            P(("parts", "ep"), None, None),
            P(("parts", "ep")),
            P("tp", None, None),
            P("tp", "ep"),
            P("parts", "ep"),
            P("ep"),
            P("parts", None),
            P("parts", None),
            P("ep", None, "tp"),
            P("ep", None, "tp"),
            P("ep", "tp", None),
        ),
        out_specs=(P(("parts", "tp"), "ep"), P(("parts", "tp"), "ep")),
        check_vma=False,
    )
```

```python
import functools

import jax
import jax.numpy as jnp
from jax import lax
from jax.experimental import pallas as pl
from jax.experimental.pallas import tpu as pltpu
from jax.sharding import PartitionSpec as P

score_scale = 1.0 / 192.0**0.5
norm_epsilon = 1e-06
MIB = 1 << 20


def in_hbm(value):
    return pltpu.with_memory_space_constraint(value, pltpu.HBM)


def in_vmem(value):
    return pltpu.with_memory_space_constraint(value, pltpu.VMEM)


def fetch_kernel(parts, *refs):
    source, target, sems = refs[0], refs[-2], refs[-1]
    step = source.shape[-2] // parts
    copies = []
    for i in range(parts):
        cut = (slice(None),) * (len(source.shape) - 2) + (pl.ds(i * step, step),)
        copies.append(pltpu.make_async_copy(source.at[cut], target.at[cut], sems.at[i]))
    for copy in copies:
        copy.start()
    for copy in copies:
        copy.wait()


def fetch(value, after):
    parts = 4
    return pl.pallas_call(
        functools.partial(fetch_kernel, parts),
        out_shape=pltpu.VMEM(value.shape, value.dtype),
        in_specs=[pl.BlockSpec(memory_space=pl.ANY)] * (1 + len(after)),
        out_specs=pl.BlockSpec(memory_space=pltpu.VMEM),
        scratch_shapes=[pltpu.SemaphoreType.DMA((parts,))],
        cost_estimate=pl.CostEstimate(flops=0, bytes_accessed=4 * value.size, transcendentals=0),
        compiler_params=pltpu.CompilerParams(vmem_limit_bytes=1 * MIB),
        name="fetch",
    )(in_hbm(value), *after)


def attention_kernel(step_rows, pieces, ahead, lengths, q_ref, qr_ref, k_hbm, kr_hbm, up_hbm, *refs):
    out_ref, latent, rope, k_ref, kr_ref, up_ref, sems, up_sem = refs[-8:]
    step = pl.program_id(0)
    steps = k_ref.shape[0] // step_rows
    heads, positions = q_ref.shape[1], k_ref.shape[1]
    rope_width = kr_ref.shape[1]

    def copies(at):
        whole = pl.ds(at * step_rows, step_rows)
        made = [pltpu.make_async_copy(kr_hbm.at[whole], kr_ref.at[whole], sems.at[at, pieces])]
        for i in range(pieces):
            part = pl.ds(at * step_rows + i * (step_rows // pieces), step_rows // pieces)
            made.append(pltpu.make_async_copy(k_hbm.at[part], k_ref.at[part], sems.at[at, i]))
        return made

    @pl.when(step == 0)
    def _():
        for at in range(min(ahead, steps)):
            for copy in copies(at):
                copy.start()
        pltpu.make_async_copy(up_hbm, up_ref, up_sem).start()
        all_rows = qr_ref.shape[0]
        width = heads * rope_width
        lane = lax.broadcasted_iota(jnp.int32, (heads, width), 1)
        head = lax.broadcasted_iota(jnp.int32, (heads, width), 0)
        own = jnp.where(lane // rope_width == head, 1.0, 0.0)
        spread = qr_ref[...].astype(jnp.float32)[:, None, :] * own[None, :, :]
        spread = spread.reshape(all_rows * heads, width).astype(jnp.bfloat16)
        lane = lax.broadcasted_iota(jnp.int32, (width, rope_width), 0)
        column = lax.broadcasted_iota(jnp.int32, (width, rope_width), 1)
        fold = jnp.where(lane % rope_width == column, 1.0, 0.0).astype(jnp.bfloat16)
        rope[...] = jnp.dot(spread, fold, preferred_element_type=jnp.float32)

    @pl.when(step + ahead < steps)
    def _():
        for copy in copies(step + ahead):
            copy.start()

    for copy in copies(step):
        copy.wait()
    place = lax.broadcasted_iota(jnp.int32, (heads, positions), 1)
    lanes = latent.shape[2]
    lanes = latent.shape[2]
    scores = []
    for r in range(step_rows):
        first = pl.multiple_of((step * step_rows + r) * heads, heads)
        score = lax.dot_general(
            q_ref[r], k_ref[step * step_rows + r], (((1,), (1,)), ((), ())), preferred_element_type=jnp.float32
        )
        score += jnp.dot(
            rope[pl.ds(first, heads), :].astype(jnp.bfloat16), kr_ref[step * step_rows + r], preferred_element_type=jnp.float32
        )
        scores.append(score)
    probabilities = []
    for r in range(step_rows):
        visible = place < lengths[step * step_rows + r]
        score = jnp.where(visible, scores[r] * score_scale, -jnp.inf)
        weight = jnp.exp(score - jnp.max(score, axis=-1, keepdims=True))
        total = jnp.sum(weight, axis=-1, keepdims=True)
        probabilities.append((weight / total).astype(jnp.bfloat16))
    for r in range(step_rows):
        first = pl.multiple_of((step * step_rows + r) * heads, heads)
        mixed = jnp.dot(probabilities[r], k_ref[step * step_rows + r], preferred_element_type=jnp.float32)
        for c in range(latent.shape[0]):
            latent[c, pl.ds(first, heads), :] = mixed[:, c * lanes : (c + 1) * lanes]

    @pl.when(step == pl.num_programs(0) - 1)
    def _():
        pltpu.make_async_copy(up_hbm, up_ref, up_sem).wait()
        rows = out_ref.shape[0]
        width = up_ref.shape[2]
        for h in range(heads):
            parts = [latent[c, pl.ds(h, rows, stride=heads), :] for c in range(latent.shape[0])]
            part = jnp.concatenate(parts, axis=1).astype(jnp.bfloat16)
            out_ref[:, h * width : (h + 1) * width] = jnp.dot(
                part, up_ref[h], preferred_element_type=jnp.float32
            ).astype(jnp.bfloat16)


def attend(query_latent, query_rope, cache_latent, cache_rope, cache_length, value_up, after):
    rows, heads, latent_width = query_latent.shape
    rope_width = cache_rope.shape[1]
    value_width = value_up.shape[2]
    step_rows, pieces, ahead = 8, 1, 3
    by_row = lambda i, lengths: (i, 0, 0)
    return pl.pallas_call(
        functools.partial(attention_kernel, step_rows, pieces, ahead),
        out_shape=jax.ShapeDtypeStruct((rows, heads * value_width), jnp.bfloat16),
        grid_spec=pltpu.PrefetchScalarGridSpec(
            num_scalar_prefetch=1,
            grid=(rows // step_rows,),
            in_specs=[
                pl.BlockSpec((step_rows, heads, latent_width), by_row),
                pl.BlockSpec(query_rope.shape, lambda i, lengths: (0, 0)),
                pl.BlockSpec(memory_space=pl.ANY),
                pl.BlockSpec(memory_space=pl.ANY),
                pl.BlockSpec(memory_space=pl.ANY),
            ]
            + [pl.BlockSpec(memory_space=pl.ANY)] * len(after),
            out_specs=pl.BlockSpec((rows, heads * value_width), lambda i, lengths: (0, 0)),
            scratch_shapes=[
                pltpu.VMEM((latent_width // 128, rows * heads, 128), jnp.float32),
                pltpu.VMEM((rows * heads, rope_width), jnp.float32),
                pltpu.VMEM(cache_latent.shape, jnp.bfloat16),
                pltpu.VMEM(cache_rope.shape, jnp.bfloat16),
                pltpu.VMEM(value_up.shape, jnp.bfloat16),
                pltpu.SemaphoreType.DMA((rows // step_rows, pieces + 1)),
                pltpu.SemaphoreType.DMA,
            ],
        ),
        cost_estimate=pl.CostEstimate(
            flops=64 * heads * cache_latent.size, bytes_accessed=2 * cache_latent.size, transcendentals=0
        ),
        compiler_params=pltpu.CompilerParams(vmem_limit_bytes=28 * MIB),
        name="attention",
    )(
        cache_length,
        in_hbm(query_latent),
        in_hbm(query_rope),
        in_hbm(cache_latent),
        in_hbm(cache_rope),
        in_hbm(value_up),
        *after,
    )


def projection_kernel(count, out_count, places, *refs):
    blocks, weight, outs = refs[:count], refs[count], refs[-2 - out_count : -2]
    gathered, result = refs[-2:]
    height = blocks[0].shape[0]
    for k in range(count):
        first = pl.multiple_of(places[k] * height, height)
        gathered[pl.ds(first, height), :] = blocks[k][...]
    columns = weight.shape[1]
    tile = 256 if columns % 256 == 0 else 128
    for j in range(columns // tile):
        result[:, j * tile : (j + 1) * tile] = jnp.dot(
            gathered[...], weight[:, j * tile : (j + 1) * tile], preferred_element_type=jnp.float32
        ).astype(jnp.bfloat16)
    out_height = outs[0].shape[0]
    for s in range(len(outs)):
        first = pl.multiple_of(places[count + s] * out_height, out_height)
        outs[s][...] = result[pl.ds(first, out_height), :]


def project(places, blocks, weight, out_count):
    count = len(blocks)
    height, depth = blocks[0].shape
    rows, columns = height * count, weight.shape[1]
    whole = pl.BlockSpec(memory_space=pltpu.VMEM)
    return pl.pallas_call(
        functools.partial(projection_kernel, count, out_count),
        out_shape=[jax.ShapeDtypeStruct((rows // out_count, columns), jnp.bfloat16)] * out_count,
        in_specs=[pl.BlockSpec(memory_space=pltpu.SMEM)] + [whole] * (count + 1),
        out_specs=[whole] * out_count,
        scratch_shapes=[
            pltpu.VMEM((rows, depth), jnp.bfloat16),
            pltpu.VMEM((rows, columns), jnp.bfloat16),
        ],
        cost_estimate=pl.CostEstimate(flops=2 * rows * depth * columns, bytes_accessed=4 * MIB, transcendentals=0),
        compiler_params=pltpu.CompilerParams(vmem_limit_bytes=8 * MIB),
        name="projection",
    )(places, *blocks, in_vmem(weight))


def gate_kernel(row_blocks, first, count, offset, model_width, places, *refs):
    blocks, gains = refs[: row_blocks * count], refs[row_blocks * count : (row_blocks + 1) * count]
    refs = refs[(row_blocks + 1) * count :]
    gate, up, refs = refs[0], refs[1], refs[2:]
    if first:
        before, (active, x) = refs[:3], refs[-2:]
        gate_sum, up_sum, squares = before
    else:
        gate_sum, up_sum, squares, x = refs[-4:]
    height, width = blocks[0].shape
    hidden = gate.shape[2]
    tile = min(256, hidden)
    sums = [[None] * (hidden // tile), [None] * (hidden // tile)]
    mine = slice(offset, offset + row_blocks * height)
    totals = [0.0] * row_blocks
    if first:
        totals = [squares[offset + s * height : offset + (s + 1) * height, :] for s in range(row_blocks)]
    for k in range(count):
        for s in range(row_blocks):
            wide = blocks[s * count + k][...].astype(jnp.float32)
            totals[s] += jnp.sum(wide * wide, axis=-1, keepdims=True)
            x[s * height : (s + 1) * height, k * width : (k + 1) * width] = (wide * gains[k][...]).astype(jnp.bfloat16)
    for w, (weight, start) in enumerate(((gate, gate_sum), (up, up_sum))):
        for j in range(hidden // tile):
            cut = slice(j * tile, (j + 1) * tile)
            total = start[mine, cut] if first else None
            for k in range(count):
                depth = pl.ds(pl.multiple_of(places[first + k] * width, 128), width)
                product = jnp.dot(
                    x[:, k * width : (k + 1) * width], weight[0, depth, cut], preferred_element_type=jnp.float32
                )
                total = product if total is None else total + product
            sums[w][j] = total
            if not first:
                start[:, cut] = total
    if not first:
        for s in range(row_blocks):
            squares[s * height : (s + 1) * height, :] = totals[s]
        return
    scale = jnp.concatenate([lax.rsqrt(t / model_width + norm_epsilon) for t in totals], axis=0)
    for j in range(hidden // tile):
        gate_part = sums[0][j] * scale
        up_part = sums[1][j] * scale
        active[:, j * tile : (j + 1) * tile] = (gate_part / (1.0 + jnp.exp(-gate_part)) * up_part).astype(jnp.bfloat16)


def activate(places, blocks, gains, gate_weight, up_weight, first, offset, before, after):
    row_blocks, count = len(blocks), len(blocks[0])
    height, width = blocks[0][0].shape
    rows = row_blocks * height
    model_width, hidden = gate_weight.shape[1:]
    whole = pl.BlockSpec(memory_space=pltpu.VMEM)
    if first:
        kinds = jax.ShapeDtypeStruct((rows, hidden), jnp.bfloat16)
    else:
        kinds = [jax.ShapeDtypeStruct((rows, n), jnp.float32) for n in (hidden, hidden, 1)]
    return pl.pallas_call(
        functools.partial(gate_kernel, row_blocks, first, count, offset, model_width),
        out_shape=kinds,
        in_specs=[pl.BlockSpec(memory_space=pltpu.SMEM)] + [whole] * ((row_blocks + 1) * count + 2 + len(before))
        + [pl.BlockSpec(memory_space=pl.ANY)] * len(after),
        out_specs=whole if first else [whole] * 3,
        scratch_shapes=[pltpu.VMEM((rows, count * width), jnp.bfloat16)],
        cost_estimate=pl.CostEstimate(
            flops=4 * rows * hidden * count * width, bytes_accessed=4 * hidden * count * width, transcendentals=0
        ),
        compiler_params=pltpu.CompilerParams(vmem_limit_bytes=2 * rows * (count * width + 8 * hidden) + 12 * MIB),
        name="activate",
    )(places, *[b for row in blocks for b in row], *gains, in_vmem(gate_weight), in_vmem(up_weight), *before, *after)


def down_kernel(slots, at, column_blocks, cores, places, active, row_weight, down, *refs):
    row_blocks = len(slots)
    outs = refs[-row_blocks * cores :]
    width = down.shape[2] // column_blocks
    height = outs[0].shape[0] * cores // column_blocks
    mine = slice(at * row_blocks * height, (at + 1) * row_blocks * height)
    order = [b * cores + c for c in reversed(range(cores)) for b in range(column_blocks // cores)]
    tile = 256 if width % 256 == 0 else 128
    weights = []
    for s in range(row_blocks):
        first = pl.multiple_of(places[column_blocks + slots[s]] * height, height)
        weights.append(row_weight[pl.ds(first, height), :])
    for k in order:
        b, c = k // cores, k % cores
        start = pl.multiple_of(places[k] * width, 128)
        for j in range(width // tile):
            cut = slice(j * tile, (j + 1) * tile)
            product = jnp.dot(
                active[mine, :], down[0, :, pl.ds(start + j * tile, tile)], preferred_element_type=jnp.float32
            )
            for s in range(row_blocks):
                part = product[s * height : (s + 1) * height, :] * weights[s]
                outs[s * cores + c][b * height : (b + 1) * height, cut] = part.astype(jnp.bfloat16)


def project_down(places, active, row_weight, down_weight, slots, at, height, column_blocks, cores, after):
    row_blocks = len(slots)
    rows = row_blocks * height
    width = down_weight.shape[2] // column_blocks
    whole = pl.BlockSpec(memory_space=pltpu.VMEM)
    out = jax.ShapeDtypeStruct((height * (column_blocks // cores), width), jnp.bfloat16)
    outs = pl.pallas_call(
        functools.partial(down_kernel, slots, at, column_blocks, cores),
        out_shape=[out] * (row_blocks * cores),
        in_specs=[pl.BlockSpec(memory_space=pltpu.SMEM)]
        + [whole] * 3
        + [pl.BlockSpec(memory_space=pl.ANY)] * len(after),
        out_specs=[whole] * (row_blocks * cores),
        cost_estimate=pl.CostEstimate(
            flops=2 * rows * down_weight.size, bytes_accessed=2 * down_weight.size, transcendentals=0
        ),
        compiler_params=pltpu.CompilerParams(vmem_limit_bytes=4 * MIB),
        name="down",
    )(places, active, row_weight, in_vmem(down_weight), *after)
    return [outs[s * cores : (s + 1) * cores] for s in range(row_blocks)]


def add_kernel(groups, *refs):
    used = sum(len(g) for g in groups)
    outs = refs[-len(groups) :]
    at = 0
    for group, out in zip(groups, outs):
        total = None
        for first in group:
            value = refs[at][first : first + out.shape[0], :].astype(jnp.float32)
            total = value if total is None else total + value
            at += 1
        out[...] = total.astype(out.dtype)


def add(groups, height, after=(), kind=jnp.bfloat16):
    values = [value for group in groups for value, _ in group]
    width = values[0].shape[1]
    whole = pl.BlockSpec(memory_space=pltpu.VMEM)
    return pl.pallas_call(
        functools.partial(add_kernel, [[first for _, first in group] for group in groups]),
        out_shape=[jax.ShapeDtypeStruct((height, width), kind)] * len(groups),
        in_specs=[whole] * len(values) + [pl.BlockSpec(memory_space=pl.ANY)] * len(after),
        out_specs=[whole] * len(groups),
        compiler_params=pltpu.CompilerParams(vmem_limit_bytes=8 * MIB),
        name="add",
    )(*values, *after)


def shards(
    query_latent,
    query_rope,
    cache_latent,
    cache_rope,
    cache_length,
    value_up,
    output_weight,
    residual,
    norm_gain,
    routed_experts,
    expert_gates,
    gate_weight,
    up_weight,
    down_weight,
):
    ep_count = lax.axis_size("ep")
    tp_count = lax.axis_size("tp")
    ep_index = lax.axis_index("ep")
    tp_index = lax.axis_index("tp")
    row_total = routed_experts.shape[0]
    block_rows = row_total // tp_count
    cores = 2
    chips = ep_count // cores

    def from_core(value):
        return lax.ppermute(value, "ep", [(i, i ^ 1) for i in range(ep_count)])

    def from_chip(value, back):
        step = cores * back
        return lax.ppermute(value, "ep", [(i, (i + step) % ep_count) for i in range(ep_count)])

    def from_tp(value, bits):
        return lax.ppermute(value, "tp", [(i, i ^ bits) for i in range(tp_count)])

    def gather_ep(value, after=()):
        same = [value] + [from_chip(value, b) for b in range(1, chips)]
        if after:
            same[1:] = [add([[(v, 0)]], v.shape[0], after)[0] for v in same[1:]]
        other = [from_core(v) for v in same]
        return [v for pair in zip(same, other) for v in pair]

    chip, core = ep_index // cores, ep_index % cores
    ep_places = [
        (chip - b + chips) % chips * cores + (core if c == 0 else 1 - core)
        for b in range(chips)
        for c in range(cores)
    ]
    tp_places = [tp_index ^ k for k in range(tp_count)]
    places = jnp.stack(ep_places + tp_places).astype(jnp.int32)

    gain = norm_gain.reshape(1, -1)
    gains = gather_ep(gain)
    own_residual = lax.dynamic_slice_in_dim(residual, tp_index * block_rows, block_rows, 0)
    row_weight = jnp.sum(jnp.where(routed_experts == ep_index, expert_gates, 0.0), axis=-1, keepdims=True)

    head_out = attend(query_latent, query_rope, cache_latent, cache_rope, cache_length, value_up, [places])
    output_weight = fetch(output_weight, [head_out, row_weight, own_residual, gain])
    partial = project(places, gather_ep(head_out, [output_weight]), output_weight, tp_count)

    gate_weight = fetch(gate_weight, [partial[0]])
    terms = [[(value, 0)] for value in partial]
    for k in reversed(range(1, tp_count)):
        total = terms[k][0][0]
        if len(terms[k]) > 1 or k == 1:
            (total,) = add([terms[k]], block_rows, [gate_weight] if k == 1 else [])
        low = k & -k
        arrived = from_tp(total, low)
        terms[k ^ low].append((arrived, 0))
    up_weight = fetch(up_weight, [total])
    down_weight = fetch(down_weight, [total])
    stream_terms = terms[0] + [(own_residual, 0)]
    stream, stream_out = add([stream_terms, stream_terms], block_rows, gains + [gate_weight, up_weight, down_weight])

    rows_of = {0: stream}
    crossed = [from_chip(stream, b) for b in range(1, chips)]
    for k in range(1, tp_count):
        low = k & -k
        source = rows_of[k ^ low]
        if k == tp_count - 1:
            (source,) = add([[(source, 0)]], block_rows, crossed)
        rows_of[k] = from_tp(source, low)
    slots = list(reversed(range(tp_count)))
    near = {k: [rows_of[k], from_core(rows_of[k])] for k in slots}
    half = tp_count // 2
    early = [k for k in slots if k % half == 0] if tp_count == 4 else slots[half:]
    late = [k for k in slots if k not in early]
    ordered = late + early
    sums = activate(places, [near[k] for k in ordered], gains[:cores], gate_weight, up_weight, 0, 0, [], [])

    def run_expert(group, after):
        active = activate(
            places,
            [far[k] for k in group],
            gains[cores:],
            gate_weight,
            up_weight,
            cores,
            ordered.index(group[0]) * block_rows,
            sums,
            after,
        )
        got = project_down(places, active, row_weight, down_weight, group, 0, block_rows, ep_count, cores, [])
        outs.update(zip(group, got))
        return got[0][:1]

    far, outs = {}, {}
    last = tp_count - 1
    for k in early + late[::-1]:
        far[k] = []
        if k == last:
            done = run_expert(early, [])
        for b in range(1, chips):
            if k == 0:
                value = crossed[b - 1]
            elif k == 1:
                (source,) = add([[(crossed[b - 1], 0)]], block_rows, near[last][1:])
                value = from_tp(source, 1)
            else:
                value = from_chip(rows_of[k], b)
            (later,) = add([[(value, 0)]], block_rows, done) if k == last else (value,)
            far[k] += [value, from_core(later)]
    run_expert(late, done)

    def send_back(k, after):
        total = list(add([terms[k]], block_rows, after))
        low = k & -k
        terms[k ^ low].append((from_tp(total[0], low), 0))
        return total

    terms = [[] for _ in range(tp_count)]
    arrivals, sent = [], []
    swapped = {k: from_core(outs[k][1]) for k in slots}
    def core_sums(k, after):
        rows = [[(outs[k][0], c * block_rows), (swapped[k], c * block_rows)] for c in range(chips)]
        return rows, after

    def cross(k, extra, after):
        rows, after = core_sums(k, after)
        added = add([row + more for row, more in zip(rows, extra)], block_rows, after)
        across = [from_chip(added[c], chips - c) for c in range(1, chips)]
        arrivals.append(across)
        terms[k] += [(value, 0) for value in [added[0]] + across]

    none = [[] for _ in range(chips)]
    for k in slots[:-2]:
        cross(k, none, arrivals[-2] if len(arrivals) > 1 else [])
    rows, _ = core_sums(1, [])
    added = add(rows, block_rows)
    joined = [[]] + [[(from_tp(added[c], 1), 0)] for c in range(1, chips)]
    early = [value for more in joined for value, _ in more]
    sent = send_back(slots[0], early)
    cross(0, joined, sent)
    for k in slots[1:-2]:
        send_back(k, [])
    terms[1].insert(0, (added[0], 0))
    (kept,) = add([terms[1]], block_rows) if len(terms[1]) > 1 else (added[0],)
    (most,) = add([terms[0]], block_rows, (), jnp.float32)
    (mixed,) = add([[(most, 0), (from_tp(kept, 1), 0)]], block_rows)
    return (stream_out, mixed)


def solution(mesh):
    return jax.shard_map(
        shards,
        mesh=mesh,
        in_specs=(
            P(("parts", "ep"), "tp", None),
            P(("parts", "ep"), "tp"),
            P(("parts", "ep"), None, None),
            P(("parts", "ep"), None, None),
            P(("parts", "ep")),
            P("tp", None, None),
            P("tp", "ep"),
            P("parts", "ep"),
            P("ep"),
            P("parts", None),
            P("parts", None),
            P("ep", None, "tp"),
            P("ep", None, "tp"),
            P("ep", "tp", None),
        ),
        out_specs=(P(("parts", "tp"), "ep"), P(("parts", "tp"), "ep")),
        check_vma=False,
    )
```

```python
import functools

import jax
import jax.numpy as jnp
from jax import lax
from jax.experimental import pallas as pl
from jax.experimental.pallas import tpu as pltpu
from jax.sharding import PartitionSpec as P

score_scale = 1.0 / 192.0**0.5
norm_epsilon = 1e-06
MIB = 1 << 20


def in_hbm(value):
    return pltpu.with_memory_space_constraint(value, pltpu.HBM)


def in_vmem(value):
    return pltpu.with_memory_space_constraint(value, pltpu.VMEM)


def fetch_kernel(parts, *refs):
    source, target, sems = refs[0], refs[-2], refs[-1]
    step = source.shape[-2] // parts
    copies = []
    for i in range(parts):
        cut = (slice(None),) * (len(source.shape) - 2) + (pl.ds(i * step, step),)
        copies.append(pltpu.make_async_copy(source.at[cut], target.at[cut], sems.at[i]))
    for copy in copies:
        copy.start()
    for copy in copies:
        copy.wait()


def fetch(value, after):
    parts = 4
    return pl.pallas_call(
        functools.partial(fetch_kernel, parts),
        out_shape=pltpu.VMEM(value.shape, value.dtype),
        in_specs=[pl.BlockSpec(memory_space=pl.ANY)] * (1 + len(after)),
        out_specs=pl.BlockSpec(memory_space=pltpu.VMEM),
        scratch_shapes=[pltpu.SemaphoreType.DMA((parts,))],
        cost_estimate=pl.CostEstimate(flops=0, bytes_accessed=4 * value.size, transcendentals=0),
        compiler_params=pltpu.CompilerParams(vmem_limit_bytes=1 * MIB),
        name="fetch",
    )(in_hbm(value), *after)


def attention_kernel(step_rows, pieces, ahead, lengths, q_ref, qr_ref, k_hbm, kr_hbm, up_hbm, *refs):
    out_ref, latent, rope, k_ref, kr_ref, up_ref, sems, up_sem = refs[-8:]
    step = pl.program_id(0)
    steps = k_ref.shape[0] // step_rows
    heads, positions = q_ref.shape[1], k_ref.shape[1]
    rope_width = kr_ref.shape[1]

    def copies(at):
        whole = pl.ds(at * step_rows, step_rows)
        made = [pltpu.make_async_copy(kr_hbm.at[whole], kr_ref.at[whole], sems.at[at, pieces])]
        for i in range(pieces):
            part = pl.ds(at * step_rows + i * (step_rows // pieces), step_rows // pieces)
            made.append(pltpu.make_async_copy(k_hbm.at[part], k_ref.at[part], sems.at[at, i]))
        return made

    @pl.when(step == 0)
    def _():
        for at in range(min(ahead, steps)):
            for copy in copies(at):
                copy.start()
        pltpu.make_async_copy(up_hbm, up_ref, up_sem).start()
        all_rows = qr_ref.shape[0]
        width = heads * rope_width
        lane = lax.broadcasted_iota(jnp.int32, (heads, width), 1)
        head = lax.broadcasted_iota(jnp.int32, (heads, width), 0)
        own = jnp.where(lane // rope_width == head, 1.0, 0.0)
        spread = qr_ref[...].astype(jnp.float32)[:, None, :] * own[None, :, :]
        spread = spread.reshape(all_rows * heads, width).astype(jnp.bfloat16)
        lane = lax.broadcasted_iota(jnp.int32, (width, rope_width), 0)
        column = lax.broadcasted_iota(jnp.int32, (width, rope_width), 1)
        fold = jnp.where(lane % rope_width == column, 1.0, 0.0).astype(jnp.bfloat16)
        rope[...] = jnp.dot(spread, fold, preferred_element_type=jnp.float32)

    @pl.when(step + ahead < steps)
    def _():
        for copy in copies(step + ahead):
            copy.start()

    for copy in copies(step):
        copy.wait()
    place = lax.broadcasted_iota(jnp.int32, (heads, positions), 1)
    lanes = latent.shape[2]
    lanes = latent.shape[2]
    scores = []
    for r in range(step_rows):
        first = pl.multiple_of((step * step_rows + r) * heads, heads)
        score = lax.dot_general(
            q_ref[r], k_ref[step * step_rows + r], (((1,), (1,)), ((), ())), preferred_element_type=jnp.float32
        )
        score += jnp.dot(
            rope[pl.ds(first, heads), :].astype(jnp.bfloat16), kr_ref[step * step_rows + r], preferred_element_type=jnp.float32
        )
        scores.append(score)
    probabilities = []
    for r in range(step_rows):
        visible = place < lengths[step * step_rows + r]
        score = jnp.where(visible, scores[r] * score_scale, -jnp.inf)
        weight = jnp.exp(score - jnp.max(score, axis=-1, keepdims=True))
        total = jnp.sum(weight, axis=-1, keepdims=True)
        probabilities.append((weight / total).astype(jnp.bfloat16))
    for r in range(step_rows):
        first = pl.multiple_of((step * step_rows + r) * heads, heads)
        mixed = jnp.dot(probabilities[r], k_ref[step * step_rows + r], preferred_element_type=jnp.float32)
        for c in range(latent.shape[0]):
            latent[c, pl.ds(first, heads), :] = mixed[:, c * lanes : (c + 1) * lanes]

    @pl.when(step == pl.num_programs(0) - 1)
    def _():
        pltpu.make_async_copy(up_hbm, up_ref, up_sem).wait()
        rows = out_ref.shape[0]
        width = up_ref.shape[2]
        for h in range(heads):
            parts = [latent[c, pl.ds(h, rows, stride=heads), :] for c in range(latent.shape[0])]
            part = jnp.concatenate(parts, axis=1).astype(jnp.bfloat16)
            out_ref[:, h * width : (h + 1) * width] = jnp.dot(
                part, up_ref[h], preferred_element_type=jnp.float32
            ).astype(jnp.bfloat16)


def attend(query_latent, query_rope, cache_latent, cache_rope, cache_length, value_up, after):
    rows, heads, latent_width = query_latent.shape
    rope_width = cache_rope.shape[1]
    value_width = value_up.shape[2]
    step_rows, pieces, ahead = 8, 1, 3
    by_row = lambda i, lengths: (i, 0, 0)
    return pl.pallas_call(
        functools.partial(attention_kernel, step_rows, pieces, ahead),
        out_shape=jax.ShapeDtypeStruct((rows, heads * value_width), jnp.bfloat16),
        grid_spec=pltpu.PrefetchScalarGridSpec(
            num_scalar_prefetch=1,
            grid=(rows // step_rows,),
            in_specs=[
                pl.BlockSpec((step_rows, heads, latent_width), by_row),
                pl.BlockSpec(query_rope.shape, lambda i, lengths: (0, 0)),
                pl.BlockSpec(memory_space=pl.ANY),
                pl.BlockSpec(memory_space=pl.ANY),
                pl.BlockSpec(memory_space=pl.ANY),
            ]
            + [pl.BlockSpec(memory_space=pl.ANY)] * len(after),
            out_specs=pl.BlockSpec((rows, heads * value_width), lambda i, lengths: (0, 0)),
            scratch_shapes=[
                pltpu.VMEM((latent_width // 128, rows * heads, 128), jnp.float32),
                pltpu.VMEM((rows * heads, rope_width), jnp.float32),
                pltpu.VMEM(cache_latent.shape, jnp.bfloat16),
                pltpu.VMEM(cache_rope.shape, jnp.bfloat16),
                pltpu.VMEM(value_up.shape, jnp.bfloat16),
                pltpu.SemaphoreType.DMA((rows // step_rows, pieces + 1)),
                pltpu.SemaphoreType.DMA,
            ],
        ),
        cost_estimate=pl.CostEstimate(
            flops=64 * heads * cache_latent.size, bytes_accessed=2 * cache_latent.size, transcendentals=0
        ),
        compiler_params=pltpu.CompilerParams(vmem_limit_bytes=28 * MIB),
        name="attention",
    )(
        in_hbm(cache_length),
        in_hbm(query_latent),
        in_hbm(query_rope),
        in_hbm(cache_latent),
        in_hbm(cache_rope),
        in_hbm(value_up),
        *after,
    )


def projection_kernel(count, out_count, places, *refs):
    blocks, weight, outs = refs[:count], refs[count], refs[-2 - out_count : -2]
    gathered, result = refs[-2:]
    height = blocks[0].shape[0]
    for k in range(count):
        first = pl.multiple_of(places[k] * height, height)
        gathered[pl.ds(first, height), :] = blocks[k][...]
    columns = weight.shape[1]
    tile = 256 if columns % 256 == 0 else 128
    for j in range(columns // tile):
        result[:, j * tile : (j + 1) * tile] = jnp.dot(
            gathered[...], weight[:, j * tile : (j + 1) * tile], preferred_element_type=jnp.float32
        ).astype(jnp.bfloat16)
    out_height = outs[0].shape[0]
    for s in range(len(outs)):
        first = pl.multiple_of(places[count + s] * out_height, out_height)
        outs[s][...] = result[pl.ds(first, out_height), :]


def project(places, blocks, weight, out_count):
    count = len(blocks)
    height, depth = blocks[0].shape
    rows, columns = height * count, weight.shape[1]
    whole = pl.BlockSpec(memory_space=pltpu.VMEM)
    return pl.pallas_call(
        functools.partial(projection_kernel, count, out_count),
        out_shape=[jax.ShapeDtypeStruct((rows // out_count, columns), jnp.bfloat16)] * out_count,
        in_specs=[pl.BlockSpec(memory_space=pltpu.SMEM)] + [whole] * (count + 1),
        out_specs=[whole] * out_count,
        scratch_shapes=[
            pltpu.VMEM((rows, depth), jnp.bfloat16),
            pltpu.VMEM((rows, columns), jnp.bfloat16),
        ],
        cost_estimate=pl.CostEstimate(flops=2 * rows * depth * columns, bytes_accessed=4 * MIB, transcendentals=0),
        compiler_params=pltpu.CompilerParams(vmem_limit_bytes=8 * MIB),
        name="projection",
    )(places, *blocks, in_vmem(weight))


def gate_kernel(row_blocks, cores, first, count, model_width, places, *refs):
    blocks, gains = refs[: row_blocks * count], refs[row_blocks * count : (row_blocks + 1) * count]
    refs = refs[(row_blocks + 1) * count :]
    gate, up, refs = refs[0], refs[1], refs[2:]
    if first:
        before, (active, x) = refs[:3], refs[-2:]
        gate_sum, up_sum, squares = before
    else:
        gate_sum, up_sum, squares, x = refs[-4:]
    height, width = blocks[0].shape
    hidden = gate.shape[2]
    tile = min(256, hidden)
    sums = [[None] * (hidden // tile), [None] * (hidden // tile)]
    totals = [squares[s * height : (s + 1) * height, :] if first else 0.0 for s in range(row_blocks)]
    for k in range(count):
        for s in range(row_blocks):
            wide = blocks[s * count + k][...].astype(jnp.float32)
            totals[s] += jnp.sum(wide * wide, axis=-1, keepdims=True)
            x[s * height : (s + 1) * height, k * width : (k + 1) * width] = (wide * gains[k][...]).astype(jnp.bfloat16)
    for w, (weight, start) in enumerate(((gate, gate_sum), (up, up_sum))):
        for j in range(hidden // tile):
            cut = slice(j * tile, (j + 1) * tile)
            total = start[:, cut] if first else None
            for k in range(count):
                depth = pl.ds(pl.multiple_of(places[first + k] * width, 128), width)
                product = jnp.dot(
                    x[:, k * width : (k + 1) * width], weight[0, depth, cut], preferred_element_type=jnp.float32
                )
                total = product if total is None else total + product
            sums[w][j] = total
            if not first:
                start[:, cut] = total
    if not first:
        for s in range(row_blocks):
            squares[s * height : (s + 1) * height, :] = totals[s]
        return
    scale = jnp.concatenate([lax.rsqrt(t / model_width + norm_epsilon) for t in totals], axis=0)
    for j in range(hidden // tile):
        gate_part = sums[0][j] * scale
        up_part = sums[1][j] * scale
        active[:, j * tile : (j + 1) * tile] = (gate_part / (1.0 + jnp.exp(-gate_part)) * up_part).astype(jnp.bfloat16)


def activate(places, blocks, gains, gate_weight, up_weight, cores, first, before, after):
    row_blocks, count = len(blocks), len(blocks[0])
    height, width = blocks[0][0].shape
    rows = row_blocks * height
    model_width, hidden = gate_weight.shape[1:]
    whole = pl.BlockSpec(memory_space=pltpu.VMEM)
    if first:
        kinds = jax.ShapeDtypeStruct((rows, hidden), jnp.bfloat16)
    else:
        kinds = [jax.ShapeDtypeStruct((rows, n), jnp.float32) for n in (hidden, hidden, 1)]
    return pl.pallas_call(
        functools.partial(gate_kernel, row_blocks, cores, first, count, model_width),
        out_shape=kinds,
        in_specs=[pl.BlockSpec(memory_space=pltpu.SMEM)] + [whole] * ((row_blocks + 1) * count + 2 + len(before))
        + [pl.BlockSpec(memory_space=pl.ANY)] * len(after),
        out_specs=whole if first else [whole] * 3,
        scratch_shapes=[pltpu.VMEM((rows, count * width), jnp.bfloat16)],
        cost_estimate=pl.CostEstimate(
            flops=4 * rows * hidden * count * width, bytes_accessed=4 * hidden * count * width, transcendentals=0
        ),
        compiler_params=pltpu.CompilerParams(vmem_limit_bytes=2 * rows * (count * width + 8 * hidden) + 12 * MIB),
        name="activate",
    )(places, *[b for row in blocks for b in row], *gains, in_vmem(gate_weight), in_vmem(up_weight), *before, *after)


def down_kernel(slots, at, column_blocks, cores, places, active, row_weight, down, *refs):
    row_blocks = len(slots)
    outs = refs[-row_blocks * cores :]
    width = down.shape[2] // column_blocks
    height = outs[0].shape[0] * cores // column_blocks
    mine = slice(at * row_blocks * height, (at + 1) * row_blocks * height)
    order = [b * cores + c for c in reversed(range(cores)) for b in range(column_blocks // cores)]
    tile = 256 if width % 256 == 0 else 128
    weights = []
    for s in range(row_blocks):
        first = pl.multiple_of(places[column_blocks + slots[s]] * height, height)
        weights.append(row_weight[pl.ds(first, height), :])
    for k in order:
        b, c = k // cores, k % cores
        start = pl.multiple_of(places[k] * width, 128)
        for j in range(width // tile):
            cut = slice(j * tile, (j + 1) * tile)
            product = jnp.dot(
                active[mine, :], down[0, :, pl.ds(start + j * tile, tile)], preferred_element_type=jnp.float32
            )
            for s in range(row_blocks):
                part = product[s * height : (s + 1) * height, :] * weights[s]
                outs[s * cores + c][b * height : (b + 1) * height, cut] = part.astype(jnp.bfloat16)


def project_down(places, active, row_weight, down_weight, slots, at, height, column_blocks, cores, after):
    row_blocks = len(slots)
    rows = row_blocks * height
    width = down_weight.shape[2] // column_blocks
    whole = pl.BlockSpec(memory_space=pltpu.VMEM)
    out = jax.ShapeDtypeStruct((height * (column_blocks // cores), width), jnp.bfloat16)
    outs = pl.pallas_call(
        functools.partial(down_kernel, slots, at, column_blocks, cores),
        out_shape=[out] * (row_blocks * cores),
        in_specs=[pl.BlockSpec(memory_space=pltpu.SMEM)]
        + [whole] * 3
        + [pl.BlockSpec(memory_space=pl.ANY)] * len(after),
        out_specs=[whole] * (row_blocks * cores),
        cost_estimate=pl.CostEstimate(
            flops=2 * rows * down_weight.size, bytes_accessed=2 * down_weight.size, transcendentals=0
        ),
        compiler_params=pltpu.CompilerParams(vmem_limit_bytes=4 * MIB),
        name="down",
    )(places, active, row_weight, in_vmem(down_weight), *after)
    return [outs[s * cores : (s + 1) * cores] for s in range(row_blocks)]


def add_kernel(groups, *refs):
    used = sum(len(g) for g in groups)
    outs = refs[-len(groups) :]
    at = 0
    for group, out in zip(groups, outs):
        total = None
        for first in group:
            value = refs[at][first : first + out.shape[0], :].astype(jnp.float32)
            total = value if total is None else total + value
            at += 1
        out[...] = total.astype(out.dtype)


def add(groups, height, after=(), kind=jnp.bfloat16):
    values = [value for group in groups for value, _ in group]
    width = values[0].shape[1]
    whole = pl.BlockSpec(memory_space=pltpu.VMEM)
    return pl.pallas_call(
        functools.partial(add_kernel, [[first for _, first in group] for group in groups]),
        out_shape=[jax.ShapeDtypeStruct((height, width), kind)] * len(groups),
        in_specs=[whole] * len(values) + [pl.BlockSpec(memory_space=pl.ANY)] * len(after),
        out_specs=[whole] * len(groups),
        compiler_params=pltpu.CompilerParams(vmem_limit_bytes=8 * MIB),
        name="add",
    )(*values, *after)


def shards(
    query_latent,
    query_rope,
    cache_latent,
    cache_rope,
    cache_length,
    value_up,
    output_weight,
    residual,
    norm_gain,
    routed_experts,
    expert_gates,
    gate_weight,
    up_weight,
    down_weight,
):
    ep_count = lax.axis_size("ep")
    tp_count = lax.axis_size("tp")
    ep_index = lax.axis_index("ep")
    tp_index = lax.axis_index("tp")
    row_total = routed_experts.shape[0]
    block_rows = row_total // tp_count
    cores = 2
    chips = ep_count // cores

    def from_core(value):
        return lax.ppermute(value, "ep", [(i, i ^ 1) for i in range(ep_count)])

    def from_chip(value, back):
        step = cores * back
        return lax.ppermute(value, "ep", [(i, (i + step) % ep_count) for i in range(ep_count)])

    def from_tp(value, bits):
        return lax.ppermute(value, "tp", [(i, i ^ bits) for i in range(tp_count)])

    def gather_ep(value, after=()):
        same = [value] + [from_chip(value, b) for b in range(1, chips)]
        if after:
            same[1:] = [add([[(v, 0)]], v.shape[0], after)[0] for v in same[1:]]
        other = [from_core(v) for v in same]
        return [v for pair in zip(same, other) for v in pair]

    chip, core = ep_index // cores, ep_index % cores
    ep_places = [
        (chip - b + chips) % chips * cores + (core if c == 0 else 1 - core)
        for b in range(chips)
        for c in range(cores)
    ]
    tp_places = [tp_index ^ k for k in range(tp_count)]
    places = jnp.stack(ep_places + tp_places).astype(jnp.int32)

    gain = norm_gain.reshape(1, -1)
    gains = gather_ep(gain)
    own_residual = lax.dynamic_slice_in_dim(residual, tp_index * block_rows, block_rows, 0)
    row_weight = jnp.sum(jnp.where(routed_experts == ep_index, expert_gates, 0.0), axis=-1, keepdims=True)

    head_out = attend(query_latent, query_rope, cache_latent, cache_rope, cache_length, value_up, [places])
    output_weight = fetch(output_weight, [head_out, row_weight, own_residual, gain])
    partial = project(places, gather_ep(head_out, [output_weight]), output_weight, tp_count)

    gate_weight = fetch(gate_weight, [partial[0]])
    terms = [[(value, 0)] for value in partial]
    for k in reversed(range(1, tp_count)):
        total = terms[k][0][0]
        if len(terms[k]) > 1 or k == 1:
            (total,) = add([terms[k]], block_rows, [gate_weight] if k == 1 else [])
        low = k & -k
        arrived = from_tp(total, low)
        terms[k ^ low].append((arrived, 0))
    up_weight = fetch(up_weight, [total])
    stream_terms = terms[0] + [(own_residual, 0)]
    stream, stream_out = add([stream_terms, stream_terms], block_rows, gains + [gate_weight, up_weight])
    down_weight = fetch(down_weight, [stream])

    rows_of = {0: stream}
    crossed = [from_chip(stream, b) for b in range(1, chips)]
    for k in range(1, tp_count):
        low = k & -k
        source = rows_of[k ^ low]
        if k == tp_count - 1:
            (source,) = add([[(source, 0)]], block_rows, crossed)
        rows_of[k] = from_tp(source, low)
    slots = list(reversed(range(tp_count)))
    near = {k: [rows_of[k], from_core(rows_of[k])] for k in slots}
    sums = activate(places, [near[k] for k in slots], gains[:cores], gate_weight, up_weight, cores, 0, [], [down_weight])
    far = {}
    for k in [0] + slots[:-1]:
        far[k] = []
        for b in range(1, chips):
            if k == 0:
                value = crossed[b - 1]
            elif k == 1:
                (source,) = add([[(crossed[b - 1], 0)]], block_rows, [rows_of[tp_count - 1]])
                value = from_tp(source, 1)
            else:
                value = from_chip(rows_of[k], b)
            (later,) = add([[(value, 0)]], block_rows, sums[-1:]) if k == tp_count - 1 else (value,)
            far[k] += [value, from_core(later)]
    active = activate(places, [far[k] for k in slots], gains[cores:], gate_weight, up_weight, cores, cores, sums, [])

    def send_back(k, after):
        total = list(add([terms[k]], block_rows, after))
        low = k & -k
        terms[k ^ low].append((from_tp(total[0], low), 0))
        return total

    terms = [[] for _ in range(tp_count)]
    arrivals, sent = [], []
    outs = project_down(places, active, row_weight, down_weight, slots, 0, block_rows, ep_count, cores, [])
    swapped = [from_core(out[1]) for out in outs]
    def core_sums(k, after):
        at = slots.index(k)
        rows = [[(outs[at][0], c * block_rows), (swapped[at], c * block_rows)] for c in range(chips)]
        return rows, after

    def cross(k, extra, after):
        rows, after = core_sums(k, after)
        added = add([row + more for row, more in zip(rows, extra)], block_rows, after)
        across = [from_chip(added[c], chips - c) for c in range(1, chips)]
        arrivals.append(across)
        terms[k] += [(value, 0) for value in [added[0]] + across]

    none = [[] for _ in range(chips)]
    for k in slots[:-2]:
        cross(k, none, arrivals[-2] if len(arrivals) > 1 else [])
    rows, _ = core_sums(1, [])
    added = add(rows, block_rows)
    joined = [[]] + [[(from_tp(added[c], 1), 0)] for c in range(1, chips)]
    early = [value for more in joined for value, _ in more]
    sent = send_back(slots[0], early)
    cross(0, joined, sent)
    for k in slots[1:-2]:
        send_back(k, [])
    terms[1].insert(0, (added[0], 0))
    (kept,) = add([terms[1]], block_rows) if len(terms[1]) > 1 else (added[0],)
    (most,) = add([terms[0]], block_rows, (), jnp.float32)
    (mixed,) = add([[(most, 0), (from_tp(kept, 1), 0)]], block_rows)
    return (stream_out, mixed)


def solution(mesh):
    return jax.shard_map(
        shards,
        mesh=mesh,
        in_specs=(
            P(("parts", "ep"), "tp", None),
            P(("parts", "ep"), "tp"),
            P(("parts", "ep"), None, None),
            P(("parts", "ep"), None, None),
            P(("parts", "ep")),
            P("tp", None, None),
            P("tp", "ep"),
            P("parts", "ep"),
            P("ep"),
            P("parts", None),
            P("parts", None),
            P("ep", None, "tp"),
            P("ep", None, "tp"),
            P("ep", "tp", None),
        ),
        out_specs=(P(("parts", "tp"), "ep"), P(("parts", "tp"), "ep")),
        check_vma=False,
    )
```

```python
import functools

import jax
import jax.numpy as jnp
from jax import lax
from jax.experimental import pallas as pl
from jax.experimental.pallas import tpu as pltpu
from jax.sharding import PartitionSpec as P

score_scale = 1.0 / 192.0**0.5
norm_epsilon = 1e-06
MIB = 1 << 20


def in_hbm(value):
    return pltpu.with_memory_space_constraint(value, pltpu.HBM)


def in_vmem(value):
    return pltpu.with_memory_space_constraint(value, pltpu.VMEM)


def fetch_kernel(parts, *refs):
    source, target, sems = refs[0], refs[-2], refs[-1]
    step = source.shape[-2] // parts
    copies = []
    for i in range(parts):
        cut = (slice(None),) * (len(source.shape) - 2) + (pl.ds(i * step, step),)
        copies.append(pltpu.make_async_copy(source.at[cut], target.at[cut], sems.at[i]))
    for copy in copies:
        copy.start()
    for copy in copies:
        copy.wait()


def fetch(value, after):
    parts = 4
    return pl.pallas_call(
        functools.partial(fetch_kernel, parts),
        out_shape=pltpu.VMEM(value.shape, value.dtype),
        in_specs=[pl.BlockSpec(memory_space=pl.ANY)] * (1 + len(after)),
        out_specs=pl.BlockSpec(memory_space=pltpu.VMEM),
        scratch_shapes=[pltpu.SemaphoreType.DMA((parts,))],
        cost_estimate=pl.CostEstimate(flops=0, bytes_accessed=4 * value.size, transcendentals=0),
        compiler_params=pltpu.CompilerParams(vmem_limit_bytes=1 * MIB),
        name="fetch",
    )(in_hbm(value), *after)


def attention_kernel(step_rows, pieces, ahead, lengths, q_ref, qr_ref, k_hbm, kr_hbm, up_hbm, *refs):
    out_ref, latent, rope, k_ref, kr_ref, up_ref, sems, up_sem = refs[-8:]
    step = pl.program_id(0)
    steps = k_ref.shape[0] // step_rows
    heads, positions = q_ref.shape[1], k_ref.shape[1]
    rope_width = kr_ref.shape[1]

    def copies(at):
        whole = pl.ds(at * step_rows, step_rows)
        made = [pltpu.make_async_copy(kr_hbm.at[whole], kr_ref.at[whole], sems.at[at, pieces])]
        for i in range(pieces):
            part = pl.ds(at * step_rows + i * (step_rows // pieces), step_rows // pieces)
            made.append(pltpu.make_async_copy(k_hbm.at[part], k_ref.at[part], sems.at[at, i]))
        return made

    @pl.when(step == 0)
    def _():
        for at in range(min(ahead, steps)):
            for copy in copies(at):
                copy.start()
        pltpu.make_async_copy(up_hbm, up_ref, up_sem).start()
        all_rows = qr_ref.shape[0]
        width = heads * rope_width
        lane = lax.broadcasted_iota(jnp.int32, (heads, width), 1)
        head = lax.broadcasted_iota(jnp.int32, (heads, width), 0)
        own = jnp.where(lane // rope_width == head, 1.0, 0.0)
        spread = qr_ref[...].astype(jnp.float32)[:, None, :] * own[None, :, :]
        spread = spread.reshape(all_rows * heads, width).astype(jnp.bfloat16)
        lane = lax.broadcasted_iota(jnp.int32, (width, rope_width), 0)
        column = lax.broadcasted_iota(jnp.int32, (width, rope_width), 1)
        fold = jnp.where(lane % rope_width == column, 1.0, 0.0).astype(jnp.bfloat16)
        rope[...] = jnp.dot(spread, fold, preferred_element_type=jnp.float32)

    @pl.when(step + ahead < steps)
    def _():
        for copy in copies(step + ahead):
            copy.start()

    for copy in copies(step):
        copy.wait()
    place = lax.broadcasted_iota(jnp.int32, (heads, positions), 1)
    lanes = latent.shape[2]
    lanes = latent.shape[2]
    scores = []
    for r in range(step_rows):
        first = pl.multiple_of((step * step_rows + r) * heads, heads)
        score = lax.dot_general(
            q_ref[r], k_ref[step * step_rows + r], (((1,), (1,)), ((), ())), preferred_element_type=jnp.float32
        )
        score += jnp.dot(
            rope[pl.ds(first, heads), :].astype(jnp.bfloat16), kr_ref[step * step_rows + r], preferred_element_type=jnp.float32
        )
        scores.append(score)
    probabilities = []
    for r in range(step_rows):
        visible = place < lengths[step * step_rows + r]
        score = jnp.where(visible, scores[r] * score_scale, -jnp.inf)
        weight = jnp.exp(score - jnp.max(score, axis=-1, keepdims=True))
        total = jnp.sum(weight, axis=-1, keepdims=True)
        probabilities.append((weight / total).astype(jnp.bfloat16))
    for r in range(step_rows):
        first = pl.multiple_of((step * step_rows + r) * heads, heads)
        mixed = jnp.dot(probabilities[r], k_ref[step * step_rows + r], preferred_element_type=jnp.float32)
        for c in range(latent.shape[0]):
            latent[c, pl.ds(first, heads), :] = mixed[:, c * lanes : (c + 1) * lanes]

    @pl.when(step == pl.num_programs(0) - 1)
    def _():
        pltpu.make_async_copy(up_hbm, up_ref, up_sem).wait()
        rows = out_ref.shape[0]
        width = up_ref.shape[2]
        for h in range(heads):
            parts = [latent[c, pl.ds(h, rows, stride=heads), :] for c in range(latent.shape[0])]
            part = jnp.concatenate(parts, axis=1).astype(jnp.bfloat16)
            out_ref[:, h * width : (h + 1) * width] = jnp.dot(
                part, up_ref[h], preferred_element_type=jnp.float32
            ).astype(jnp.bfloat16)


def attend(query_latent, query_rope, cache_latent, cache_rope, cache_length, value_up, after):
    rows, heads, latent_width = query_latent.shape
    rope_width = cache_rope.shape[1]
    value_width = value_up.shape[2]
    step_rows, pieces, ahead = 8, 1, 3
    by_row = lambda i, lengths: (i, 0, 0)
    return pl.pallas_call(
        functools.partial(attention_kernel, step_rows, pieces, ahead),
        out_shape=jax.ShapeDtypeStruct((rows, heads * value_width), jnp.bfloat16),
        grid_spec=pltpu.PrefetchScalarGridSpec(
            num_scalar_prefetch=1,
            grid=(rows // step_rows,),
            in_specs=[
                pl.BlockSpec((step_rows, heads, latent_width), by_row),
                pl.BlockSpec(query_rope.shape, lambda i, lengths: (0, 0)),
                pl.BlockSpec(memory_space=pl.ANY),
                pl.BlockSpec(memory_space=pl.ANY),
                pl.BlockSpec(memory_space=pl.ANY),
            ]
            + [pl.BlockSpec(memory_space=pl.ANY)] * len(after),
            out_specs=pl.BlockSpec((rows, heads * value_width), lambda i, lengths: (0, 0)),
            scratch_shapes=[
                pltpu.VMEM((latent_width // 128, rows * heads, 128), jnp.float32),
                pltpu.VMEM((rows * heads, rope_width), jnp.float32),
                pltpu.VMEM(cache_latent.shape, jnp.bfloat16),
                pltpu.VMEM(cache_rope.shape, jnp.bfloat16),
                pltpu.VMEM(value_up.shape, jnp.bfloat16),
                pltpu.SemaphoreType.DMA((rows // step_rows, pieces + 1)),
                pltpu.SemaphoreType.DMA,
            ],
        ),
        cost_estimate=pl.CostEstimate(
            flops=64 * heads * cache_latent.size, bytes_accessed=2 * cache_latent.size, transcendentals=0
        ),
        compiler_params=pltpu.CompilerParams(vmem_limit_bytes=28 * MIB),
        name="attention",
    )(
        in_hbm(cache_length),
        in_hbm(query_latent),
        in_hbm(query_rope),
        in_hbm(cache_latent),
        in_hbm(cache_rope),
        in_hbm(value_up),
        *after,
    )


def projection_kernel(count, out_count, places, *refs):
    blocks, weight, outs = refs[:count], refs[count], refs[-2 - out_count : -2]
    gathered, result = refs[-2:]
    height = blocks[0].shape[0]
    for k in range(count):
        first = pl.multiple_of(places[k] * height, height)
        gathered[pl.ds(first, height), :] = blocks[k][...]
    columns = weight.shape[1]
    tile = 256 if columns % 256 == 0 else 128
    for j in range(columns // tile):
        result[:, j * tile : (j + 1) * tile] = jnp.dot(
            gathered[...], weight[:, j * tile : (j + 1) * tile], preferred_element_type=jnp.float32
        ).astype(jnp.bfloat16)
    out_height = outs[0].shape[0]
    for s in range(len(outs)):
        first = pl.multiple_of(places[count + s] * out_height, out_height)
        outs[s][...] = result[pl.ds(first, out_height), :]


def project(places, blocks, weight, out_count):
    count = len(blocks)
    height, depth = blocks[0].shape
    rows, columns = height * count, weight.shape[1]
    whole = pl.BlockSpec(memory_space=pltpu.VMEM)
    return pl.pallas_call(
        functools.partial(projection_kernel, count, out_count),
        out_shape=[jax.ShapeDtypeStruct((rows // out_count, columns), jnp.bfloat16)] * out_count,
        in_specs=[pl.BlockSpec(memory_space=pltpu.SMEM)] + [whole] * (count + 1),
        out_specs=[whole] * out_count,
        scratch_shapes=[
            pltpu.VMEM((rows, depth), jnp.bfloat16),
            pltpu.VMEM((rows, columns), jnp.bfloat16),
        ],
        cost_estimate=pl.CostEstimate(flops=2 * rows * depth * columns, bytes_accessed=4 * MIB, transcendentals=0),
        compiler_params=pltpu.CompilerParams(vmem_limit_bytes=8 * MIB),
        name="projection",
    )(places, *blocks, in_vmem(weight))


def gate_kernel(row_blocks, cores, first, count, model_width, places, *refs):
    blocks, gains = refs[: row_blocks * count], refs[row_blocks * count : (row_blocks + 1) * count]
    refs = refs[(row_blocks + 1) * count :]
    gate, up, refs = refs[0], refs[1], refs[2:]
    if first:
        before, (active, x) = refs[:3], refs[-2:]
        gate_sum, up_sum, squares = before
    else:
        gate_sum, up_sum, squares, x = refs[-4:]
    height, width = blocks[0].shape
    hidden = gate.shape[2]
    tile = min(256, hidden)
    sums = [[None] * (hidden // tile), [None] * (hidden // tile)]
    totals = [squares[s * height : (s + 1) * height, :] if first else 0.0 for s in range(row_blocks)]
    for k in range(count):
        for s in range(row_blocks):
            wide = blocks[s * count + k][...].astype(jnp.float32)
            totals[s] += jnp.sum(wide * wide, axis=-1, keepdims=True)
            x[s * height : (s + 1) * height, k * width : (k + 1) * width] = (wide * gains[k][...]).astype(jnp.bfloat16)
    for w, (weight, start) in enumerate(((gate, gate_sum), (up, up_sum))):
        for j in range(hidden // tile):
            cut = slice(j * tile, (j + 1) * tile)
            total = start[:, cut] if first else None
            for k in range(count):
                depth = pl.ds(pl.multiple_of(places[first + k] * width, 128), width)
                product = jnp.dot(
                    x[:, k * width : (k + 1) * width], weight[0, depth, cut], preferred_element_type=jnp.float32
                )
                total = product if total is None else total + product
            sums[w][j] = total
            if not first:
                start[:, cut] = total
    if not first:
        for s in range(row_blocks):
            squares[s * height : (s + 1) * height, :] = totals[s]
        return
    scale = jnp.concatenate([lax.rsqrt(t / model_width + norm_epsilon) for t in totals], axis=0)
    for j in range(hidden // tile):
        gate_part = sums[0][j] * scale
        up_part = sums[1][j] * scale
        active[:, j * tile : (j + 1) * tile] = (gate_part / (1.0 + jnp.exp(-gate_part)) * up_part).astype(jnp.bfloat16)


def activate(places, blocks, gains, gate_weight, up_weight, cores, first, before, after):
    row_blocks, count = len(blocks), len(blocks[0])
    height, width = blocks[0][0].shape
    rows = row_blocks * height
    model_width, hidden = gate_weight.shape[1:]
    whole = pl.BlockSpec(memory_space=pltpu.VMEM)
    if first:
        kinds = jax.ShapeDtypeStruct((rows, hidden), jnp.bfloat16)
    else:
        kinds = [jax.ShapeDtypeStruct((rows, n), jnp.float32) for n in (hidden, hidden, 1)]
    return pl.pallas_call(
        functools.partial(gate_kernel, row_blocks, cores, first, count, model_width),
        out_shape=kinds,
        in_specs=[pl.BlockSpec(memory_space=pltpu.SMEM)] + [whole] * ((row_blocks + 1) * count + 2 + len(before))
        + [pl.BlockSpec(memory_space=pl.ANY)] * len(after),
        out_specs=whole if first else [whole] * 3,
        scratch_shapes=[pltpu.VMEM((rows, count * width), jnp.bfloat16)],
        cost_estimate=pl.CostEstimate(
            flops=4 * rows * hidden * count * width, bytes_accessed=4 * hidden * count * width, transcendentals=0
        ),
        compiler_params=pltpu.CompilerParams(vmem_limit_bytes=2 * rows * (count * width + 8 * hidden) + 12 * MIB),
        name="activate",
    )(places, *[b for row in blocks for b in row], *gains, in_vmem(gate_weight), in_vmem(up_weight), *before, *after)


def down_kernel(slots, at, column_blocks, cores, places, active, row_weight, down, *refs):
    row_blocks = len(slots)
    outs = refs[-row_blocks * cores :]
    width = down.shape[2] // column_blocks
    height = outs[0].shape[0] * cores // column_blocks
    mine = slice(at * row_blocks * height, (at + 1) * row_blocks * height)
    order = [b * cores + c for c in reversed(range(cores)) for b in range(column_blocks // cores)]
    tile = 256 if width % 256 == 0 else 128
    weights = []
    for s in range(row_blocks):
        first = pl.multiple_of(places[column_blocks + slots[s]] * height, height)
        weights.append(row_weight[pl.ds(first, height), :])
    for k in order:
        b, c = k // cores, k % cores
        start = pl.multiple_of(places[k] * width, 128)
        for j in range(width // tile):
            cut = slice(j * tile, (j + 1) * tile)
            product = jnp.dot(
                active[mine, :], down[0, :, pl.ds(start + j * tile, tile)], preferred_element_type=jnp.float32
            )
            for s in range(row_blocks):
                part = product[s * height : (s + 1) * height, :] * weights[s]
                outs[s * cores + c][b * height : (b + 1) * height, cut] = part.astype(jnp.bfloat16)


def project_down(places, active, row_weight, down_weight, slots, at, height, column_blocks, cores, after):
    row_blocks = len(slots)
    rows = row_blocks * height
    width = down_weight.shape[2] // column_blocks
    whole = pl.BlockSpec(memory_space=pltpu.VMEM)
    out = jax.ShapeDtypeStruct((height * (column_blocks // cores), width), jnp.bfloat16)
    outs = pl.pallas_call(
        functools.partial(down_kernel, slots, at, column_blocks, cores),
        out_shape=[out] * (row_blocks * cores),
        in_specs=[pl.BlockSpec(memory_space=pltpu.SMEM)]
        + [whole] * 3
        + [pl.BlockSpec(memory_space=pl.ANY)] * len(after),
        out_specs=[whole] * (row_blocks * cores),
        cost_estimate=pl.CostEstimate(
            flops=2 * rows * down_weight.size, bytes_accessed=2 * down_weight.size, transcendentals=0
        ),
        compiler_params=pltpu.CompilerParams(vmem_limit_bytes=4 * MIB),
        name="down",
    )(places, active, row_weight, in_vmem(down_weight), *after)
    return [outs[s * cores : (s + 1) * cores] for s in range(row_blocks)]


def add_kernel(groups, *refs):
    used = sum(len(g) for g in groups)
    outs = refs[-len(groups) :]
    at = 0
    for group, out in zip(groups, outs):
        total = None
        for first in group:
            value = refs[at][first : first + out.shape[0], :].astype(jnp.float32)
            total = value if total is None else total + value
            at += 1
        out[...] = total.astype(out.dtype)


def add(groups, height, after=(), kind=jnp.bfloat16):
    values = [value for group in groups for value, _ in group]
    width = values[0].shape[1]
    whole = pl.BlockSpec(memory_space=pltpu.VMEM)
    return pl.pallas_call(
        functools.partial(add_kernel, [[first for _, first in group] for group in groups]),
        out_shape=[jax.ShapeDtypeStruct((height, width), kind)] * len(groups),
        in_specs=[whole] * len(values) + [pl.BlockSpec(memory_space=pl.ANY)] * len(after),
        out_specs=[whole] * len(groups),
        compiler_params=pltpu.CompilerParams(vmem_limit_bytes=8 * MIB),
        name="add",
    )(*values, *after)


def shards(
    query_latent,
    query_rope,
    cache_latent,
    cache_rope,
    cache_length,
    value_up,
    output_weight,
    residual,
    norm_gain,
    routed_experts,
    expert_gates,
    gate_weight,
    up_weight,
    down_weight,
):
    ep_count = lax.axis_size("ep")
    tp_count = lax.axis_size("tp")
    ep_index = lax.axis_index("ep")
    tp_index = lax.axis_index("tp")
    row_total = routed_experts.shape[0]
    block_rows = row_total // tp_count
    cores = 2
    chips = ep_count // cores

    def from_core(value):
        return lax.ppermute(value, "ep", [(i, i ^ 1) for i in range(ep_count)])

    def from_chip(value, back):
        step = cores * back
        return lax.ppermute(value, "ep", [(i, (i + step) % ep_count) for i in range(ep_count)])

    def from_tp(value, bits):
        return lax.ppermute(value, "tp", [(i, i ^ bits) for i in range(tp_count)])

    def gather_ep(value, after=()):
        same = [value] + [from_chip(value, b) for b in range(1, chips)]
        if after:
            same[1:] = [add([[(v, 0)]], v.shape[0], after)[0] for v in same[1:]]
        other = [from_core(v) for v in same]
        return [v for pair in zip(same, other) for v in pair]

    chip, core = ep_index // cores, ep_index % cores
    ep_places = [
        (chip - b + chips) % chips * cores + (core if c == 0 else 1 - core)
        for b in range(chips)
        for c in range(cores)
    ]
    tp_places = [tp_index ^ k for k in range(tp_count)]
    places = jnp.stack(ep_places + tp_places).astype(jnp.int32)

    gain = norm_gain.reshape(1, -1)
    gains = gather_ep(gain)
    own_residual = lax.dynamic_slice_in_dim(residual, tp_index * block_rows, block_rows, 0)
    row_weight = jnp.sum(jnp.where(routed_experts == ep_index, expert_gates, 0.0), axis=-1, keepdims=True)

    head_out = attend(query_latent, query_rope, cache_latent, cache_rope, cache_length, value_up, [places])
    output_weight = fetch(output_weight, [head_out, row_weight, own_residual, gain])
    partial = project(places, gather_ep(head_out, [output_weight]), output_weight, tp_count)

    gate_weight = fetch(gate_weight, [partial[0]])
    terms = [[(value, 0)] for value in partial]
    for k in reversed(range(1, tp_count)):
        total = terms[k][0][0]
        if len(terms[k]) > 1 or k == 1:
            (total,) = add([terms[k]], block_rows, [gate_weight] if k == 1 else [])
        low = k & -k
        arrived = from_tp(total, low)
        terms[k ^ low].append((arrived, 0))
    stream_terms = terms[0] + [(own_residual, 0)]
    stream, stream_out = add([stream_terms, stream_terms], block_rows, gains + [gate_weight])
    up_weight = fetch(up_weight, [stream])
    down_weight = fetch(down_weight, [stream])

    rows_of = {0: stream}
    crossed = [from_chip(stream, b) for b in range(1, chips)]
    for k in range(1, tp_count):
        low = k & -k
        source = rows_of[k ^ low]
        if k == tp_count - 1:
            (source,) = add([[(source, 0)]], block_rows, crossed + [up_weight])
        rows_of[k] = from_tp(source, low)
    slots = list(reversed(range(tp_count)))
    near = {k: [rows_of[k], from_core(rows_of[k])] for k in slots}
    sums = activate(places, [near[k] for k in slots], gains[:cores], gate_weight, up_weight, cores, 0, [], [down_weight])
    far = {}
    for k in [0] + slots[:-1]:
        far[k] = []
        for b in range(1, chips):
            if k == 0:
                value = crossed[b - 1]
            elif k == 1:
                (source,) = add([[(crossed[b - 1], 0)]], block_rows, [rows_of[tp_count - 1]])
                value = from_tp(source, 1)
            else:
                value = from_chip(rows_of[k], b)
            (later,) = add([[(value, 0)]], block_rows, sums[-1:]) if k == tp_count - 1 else (value,)
            far[k] += [value, from_core(later)]
    active = activate(places, [far[k] for k in slots], gains[cores:], gate_weight, up_weight, cores, cores, sums, [])

    def send_back(k, after):
        total = list(add([terms[k]], block_rows, after))
        low = k & -k
        terms[k ^ low].append((from_tp(total[0], low), 0))
        return total

    terms = [[] for _ in range(tp_count)]
    arrivals, sent = [], []
    outs = project_down(places, active, row_weight, down_weight, slots, 0, block_rows, ep_count, cores, [])
    swapped = [from_core(out[1]) for out in outs]
    def core_sums(k, after):
        at = slots.index(k)
        rows = [[(outs[at][0], c * block_rows), (swapped[at], c * block_rows)] for c in range(chips)]
        return rows, after

    def cross(k, extra, after):
        rows, after = core_sums(k, after)
        added = add([row + more for row, more in zip(rows, extra)], block_rows, after)
        across = [from_chip(added[c], chips - c) for c in range(1, chips)]
        arrivals.append(across)
        terms[k] += [(value, 0) for value in [added[0]] + across]

    none = [[] for _ in range(chips)]
    for k in slots[:-2]:
        cross(k, none, arrivals[-2] if len(arrivals) > 1 else [])
    rows, _ = core_sums(1, [])
    added = add(rows, block_rows)
    joined = [[]] + [[(from_tp(added[c], 1), 0)] for c in range(1, chips)]
    early = [value for more in joined for value, _ in more]
    sent = send_back(slots[0], early)
    cross(0, joined, sent)
    for k in slots[1:-2]:
        send_back(k, [])
    terms[1].insert(0, (added[0], 0))
    (kept,) = add([terms[1]], block_rows) if len(terms[1]) > 1 else (added[0],)
    (most,) = add([terms[0]], block_rows, (), jnp.float32)
    (mixed,) = add([[(most, 0), (from_tp(kept, 1), 0)]], block_rows)
    return (stream_out, mixed)


def solution(mesh):
    return jax.shard_map(
        shards,
        mesh=mesh,
        in_specs=(
            P(("parts", "ep"), "tp", None),
            P(("parts", "ep"), "tp"),
            P(("parts", "ep"), None, None),
            P(("parts", "ep"), None, None),
            P(("parts", "ep")),
            P("tp", None, None),
            P("tp", "ep"),
            P("parts", "ep"),
            P("ep"),
            P("parts", None),
            P("parts", None),
            P("ep", None, "tp"),
            P("ep", None, "tp"),
            P("ep", "tp", None),
        ),
        out_specs=(P(("parts", "tp"), "ep"), P(("parts", "tp"), "ep")),
        check_vma=False,
    )
```

```python
import functools

import jax
import jax.numpy as jnp
from jax import lax
from jax.experimental import pallas as pl
from jax.experimental.pallas import tpu as pltpu
from jax.sharding import PartitionSpec as P

score_scale = 1.0 / 192.0**0.5
norm_epsilon = 1e-06
MIB = 1 << 20


def in_hbm(value):
    return pltpu.with_memory_space_constraint(value, pltpu.HBM)


def in_vmem(value):
    return pltpu.with_memory_space_constraint(value, pltpu.VMEM)


def fetch_kernel(parts, *refs):
    source, target, sems = refs[0], refs[-2], refs[-1]
    step = source.shape[-2] // parts
    copies = []
    for i in range(parts):
        cut = (slice(None),) * (len(source.shape) - 2) + (pl.ds(i * step, step),)
        copies.append(pltpu.make_async_copy(source.at[cut], target.at[cut], sems.at[i]))
    for copy in copies:
        copy.start()
    for copy in copies:
        copy.wait()


def fetch(value, after):
    parts = 4
    return pl.pallas_call(
        functools.partial(fetch_kernel, parts),
        out_shape=pltpu.VMEM(value.shape, value.dtype),
        in_specs=[pl.BlockSpec(memory_space=pl.ANY)] * (1 + len(after)),
        out_specs=pl.BlockSpec(memory_space=pltpu.VMEM),
        scratch_shapes=[pltpu.SemaphoreType.DMA((parts,))],
        cost_estimate=pl.CostEstimate(flops=0, bytes_accessed=4 * value.size, transcendentals=0),
        compiler_params=pltpu.CompilerParams(vmem_limit_bytes=1 * MIB),
        name="fetch",
    )(in_hbm(value), *after)


def attention_kernel(step_rows, pieces, ahead, lengths, q_ref, qr_ref, k_hbm, kr_hbm, up_hbm, *refs):
    out_ref, latent, rope, k_ref, kr_ref, up_ref, sems, up_sem = refs[-8:]
    step = pl.program_id(0)
    steps = k_ref.shape[0] // step_rows
    heads, positions = q_ref.shape[1], k_ref.shape[1]
    rope_width = kr_ref.shape[1]

    def copies(at):
        whole = pl.ds(at * step_rows, step_rows)
        made = [pltpu.make_async_copy(kr_hbm.at[whole], kr_ref.at[whole], sems.at[at, pieces])]
        for i in range(pieces):
            part = pl.ds(at * step_rows + i * (step_rows // pieces), step_rows // pieces)
            made.append(pltpu.make_async_copy(k_hbm.at[part], k_ref.at[part], sems.at[at, i]))
        return made

    @pl.when(step == 0)
    def _():
        for at in range(min(ahead, steps)):
            for copy in copies(at):
                copy.start()
        pltpu.make_async_copy(up_hbm, up_ref, up_sem).start()
        all_rows = qr_ref.shape[0]
        width = heads * rope_width
        lane = lax.broadcasted_iota(jnp.int32, (heads, width), 1)
        head = lax.broadcasted_iota(jnp.int32, (heads, width), 0)
        own = jnp.where(lane // rope_width == head, 1.0, 0.0)
        spread = qr_ref[...].astype(jnp.float32)[:, None, :] * own[None, :, :]
        spread = spread.reshape(all_rows * heads, width).astype(jnp.bfloat16)
        lane = lax.broadcasted_iota(jnp.int32, (width, rope_width), 0)
        column = lax.broadcasted_iota(jnp.int32, (width, rope_width), 1)
        fold = jnp.where(lane % rope_width == column, 1.0, 0.0).astype(jnp.bfloat16)
        rope[...] = jnp.dot(spread, fold, preferred_element_type=jnp.float32)

    @pl.when(step + ahead < steps)
    def _():
        for copy in copies(step + ahead):
            copy.start()

    for copy in copies(step):
        copy.wait()
    place = lax.broadcasted_iota(jnp.int32, (heads, positions), 1)
    lanes = latent.shape[2]
    lanes = latent.shape[2]
    scores = []
    for r in range(step_rows):
        first = pl.multiple_of((step * step_rows + r) * heads, heads)
        score = lax.dot_general(
            q_ref[r], k_ref[step * step_rows + r], (((1,), (1,)), ((), ())), preferred_element_type=jnp.float32
        )
        score += jnp.dot(
            rope[pl.ds(first, heads), :].astype(jnp.bfloat16), kr_ref[step * step_rows + r], preferred_element_type=jnp.float32
        )
        scores.append(score)
    probabilities = []
    for r in range(step_rows):
        visible = place < lengths[step * step_rows + r]
        score = jnp.where(visible, scores[r] * score_scale, -jnp.inf)
        weight = jnp.exp(score - jnp.max(score, axis=-1, keepdims=True))
        total = jnp.sum(weight, axis=-1, keepdims=True)
        probabilities.append((weight / total).astype(jnp.bfloat16))
    for r in range(step_rows):
        first = pl.multiple_of((step * step_rows + r) * heads, heads)
        mixed = jnp.dot(probabilities[r], k_ref[step * step_rows + r], preferred_element_type=jnp.float32)
        for c in range(latent.shape[0]):
            latent[c, pl.ds(first, heads), :] = mixed[:, c * lanes : (c + 1) * lanes]

    @pl.when(step == pl.num_programs(0) - 1)
    def _():
        pltpu.make_async_copy(up_hbm, up_ref, up_sem).wait()
        rows = out_ref.shape[0]
        width = up_ref.shape[2]
        for h in range(heads):
            parts = [latent[c, pl.ds(h, rows, stride=heads), :] for c in range(latent.shape[0])]
            part = jnp.concatenate(parts, axis=1).astype(jnp.bfloat16)
            out_ref[:, h * width : (h + 1) * width] = jnp.dot(
                part, up_ref[h], preferred_element_type=jnp.float32
            ).astype(jnp.bfloat16)


def attend(query_latent, query_rope, cache_latent, cache_rope, cache_length, value_up, after):
    rows, heads, latent_width = query_latent.shape
    rope_width = cache_rope.shape[1]
    value_width = value_up.shape[2]
    step_rows, pieces, ahead = 8, 1, 3
    by_row = lambda i, lengths: (i, 0, 0)
    return pl.pallas_call(
        functools.partial(attention_kernel, step_rows, pieces, ahead),
        out_shape=jax.ShapeDtypeStruct((rows, heads * value_width), jnp.bfloat16),
        grid_spec=pltpu.PrefetchScalarGridSpec(
            num_scalar_prefetch=1,
            grid=(rows // step_rows,),
            in_specs=[
                pl.BlockSpec((step_rows, heads, latent_width), by_row),
                pl.BlockSpec(query_rope.shape, lambda i, lengths: (0, 0)),
                pl.BlockSpec(memory_space=pl.ANY),
                pl.BlockSpec(memory_space=pl.ANY),
                pl.BlockSpec(memory_space=pl.ANY),
            ]
            + [pl.BlockSpec(memory_space=pl.ANY)] * len(after),
            out_specs=pl.BlockSpec((rows, heads * value_width), lambda i, lengths: (0, 0)),
            scratch_shapes=[
                pltpu.VMEM((latent_width // 128, rows * heads, 128), jnp.float32),
                pltpu.VMEM((rows * heads, rope_width), jnp.float32),
                pltpu.VMEM(cache_latent.shape, jnp.bfloat16),
                pltpu.VMEM(cache_rope.shape, jnp.bfloat16),
                pltpu.VMEM(value_up.shape, jnp.bfloat16),
                pltpu.SemaphoreType.DMA((rows // step_rows, pieces + 1)),
                pltpu.SemaphoreType.DMA,
            ],
        ),
        cost_estimate=pl.CostEstimate(
            flops=64 * heads * cache_latent.size, bytes_accessed=2 * cache_latent.size, transcendentals=0
        ),
        compiler_params=pltpu.CompilerParams(vmem_limit_bytes=28 * MIB),
        name="attention",
    )(
        in_hbm(cache_length),
        in_hbm(query_latent),
        in_hbm(query_rope),
        in_hbm(cache_latent),
        in_hbm(cache_rope),
        in_hbm(value_up),
        *after,
    )


def projection_kernel(count, out_count, places, *refs):
    blocks, weight, outs = refs[:count], refs[count], refs[-2 - out_count : -2]
    gathered, result = refs[-2:]
    height = blocks[0].shape[0]
    for k in range(count):
        first = pl.multiple_of(places[k] * height, height)
        gathered[pl.ds(first, height), :] = blocks[k][...]
    columns = weight.shape[1]
    tile = 256 if columns % 256 == 0 else 128
    for j in range(columns // tile):
        result[:, j * tile : (j + 1) * tile] = jnp.dot(
            gathered[...], weight[:, j * tile : (j + 1) * tile], preferred_element_type=jnp.float32
        ).astype(jnp.bfloat16)
    out_height = outs[0].shape[0]
    for s in range(len(outs)):
        first = pl.multiple_of(places[count + s] * out_height, out_height)
        outs[s][...] = result[pl.ds(first, out_height), :]


def project(places, blocks, weight, out_count):
    count = len(blocks)
    height, depth = blocks[0].shape
    rows, columns = height * count, weight.shape[1]
    whole = pl.BlockSpec(memory_space=pltpu.VMEM)
    return pl.pallas_call(
        functools.partial(projection_kernel, count, out_count),
        out_shape=[jax.ShapeDtypeStruct((rows // out_count, columns), jnp.bfloat16)] * out_count,
        in_specs=[pl.BlockSpec(memory_space=pltpu.SMEM)] + [whole] * (count + 1),
        out_specs=[whole] * out_count,
        scratch_shapes=[
            pltpu.VMEM((rows, depth), jnp.bfloat16),
            pltpu.VMEM((rows, columns), jnp.bfloat16),
        ],
        cost_estimate=pl.CostEstimate(flops=2 * rows * depth * columns, bytes_accessed=4 * MIB, transcendentals=0),
        compiler_params=pltpu.CompilerParams(vmem_limit_bytes=8 * MIB),
        name="projection",
    )(places, *blocks, in_vmem(weight))


def gate_kernel(row_blocks, first, count, model_width, places, *refs):
    blocks, gains = refs[: row_blocks * count], refs[row_blocks * count : (row_blocks + 1) * count]
    refs = refs[(row_blocks + 1) * count :]
    gate, up, refs = refs[0], refs[1], refs[2:]
    if first:
        before, (active, x) = refs[:3], refs[-2:]
        gate_sum, up_sum, squares = before
    else:
        source, (gate_sum, up_sum, squares, target, x, sems) = refs[0], refs[-6:]
        parts = sems.shape[0]
        step = source.shape[1] // parts
        copies = []
        for i in range(parts):
            cut = pl.ds(i * step, step)
            copies.append(pltpu.make_async_copy(source.at[:, cut], target.at[:, cut], sems.at[i]))
            copies[i].start()
    height, width = blocks[0].shape
    hidden = gate.shape[2]
    tile = min(256, hidden)
    sums = [[None] * (hidden // tile), [None] * (hidden // tile)]
    totals = [squares[s * height : (s + 1) * height, :] if first else 0.0 for s in range(row_blocks)]
    for k in range(count):
        for s in range(row_blocks):
            wide = blocks[s * count + k][...].astype(jnp.float32)
            totals[s] += jnp.sum(wide * wide, axis=-1, keepdims=True)
            x[s * height : (s + 1) * height, k * width : (k + 1) * width] = (wide * gains[k][...]).astype(jnp.bfloat16)
    for w, (weight, start) in enumerate(((gate, gate_sum), (up, up_sum))):
        for j in range(hidden // tile):
            cut = slice(j * tile, (j + 1) * tile)
            total = start[:, cut] if first else None
            for k in range(count):
                depth = pl.ds(pl.multiple_of(places[first + k] * width, 128), width)
                product = jnp.dot(
                    x[:, k * width : (k + 1) * width], weight[0, depth, cut], preferred_element_type=jnp.float32
                )
                total = product if total is None else total + product
            sums[w][j] = total
            if not first:
                start[:, cut] = total
    if not first:
        for s in range(row_blocks):
            squares[s * height : (s + 1) * height, :] = totals[s]
        for copy in copies:
            copy.wait()
        return
    scale = jnp.concatenate([lax.rsqrt(t / model_width + norm_epsilon) for t in totals], axis=0)
    for j in range(hidden // tile):
        gate_part = sums[0][j] * scale
        up_part = sums[1][j] * scale
        active[:, j * tile : (j + 1) * tile] = (gate_part / (1.0 + jnp.exp(-gate_part)) * up_part).astype(jnp.bfloat16)


def activate(places, blocks, gains, gate_weight, up_weight, first, before, following=None):
    row_blocks, count = len(blocks), len(blocks[0])
    height, width = blocks[0][0].shape
    rows = row_blocks * height
    model_width, hidden = gate_weight.shape[1:]
    whole = pl.BlockSpec(memory_space=pltpu.VMEM)
    rest = [] if first else [in_hbm(following)]
    if first:
        kinds = jax.ShapeDtypeStruct((rows, hidden), jnp.bfloat16)
    else:
        kinds = [jax.ShapeDtypeStruct((rows, n), jnp.float32) for n in (hidden, hidden, 1)]
        kinds.append(pltpu.VMEM(following.shape, following.dtype))
    return pl.pallas_call(
        functools.partial(gate_kernel, row_blocks, first, count, model_width),
        out_shape=kinds,
        in_specs=[pl.BlockSpec(memory_space=pltpu.SMEM)] + [whole] * ((row_blocks + 1) * count + 2 + len(before))
        + [pl.BlockSpec(memory_space=pl.ANY)] * (0 if first else 1),
        out_specs=whole if first else [whole] * 4,
        scratch_shapes=[pltpu.VMEM((rows, count * width), jnp.bfloat16)]
        + [pltpu.SemaphoreType.DMA((4,))] * (0 if first else 1),
        cost_estimate=pl.CostEstimate(
            flops=4 * rows * hidden * count * width, bytes_accessed=4 * hidden * count * width, transcendentals=0
        ),
        compiler_params=pltpu.CompilerParams(vmem_limit_bytes=2 * rows * (count * width + 8 * hidden) + 12 * MIB),
        name="activate",
    )(places, *[b for row in blocks for b in row], *gains, in_vmem(gate_weight), in_vmem(up_weight), *before, *rest)


def down_kernel(slots, at, column_blocks, cores, places, active, row_weight, down, *refs):
    row_blocks = len(slots)
    outs = refs[-row_blocks * cores :]
    width = down.shape[2] // column_blocks
    height = outs[0].shape[0] * cores // column_blocks
    mine = slice(at * row_blocks * height, (at + 1) * row_blocks * height)
    order = [b * cores + c for c in reversed(range(cores)) for b in range(column_blocks // cores)]
    tile = 256 if width % 256 == 0 else 128
    weights = []
    for s in range(row_blocks):
        first = pl.multiple_of(places[column_blocks + slots[s]] * height, height)
        weights.append(row_weight[pl.ds(first, height), :])
    for k in order:
        b, c = k // cores, k % cores
        start = pl.multiple_of(places[k] * width, 128)
        for j in range(width // tile):
            cut = slice(j * tile, (j + 1) * tile)
            product = jnp.dot(
                active[mine, :], down[0, :, pl.ds(start + j * tile, tile)], preferred_element_type=jnp.float32
            )
            for s in range(row_blocks):
                part = product[s * height : (s + 1) * height, :] * weights[s]
                outs[s * cores + c][b * height : (b + 1) * height, cut] = part.astype(jnp.bfloat16)


def project_down(places, active, row_weight, down_weight, slots, at, height, column_blocks, cores, after):
    row_blocks = len(slots)
    rows = row_blocks * height
    width = down_weight.shape[2] // column_blocks
    whole = pl.BlockSpec(memory_space=pltpu.VMEM)
    out = jax.ShapeDtypeStruct((height * (column_blocks // cores), width), jnp.bfloat16)
    outs = pl.pallas_call(
        functools.partial(down_kernel, slots, at, column_blocks, cores),
        out_shape=[out] * (row_blocks * cores),
        in_specs=[pl.BlockSpec(memory_space=pltpu.SMEM)]
        + [whole] * 3
        + [pl.BlockSpec(memory_space=pl.ANY)] * len(after),
        out_specs=[whole] * (row_blocks * cores),
        cost_estimate=pl.CostEstimate(
            flops=2 * rows * down_weight.size, bytes_accessed=2 * down_weight.size, transcendentals=0
        ),
        compiler_params=pltpu.CompilerParams(vmem_limit_bytes=4 * MIB),
        name="down",
    )(places, active, row_weight, in_vmem(down_weight), *after)
    return [outs[s * cores : (s + 1) * cores] for s in range(row_blocks)]


def add_kernel(groups, *refs):
    used = sum(len(g) for g in groups)
    outs = refs[-len(groups) :]
    at = 0
    for group, out in zip(groups, outs):
        total = None
        for first in group:
            value = refs[at][first : first + out.shape[0], :].astype(jnp.float32)
            total = value if total is None else total + value
            at += 1
        out[...] = total.astype(out.dtype)


def add(groups, height, after=(), kind=jnp.bfloat16):
    values = [value for group in groups for value, _ in group]
    width = values[0].shape[1]
    whole = pl.BlockSpec(memory_space=pltpu.VMEM)
    return pl.pallas_call(
        functools.partial(add_kernel, [[first for _, first in group] for group in groups]),
        out_shape=[jax.ShapeDtypeStruct((height, width), kind)] * len(groups),
        in_specs=[whole] * len(values) + [pl.BlockSpec(memory_space=pl.ANY)] * len(after),
        out_specs=[whole] * len(groups),
        compiler_params=pltpu.CompilerParams(vmem_limit_bytes=8 * MIB),
        name="add",
    )(*values, *after)


def shards(
    query_latent,
    query_rope,
    cache_latent,
    cache_rope,
    cache_length,
    value_up,
    output_weight,
    residual,
    norm_gain,
    routed_experts,
    expert_gates,
    gate_weight,
    up_weight,
    down_weight,
):
    ep_count = lax.axis_size("ep")
    tp_count = lax.axis_size("tp")
    ep_index = lax.axis_index("ep")
    tp_index = lax.axis_index("tp")
    row_total = routed_experts.shape[0]
    block_rows = row_total // tp_count
    cores = 2
    chips = ep_count // cores

    def from_core(value):
        return lax.ppermute(value, "ep", [(i, i ^ 1) for i in range(ep_count)])

    def from_chip(value, back):
        step = cores * back
        return lax.ppermute(value, "ep", [(i, (i + step) % ep_count) for i in range(ep_count)])

    def from_tp(value, bits):
        return lax.ppermute(value, "tp", [(i, i ^ bits) for i in range(tp_count)])

    def gather_ep(value, after=()):
        same = [value] + [from_chip(value, b) for b in range(1, chips)]
        if after:
            same[1:] = [add([[(v, 0)]], v.shape[0], after)[0] for v in same[1:]]
        other = [from_core(v) for v in same]
        return [v for pair in zip(same, other) for v in pair]

    chip, core = ep_index // cores, ep_index % cores
    ep_places = [
        (chip - b + chips) % chips * cores + (core if c == 0 else 1 - core)
        for b in range(chips)
        for c in range(cores)
    ]
    tp_places = [tp_index ^ k for k in range(tp_count)]
    places = jnp.stack(ep_places + tp_places).astype(jnp.int32)

    gain = norm_gain.reshape(1, -1)
    gains = gather_ep(gain)
    own_residual = lax.dynamic_slice_in_dim(residual, tp_index * block_rows, block_rows, 0)
    row_weight = jnp.sum(jnp.where(routed_experts == ep_index, expert_gates, 0.0), axis=-1, keepdims=True)

    head_out = attend(query_latent, query_rope, cache_latent, cache_rope, cache_length, value_up, [places])
    output_weight = fetch(output_weight, [head_out, row_weight, own_residual, gain])
    partial = project(places, gather_ep(head_out, [output_weight]), output_weight, tp_count)

    gate_weight = fetch(gate_weight, [partial[0]])
    terms = [[(value, 0)] for value in partial]
    for k in reversed(range(1, tp_count)):
        total = terms[k][0][0]
        if len(terms[k]) > 1 or k == 1:
            (total,) = add([terms[k]], block_rows, [gate_weight] if k == 1 else [])
        low = k & -k
        arrived = from_tp(total, low)
        terms[k ^ low].append((arrived, 0))
    stream_terms = terms[0] + [(own_residual, 0)]
    stream, stream_out = add([stream_terms, stream_terms], block_rows, gains + [gate_weight])
    up_weight = fetch(up_weight, [stream])

    rows_of = {0: stream}
    crossed = [from_chip(stream, b) for b in range(1, chips)]
    for k in range(1, tp_count):
        low = k & -k
        source = rows_of[k ^ low]
        if k == tp_count - 1:
            (source,) = add([[(source, 0)]], block_rows, crossed + [up_weight])
        rows_of[k] = from_tp(source, low)
    slots = list(reversed(range(tp_count)))
    near = {k: [rows_of[k], from_core(rows_of[k])] for k in slots}
    *sums, down_weight = activate(
        places, [near[k] for k in slots], gains[:cores], gate_weight, up_weight, 0, [], down_weight
    )
    far = {}
    for k in [0] + slots[:-1]:
        far[k] = []
        for b in range(1, chips):
            if k == 0:
                value = crossed[b - 1]
            elif k == 1:
                (source,) = add([[(crossed[b - 1], 0)]], block_rows, [rows_of[tp_count - 1]])
                value = from_tp(source, 1)
            else:
                value = from_chip(rows_of[k], b)
            (later,) = add([[(value, 0)]], block_rows, sums[-1:]) if k == tp_count - 1 else (value,)
            far[k] += [value, from_core(later)]
    active = activate(places, [far[k] for k in slots], gains[cores:], gate_weight, up_weight, cores, sums)

    def send_back(k, after):
        total = list(add([terms[k]], block_rows, after))
        low = k & -k
        terms[k ^ low].append((from_tp(total[0], low), 0))
        return total

    terms = [[] for _ in range(tp_count)]
    arrivals, sent = [], []
    outs = project_down(places, active, row_weight, down_weight, slots, 0, block_rows, ep_count, cores, [])
    swapped = [from_core(out[1]) for out in outs]
    def core_sums(k, after):
        at = slots.index(k)
        rows = [[(outs[at][0], c * block_rows), (swapped[at], c * block_rows)] for c in range(chips)]
        return rows, after

    def cross(k, extra, after):
        rows, after = core_sums(k, after)
        added = add([row + more for row, more in zip(rows, extra)], block_rows, after)
        across = [from_chip(added[c], chips - c) for c in range(1, chips)]
        arrivals.append(across)
        terms[k] += [(value, 0) for value in [added[0]] + across]

    none = [[] for _ in range(chips)]
    for k in slots[:-2]:
        cross(k, none, arrivals[-2] if len(arrivals) > 1 else [])
    rows, _ = core_sums(1, [])
    added = add(rows, block_rows)
    joined = [[]] + [[(from_tp(added[c], 1), 0)] for c in range(1, chips)]
    early = [value for more in joined for value, _ in more]
    sent = send_back(slots[0], early)
    cross(0, joined, sent)
    for k in slots[1:-2]:
        send_back(k, [])
    terms[1].insert(0, (added[0], 0))
    (kept,) = add([terms[1]], block_rows) if len(terms[1]) > 1 else (added[0],)
    (most,) = add([terms[0]], block_rows, (), jnp.float32)
    (mixed,) = add([[(most, 0), (from_tp(kept, 1), 0)]], block_rows)
    return (stream_out, mixed)


def solution(mesh):
    return jax.shard_map(
        shards,
        mesh=mesh,
        in_specs=(
            P(("parts", "ep"), "tp", None),
            P(("parts", "ep"), "tp"),
            P(("parts", "ep"), None, None),
            P(("parts", "ep"), None, None),
            P(("parts", "ep")),
            P("tp", None, None),
            P("tp", "ep"),
            P("parts", "ep"),
            P("ep"),
            P("parts", None),
            P("parts", None),
            P("ep", None, "tp"),
            P("ep", None, "tp"),
            P("ep", "tp", None),
        ),
        out_specs=(P(("parts", "tp"), "ep"), P(("parts", "tp"), "ep")),
        check_vma=False,
    )
```

```python
import functools

import jax
import jax.numpy as jnp
from jax import lax
from jax.experimental import pallas as pl
from jax.experimental.pallas import tpu as pltpu
from jax.sharding import PartitionSpec as P

score_scale = 1.0 / 192.0**0.5
norm_epsilon = 1e-06
MIB = 1 << 20


def in_hbm(value):
    return pltpu.with_memory_space_constraint(value, pltpu.HBM)


def in_vmem(value):
    return pltpu.with_memory_space_constraint(value, pltpu.VMEM)


def fetch_kernel(parts, *refs):
    source, target, sems = refs[0], refs[-2], refs[-1]
    step = source.shape[-2] // parts
    copies = []
    for i in range(parts):
        cut = (slice(None),) * (len(source.shape) - 2) + (pl.ds(i * step, step),)
        copies.append(pltpu.make_async_copy(source.at[cut], target.at[cut], sems.at[i]))
    for copy in copies:
        copy.start()
    for copy in copies:
        copy.wait()


def fetch(value, after):
    parts = 4
    return pl.pallas_call(
        functools.partial(fetch_kernel, parts),
        out_shape=pltpu.VMEM(value.shape, value.dtype),
        in_specs=[pl.BlockSpec(memory_space=pl.ANY)] * (1 + len(after)),
        out_specs=pl.BlockSpec(memory_space=pltpu.VMEM),
        scratch_shapes=[pltpu.SemaphoreType.DMA((parts,))],
        cost_estimate=pl.CostEstimate(flops=0, bytes_accessed=4 * value.size, transcendentals=0),
        compiler_params=pltpu.CompilerParams(vmem_limit_bytes=1 * MIB),
        name="fetch",
    )(in_hbm(value), *after)


def attention_kernel(step_rows, pieces, ahead, lengths, q_ref, qr_ref, k_hbm, kr_hbm, up_hbm, *refs):
    out_ref, latent, rope, k_ref, kr_ref, up_ref, sems, up_sem = refs[-8:]
    step = pl.program_id(0)
    steps = k_ref.shape[0] // step_rows
    heads, positions = q_ref.shape[1], k_ref.shape[1]
    rope_width = kr_ref.shape[1]

    def copies(at):
        whole = pl.ds(at * step_rows, step_rows)
        made = [pltpu.make_async_copy(kr_hbm.at[whole], kr_ref.at[whole], sems.at[at, pieces])]
        for i in range(pieces):
            part = pl.ds(at * step_rows + i * (step_rows // pieces), step_rows // pieces)
            made.append(pltpu.make_async_copy(k_hbm.at[part], k_ref.at[part], sems.at[at, i]))
        return made

    @pl.when(step == 0)
    def _():
        for at in range(min(ahead, steps)):
            for copy in copies(at):
                copy.start()
        pltpu.make_async_copy(up_hbm, up_ref, up_sem).start()
        all_rows = qr_ref.shape[0]
        width = heads * rope_width
        lane = lax.broadcasted_iota(jnp.int32, (heads, width), 1)
        head = lax.broadcasted_iota(jnp.int32, (heads, width), 0)
        own = jnp.where(lane // rope_width == head, 1.0, 0.0)
        spread = qr_ref[...].astype(jnp.float32)[:, None, :] * own[None, :, :]
        spread = spread.reshape(all_rows * heads, width).astype(jnp.bfloat16)
        lane = lax.broadcasted_iota(jnp.int32, (width, rope_width), 0)
        column = lax.broadcasted_iota(jnp.int32, (width, rope_width), 1)
        fold = jnp.where(lane % rope_width == column, 1.0, 0.0).astype(jnp.bfloat16)
        rope[...] = jnp.dot(spread, fold, preferred_element_type=jnp.float32)

    @pl.when(step + ahead < steps)
    def _():
        for copy in copies(step + ahead):
            copy.start()

    for copy in copies(step):
        copy.wait()
    place = lax.broadcasted_iota(jnp.int32, (heads, positions), 1)
    lanes = latent.shape[2]
    lanes = latent.shape[2]
    scores = []
    for r in range(step_rows):
        first = pl.multiple_of((step * step_rows + r) * heads, heads)
        score = lax.dot_general(
            q_ref[r], k_ref[step * step_rows + r], (((1,), (1,)), ((), ())), preferred_element_type=jnp.float32
        )
        score += jnp.dot(
            rope[pl.ds(first, heads), :].astype(jnp.bfloat16), kr_ref[step * step_rows + r], preferred_element_type=jnp.float32
        )
        scores.append(score)
    probabilities = []
    for r in range(step_rows):
        visible = place < lengths[step * step_rows + r]
        score = jnp.where(visible, scores[r] * score_scale, -jnp.inf)
        weight = jnp.exp(score - jnp.max(score, axis=-1, keepdims=True))
        total = jnp.sum(weight, axis=-1, keepdims=True)
        probabilities.append((weight / total).astype(jnp.bfloat16))
    for r in range(step_rows):
        first = pl.multiple_of((step * step_rows + r) * heads, heads)
        mixed = jnp.dot(probabilities[r], k_ref[step * step_rows + r], preferred_element_type=jnp.float32)
        for c in range(latent.shape[0]):
            latent[c, pl.ds(first, heads), :] = mixed[:, c * lanes : (c + 1) * lanes]

    @pl.when(step == pl.num_programs(0) - 1)
    def _():
        pltpu.make_async_copy(up_hbm, up_ref, up_sem).wait()
        rows = out_ref.shape[0]
        width = up_ref.shape[2]
        for h in range(heads):
            parts = [latent[c, pl.ds(h, rows, stride=heads), :] for c in range(latent.shape[0])]
            part = jnp.concatenate(parts, axis=1).astype(jnp.bfloat16)
            out_ref[:, h * width : (h + 1) * width] = jnp.dot(
                part, up_ref[h], preferred_element_type=jnp.float32
            ).astype(jnp.bfloat16)


def attend(query_latent, query_rope, cache_latent, cache_rope, cache_length, value_up, after):
    rows, heads, latent_width = query_latent.shape
    rope_width = cache_rope.shape[1]
    value_width = value_up.shape[2]
    step_rows, pieces, ahead = 8, 1, 3
    by_row = lambda i, lengths: (i, 0, 0)
    return pl.pallas_call(
        functools.partial(attention_kernel, step_rows, pieces, ahead),
        out_shape=jax.ShapeDtypeStruct((rows, heads * value_width), jnp.bfloat16),
        grid_spec=pltpu.PrefetchScalarGridSpec(
            num_scalar_prefetch=1,
            grid=(rows // step_rows,),
            in_specs=[
                pl.BlockSpec((step_rows, heads, latent_width), by_row),
                pl.BlockSpec(query_rope.shape, lambda i, lengths: (0, 0)),
                pl.BlockSpec(memory_space=pl.ANY),
                pl.BlockSpec(memory_space=pl.ANY),
                pl.BlockSpec(memory_space=pl.ANY),
            ]
            + [pl.BlockSpec(memory_space=pl.ANY)] * len(after),
            out_specs=pl.BlockSpec((rows, heads * value_width), lambda i, lengths: (0, 0)),
            scratch_shapes=[
                pltpu.VMEM((latent_width // 128, rows * heads, 128), jnp.float32),
                pltpu.VMEM((rows * heads, rope_width), jnp.float32),
                pltpu.VMEM(cache_latent.shape, jnp.bfloat16),
                pltpu.VMEM(cache_rope.shape, jnp.bfloat16),
                pltpu.VMEM(value_up.shape, jnp.bfloat16),
                pltpu.SemaphoreType.DMA((rows // step_rows, pieces + 1)),
                pltpu.SemaphoreType.DMA,
            ],
        ),
        cost_estimate=pl.CostEstimate(
            flops=64 * heads * cache_latent.size, bytes_accessed=2 * cache_latent.size, transcendentals=0
        ),
        compiler_params=pltpu.CompilerParams(vmem_limit_bytes=28 * MIB),
        name="attention",
    )(
        in_hbm(cache_length),
        in_hbm(query_latent),
        in_hbm(query_rope),
        in_hbm(cache_latent),
        in_hbm(cache_rope),
        in_hbm(value_up),
        *after,
    )


def projection_kernel(count, out_count, places, *refs):
    blocks, weight, outs = refs[:count], refs[count], refs[-2 - out_count : -2]
    gathered, result = refs[-2:]
    height = blocks[0].shape[0]
    for k in range(count):
        first = pl.multiple_of(places[k] * height, height)
        gathered[pl.ds(first, height), :] = blocks[k][...]
    columns = weight.shape[1]
    tile = 256 if columns % 256 == 0 else 128
    for j in range(columns // tile):
        result[:, j * tile : (j + 1) * tile] = jnp.dot(
            gathered[...], weight[:, j * tile : (j + 1) * tile], preferred_element_type=jnp.float32
        ).astype(jnp.bfloat16)
    out_height = outs[0].shape[0]
    for s in range(len(outs)):
        first = pl.multiple_of(places[count + s] * out_height, out_height)
        outs[s][...] = result[pl.ds(first, out_height), :]


def project(places, blocks, weight, out_count):
    count = len(blocks)
    height, depth = blocks[0].shape
    rows, columns = height * count, weight.shape[1]
    whole = pl.BlockSpec(memory_space=pltpu.VMEM)
    return pl.pallas_call(
        functools.partial(projection_kernel, count, out_count),
        out_shape=[jax.ShapeDtypeStruct((rows // out_count, columns), jnp.bfloat16)] * out_count,
        in_specs=[pl.BlockSpec(memory_space=pltpu.SMEM)] + [whole] * (count + 1),
        out_specs=[whole] * out_count,
        scratch_shapes=[
            pltpu.VMEM((rows, depth), jnp.bfloat16),
            pltpu.VMEM((rows, columns), jnp.bfloat16),
        ],
        cost_estimate=pl.CostEstimate(flops=2 * rows * depth * columns, bytes_accessed=4 * MIB, transcendentals=0),
        compiler_params=pltpu.CompilerParams(vmem_limit_bytes=8 * MIB),
        name="projection",
    )(places, *blocks, in_vmem(weight))


def gate_kernel(row_blocks, cores, first, count, model_width, places, *refs):
    blocks, gains = refs[: row_blocks * count], refs[row_blocks * count : (row_blocks + 1) * count]
    refs = refs[(row_blocks + 1) * count :]
    gate, up, refs = refs[0], refs[1], refs[2:]
    if first:
        before, (active, x) = refs[:3], refs[-2:]
        gate_sum, up_sum, squares = before
    else:
        gate_sum, up_sum, squares, x = refs[-4:]
    height, width = blocks[0].shape
    hidden = gate.shape[2]
    tile = min(256, hidden)
    sums = [[None] * (hidden // tile), [None] * (hidden // tile)]
    totals = [squares[s * height : (s + 1) * height, :] if first else 0.0 for s in range(row_blocks)]
    for k in range(count):
        for s in range(row_blocks):
            wide = blocks[s * count + k][...].astype(jnp.float32)
            totals[s] += jnp.sum(wide * wide, axis=-1, keepdims=True)
            x[s * height : (s + 1) * height, k * width : (k + 1) * width] = (wide * gains[k][...]).astype(jnp.bfloat16)
    for w, (weight, start) in enumerate(((gate, gate_sum), (up, up_sum))):
        for j in range(hidden // tile):
            cut = slice(j * tile, (j + 1) * tile)
            total = start[:, cut] if first else None
            for k in range(count):
                depth = pl.ds(pl.multiple_of(places[first + k] * width, 128), width)
                product = jnp.dot(
                    x[:, k * width : (k + 1) * width], weight[0, depth, cut], preferred_element_type=jnp.float32
                )
                total = product if total is None else total + product
            sums[w][j] = total
            if not first:
                start[:, cut] = total
    if not first:
        for s in range(row_blocks):
            squares[s * height : (s + 1) * height, :] = totals[s]
        return
    scale = jnp.concatenate([lax.rsqrt(t / model_width + norm_epsilon) for t in totals], axis=0)
    for j in range(hidden // tile):
        gate_part = sums[0][j] * scale
        up_part = sums[1][j] * scale
        active[:, j * tile : (j + 1) * tile] = (gate_part / (1.0 + jnp.exp(-gate_part)) * up_part).astype(jnp.bfloat16)


def activate(places, blocks, gains, gate_weight, up_weight, cores, first, before, after):
    row_blocks, count = len(blocks), len(blocks[0])
    height, width = blocks[0][0].shape
    rows = row_blocks * height
    model_width, hidden = gate_weight.shape[1:]
    whole = pl.BlockSpec(memory_space=pltpu.VMEM)
    if first:
        kinds = jax.ShapeDtypeStruct((rows, hidden), jnp.bfloat16)
    else:
        kinds = [jax.ShapeDtypeStruct((rows, n), jnp.float32) for n in (hidden, hidden, 1)]
    return pl.pallas_call(
        functools.partial(gate_kernel, row_blocks, cores, first, count, model_width),
        out_shape=kinds,
        in_specs=[pl.BlockSpec(memory_space=pltpu.SMEM)] + [whole] * ((row_blocks + 1) * count + 2 + len(before))
        + [pl.BlockSpec(memory_space=pl.ANY)] * len(after),
        out_specs=whole if first else [whole] * 3,
        scratch_shapes=[pltpu.VMEM((rows, count * width), jnp.bfloat16)],
        cost_estimate=pl.CostEstimate(
            flops=4 * rows * hidden * count * width, bytes_accessed=4 * hidden * count * width, transcendentals=0
        ),
        compiler_params=pltpu.CompilerParams(vmem_limit_bytes=2 * rows * (count * width + 8 * hidden) + 12 * MIB),
        name="activate",
    )(places, *[b for row in blocks for b in row], *gains, in_vmem(gate_weight), in_vmem(up_weight), *before, *after)


def down_kernel(slots, at, column_blocks, cores, places, active, row_weight, down, *refs):
    row_blocks = len(slots)
    outs = refs[-row_blocks * cores :]
    width = down.shape[2] // column_blocks
    height = outs[0].shape[0] * cores // column_blocks
    mine = slice(at * row_blocks * height, (at + 1) * row_blocks * height)
    order = [b * cores + c for c in reversed(range(cores)) for b in range(column_blocks // cores)]
    tile = 256 if width % 256 == 0 else 128
    weights = []
    for s in range(row_blocks):
        first = pl.multiple_of(places[column_blocks + slots[s]] * height, height)
        weights.append(row_weight[pl.ds(first, height), :])
    for k in order:
        b, c = k // cores, k % cores
        start = pl.multiple_of(places[k] * width, 128)
        for j in range(width // tile):
            cut = slice(j * tile, (j + 1) * tile)
            product = jnp.dot(
                active[mine, :], down[0, :, pl.ds(start + j * tile, tile)], preferred_element_type=jnp.float32
            )
            for s in range(row_blocks):
                part = product[s * height : (s + 1) * height, :] * weights[s]
                outs[s * cores + c][b * height : (b + 1) * height, cut] = part.astype(jnp.bfloat16)


def project_down(places, active, row_weight, down_weight, slots, at, height, column_blocks, cores, after):
    row_blocks = len(slots)
    rows = row_blocks * height
    width = down_weight.shape[2] // column_blocks
    whole = pl.BlockSpec(memory_space=pltpu.VMEM)
    out = jax.ShapeDtypeStruct((height * (column_blocks // cores), width), jnp.bfloat16)
    outs = pl.pallas_call(
        functools.partial(down_kernel, slots, at, column_blocks, cores),
        out_shape=[out] * (row_blocks * cores),
        in_specs=[pl.BlockSpec(memory_space=pltpu.SMEM)]
        + [whole] * 3
        + [pl.BlockSpec(memory_space=pl.ANY)] * len(after),
        out_specs=[whole] * (row_blocks * cores),
        cost_estimate=pl.CostEstimate(
            flops=2 * rows * down_weight.size, bytes_accessed=2 * down_weight.size, transcendentals=0
        ),
        compiler_params=pltpu.CompilerParams(vmem_limit_bytes=4 * MIB),
        name="down",
    )(places, active, row_weight, in_vmem(down_weight), *after)
    return [outs[s * cores : (s + 1) * cores] for s in range(row_blocks)]


def add_kernel(groups, *refs):
    used = sum(len(g) for g in groups)
    outs = refs[-len(groups) :]
    at = 0
    for group, out in zip(groups, outs):
        total = None
        for first in group:
            value = refs[at][first : first + out.shape[0], :].astype(jnp.float32)
            total = value if total is None else total + value
            at += 1
        out[...] = total.astype(out.dtype)


def add(groups, height, after=(), kind=jnp.bfloat16):
    values = [value for group in groups for value, _ in group]
    width = values[0].shape[1]
    whole = pl.BlockSpec(memory_space=pltpu.VMEM)
    return pl.pallas_call(
        functools.partial(add_kernel, [[first for _, first in group] for group in groups]),
        out_shape=[jax.ShapeDtypeStruct((height, width), kind)] * len(groups),
        in_specs=[whole] * len(values) + [pl.BlockSpec(memory_space=pl.ANY)] * len(after),
        out_specs=[whole] * len(groups),
        compiler_params=pltpu.CompilerParams(vmem_limit_bytes=8 * MIB),
        name="add",
    )(*values, *after)


def shards(
    query_latent,
    query_rope,
    cache_latent,
    cache_rope,
    cache_length,
    value_up,
    output_weight,
    residual,
    norm_gain,
    routed_experts,
    expert_gates,
    gate_weight,
    up_weight,
    down_weight,
):
    ep_count = lax.axis_size("ep")
    tp_count = lax.axis_size("tp")
    ep_index = lax.axis_index("ep")
    tp_index = lax.axis_index("tp")
    row_total = routed_experts.shape[0]
    block_rows = row_total // tp_count
    cores = 2
    chips = ep_count // cores

    def from_core(value):
        return lax.ppermute(value, "ep", [(i, i ^ 1) for i in range(ep_count)])

    def from_chip(value, back):
        step = cores * back
        return lax.ppermute(value, "ep", [(i, (i + step) % ep_count) for i in range(ep_count)])

    def from_tp(value, bits):
        return lax.ppermute(value, "tp", [(i, i ^ bits) for i in range(tp_count)])

    def gather_ep(value, after=()):
        same = [value] + [from_chip(value, b) for b in range(1, chips)]
        if after:
            same[1:] = [add([[(v, 0)]], v.shape[0], after)[0] for v in same[1:]]
        other = [from_core(v) for v in same]
        return [v for pair in zip(same, other) for v in pair]

    chip, core = ep_index // cores, ep_index % cores
    ep_places = [
        (chip - b + chips) % chips * cores + (core if c == 0 else 1 - core)
        for b in range(chips)
        for c in range(cores)
    ]
    tp_places = [tp_index ^ k for k in range(tp_count)]
    places = jnp.stack(ep_places + tp_places).astype(jnp.int32)

    gain = norm_gain.reshape(1, -1)
    gains = gather_ep(gain)
    own_residual = lax.dynamic_slice_in_dim(residual, tp_index * block_rows, block_rows, 0)
    row_weight = jnp.sum(jnp.where(routed_experts == ep_index, expert_gates, 0.0), axis=-1, keepdims=True)

    head_out = attend(query_latent, query_rope, cache_latent, cache_rope, cache_length, value_up, [places])
    output_weight = fetch(output_weight, [head_out, row_weight, own_residual, gain])
    partial = project(places, gather_ep(head_out, [output_weight]), output_weight, tp_count)

    gate_weight = fetch(gate_weight, [partial[0]])
    terms = [[(value, 0)] for value in partial]
    for k in reversed(range(1, tp_count)):
        total = terms[k][0][0]
        if len(terms[k]) > 1 or k == 1:
            (total,) = add([terms[k]], block_rows, [gate_weight] if k == 1 else [])
        low = k & -k
        arrived = from_tp(total, low)
        terms[k ^ low].append((arrived, 0))
    up_weight = fetch(up_weight, [total])
    stream_terms = terms[0] + [(own_residual, 0)]
    stream, stream_out = add([stream_terms, stream_terms], block_rows, gains + [gate_weight, up_weight])
    down_weight = fetch(down_weight, [stream])

    rows_of = {0: stream}
    crossed = [from_chip(stream, b) for b in range(1, chips)]
    for k in range(1, tp_count):
        low = k & -k
        source = rows_of[k ^ low]
        if k == tp_count - 1:
            (source,) = add([[(source, 0)]], block_rows, crossed + [down_weight])
        rows_of[k] = from_tp(source, low)
    slots = list(reversed(range(tp_count)))
    near = {k: [rows_of[k], from_core(rows_of[k])] for k in slots}
    sums = activate(places, [near[k] for k in slots], gains[:cores], gate_weight, up_weight, cores, 0, [], [down_weight])
    far = {}
    for k in [0] + slots[:-1]:
        far[k] = []
        for b in range(1, chips):
            if k == 0:
                value = crossed[b - 1]
            elif k == 1:
                (source,) = add([[(crossed[b - 1], 0)]], block_rows, [rows_of[tp_count - 1]])
                value = from_tp(source, 1)
            else:
                value = from_chip(rows_of[k], b)
            (later,) = add([[(value, 0)]], block_rows, sums[-1:]) if k == tp_count - 1 else (value,)
            far[k] += [value, from_core(later)]
    active = activate(places, [far[k] for k in slots], gains[cores:], gate_weight, up_weight, cores, cores, sums, [])

    def send_back(k, after):
        total = list(add([terms[k]], block_rows, after))
        low = k & -k
        terms[k ^ low].append((from_tp(total[0], low), 0))
        return total

    terms = [[] for _ in range(tp_count)]
    arrivals, sent = [], []
    outs = project_down(places, active, row_weight, down_weight, slots, 0, block_rows, ep_count, cores, [])
    swapped = [from_core(out[1]) for out in outs]
    def core_sums(k, after):
        at = slots.index(k)
        rows = [[(outs[at][0], c * block_rows), (swapped[at], c * block_rows)] for c in range(chips)]
        return rows, after

    def cross(k, extra, after):
        rows, after = core_sums(k, after)
        added = add([row + more for row, more in zip(rows, extra)], block_rows, after)
        across = [from_chip(added[c], chips - c) for c in range(1, chips)]
        arrivals.append(across)
        terms[k] += [(value, 0) for value in [added[0]] + across]

    none = [[] for _ in range(chips)]
    for k in slots[:-2]:
        cross(k, none, arrivals[-2] if len(arrivals) > 1 else [])
    rows, _ = core_sums(1, [])
    added = add(rows, block_rows)
    joined = [[]] + [[(from_tp(added[c], 1), 0)] for c in range(1, chips)]
    early = [value for more in joined for value, _ in more]
    sent = send_back(slots[0], early)
    cross(0, joined, sent)
    for k in slots[1:-2]:
        send_back(k, [])
    terms[1].insert(0, (added[0], 0))
    (kept,) = add([terms[1]], block_rows) if len(terms[1]) > 1 else (added[0],)
    (most,) = add([terms[0]], block_rows, (), jnp.float32)
    (mixed,) = add([[(most, 0), (from_tp(kept, 1), 0)]], block_rows)
    return (stream_out, mixed)


def solution(mesh):
    return jax.shard_map(
        shards,
        mesh=mesh,
        in_specs=(
            P(("parts", "ep"), "tp", None),
            P(("parts", "ep"), "tp"),
            P(("parts", "ep"), None, None),
            P(("parts", "ep"), None, None),
            P(("parts", "ep")),
            P("tp", None, None),
            P("tp", "ep"),
            P("parts", "ep"),
            P("ep"),
            P("parts", None),
            P("parts", None),
            P("ep", None, "tp"),
            P("ep", None, "tp"),
            P("ep", "tp", None),
        ),
        out_specs=(P(("parts", "tp"), "ep"), P(("parts", "tp"), "ep")),
        check_vma=False,
    )
```

```python
import functools

import jax
import jax.numpy as jnp
from jax import lax
from jax.experimental import pallas as pl
from jax.experimental.pallas import tpu as pltpu
from jax.sharding import PartitionSpec as P

score_scale = 1.0 / 192.0**0.5
norm_epsilon = 1e-06
MIB = 1 << 20


def in_hbm(value):
    return pltpu.with_memory_space_constraint(value, pltpu.HBM)


def in_vmem(value):
    return pltpu.with_memory_space_constraint(value, pltpu.VMEM)


def fetch_kernel(parts, *refs):
    source, target, sems = refs[0], refs[-2], refs[-1]
    step = source.shape[-2] // parts
    copies = []
    for i in range(parts):
        cut = (slice(None),) * (len(source.shape) - 2) + (pl.ds(i * step, step),)
        copies.append(pltpu.make_async_copy(source.at[cut], target.at[cut], sems.at[i]))
    for copy in copies:
        copy.start()
    for copy in copies:
        copy.wait()


def fetch(value, after):
    parts = 4
    return pl.pallas_call(
        functools.partial(fetch_kernel, parts),
        out_shape=pltpu.VMEM(value.shape, value.dtype),
        in_specs=[pl.BlockSpec(memory_space=pl.ANY)] * (1 + len(after)),
        out_specs=pl.BlockSpec(memory_space=pltpu.VMEM),
        scratch_shapes=[pltpu.SemaphoreType.DMA((parts,))],
        cost_estimate=pl.CostEstimate(flops=0, bytes_accessed=4 * value.size, transcendentals=0),
        compiler_params=pltpu.CompilerParams(vmem_limit_bytes=1 * MIB),
        name="fetch",
    )(in_hbm(value), *after)


def attention_kernel(step_rows, pieces, ahead, lengths, q_ref, qr_ref, k_hbm, kr_hbm, up_hbm, *refs):
    out_ref, latent, rope, k_ref, kr_ref, up_ref, sems, up_sem = refs[-8:]
    step = pl.program_id(0)
    steps = k_ref.shape[0] // step_rows
    heads, positions = q_ref.shape[1], k_ref.shape[1]
    rope_width = kr_ref.shape[1]

    def copies(at):
        whole = pl.ds(at * step_rows, step_rows)
        made = [pltpu.make_async_copy(kr_hbm.at[whole], kr_ref.at[whole], sems.at[at, pieces])]
        for i in range(pieces):
            part = pl.ds(at * step_rows + i * (step_rows // pieces), step_rows // pieces)
            made.append(pltpu.make_async_copy(k_hbm.at[part], k_ref.at[part], sems.at[at, i]))
        return made

    @pl.when(step == 0)
    def _():
        for copy in copies(0):
            copy.start()
        all_rows = qr_ref.shape[0]
        width = heads * rope_width
        lane = lax.broadcasted_iota(jnp.int32, (heads, width), 1)
        head = lax.broadcasted_iota(jnp.int32, (heads, width), 0)
        own = jnp.where(lane // rope_width == head, 1.0, 0.0)
        spread = qr_ref[...].astype(jnp.float32)[:, None, :] * own[None, :, :]
        spread = spread.reshape(all_rows * heads, width).astype(jnp.bfloat16)
        lane = lax.broadcasted_iota(jnp.int32, (width, rope_width), 0)
        column = lax.broadcasted_iota(jnp.int32, (width, rope_width), 1)
        fold = jnp.where(lane % rope_width == column, 1.0, 0.0).astype(jnp.bfloat16)
        rope[...] = jnp.dot(spread, fold, preferred_element_type=jnp.float32)

    @pl.when(step == 0)
    def _():
        for at in range(1, min(ahead, steps)):
            for copy in copies(at):
                copy.start()

    for copy in copies(step):
        copy.wait()

    @pl.when(step + ahead < steps)
    def _():
        for copy in copies(step + ahead):
            copy.start()

    @pl.when(step == steps // 2)
    def _():
        pltpu.make_async_copy(up_hbm, up_ref, up_sem).start()

    place = lax.broadcasted_iota(jnp.int32, (heads, positions), 1)
    lanes = latent.shape[2]
    lanes = latent.shape[2]
    scores = []
    for r in range(step_rows):
        first = pl.multiple_of((step * step_rows + r) * heads, heads)
        score = lax.dot_general(
            q_ref[r], k_ref[step * step_rows + r], (((1,), (1,)), ((), ())), preferred_element_type=jnp.float32
        )
        score += jnp.dot(
            rope[pl.ds(first, heads), :].astype(jnp.bfloat16), kr_ref[step * step_rows + r], preferred_element_type=jnp.float32
        )
        scores.append(score)
    probabilities = []
    for r in range(step_rows):
        visible = place < lengths[step * step_rows + r]
        score = jnp.where(visible, scores[r] * score_scale, -jnp.inf)
        weight = jnp.exp(score - jnp.max(score, axis=-1, keepdims=True))
        total = jnp.sum(weight, axis=-1, keepdims=True)
        probabilities.append((weight / total).astype(jnp.bfloat16))
    for r in range(step_rows):
        first = pl.multiple_of((step * step_rows + r) * heads, heads)
        mixed = jnp.dot(probabilities[r], k_ref[step * step_rows + r], preferred_element_type=jnp.float32)
        for c in range(latent.shape[0]):
            latent[c, pl.ds(first, heads), :] = mixed[:, c * lanes : (c + 1) * lanes]

    @pl.when(step == pl.num_programs(0) - 1)
    def _():
        pltpu.make_async_copy(up_hbm, up_ref, up_sem).wait()
        rows = out_ref.shape[0]
        width = up_ref.shape[2]
        for h in range(heads):
            parts = [latent[c, pl.ds(h, rows, stride=heads), :] for c in range(latent.shape[0])]
            part = jnp.concatenate(parts, axis=1).astype(jnp.bfloat16)
            out_ref[:, h * width : (h + 1) * width] = jnp.dot(
                part, up_ref[h], preferred_element_type=jnp.float32
            ).astype(jnp.bfloat16)


def attend(query_latent, query_rope, cache_latent, cache_rope, cache_length, value_up, after):
    rows, heads, latent_width = query_latent.shape
    rope_width = cache_rope.shape[1]
    value_width = value_up.shape[2]
    step_rows, pieces, ahead = 8, 1, 2
    by_row = lambda i, lengths: (i, 0, 0)
    return pl.pallas_call(
        functools.partial(attention_kernel, step_rows, pieces, ahead),
        out_shape=jax.ShapeDtypeStruct((rows, heads * value_width), jnp.bfloat16),
        grid_spec=pltpu.PrefetchScalarGridSpec(
            num_scalar_prefetch=1,
            grid=(rows // step_rows,),
            in_specs=[
                pl.BlockSpec((step_rows, heads, latent_width), by_row),
                pl.BlockSpec(query_rope.shape, lambda i, lengths: (0, 0)),
                pl.BlockSpec(memory_space=pl.ANY),
                pl.BlockSpec(memory_space=pl.ANY),
                pl.BlockSpec(memory_space=pl.ANY),
            ]
            + [pl.BlockSpec(memory_space=pl.ANY)] * len(after),
            out_specs=pl.BlockSpec((rows, heads * value_width), lambda i, lengths: (0, 0)),
            scratch_shapes=[
                pltpu.VMEM((latent_width // 128, rows * heads, 128), jnp.float32),
                pltpu.VMEM((rows * heads, rope_width), jnp.float32),
                pltpu.VMEM(cache_latent.shape, jnp.bfloat16),
                pltpu.VMEM(cache_rope.shape, jnp.bfloat16),
                pltpu.VMEM(value_up.shape, jnp.bfloat16),
                pltpu.SemaphoreType.DMA((rows // step_rows, pieces + 1)),
                pltpu.SemaphoreType.DMA,
            ],
        ),
        cost_estimate=pl.CostEstimate(
            flops=64 * heads * cache_latent.size, bytes_accessed=2 * cache_latent.size, transcendentals=0
        ),
        compiler_params=pltpu.CompilerParams(vmem_limit_bytes=28 * MIB),
        name="attention",
    )(
        in_hbm(cache_length),
        in_hbm(query_latent),
        in_hbm(query_rope),
        in_hbm(cache_latent),
        in_hbm(cache_rope),
        in_hbm(value_up),
        *after,
    )


def projection_kernel(count, out_count, places, *refs):
    blocks, weight, outs = refs[:count], refs[count], refs[-2 - out_count : -2]
    gathered, result = refs[-2:]
    height = blocks[0].shape[0]
    for k in range(count):
        first = pl.multiple_of(places[k] * height, height)
        gathered[pl.ds(first, height), :] = blocks[k][...]
    columns = weight.shape[1]
    tile = 256 if columns % 256 == 0 else 128
    for j in range(columns // tile):
        result[:, j * tile : (j + 1) * tile] = jnp.dot(
            gathered[...], weight[:, j * tile : (j + 1) * tile], preferred_element_type=jnp.float32
        ).astype(jnp.bfloat16)
    out_height = outs[0].shape[0]
    for s in range(len(outs)):
        first = pl.multiple_of(places[count + s] * out_height, out_height)
        outs[s][...] = result[pl.ds(first, out_height), :]


def project(places, blocks, weight, out_count):
    count = len(blocks)
    height, depth = blocks[0].shape
    rows, columns = height * count, weight.shape[1]
    whole = pl.BlockSpec(memory_space=pltpu.VMEM)
    return pl.pallas_call(
        functools.partial(projection_kernel, count, out_count),
        out_shape=[jax.ShapeDtypeStruct((rows // out_count, columns), jnp.bfloat16)] * out_count,
        in_specs=[pl.BlockSpec(memory_space=pltpu.SMEM)] + [whole] * (count + 1),
        out_specs=[whole] * out_count,
        scratch_shapes=[
            pltpu.VMEM((rows, depth), jnp.bfloat16),
            pltpu.VMEM((rows, columns), jnp.bfloat16),
        ],
        cost_estimate=pl.CostEstimate(flops=2 * rows * depth * columns, bytes_accessed=4 * MIB, transcendentals=0),
        compiler_params=pltpu.CompilerParams(vmem_limit_bytes=8 * MIB),
        name="projection",
    )(places, *blocks, in_vmem(weight))


def gate_kernel(row_blocks, cores, first, count, model_width, places, *refs):
    blocks, gains = refs[: row_blocks * count], refs[row_blocks * count : (row_blocks + 1) * count]
    refs = refs[(row_blocks + 1) * count :]
    gate, up, refs = refs[0], refs[1], refs[2:]
    if first:
        before, (active, x) = refs[:3], refs[-2:]
        gate_sum, up_sum, squares = before
    else:
        gate_sum, up_sum, squares, x = refs[-4:]
    height, width = blocks[0].shape
    hidden = gate.shape[2]
    tile = min(256, hidden)
    sums = [[None] * (hidden // tile), [None] * (hidden // tile)]
    totals = [squares[s * height : (s + 1) * height, :] if first else 0.0 for s in range(row_blocks)]
    for k in range(count):
        for s in range(row_blocks):
            wide = blocks[s * count + k][...].astype(jnp.float32)
            totals[s] += jnp.sum(wide * wide, axis=-1, keepdims=True)
            x[s * height : (s + 1) * height, k * width : (k + 1) * width] = (wide * gains[k][...]).astype(jnp.bfloat16)
    for w, (weight, start) in enumerate(((gate, gate_sum), (up, up_sum))):
        for j in range(hidden // tile):
            cut = slice(j * tile, (j + 1) * tile)
            total = start[:, cut] if first else None
            for k in range(count):
                depth = pl.ds(pl.multiple_of(places[first + k] * width, 128), width)
                product = jnp.dot(
                    x[:, k * width : (k + 1) * width], weight[0, depth, cut], preferred_element_type=jnp.float32
                )
                total = product if total is None else total + product
            sums[w][j] = total
            if not first:
                start[:, cut] = total
    if not first:
        for s in range(row_blocks):
            squares[s * height : (s + 1) * height, :] = totals[s]
        return
    scale = jnp.concatenate([lax.rsqrt(t / model_width + norm_epsilon) for t in totals], axis=0)
    for j in range(hidden // tile):
        gate_part = sums[0][j] * scale
        up_part = sums[1][j] * scale
        active[:, j * tile : (j + 1) * tile] = (gate_part / (1.0 + jnp.exp(-gate_part)) * up_part).astype(jnp.bfloat16)


def activate(places, blocks, gains, gate_weight, up_weight, cores, first, before, after):
    row_blocks, count = len(blocks), len(blocks[0])
    height, width = blocks[0][0].shape
    rows = row_blocks * height
    model_width, hidden = gate_weight.shape[1:]
    whole = pl.BlockSpec(memory_space=pltpu.VMEM)
    if first:
        kinds = jax.ShapeDtypeStruct((rows, hidden), jnp.bfloat16)
    else:
        kinds = [jax.ShapeDtypeStruct((rows, n), jnp.float32) for n in (hidden, hidden, 1)]
    return pl.pallas_call(
        functools.partial(gate_kernel, row_blocks, cores, first, count, model_width),
        out_shape=kinds,
        in_specs=[pl.BlockSpec(memory_space=pltpu.SMEM)] + [whole] * ((row_blocks + 1) * count + 2 + len(before))
        + [pl.BlockSpec(memory_space=pl.ANY)] * len(after),
        out_specs=whole if first else [whole] * 3,
        scratch_shapes=[pltpu.VMEM((rows, count * width), jnp.bfloat16)],
        cost_estimate=pl.CostEstimate(
            flops=4 * rows * hidden * count * width, bytes_accessed=4 * hidden * count * width, transcendentals=0
        ),
        compiler_params=pltpu.CompilerParams(vmem_limit_bytes=2 * rows * (count * width + 8 * hidden) + 12 * MIB),
        name="activate",
    )(places, *[b for row in blocks for b in row], *gains, in_vmem(gate_weight), in_vmem(up_weight), *before, *after)


def down_kernel(slots, at, column_blocks, cores, places, active, row_weight, down, *refs):
    row_blocks = len(slots)
    outs = refs[-row_blocks * cores :]
    width = down.shape[2] // column_blocks
    height = outs[0].shape[0] * cores // column_blocks
    mine = slice(at * row_blocks * height, (at + 1) * row_blocks * height)
    order = [b * cores + c for c in reversed(range(cores)) for b in range(column_blocks // cores)]
    tile = 256 if width % 256 == 0 else 128
    weights = []
    for s in range(row_blocks):
        first = pl.multiple_of(places[column_blocks + slots[s]] * height, height)
        weights.append(row_weight[pl.ds(first, height), :])
    for k in order:
        b, c = k // cores, k % cores
        start = pl.multiple_of(places[k] * width, 128)
        for j in range(width // tile):
            cut = slice(j * tile, (j + 1) * tile)
            product = jnp.dot(
                active[mine, :], down[0, :, pl.ds(start + j * tile, tile)], preferred_element_type=jnp.float32
            )
            for s in range(row_blocks):
                part = product[s * height : (s + 1) * height, :] * weights[s]
                outs[s * cores + c][b * height : (b + 1) * height, cut] = part.astype(jnp.bfloat16)


def project_down(places, active, row_weight, down_weight, slots, at, height, column_blocks, cores, after):
    row_blocks = len(slots)
    rows = row_blocks * height
    width = down_weight.shape[2] // column_blocks
    whole = pl.BlockSpec(memory_space=pltpu.VMEM)
    out = jax.ShapeDtypeStruct((height * (column_blocks // cores), width), jnp.bfloat16)
    outs = pl.pallas_call(
        functools.partial(down_kernel, slots, at, column_blocks, cores),
        out_shape=[out] * (row_blocks * cores),
        in_specs=[pl.BlockSpec(memory_space=pltpu.SMEM)]
        + [whole] * 3
        + [pl.BlockSpec(memory_space=pl.ANY)] * len(after),
        out_specs=[whole] * (row_blocks * cores),
        cost_estimate=pl.CostEstimate(
            flops=2 * rows * down_weight.size, bytes_accessed=2 * down_weight.size, transcendentals=0
        ),
        compiler_params=pltpu.CompilerParams(vmem_limit_bytes=4 * MIB),
        name="down",
    )(places, active, row_weight, in_vmem(down_weight), *after)
    return [outs[s * cores : (s + 1) * cores] for s in range(row_blocks)]


def add_kernel(groups, *refs):
    used = sum(len(g) for g in groups)
    outs = refs[-len(groups) :]
    at = 0
    for group, out in zip(groups, outs):
        total = None
        for first in group:
            value = refs[at][first : first + out.shape[0], :].astype(jnp.float32)
            total = value if total is None else total + value
            at += 1
        out[...] = total.astype(out.dtype)


def add(groups, height, after=(), kind=jnp.bfloat16):
    values = [value for group in groups for value, _ in group]
    width = values[0].shape[1]
    whole = pl.BlockSpec(memory_space=pltpu.VMEM)
    return pl.pallas_call(
        functools.partial(add_kernel, [[first for _, first in group] for group in groups]),
        out_shape=[jax.ShapeDtypeStruct((height, width), kind)] * len(groups),
        in_specs=[whole] * len(values) + [pl.BlockSpec(memory_space=pl.ANY)] * len(after),
        out_specs=[whole] * len(groups),
        compiler_params=pltpu.CompilerParams(vmem_limit_bytes=8 * MIB),
        name="add",
    )(*values, *after)


def shards(
    query_latent,
    query_rope,
    cache_latent,
    cache_rope,
    cache_length,
    value_up,
    output_weight,
    residual,
    norm_gain,
    routed_experts,
    expert_gates,
    gate_weight,
    up_weight,
    down_weight,
):
    ep_count = lax.axis_size("ep")
    tp_count = lax.axis_size("tp")
    ep_index = lax.axis_index("ep")
    tp_index = lax.axis_index("tp")
    row_total = routed_experts.shape[0]
    block_rows = row_total // tp_count
    cores = 2
    chips = ep_count // cores

    def from_core(value):
        return lax.ppermute(value, "ep", [(i, i ^ 1) for i in range(ep_count)])

    def from_chip(value, back):
        step = cores * back
        return lax.ppermute(value, "ep", [(i, (i + step) % ep_count) for i in range(ep_count)])

    def from_tp(value, bits):
        return lax.ppermute(value, "tp", [(i, i ^ bits) for i in range(tp_count)])

    def gather_ep(value, after=()):
        same = [value] + [from_chip(value, b) for b in range(1, chips)]
        if after:
            same[1:] = [add([[(v, 0)]], v.shape[0], after)[0] for v in same[1:]]
        other = [from_core(v) for v in same]
        return [v for pair in zip(same, other) for v in pair]

    chip, core = ep_index // cores, ep_index % cores
    ep_places = [
        (chip - b + chips) % chips * cores + (core if c == 0 else 1 - core)
        for b in range(chips)
        for c in range(cores)
    ]
    tp_places = [tp_index ^ k for k in range(tp_count)]
    places = jnp.stack(ep_places + tp_places).astype(jnp.int32)

    gain = norm_gain.reshape(1, -1)
    gains = gather_ep(gain)
    own_residual = lax.dynamic_slice_in_dim(residual, tp_index * block_rows, block_rows, 0)
    row_weight = jnp.sum(jnp.where(routed_experts == ep_index, expert_gates, 0.0), axis=-1, keepdims=True)

    head_out = attend(query_latent, query_rope, cache_latent, cache_rope, cache_length, value_up, [places])
    output_weight = fetch(output_weight, [head_out, row_weight, own_residual, gain])
    partial = project(places, gather_ep(head_out, [output_weight]), output_weight, tp_count)

    gate_weight = fetch(gate_weight, [partial[0]])
    terms = [[(value, 0)] for value in partial]
    for k in reversed(range(1, tp_count)):
        total = terms[k][0][0]
        if len(terms[k]) > 1 or k == 1:
            (total,) = add([terms[k]], block_rows, [gate_weight] if k == 1 else [])
        low = k & -k
        arrived = from_tp(total, low)
        terms[k ^ low].append((arrived, 0))
    stream_terms = terms[0] + [(own_residual, 0)]
    stream, stream_out = add([stream_terms, stream_terms], block_rows, gains + [gate_weight])
    up_weight = fetch(up_weight, [stream])
    down_weight = fetch(down_weight, [stream])

    rows_of = {0: stream}
    crossed = [from_chip(stream, b) for b in range(1, chips)]
    for k in range(1, tp_count):
        low = k & -k
        source = rows_of[k ^ low]
        if k == tp_count - 1:
            (source,) = add([[(source, 0)]], block_rows, crossed + [up_weight])
        rows_of[k] = from_tp(source, low)
    slots = list(reversed(range(tp_count)))
    near = {k: [rows_of[k], from_core(rows_of[k])] for k in slots}
    sums = activate(places, [near[k] for k in slots], gains[:cores], gate_weight, up_weight, cores, 0, [], [down_weight])
    far = {}
    for k in [0] + slots[:-1]:
        far[k] = []
        for b in range(1, chips):
            if k == 0:
                value = crossed[b - 1]
            elif k == 1:
                (source,) = add([[(crossed[b - 1], 0)]], block_rows, [rows_of[tp_count - 1]])
                value = from_tp(source, 1)
            else:
                value = from_chip(rows_of[k], b)
            (later,) = add([[(value, 0)]], block_rows, sums[-1:]) if k == tp_count - 1 else (value,)
            far[k] += [value, from_core(later)]
    active = activate(places, [far[k] for k in slots], gains[cores:], gate_weight, up_weight, cores, cores, sums, [])

    def send_back(k, after):
        total = list(add([terms[k]], block_rows, after))
        low = k & -k
        terms[k ^ low].append((from_tp(total[0], low), 0))
        return total

    terms = [[] for _ in range(tp_count)]
    arrivals, sent = [], []
    outs = project_down(places, active, row_weight, down_weight, slots, 0, block_rows, ep_count, cores, [])
    swapped = [from_core(out[1]) for out in outs]
    def core_sums(k, after):
        at = slots.index(k)
        rows = [[(outs[at][0], c * block_rows), (swapped[at], c * block_rows)] for c in range(chips)]
        return rows, after

    def cross(k, extra, after):
        rows, after = core_sums(k, after)
        added = add([row + more for row, more in zip(rows, extra)], block_rows, after)
        across = [from_chip(added[c], chips - c) for c in range(1, chips)]
        arrivals.append(across)
        terms[k] += [(value, 0) for value in [added[0]] + across]

    none = [[] for _ in range(chips)]
    for k in slots[:-2]:
        cross(k, none, arrivals[-2] if len(arrivals) > 1 else [])
    rows, _ = core_sums(1, [])
    added = add(rows, block_rows)
    joined = [[]] + [[(from_tp(added[c], 1), 0)] for c in range(1, chips)]
    early = [value for more in joined for value, _ in more]
    sent = send_back(slots[0], early)
    cross(0, joined, sent)
    for k in slots[1:-2]:
        send_back(k, [])
    terms[1].insert(0, (added[0], 0))
    (kept,) = add([terms[1]], block_rows) if len(terms[1]) > 1 else (added[0],)
    (most,) = add([terms[0]], block_rows, (), jnp.float32)
    (mixed,) = add([[(most, 0), (from_tp(kept, 1), 0)]], block_rows)
    return (stream_out, mixed)


def solution(mesh):
    return jax.shard_map(
        shards,
        mesh=mesh,
        in_specs=(
            P(("parts", "ep"), "tp", None),
            P(("parts", "ep"), "tp"),
            P(("parts", "ep"), None, None),
            P(("parts", "ep"), None, None),
            P(("parts", "ep")),
            P("tp", None, None),
            P("tp", "ep"),
            P("parts", "ep"),
            P("ep"),
            P("parts", None),
            P("parts", None),
            P("ep", None, "tp"),
            P("ep", None, "tp"),
            P("ep", "tp", None),
        ),
        out_specs=(P(("parts", "tp"), "ep"), P(("parts", "tp"), "ep")),
        check_vma=False,
    )
```
